32 devices in a mesh: seq: 8 (over z, y), mp: 4 (over x, core).
Axes of the slice: x: 2, y: 2, z: 4, core: 2. Of those that a mesh axis runs over, the one named last changes fastest.
Arguments:
- mixed_in: bfloat16 [4096, 2048], P('seq'), may hold values from -6 to 6
- w_query: bfloat16 [2048, 2048], P(None, 'mp'), may hold values from -0.1875 to 0.1875
- w_key: bfloat16 [2048, 2048], P(None, 'mp'), may hold values from -0.1875 to 0.1875
- w_value: bfloat16 [2048, 2048], P(None, 'mp'), may hold values from -0.125 to 0.125
- w_out: bfloat16 [2048, 2048], P('mp'), may hold values from -0.375 to 0.375
- gain_attn: float32 [2048], replicated, may hold values from 0.1 to 1.9
- w_gate: bfloat16 [2048, 8192], P(None, 'mp'), may hold values from -0.125 to 0.125
- w_up: bfloat16 [2048, 8192], P(None, 'mp'), may hold values from -0.125 to 0.125
- w_down: bfloat16 [8192, 2048], P('mp'), may hold values from -0.125 to 0.125
- gain_mlp: float32 [2048], replicated, may hold values from 0.1 to 1.9
- doc_ends: int32 [5], replicated, may hold values from 1 to 4096, as said below
- cotangent: bfloat16 [4096, 2048], P('seq'), may hold values from -6 to 6
Outputs:
- mixed_out: bfloat16 [4096, 2048], P('seq')
- input_grad: bfloat16 [4096, 2048], P('seq')
- grad_query: float32 [2048, 2048], P('seq', 'mp')
- grad_key: float32 [2048, 2048], P('seq', 'mp')
- grad_value: float32 [2048, 2048], P('seq', 'mp')
- grad_out: float32 [2048, 2048], P('mp', 'seq')
- grad_gain_attn: float32 [2048], P('seq')
- grad_gate: float32 [2048, 8192], P('seq', 'mp')
- grad_up: float32 [2048, 8192], P('seq', 'mp')
- grad_down: float32 [8192, 2048], P('mp', 'seq')
- grad_gain_mlp: float32 [2048], P('seq')
The draws below stay inside these ranges and needn't reach their ends.
Inputs may be any that keep to these rules, and one draw needn't show every extreme that they name: `doc_ends`: rising ends of the 5 packed documents; the last is 4096; one document begins within the first 512 tokens and ends within the last 512 tokens; each of the others holds 1 to 128 tokens.
All inputs are finite; a program needn't handle non-finite values.
Results may differ from the reference program's by a relative error of at most 0.017.
Values may be sent and summed in bfloat16 or wider, within the bound.
No kernel may reach another device: no remote copies, remote signals or barrier semaphores. Data moves between devices by JAX's collectives and lax.ppermute only.
A program may use at most 256 MiB of HBM per device.

```python
import math
import jax
import jax.numpy as jnp
from jax import lax

D = 2048
HEADS = 16
HD = 128
FF = 8192
TOK_DEV = 512
TOKENS = 4096


def draw_doc_ends(key, part):
    key = jax.random.fold_in(key, 7)
    place_key, length_key = jax.random.split(key, 2)
    where_long = jax.random.randint(place_key, (), 1, 4).astype(jnp.int32)
    shorts = jax.random.randint(length_key, (4,), 1, TOK_DEV // 4 + 1).astype(jnp.int32)
    slots = jnp.arange(5, dtype=jnp.int32)
    is_long = slots == where_long
    short_slot = jnp.clip(slots - (slots > where_long).astype(jnp.int32), 0, 3).astype(jnp.int32)
    lengths = jnp.where(is_long, 0, shorts[short_slot]).astype(jnp.int32)
    long_length = (TOKENS - jnp.sum(lengths)).astype(jnp.int32)
    lengths = jnp.where(is_long, long_length, lengths).astype(jnp.int32)
    return jnp.cumsum(lengths).astype(jnp.int32)


def spiked(entries, own_key, source, target, blocks, factor):
    owner, partner = [(jnp.arange(entries.shape[axis_at]) // (entries.shape[axis_at] // blocks)).reshape([-1 if axis == axis_at else 1 for axis in range(entries.ndim)]) for axis_at in (source, target)]
    chosen = jax.random.permutation(own_key, blocks)[partner]
    strong = (owner == chosen) | (owner == (partner + blocks // 2) % blocks)
    return jnp.where(strong, factor * entries, entries)


def steps_of(stream_key, shape, cuts, smallest, high):
    loudness = 1.0
    for dim, shards_of in cuts:
        heights = jax.random.uniform(jax.random.fold_in(jax.random.fold_in(stream_key, 6), dim), (shards_of,), jnp.float32, smallest / len(cuts), high / len(cuts))
        loudness = loudness * jnp.repeat(jnp.exp(heights), shape[dim] // shards_of).reshape((-1,) + (1,) * (len(shape) - 1 - dim))
    return loudness


def bell_draw(key, extent, deviation, bound, cuts=(), held_as=jnp.bfloat16):
    drawn = jax.random.normal(key, extent, jnp.float32) * deviation
    if len(cuts) > 0:
        drawn = steps_of(key, extent, cuts, -0.22, 0.18) * drawn
    return jnp.clip(drawn, min=-bound, max=bound).astype(held_as)


def bell_draw_with(own_key, shape, scale, bound, pieces, heavy, held_as=jnp.bfloat16):
    result = scale * jax.random.normal(own_key, shape, jnp.float32)
    if pieces:
        result = result * steps_of(own_key, shape, pieces, -0.22, 0.18)
    return jnp.clip(spiked(result, jax.random.fold_in(own_key, 3), *heavy), -bound, bound).astype(held_as)


def setup_inputs(seed: int = 0) -> dict:
    streams_of = jax.random.split(jax.random.key(seed), 13)
    return {
        "mixed_in": bell_draw_with(streams_of[0], (TOKENS, D), 1.0, 6.0, ((0, 8),), (0, 1, 8, 2.0)),
        "w_query": bell_draw(streams_of[1], (D, HEADS * HD), (D // 2) ** -0.5, 0.1875, ((1, 4),)),
        "w_key": bell_draw(streams_of[2], (D, HEADS * HD), (D // 2) ** -0.5, 0.1875, ((1, 4),)),
        "w_value": bell_draw(streams_of[3], (D, HEADS * HD), D ** -0.5, 0.125, ((1, 4),)),
        "w_out": bell_draw(streams_of[4], (HEADS * HD, D), (HEADS * HD // 8) ** -0.5, 0.375, ((0, 4),)),
        "gain_attn": jnp.clip(1.0 + 0.18 * jax.random.normal(streams_of[5], (D,), jnp.float32), 0.1, 1.9),
        "w_gate": bell_draw(streams_of[6], (D, FF), D ** -0.5, 0.125, ((1, 4),)),
        "w_up": bell_draw(streams_of[7], (D, FF), D ** -0.5, 0.125, ((1, 4),)),
        "w_down": bell_draw(streams_of[8], (FF, D), (FF // 4) ** -0.5, 0.125, ((0, 4),)),
        "gain_mlp": jnp.clip(1.0 + 0.18 * jax.random.normal(streams_of[9], (D,), jnp.float32), 0.1, 1.9),
        "doc_ends": draw_doc_ends(jax.random.fold_in(streams_of[12], 71), 0),
        "cotangent": bell_draw_with(streams_of[11], (TOKENS, D), 1.0, 6.0, ((0, 8),), (0, 1, 8, 2.0)),
    }


EPSILON = 1e-05
THETA = 10000.0
HIGHEST = lax.Precision.HIGHEST

@jax.custom_vjp
def low(v):
    return lax.optimization_barrier(v.astype(jnp.bfloat16)).astype(jnp.float32)

@jax.custom_vjp
def low_back(v):
    return v

def low_keep(v):
    return (low(v), None)

def low_pass(kept, grad):
    return (grad,)

def back_keep(v):
    return (v, None)

def back_low(kept, grad):
    return (low(grad),)
low.defvjp(low_keep, low_pass)
low_back.defvjp(back_keep, back_low)

def doc_segment(token_index, doc_ends):
    return lax.optimization_barrier(jnp.sum((token_index[:, None] >= doc_ends[None, :]).astype(jnp.int32), axis=1))

def doc_info(token_index, doc_ends):
    segment = doc_segment(token_index, doc_ends)
    below = doc_ends[None, :] <= token_index[:, None]
    begin = lax.optimization_barrier(jnp.max(jnp.where(below, doc_ends[None, :], 0), axis=1))
    finish = lax.optimization_barrier(jnp.min(jnp.where(below, jnp.max(doc_ends), doc_ends[None, :]), axis=1))
    length = finish - begin
    return (segment, token_index - begin, -jnp.log(length.astype(jnp.float32)))

def rope_tables(position, head_size):
    middle = head_size // 2
    frequency = THETA ** (-(jnp.arange(middle, dtype=jnp.float32) * 2.0 / head_size))
    angles = position.astype(jnp.float32)[:, None] * frequency[None, :]
    cosine = jnp.concatenate([jnp.cos(angles), jnp.cos(angles)], axis=1)
    sine_table = jnp.concatenate([jnp.sin(angles), jnp.sin(angles)], axis=1)
    return (cosine, sine_table)

def rotate(values, cosine, sine_table):
    middle = values.shape[-1] // 2
    turned = jnp.concatenate([-values[..., middle:], values[..., :middle]], axis=-1)
    return values * cosine[:, None, :] + turned * sine_table[:, None, :]

def normalize(values, gain):
    return values * lax.rsqrt(lax.optimization_barrier(jnp.mean(values * values, axis=-1, keepdims=True)) + EPSILON) * gain

def matmul(left, right):
    return jnp.dot(left, right, precision=HIGHEST)

def forward(mixed, w_query, w_key, w_value, w_out, gain_attn, w_gate, w_up, w_down, gain_mlp, cosine, sine_table, segment, bias):
    factor = 1.0 / math.sqrt(HD)
    normed_attn = low(normalize(mixed, gain_attn))
    query_pre = low_back(matmul(normed_attn, w_query)).reshape(TOKENS, HEADS, HD)
    key_pre = low_back(matmul(normed_attn, w_key)).reshape(TOKENS, HEADS, HD)
    values = low(low_back(matmul(normed_attn, w_value))).reshape(TOKENS, HEADS, HD)
    queries = low(rotate(query_pre, cosine, sine_table))
    keys = low(rotate(key_pre, cosine, sine_table))
    width = math.gcd(TOKENS, 512)
    blocks = TOKENS // width
    token_index = jnp.arange(TOKENS, dtype=jnp.int32)

    def attend_block(start):
        query_block = lax.dynamic_slice_in_dim(queries, start, width, 0)
        query_index = lax.dynamic_slice_in_dim(token_index, start, width, 0)
        query_segment = lax.dynamic_slice_in_dim(segment, start, width, 0)
        query_bias = lax.dynamic_slice_in_dim(bias, start, width, 0)
        scores = jnp.einsum('qhd,khd->hqk', query_block, keys, precision=HIGHEST) * factor + query_bias[None, :, None]
        scores = low_back(scores)
        allowed = ((token_index[None, :] <= query_index[:, None]) & (segment[None, :] == query_segment[:, None])).astype(jnp.float32)
        weights = low(jax.nn.sigmoid(scores) * allowed[None, :, :])
        return jnp.einsum('hqk,khd->qhd', weights, values, precision=HIGHEST)
    attended = lax.map(jax.checkpoint(attend_block), jnp.arange(blocks, dtype=jnp.int32) * width)
    heads_out = low(low_back(attended.reshape(TOKENS, HEADS * HD)))
    residual = mixed + low_back(matmul(heads_out, w_out))
    normed_mlp = low(normalize(residual, gain_mlp))
    gate_pre = low_back(matmul(normed_mlp, w_gate))
    up_pre = low_back(matmul(normed_mlp, w_up))
    hidden = low(jax.nn.silu(gate_pre) * up_pre)
    return residual + low_back(matmul(hidden, w_down))

def reference(mixed_in, w_query, w_key, w_value, w_out, gain_attn, w_gate, w_up, w_down, gain_mlp, doc_ends, cotangent):
    token_index = jnp.arange(TOKENS, dtype=jnp.int32)
    segment, position, bias = doc_info(token_index, doc_ends)
    cosine, sine_table = rope_tables(position, HD)
    floats = [mixed_in, w_query, w_key, w_value, w_out, gain_attn, w_gate, w_up, w_down, gain_mlp]
    floats = [item.astype(jnp.float32) for item in floats]

    def layer(*weights):
        return forward(*weights, cosine, sine_table, segment, bias)
    output, pullback = jax.vjp(layer, *floats)
    grads = pullback(cotangent.astype(jnp.float32))
    return (output.astype(jnp.bfloat16), grads[0].astype(jnp.bfloat16), grads[1], grads[2], grads[3], grads[4], grads[5], grads[6], grads[7], grads[8], grads[9])
```

```python
import functools
import math

import jax
import jax.numpy as jnp
from jax import lax
from jax.experimental import pallas as pl
from jax.experimental.pallas import tpu as pltpu
from jax.sharding import PartitionSpec as P

HD = 128
EPSILON = 1e-05
THETA = 10000.0
FACTOR = 1.0 / math.sqrt(HD)
CLAMP = 80.0
VMEM_LIMIT = 56 * 1024 * 1024
F32 = jnp.float32
BF16 = jnp.bfloat16


def nn(left, right):
    return lax.dot_general(left, right, (((1,), (0,)), ((), ())), preferred_element_type=F32)


def nt(left, right):
    return lax.dot_general(left, right, (((1,), (1,)), ((), ())), preferred_element_type=F32)


def tn(left, right):
    return lax.dot_general(left, right, (((0,), (0,)), ((), ())), preferred_element_type=F32)


def call(body, out_shape, flops, moved, transcendentals=0, **kwargs):
    return pl.pallas_call(
        body,
        out_shape=out_shape,
        compiler_params=pltpu.CompilerParams(vmem_limit_bytes=VMEM_LIMIT),
        cost_estimate=pl.CostEstimate(
            flops=int(flops), bytes_accessed=int(moved), transcendentals=int(transcendentals)
        ),
        **kwargs,
    )


def rotated(values, cosine, signed):
    return values * cosine + pltpu.roll(values, HD // 2, 1) * signed


def unrotated(values, cosine, signed):
    return values * cosine - pltpu.roll(values, HD // 2, 1) * signed


def qkv_body(x_ref, w_ref, cos_ref, sin_ref, q_ref, kv_ref):
    made = nn(x_ref[...], w_ref[...])
    cosine = cos_ref[...]
    signed = sin_ref[...]
    q_ref[...] = rotated(made[:, :HD], cosine, signed).astype(BF16)
    kv_ref[:, :HD] = rotated(made[:, HD : 2 * HD], cosine, signed).astype(BF16)
    kv_ref[:, HD:] = made[:, 2 * HD :].astype(BF16)


def project_qkv(normed, weights, cosine, signed):
    rows, width = normed.shape
    tile = min(rows, 256)
    return call(
        qkv_body,
        (
            jax.ShapeDtypeStruct((rows, HD), BF16),
            jax.ShapeDtypeStruct((rows, 2 * HD), BF16),
        ),
        2 * rows * width * 3 * HD,
        2 * rows * width + 6 * width * HD + 14 * rows * HD,
        grid=(rows // tile,),
        in_specs=[
            pl.BlockSpec((tile, width), lambda i: (i, 0)),
            pl.BlockSpec((width, 3 * HD), lambda i: (0, 0)),
            pl.BlockSpec((tile, HD), lambda i: (i, 0)),
            pl.BlockSpec((tile, HD), lambda i: (i, 0)),
        ],
        out_specs=(
            pl.BlockSpec((tile, HD), lambda i: (i, 0)),
            pl.BlockSpec((tile, 2 * HD), lambda i: (i, 0)),
        ),
        name="project_qkv",
    )(normed, weights, cosine, signed)


def begin_of(index, ends_ref, count):
    begin = jnp.zeros_like(index)
    for e in range(count):
        end = ends_ref[e]
        begin = jnp.where(end <= index, jnp.maximum(begin, end), begin)
    return begin


def finish_of(index, ends_ref, count):
    finish = jnp.zeros_like(index) + ends_ref[count - 1]
    for e in range(count):
        end = ends_ref[e]
        finish = jnp.where(end > index, jnp.minimum(finish, end), finish)
    return finish


def attend_body(nz, ring, count, place_ref, ends_ref, *refs):
    n_kv = nz * ring
    q_refs, refs = refs[:nz], refs[nz:]
    kv_refs, refs = refs[:n_kv], refs[n_kv:]
    o_refs, refs = refs[:nz], refs[nz:]
    q_s, k_s, v_s, o_s, acc = refs
    z, r = place_ref[0], place_ref[1]
    rows = q_s.shape[1]
    for d in range(nz):
        q_s[d] = q_refs[d][...]
    for i in range(n_kv):
        k_s[i] = kv_refs[i][:, :HD]
        v_s[i] = kv_refs[i][:, HD:]

    @pl.loop(0, nz)
    def per_query(d):
        q_block = (z ^ d) * ring + r
        q_start = q_block * rows
        q_index = q_start + lax.broadcasted_iota(jnp.int32, (rows, 1), 0)
        begin = begin_of(q_index, ends_ref, count)
        shift = jnp.log((finish_of(q_index, ends_ref, count) - begin).astype(F32))
        first_begin = begin_of(q_start, ends_ref, count)
        last_begin = begin_of(q_start + (rows - 1), ends_ref, count)
        acc[...] = jnp.zeros_like(acc)

        @pl.loop(0, n_kv)
        def per_key(i):
            k_block = (z ^ (i & (nz - 1))) * ring + (r ^ (i // nz))
            k_start = k_block * rows
            needed = (k_block <= q_block) & (k_start + rows > first_begin)
            full = (k_block < q_block) & (k_start >= last_begin)

            def tile(masked):
                half = rows // 2
                for part in range(2):
                    at = slice(part * half, (part + 1) * half)
                    scores = nt(q_s[d, at], k_s[i])
                    grown = jnp.exp(jnp.minimum(shift[at] - scores * FACTOR, CLAMP))
                    probs = pl.reciprocal(1.0 + grown, approx=True)
                    if masked:
                        k_index = k_start + lax.broadcasted_iota(jnp.int32, (1, rows), 1)
                        allowed = (k_index <= q_index[at]) & (k_index >= begin[at])
                        probs = jnp.where(allowed, probs, 0.0)
                    acc[at] += nn(probs.astype(BF16), v_s[i])

            pl.when(needed & full)(functools.partial(tile, False))
            pl.when(needed & jnp.logical_not(full))(functools.partial(tile, True))

        o_s[d] = acc[...].astype(BF16)

    for d in range(nz):
        o_refs[d][...] = o_s[d]


def whole(memory):
    return pl.BlockSpec(memory_space=memory)


def attend(place, ends, queries, keys_values, nz, ring):
    rows = queries[0].shape[0]
    n_kv = nz * ring
    pairs = nz * n_kv / 2
    return call(
        functools.partial(attend_body, nz, ring, ends.shape[0]),
        tuple(jax.ShapeDtypeStruct((rows, HD), BF16) for _ in range(nz)),
        pairs * 4 * rows * rows * HD * 2,
        2 * (2 * nz + 2 * n_kv) * rows * HD,
        pairs * 2 * rows * rows,
        in_specs=[whole(pltpu.SMEM)] * 2 + [whole(pltpu.VMEM)] * (nz + n_kv),
        out_specs=tuple(whole(pltpu.VMEM) for _ in range(nz)),
        scratch_shapes=[
            pltpu.VMEM((nz, rows, HD), BF16),
            pltpu.VMEM((n_kv, rows, HD), BF16),
            pltpu.VMEM((n_kv, rows, HD), BF16),
            pltpu.VMEM((nz, rows, HD), BF16),
            pltpu.VMEM((rows, HD), F32),
        ],
        name="attend",
    )(place, ends, *queries, *keys_values)


def attend_back_body(nz, ring, n_dr, first_dr, chained, count, place_ref, ends_ref, *refs):
    n_kv = nz * n_dr
    q_refs, refs = refs[:nz], refs[nz:]
    do_refs, refs = refs[:nz], refs[nz:]
    kv_refs, refs = refs[:n_kv], refs[n_kv:]
    if chained:
        before_ref, refs = refs[0], refs[1:]
    dq_ref, refs = refs[0], refs[1:]
    dkv_refs, refs = refs[:n_dr], refs[n_dr:]
    q_s, do_s, k_s, v_s, begin_s, shift_s, dkv_s, dk_acc, dv_acc = refs
    z, r = place_ref[0], place_ref[1]
    rows = q_s.shape[1]
    for d in range(nz):
        q_s[d] = q_refs[d][...]
        do_s[d] = do_refs[d][...]
    for i in range(n_kv):
        k_s[i] = kv_refs[i][:, :HD]
        v_s[i] = kv_refs[i][:, HD:]
    if chained:
        dq_ref[...] = before_ref[...]
    else:
        dq_ref[...] = jnp.zeros_like(dq_ref)

    @pl.loop(0, nz)
    def tables(d):
        q_index = ((z ^ d) * ring + r) * rows + lax.broadcasted_iota(jnp.int32, (1, rows), 1)
        begin = begin_of(q_index, ends_ref, count)
        begin_s[d] = begin
        shift_s[d] = jnp.log((finish_of(q_index, ends_ref, count) - begin).astype(F32))

    @pl.loop(0, n_kv)
    def per_key(i):
        k_block = (z ^ (i & (nz - 1))) * ring + (r ^ (first_dr + i // nz))
        k_start = k_block * rows
        dk_acc[...] = jnp.zeros_like(dk_acc)
        dv_acc[...] = jnp.zeros_like(dv_acc)

        @pl.loop(0, nz)
        def per_query(d):
            q_block = (z ^ d) * ring + r
            q_start = q_block * rows
            first_begin = begin_of(q_start, ends_ref, count)
            last_begin = begin_of(q_start + (rows - 1), ends_ref, count)
            needed = (k_block <= q_block) & (k_start + rows > first_begin)
            full = (k_block < q_block) & (k_start >= last_begin)

            def tile(masked):
                half = rows // 2
                for part in range(2):
                    at = slice(part * half, (part + 1) * half)
                    keys = k_s[i, at]
                    scores = nt(keys, q_s[d])
                    grown = jnp.exp(jnp.minimum(shift_s[d] - scores * FACTOR, CLAMP))
                    probs = pl.reciprocal(1.0 + grown, approx=True)
                    if masked:
                        k_index = (
                            k_start
                            + part * half
                            + lax.broadcasted_iota(jnp.int32, (half, 1), 0)
                        )
                        q_index = q_start + lax.broadcasted_iota(jnp.int32, (1, rows), 1)
                        allowed = (k_index <= q_index) & (k_index >= begin_s[d])
                        probs = jnp.where(allowed, probs, 0.0)
                    weight_grad = nt(v_s[i, at], do_s[d])
                    score_grad = (weight_grad * (probs * probs * grown)).astype(BF16)
                    dv_acc[at] += nn(probs.astype(BF16), do_s[d])
                    dk_acc[at] += nn(score_grad, q_s[d])
                    dq_ref[d] += tn(score_grad, keys)

            pl.when(needed & full)(functools.partial(tile, False))
            pl.when(needed & jnp.logical_not(full))(functools.partial(tile, True))

        dkv_s[i, :, :HD] = (dk_acc[...] * FACTOR).astype(dkv_s.dtype)
        dkv_s[i, :, HD:] = dv_acc[...].astype(dkv_s.dtype)

    for e in range(n_dr):
        for d in range(nz):
            dkv_refs[e][d] = dkv_s[e * nz + d]


def attend_back(place, ends, queries, out_grads, keys_values, before, nz, ring, first_dr, n_dr, kept):
    rows = queries[0].shape[0]
    n_kv = nz * n_dr
    pairs = nz * n_kv / 2
    chained = before is not None
    return call(
        functools.partial(
            attend_back_body, nz, ring, n_dr, first_dr, chained, ends.shape[0]
        ),
        (jax.ShapeDtypeStruct((nz, rows, HD), F32),)
        + tuple(jax.ShapeDtypeStruct((nz, rows, 2 * HD), kept) for _ in range(n_dr)),
        pairs * 10 * rows * rows * HD * 2,
        2 * (2 * nz + 4 * n_kv) * rows * HD,
        pairs * 2 * rows * rows,
        in_specs=[whole(pltpu.SMEM)] * 2 + [whole(pltpu.VMEM)] * (2 * nz + n_kv + chained),
        out_specs=tuple(whole(pltpu.VMEM) for _ in range(1 + n_dr)),
        scratch_shapes=[
            pltpu.VMEM((nz, rows, HD), BF16),
            pltpu.VMEM((nz, rows, HD), BF16),
            pltpu.VMEM((n_kv, rows, HD), BF16),
            pltpu.VMEM((n_kv, rows, HD), BF16),
            pltpu.VMEM((nz, 1, rows), jnp.int32),
            pltpu.VMEM((nz, 1, rows), F32),
            pltpu.VMEM((n_kv, rows, 2 * HD), kept),
            pltpu.VMEM((rows, HD), F32),
            pltpu.VMEM((rows, HD), F32),
        ],
        name="attend_back",
    )(place, ends, *queries, *out_grads, *keys_values, *([before] if chained else []))


def finish_body(nz, dq_ref, dkv_ref, got_ref, cos_ref, sin_ref, *out_refs):
    for d in range(nz):
        cosine = cos_ref[d]
        signed = sin_ref[d]
        total = dkv_ref[d] + got_ref[d].astype(F32)
        out = out_refs[d]
        out[:, :HD] = unrotated(dq_ref[d] * FACTOR, cosine, signed).astype(BF16)
        out[:, HD : 2 * HD] = unrotated(total[:, :HD], cosine, signed).astype(BF16)
        out[:, 2 * HD :] = total[:, HD:].astype(BF16)


def finish_grads(dq, dkv, got, cosine, signed):
    nz, rows, _ = dq.shape
    return call(
        functools.partial(finish_body, nz),
        tuple(jax.ShapeDtypeStruct((rows, 3 * HD), BF16) for _ in range(nz)),
        12 * nz * rows * HD,
        nz * rows * HD * 30,
        in_specs=[whole(pltpu.VMEM)] * 5,
        out_specs=tuple(whole(pltpu.VMEM) for _ in range(nz)),
        name="finish_grads",
    )(dq, dkv, got, cosine, signed)


def feed_body(x_ref, wg_ref, wu_ref, dact_ref, act_ref, dg_ref, du_ref, dx_ref, acc):
    step = pl.program_id(0)
    x = x_ref[...]
    gate = nn(x, wg_ref[...])
    up = nn(x, wu_ref[...])
    dact = dact_ref[...]
    sig = jax.nn.sigmoid(gate)
    silu = gate * sig
    act_ref[...] = (silu * up).astype(BF16)
    dgate = (dact * up * sig * (1.0 + gate * (1.0 - sig))).astype(BF16)
    dup = (dact * silu).astype(BF16)
    dg_ref[...] = dgate
    du_ref[...] = dup
    part = nt(dgate, wg_ref[...]) + nt(dup, wu_ref[...])

    @pl.when(step == 0)
    def _():
        acc[...] = part

    @pl.when(step > 0)
    def _():
        acc[...] += part

    @pl.when(step == pl.num_programs(0) - 1)
    def _():
        dx_ref[...] = acc[...].astype(BF16)


def feed(normed, w_gate, w_up, dact):
    rows, width = normed.shape
    units = w_gate.shape[1]
    tile = 256
    hidden = jax.ShapeDtypeStruct((rows, units), BF16)
    return call(
        feed_body,
        (hidden, hidden, hidden, jax.ShapeDtypeStruct((rows, width), BF16)),
        8 * rows * width * units,
        4 * width * units + 10 * rows * units + 4 * rows * width,
        rows * units,
        grid=(units // tile,),
        in_specs=[
            pl.BlockSpec((rows, width), lambda j: (0, 0)),
            pl.BlockSpec((width, tile), lambda j: (0, j)),
            pl.BlockSpec((width, tile), lambda j: (0, j)),
            pl.BlockSpec((rows, tile), lambda j: (0, j)),
        ],
        out_specs=(
            pl.BlockSpec((rows, tile), lambda j: (0, j)),
            pl.BlockSpec((rows, tile), lambda j: (0, j)),
            pl.BlockSpec((rows, tile), lambda j: (0, j)),
            pl.BlockSpec((rows, width), lambda j: (0, 0)),
        ),
        scratch_shapes=[pltpu.VMEM((rows, width), F32)],
        name="feed",
    )(normed, w_gate, w_up, dact)


def weight_body(n, added, order_ref, *refs):
    xs, refs = refs[:n], refs[n:]
    ys, refs = refs[:n], refs[n:]
    total = tn(xs[0][...], ys[0][...])
    for i in range(1, n):
        total = total + tn(xs[i][...], ys[i][...])
    if added:
        total = total + refs[0][0].astype(F32)
    refs[-1][0] = total.astype(BF16)


def weight_grad(order, group, lefts, rights, width, column, add=None):
    if group % 128 != 0:
        lefts = [
            jnp.concatenate(
                [
                    lax.dynamic_slice_in_dim(left, order[p] * group, group, 1)
                    for p in range(order.shape[0])
                ],
                axis=1,
            )
            for left in lefts
        ]
        wide = lefts[0].shape[1]
        block = math.gcd(256, wide)
        order_in = jnp.arange(wide // block, dtype=jnp.int32)
    else:
        wide = order.shape[0] * group
        block = group
        order_in = order
    steps = wide // block
    n = len(lefts)
    out = jax.ShapeDtypeStruct((steps, block, width), BF16)
    tokens = sum(left.shape[0] for left in lefts)
    in_specs = [
        pl.BlockSpec((left.shape[0], block), lambda p, o: (0, o[p])) for left in lefts
    ] + [pl.BlockSpec((right.shape[0], width), lambda p, o: (0, column)) for right in rights]
    operands = [order_in, *lefts, *rights]
    if add is not None:
        in_specs.append(pl.BlockSpec((1, block, width), lambda p, o: (p, 0, 0)))
        operands.append(add.reshape(out.shape))
    made = call(
        functools.partial(weight_body, n, add is not None),
        out,
        2 * tokens * wide * width,
        2 * (tokens * wide + tokens * width + (1 + (add is not None)) * wide * width),
        grid_spec=pltpu.PrefetchScalarGridSpec(
            num_scalar_prefetch=1,
            grid=(steps,),
            in_specs=in_specs,
            out_specs=pl.BlockSpec((1, block, width), lambda p, o: (p, 0, 0)),
        ),
        name="weight_grad",
    )(*operands)
    return made.reshape(order.shape[0], group, width)


def rope_tables(position):
    middle = HD // 2
    frequency = THETA ** (-(jnp.arange(middle, dtype=F32) * 2.0 / HD))
    angles = position.astype(F32)[..., None] * frequency
    cosine = jnp.cos(angles)
    sine = jnp.sin(angles)
    return (
        jnp.concatenate([cosine, cosine], axis=-1),
        jnp.concatenate([-sine, sine], axis=-1),
    )


def rms_scale(values):
    return lax.rsqrt(jnp.mean(values * values, axis=-1, keepdims=True) + EPSILON)


def norm_back(values, scale, gain, upstream):
    normed = values * scale
    gain_grad = jnp.sum(upstream * normed, axis=0)
    weighted = upstream * gain
    return (
        gain_grad,
        scale * (weighted - normed * jnp.mean(weighted * normed, axis=-1, keepdims=True)),
    )


def in_order(own, other, bit, axis):
    return jnp.where(
        bit == 0,
        jnp.concatenate([own, other], axis=axis),
        jnp.concatenate([other, own], axis=axis),
    )


def untangle(values, index, axis):
    size = values.shape[axis]
    bits = size.bit_length() - 1
    shape = values.shape
    values = values.reshape(shape[:axis] + (2,) * bits + shape[axis + 1 :])
    for b in range(bits):
        at = axis + bits - 1 - b
        values = jnp.where((index >> b) & 1 == 1, jnp.flip(values, at), values)
    return values.reshape(shape)


def layer(
    n_seq,
    n_mp,
    mixed_in,
    w_query,
    w_key,
    w_value,
    w_out,
    gain_attn,
    w_gate,
    w_up,
    w_down,
    gain_mlp,
    doc_ends,
    cotangent,
):
    rows, width = mixed_in.shape
    nz = w_query.shape[1] // HD
    ring = n_seq // nz
    bits = n_seq.bit_length() - 1
    low_bits = ring.bit_length() - 1
    units = w_gate.shape[1]
    half_units = units // 2
    half_rows = rows // 2
    group = width // n_seq
    pair_bit = bits - 2
    pair = 1 << pair_bit

    s = lax.axis_index("seq")
    m = lax.axis_index("mp")
    z, r = s // ring, s % ring
    core = m % 2
    side = m // 2
    low = (s >> pair_bit) & 1

    def seq_swap(v, distance):
        return lax.ppermute(v, "seq", [(i, i ^ distance) for i in range(n_seq)])

    def mp_swap(v, distance):
        return lax.ppermute(v, "mp", [(i, i ^ distance) for i in range(n_mp)])

    sum_bits = list(range(pair_bit)) + [bits - 1]
    places = []
    for p in range(n_seq):
        e = 0
        for at, bit in enumerate(sum_bits + [pair_bit]):
            if (p >> (bits - 1 - at)) & 1:
                e |= 1 << bit
        places.append(e)
    order = s ^ jnp.array(places, dtype=jnp.int32)
    kept_order, sent_order = order[: n_seq // 2], order[n_seq // 2 :]

    place = jnp.stack([z, r]).astype(jnp.int32)
    inputs = mixed_in.astype(F32)
    scale_attn = rms_scale(inputs)
    normed = (inputs * scale_attn * gain_attn).astype(BF16)
    quarter = rows // n_mp
    my_quarter = lax.dynamic_slice_in_dim(normed, m * quarter, quarter, 0)
    normed_z = [normed]
    for d in range(1, nz):
        got = seq_swap(my_quarter, d * ring)
        across = mp_swap(got, 2)
        sides = in_order(got[None], across[None], side, 0)
        cores = mp_swap(sides, 1)
        normed_z.append(
            in_order(sides[:, None], cores[:, None], core, 1).reshape(rows, width)
        )

    w_heads = [
        jnp.concatenate(
            [lax.dynamic_slice_in_dim(w, (z ^ d) * HD, HD, 1) for w in (w_query, w_key, w_value)],
            axis=1,
        )
        for d in range(nz)
    ]
    w_out_heads = jnp.concatenate(
        [lax.dynamic_slice_in_dim(w_out, (z ^ d) * HD, HD, 0) for d in range(nz)], axis=0
    )
    gate_mine = lax.dynamic_slice_in_dim(w_gate, low * half_units, half_units, 1)
    up_mine = lax.dynamic_slice_in_dim(w_up, low * half_units, half_units, 1)
    down_mine = lax.dynamic_slice_in_dim(w_down, low * half_units, half_units, 0)
    gate_both = jnp.concatenate([gate_mine, mp_swap(gate_mine, 1)], axis=1)
    up_both = jnp.concatenate([up_mine, mp_swap(up_mine, 1)], axis=1)
    down_both = jnp.concatenate([down_mine, mp_swap(down_mine, 1)], axis=0)

    cot_half = lax.dynamic_slice_in_dim(cotangent, core * half_rows, half_rows, 0)
    cot = jnp.concatenate([cot_half, seq_swap(cot_half, pair)], axis=0)
    dact = nt(cot, down_both)

    blocks = (z ^ jnp.arange(nz, dtype=jnp.int32)) * ring + r
    token_index = blocks[:, None] * rows + jnp.arange(rows, dtype=jnp.int32)[None, :]
    ends_below = doc_ends[None, None, :] <= token_index[..., None]
    begin = jnp.max(jnp.where(ends_below, doc_ends, 0), axis=-1)
    cosine, signed = rope_tables(token_index - begin)
    queries, near = [], []
    for d in range(nz):
        q_d, kv_d = project_qkv(normed_z[d], w_heads[0], cosine[d], signed[d])
        queries.append(q_d)
        near.append(kv_d)
    keys_values = [near]
    for b in range(low_bits):
        keys_values = keys_values + [[seq_swap(kv, 1 << b) for kv in kvs] for kvs in keys_values]

    flat = [kv for kvs in keys_values for kv in kvs]
    outs = attend(place, doc_ends, queries, flat, nz, ring)
    heads_out = jnp.concatenate(
        [outs[0]] + [seq_swap(outs[d], d * ring) for d in range(1, nz)], axis=1
    )
    mine_at, sib_at = core * half_rows, (1 - core) * half_rows

    def over_mp(rows_of, weights, contract):
        sib = contract(rows_of(sib_at), weights).astype(BF16)
        mine = contract(rows_of(mine_at), weights)
        part = (mine + mp_swap(sib, 1).astype(F32)).astype(BF16)
        return part.astype(F32) + mp_swap(part, 2).astype(F32)

    def slicer(values):
        return lambda at: lax.dynamic_slice_in_dim(values, at, half_rows, 0)

    x_half = slicer(mixed_in)(mine_at).astype(F32)
    residual = x_half + over_mp(slicer(heads_out), w_out_heads, nn)
    scale_mlp = rms_scale(residual)
    normed_half = (residual * scale_mlp * gain_mlp).astype(BF16)
    normed_mlp = jnp.concatenate([normed_half, seq_swap(normed_half, pair)], axis=0)

    act, dgate, dup, dnormed = feed(normed_mlp, gate_both, up_both, dact)

    def over_pair(mine, theirs):
        part = (mine.astype(F32) + seq_swap(theirs, pair).astype(F32)).astype(BF16)
        return part.astype(F32) + mp_swap(part, 2).astype(F32)

    upstream = over_pair(dnormed[:half_rows], dnormed[half_rows:])
    gain_mlp_grad, norm_part = norm_back(residual, scale_mlp, gain_mlp, upstream)
    residual_grad = cot_half.astype(F32) + norm_part
    branch_half = residual_grad.astype(BF16)
    branch = in_order(branch_half, mp_swap(branch_half, 1), core, 0)

    down_theirs = nn(act[half_rows:], down_both).astype(BF16)
    down_mine_out = nn(act[:half_rows], down_both)
    out_half = (residual + over_pair(down_mine_out, down_theirs)).astype(BF16)
    mixed_out = in_order(out_half, mp_swap(out_half, 1), core, 0)

    def halve(kept, sent, first):
        total = kept.astype(F32) + seq_swap(sent, 1 << sum_bits[first]).astype(F32)
        for bit in sum_bits[first + 1 :]:
            n = total.shape[0] // 2
            low_part = total.astype(BF16)
            total = total[:n] + seq_swap(low_part[n:], 1 << bit).astype(F32)
        return total

    def hidden_grad(left, right):
        made = []
        for piece in (sent_order, kept_order):
            sib = weight_grad(piece, group, [left], [right], half_units, 1)
            made.append(
                weight_grad(piece, group, [left], [right], half_units, 0, mp_swap(sib, 1))
            )
        sent, kept = made
        total = halve(kept, sent, 0)
        theirs = seq_swap(total[1].astype(BF16), pair).astype(F32)
        return in_order(total[0], theirs, low, 1)

    down_share = hidden_grad(cot, act).T
    gate_share = hidden_grad(normed_mlp, dgate)
    up_share = hidden_grad(normed_mlp, dup)

    dheads = nt(branch, w_out_heads).astype(BF16)
    out_grads = [dheads[:, :HD]] + [
        seq_swap(dheads[:, d * HD : (d + 1) * HD], d * ring) for d in range(1, nz)
    ]
    far = [kv for kvs in keys_values[1:] for kv in kvs]
    dq_far, *dkv_far = attend_back(
        place, doc_ends, queries, out_grads, far, None, nz, ring, 1, ring - 1, BF16
    )
    dq, dkv = attend_back(
        place, doc_ends, queries, out_grads, near, dq_far, nz, ring, 0, 1, F32
    )
    pieces = [None] + list(dkv_far)
    for b in reversed(range(low_bits)):
        bit = 1 << b
        for e in range(bit):
            got = seq_swap(pieces[e | bit], bit)
            pieces[e] = (
                got
                if pieces[e] is None
                else (pieces[e].astype(F32) + got.astype(F32)).astype(BF16)
            )
    grads = finish_grads(dq, dkv, pieces[0], cosine, signed)

    wide = nz * HD
    heads_placed = untangle(heads_out.reshape(rows, nz, HD), z, 1).reshape(rows, wide)
    out_sent = weight_grad(sent_order, group, [branch], [heads_placed], wide, 0)
    out_kept = weight_grad(kept_order, group, [branch], [heads_placed], wide, 0)
    total = halve(out_kept, out_sent, 0)
    out_total = total[0] + seq_swap(total[1].astype(BF16), pair).astype(F32)
    out_share = out_total.T

    own_grads = jnp.concatenate(
        [grads[0]] + [seq_swap(grads[d], d * ring) for d in range(1, nz)], axis=1
    )
    w_all = jnp.concatenate(w_heads, axis=1)
    attn_upstream = over_mp(slicer(own_grads), w_all, nt)
    scale_half = slicer(scale_attn)(mine_at)
    gain_attn_grad, attn_part = norm_back(x_half, scale_half, gain_attn, attn_upstream)
    grad_half = (residual_grad + attn_part).astype(BF16)
    input_grad = in_order(grad_half, mp_swap(grad_half, 1), core, 0)

    sent = weight_grad(sent_order, group, normed_z, grads, 3 * HD, 0)
    kept = weight_grad(kept_order, group, normed_z, grads, 3 * HD, 0)
    total = kept.astype(F32) + seq_swap(sent, 1 << sum_bits[0]).astype(F32)
    for bit in sum_bits[1:pair_bit]:
        n = total.shape[0] // 2
        total = total[:n] + seq_swap(total[n:].astype(BF16), 1 << bit).astype(F32)
    small = total.astype(BF16)
    heads = jnp.stack(
        [total[0]] + [seq_swap(small[d], d * ring).astype(F32) for d in range(1, nz)], axis=1
    )
    heads = untangle(heads, z, 1).reshape(group, nz, 3, HD)
    shares = [heads[:, :, i].reshape(group, wide) for i in range(3)]

    def gain_share(partial):
        total = partial + mp_swap(partial, 1)
        for bit in range(bits):
            total = total + seq_swap(total, 1 << bit)
        return lax.dynamic_slice_in_dim(total, s * group, group, 0)

    return (
        mixed_out,
        input_grad,
        shares[0],
        shares[1],
        shares[2],
        out_share,
        gain_share(gain_attn_grad),
        gate_share,
        up_share,
        down_share,
        gain_share(gain_mlp_grad),
    )


def solution(mesh):
    placed = (
        P("seq", None),
        P(None, "mp"),
        P(None, "mp"),
        P(None, "mp"),
        P("mp", None),
        P(),
        P(None, "mp"),
        P(None, "mp"),
        P("mp", None),
        P(),
        P(),
        P("seq", None),
    )
    return jax.shard_map(
        functools.partial(layer, mesh.shape["seq"], mesh.shape["mp"]),
        mesh=mesh,
        in_specs=placed,
        out_specs=(
            P("seq", None),
            P("seq", None),
            P("seq", "mp"),
            P("seq", "mp"),
            P("seq", "mp"),
            P("mp", "seq"),
            P("seq"),
            P("seq", "mp"),
            P("seq", "mp"),
            P("mp", "seq"),
            P("seq"),
        ),
        check_vma=False,
    )
```

```python
import functools
import math

import jax
import jax.numpy as jnp
from jax import lax
from jax.experimental import pallas as pl
from jax.experimental.pallas import tpu as pltpu
from jax.sharding import PartitionSpec as P

HD = 128
EPSILON = 1e-05
THETA = 10000.0
FACTOR = 1.0 / math.sqrt(HD)
CLAMP = 80.0
VMEM_LIMIT = 56 * 1024 * 1024
F32 = jnp.float32
BF16 = jnp.bfloat16


def nn(left, right):
    return lax.dot_general(left, right, (((1,), (0,)), ((), ())), preferred_element_type=F32)


def nt(left, right):
    return lax.dot_general(left, right, (((1,), (1,)), ((), ())), preferred_element_type=F32)


def tn(left, right):
    return lax.dot_general(left, right, (((0,), (0,)), ((), ())), preferred_element_type=F32)


def call(body, out_shape, operands, in_specs, flops, moved, transcendentals=0, after=(), prefetch=0, **kwargs):
    n = prefetch + len(in_specs)

    def kernel(*refs):
        body(*refs[:n], *refs[n + len(after) :])

    in_specs = list(in_specs) + [pl.BlockSpec(memory_space=pl.ANY)] * len(after)
    if prefetch:
        kwargs = {
            "name": kwargs.pop("name"),
            "grid_spec": pltpu.PrefetchScalarGridSpec(
                num_scalar_prefetch=prefetch, in_specs=in_specs, **kwargs
            ),
        }
    else:
        kwargs["in_specs"] = in_specs
    return pl.pallas_call(
        kernel,
        out_shape=out_shape,
        compiler_params=pltpu.CompilerParams(vmem_limit_bytes=VMEM_LIMIT),
        cost_estimate=pl.CostEstimate(
            flops=int(flops), bytes_accessed=int(moved), transcendentals=int(transcendentals)
        ),
        **kwargs,
    )(*operands, *after)


def whole(memory):
    return pl.BlockSpec(memory_space=memory)


def rotated(values, cosine, signed):
    return values * cosine + pltpu.roll(values, HD // 2, 1) * signed


def unrotated(values, cosine, signed):
    return values * cosine - pltpu.roll(values, HD // 2, 1) * signed


def qkv_body(n, place_ref, *refs):
    pieces, refs = refs[:n], refs[n:]
    w_ref, cos_ref, sin_ref, q_ref, kv_ref, x_s = refs
    if n == 1:
        x = pieces[0][...]
    else:
        size = pieces[0].shape[0]
        for j in range(n):
            at = pl.multiple_of((place_ref[2] ^ j) * size, size)
            x_s[pl.ds(at, size), :] = pieces[j][...]
        x = x_s[...]
    made = nn(x, w_ref[...])
    cosine = cos_ref[...]
    signed = sin_ref[...]
    q_ref[...] = rotated(made[:, :HD], cosine, signed).astype(BF16)
    kv_ref[:, :HD] = rotated(made[:, HD : 2 * HD], cosine, signed).astype(BF16)
    kv_ref[:, HD:] = made[:, 2 * HD :].astype(BF16)


def project_qkv(place, pieces, weights, cosine, signed):
    n = len(pieces)
    width = pieces[0].shape[1]
    rows = n * pieces[0].shape[0]
    return call(
        functools.partial(qkv_body, n),
        (
            jax.ShapeDtypeStruct((rows, HD), BF16),
            jax.ShapeDtypeStruct((rows, 2 * HD), BF16),
        ),
        [place, *pieces, weights, cosine, signed],
        [whole(pltpu.SMEM)] + [whole(pltpu.VMEM)] * (n + 3),
        2 * rows * width * 3 * HD,
        2 * rows * width + 6 * width * HD + 14 * rows * HD,
        out_specs=(whole(pltpu.VMEM), whole(pltpu.VMEM)),
        scratch_shapes=[pltpu.VMEM((rows, width), BF16)],
        name="project_qkv",
    )


def begin_of(index, ends_ref, count):
    begin = jnp.zeros_like(index)
    for e in range(count):
        end = ends_ref[e]
        begin = jnp.where(end <= index, jnp.maximum(begin, end), begin)
    return begin


def finish_of(index, ends_ref, count):
    finish = jnp.zeros_like(index) + ends_ref[count - 1]
    for e in range(count):
        end = ends_ref[e]
        finish = jnp.where(end > index, jnp.minimum(finish, end), finish)
    return finish


def attend_body(nz, ring, count, place_ref, ends_ref, *refs):
    n_kv = nz * ring
    q_refs, refs = refs[:nz], refs[nz:]
    kv_refs, refs = refs[:n_kv], refs[n_kv:]
    o_refs, refs = refs[:nz], refs[nz:]
    q_s, k_s, v_s, o_s, acc = refs
    z, r = place_ref[0], place_ref[1]
    rows = q_s.shape[1]
    for d in range(nz):
        q_s[d] = q_refs[d][...]
    for i in range(n_kv):
        k_s[i] = kv_refs[i][:, :HD]
        v_s[i] = kv_refs[i][:, HD:]

    @pl.loop(0, nz)
    def per_query(d):
        q_block = (z ^ d) * ring + r
        q_start = q_block * rows
        q_index = q_start + lax.broadcasted_iota(jnp.int32, (rows, 1), 0)
        begin = begin_of(q_index, ends_ref, count)
        shift = jnp.log((finish_of(q_index, ends_ref, count) - begin).astype(F32))
        first_begin = begin_of(q_start, ends_ref, count)
        last_begin = begin_of(q_start + (rows - 1), ends_ref, count)
        acc[...] = jnp.zeros_like(acc)

        @pl.loop(0, n_kv)
        def per_key(i):
            k_block = (z ^ (i & (nz - 1))) * ring + (r ^ (i // nz))
            k_start = k_block * rows
            needed = (k_block <= q_block) & (k_start + rows > first_begin)
            full = (k_block < q_block) & (k_start >= last_begin)

            def tile(masked):
                half = rows // 2
                for part in range(2):
                    at = slice(part * half, (part + 1) * half)
                    scores = nt(q_s[d, at], k_s[i])
                    grown = jnp.exp(jnp.minimum(shift[at] - scores * FACTOR, CLAMP))
                    probs = pl.reciprocal(1.0 + grown, approx=True)
                    if masked:
                        k_index = k_start + lax.broadcasted_iota(jnp.int32, (1, rows), 1)
                        allowed = (k_index <= q_index[at]) & (k_index >= begin[at])
                        probs = jnp.where(allowed, probs, 0.0)
                    acc[at] += nn(probs.astype(BF16), v_s[i])

            pl.when(needed & full)(functools.partial(tile, False))
            pl.when(needed & jnp.logical_not(full))(functools.partial(tile, True))

        o_s[d] = acc[...].astype(BF16)

    for d in range(nz):
        o_refs[d][...] = o_s[d]


def attend(place, ends, queries, keys_values, nz, ring, after=()):
    rows = queries[0].shape[0]
    n_kv = nz * ring
    pairs = nz * n_kv / 2
    return call(
        functools.partial(attend_body, nz, ring, ends.shape[0]),
        tuple(jax.ShapeDtypeStruct((rows, HD), BF16) for _ in range(nz)),
        [place, ends, *queries, *keys_values],
        [whole(pltpu.SMEM)] * 2 + [whole(pltpu.VMEM)] * (nz + n_kv),
        pairs * 4 * rows * rows * HD * 2,
        2 * (2 * nz + 2 * n_kv) * rows * HD,
        pairs * 2 * rows * rows,
        after=after,
        out_specs=tuple(whole(pltpu.VMEM) for _ in range(nz)),
        scratch_shapes=[
            pltpu.VMEM((nz, rows, HD), BF16),
            pltpu.VMEM((n_kv, rows, HD), BF16),
            pltpu.VMEM((n_kv, rows, HD), BF16),
            pltpu.VMEM((nz, rows, HD), BF16),
            pltpu.VMEM((rows, HD), F32),
        ],
        name="attend",
    )


def attend_back_body(nz, ring, n_dr, first_dr, chained, count, place_ref, ends_ref, *refs):
    n_kv = nz * n_dr
    q_refs, refs = refs[:nz], refs[nz:]
    do_refs, refs = refs[:nz], refs[nz:]
    kv_refs, refs = refs[:n_kv], refs[n_kv:]
    if chained:
        before_ref, refs = refs[0], refs[1:]
    dq_ref, refs = refs[0], refs[1:]
    dkv_refs, refs = refs[:n_dr], refs[n_dr:]
    q_s, do_s, k_s, v_s, begin_s, shift_s, dkv_s, dk_acc, dv_acc = refs
    z, r = place_ref[0], place_ref[1]
    rows = q_s.shape[1]
    for d in range(nz):
        q_s[d] = q_refs[d][...]
        do_s[d] = do_refs[d][...]
    for i in range(n_kv):
        k_s[i] = kv_refs[i][:, :HD]
        v_s[i] = kv_refs[i][:, HD:]
    if chained:
        dq_ref[...] = before_ref[...]
    else:
        dq_ref[...] = jnp.zeros_like(dq_ref)

    @pl.loop(0, nz)
    def tables(d):
        q_index = ((z ^ d) * ring + r) * rows + lax.broadcasted_iota(jnp.int32, (1, rows), 1)
        begin = begin_of(q_index, ends_ref, count)
        begin_s[d] = begin
        shift_s[d] = jnp.log((finish_of(q_index, ends_ref, count) - begin).astype(F32))

    @pl.loop(0, n_kv)
    def per_key(i):
        k_block = (z ^ (i & (nz - 1))) * ring + (r ^ (first_dr + i // nz))
        k_start = k_block * rows
        dk_acc[...] = jnp.zeros_like(dk_acc)
        dv_acc[...] = jnp.zeros_like(dv_acc)

        @pl.loop(0, nz)
        def per_query(d):
            q_block = (z ^ d) * ring + r
            q_start = q_block * rows
            first_begin = begin_of(q_start, ends_ref, count)
            last_begin = begin_of(q_start + (rows - 1), ends_ref, count)
            needed = (k_block <= q_block) & (k_start + rows > first_begin)
            full = (k_block < q_block) & (k_start >= last_begin)

            def tile(masked):
                half = rows // 2
                for part in range(2):
                    at = slice(part * half, (part + 1) * half)
                    keys = k_s[i, at]
                    scores = nt(keys, q_s[d])
                    grown = jnp.exp(jnp.minimum(shift_s[d] - scores * FACTOR, CLAMP))
                    probs = pl.reciprocal(1.0 + grown, approx=True)
                    if masked:
                        k_index = (
                            k_start
                            + part * half
                            + lax.broadcasted_iota(jnp.int32, (half, 1), 0)
                        )
                        q_index = q_start + lax.broadcasted_iota(jnp.int32, (1, rows), 1)
                        allowed = (k_index <= q_index) & (k_index >= begin_s[d])
                        probs = jnp.where(allowed, probs, 0.0)
                    weight_grad = nt(v_s[i, at], do_s[d])
                    score_grad = (weight_grad * (probs * probs * grown)).astype(BF16)
                    dv_acc[at] += nn(probs.astype(BF16), do_s[d])
                    dk_acc[at] += nn(score_grad, q_s[d])
                    dq_ref[d] += tn(score_grad, keys)

            pl.when(needed & full)(functools.partial(tile, False))
            pl.when(needed & jnp.logical_not(full))(functools.partial(tile, True))

        dkv_s[i, :, :HD] = (dk_acc[...] * FACTOR).astype(dkv_s.dtype)
        dkv_s[i, :, HD:] = dv_acc[...].astype(dkv_s.dtype)

    for e in range(n_dr):
        for d in range(nz):
            dkv_refs[e][d] = dkv_s[e * nz + d]


def attend_back(
    place, ends, queries, out_grads, keys_values, before, nz, ring, first_dr, n_dr, kept, after=()
):
    rows = queries[0].shape[0]
    n_kv = nz * n_dr
    pairs = nz * n_kv / 2
    chained = before is not None
    return call(
        functools.partial(
            attend_back_body, nz, ring, n_dr, first_dr, chained, ends.shape[0]
        ),
        (jax.ShapeDtypeStruct((nz, rows, HD), F32),)
        + tuple(jax.ShapeDtypeStruct((nz, rows, 2 * HD), kept) for _ in range(n_dr)),
        [place, ends, *queries, *out_grads, *keys_values, *([before] if chained else [])],
        [whole(pltpu.SMEM)] * 2 + [whole(pltpu.VMEM)] * (2 * nz + n_kv + chained),
        pairs * 10 * rows * rows * HD * 2,
        2 * (2 * nz + 4 * n_kv) * rows * HD,
        pairs * 2 * rows * rows,
        after=after,
        out_specs=tuple(whole(pltpu.VMEM) for _ in range(1 + n_dr)),
        scratch_shapes=[
            pltpu.VMEM((nz, rows, HD), BF16),
            pltpu.VMEM((nz, rows, HD), BF16),
            pltpu.VMEM((n_kv, rows, HD), BF16),
            pltpu.VMEM((n_kv, rows, HD), BF16),
            pltpu.VMEM((nz, 1, rows), jnp.int32),
            pltpu.VMEM((nz, 1, rows), F32),
            pltpu.VMEM((n_kv, rows, 2 * HD), kept),
            pltpu.VMEM((rows, HD), F32),
            pltpu.VMEM((rows, HD), F32),
        ],
        name="attend_back",
    )


def finish_body(nz, dq_ref, dkv_ref, got_ref, cos_ref, sin_ref, *out_refs):
    for d in range(nz):
        cosine = cos_ref[d]
        signed = sin_ref[d]
        total = dkv_ref[d] + got_ref[d].astype(F32)
        out = out_refs[d]
        out[:, :HD] = unrotated(dq_ref[d] * FACTOR, cosine, signed).astype(BF16)
        out[:, HD : 2 * HD] = unrotated(total[:, :HD], cosine, signed).astype(BF16)
        out[:, 2 * HD :] = total[:, HD:].astype(BF16)


def finish_grads(dq, dkv, got, cosine, signed):
    nz, rows, _ = dq.shape
    return call(
        functools.partial(finish_body, nz),
        tuple(jax.ShapeDtypeStruct((rows, 3 * HD), BF16) for _ in range(nz)),
        [dq, dkv, got, cosine, signed],
        [whole(pltpu.VMEM)] * 5,
        12 * nz * rows * HD,
        nz * rows * HD * 30,
        out_specs=tuple(whole(pltpu.VMEM) for _ in range(nz)),
        name="finish_grads",
    )


def chosen(step, own_ref, sib_ref):
    return jnp.where(step < pl.num_programs(0) // 2, own_ref[...], sib_ref[...])


def own_columns(width, tile, steps):
    half = steps // 2
    return [
        pl.BlockSpec(
            (width, tile), lambda j, place: (0, place[3] * half + jnp.minimum(j, half - 1))
        ),
        pl.BlockSpec((width, tile), lambda j, place: (0, jnp.maximum(j - half, 0))),
    ]


def own_rows(width, tile, steps):
    half = steps // 2
    return [
        pl.BlockSpec(
            (tile, width), lambda j, place: (place[3] * half + jnp.minimum(j, half - 1), 0)
        ),
        pl.BlockSpec((tile, width), lambda j, place: (jnp.maximum(j - half, 0), 0)),
    ]


def feed_body(place_ref, x_ref, wg_ref, wg_sib, wu_ref, wu_sib, dact_ref, *refs):
    act_ref, dg_ref, du_ref, mine_ref, theirs_ref, acc = refs
    step = pl.program_id(0)
    x = x_ref[...]
    w_gate = chosen(step, wg_ref, wg_sib)
    w_up = chosen(step, wu_ref, wu_sib)
    gate = nn(x, w_gate)
    up = nn(x, w_up)
    dact = dact_ref[...]
    sig = jax.nn.sigmoid(gate)
    silu = gate * sig
    act_ref[...] = (silu * up).astype(BF16)
    dgate = (dact * up * sig * (1.0 + gate * (1.0 - sig))).astype(BF16)
    dup = (dact * silu).astype(BF16)
    dg_ref[...] = dgate
    du_ref[...] = dup
    part = nt(dgate, w_gate) + nt(dup, w_up)

    @pl.when(step == 0)
    def _():
        acc[...] = part

    @pl.when(step > 0)
    def _():
        acc[...] += part

    @pl.when(step == pl.num_programs(0) - 1)
    def _():
        half = mine_ref.shape[0]
        mine_ref[...] = acc[:half].astype(BF16)
        theirs_ref[...] = acc[half:].astype(BF16)


def feed(place, normed, w_gate, gate_sib, w_up, up_sib, dact):
    rows, width = normed.shape
    units = 2 * gate_sib.shape[1]
    tile = 256
    steps = units // tile
    hidden = jax.ShapeDtypeStruct((rows, units), BF16)
    half = jax.ShapeDtypeStruct((rows // 2, width), BF16)
    block = pl.BlockSpec((rows, tile), lambda j, place: (0, j))
    fixed = pl.BlockSpec((rows // 2, width), lambda j, place: (0, 0))
    return call(
        feed_body,
        (hidden, hidden, hidden, half, half),
        [place, normed, w_gate, gate_sib, w_up, up_sib, dact],
        [pl.BlockSpec((rows, width), lambda j, place: (0, 0))]
        + own_columns(width, tile, steps) * 2
        + [block],
        8 * rows * width * units,
        4 * width * units + 10 * rows * units + 4 * rows * width,
        rows * units,
        prefetch=1,
        grid=(steps,),
        out_specs=(block, block, block, fixed, fixed),
        scratch_shapes=[pltpu.VMEM((rows, width), F32)],
        name="feed",
    )


def down_body(place_ref, act_ref, wd_ref, wd_sib, mine_ref, theirs_ref, acc):
    step = pl.program_id(0)
    part = nn(act_ref[...], chosen(step, wd_ref, wd_sib))

    @pl.when(step == 0)
    def _():
        acc[...] = part

    @pl.when(step > 0)
    def _():
        acc[...] += part

    @pl.when(step == pl.num_programs(0) - 1)
    def _():
        half = mine_ref.shape[0]
        mine_ref[...] = acc[:half].astype(BF16)
        theirs_ref[...] = acc[half:].astype(BF16)


def down(place, act, w_down, down_sib, after=()):
    rows, units = act.shape
    width = w_down.shape[1]
    tile = 512
    steps = units // tile
    half = jax.ShapeDtypeStruct((rows // 2, width), BF16)
    fixed = pl.BlockSpec((rows // 2, width), lambda j, place: (0, 0))
    return call(
        down_body,
        (half, half),
        [place, act, w_down, down_sib],
        [pl.BlockSpec((rows, tile), lambda j, place: (0, j))] + own_rows(width, tile, steps),
        2 * rows * width * units,
        2 * width * units + 2 * rows * units + 2 * rows * width,
        after=after,
        prefetch=1,
        grid=(steps,),
        out_specs=(fixed, fixed),
        scratch_shapes=[pltpu.VMEM((rows, width), F32)],
        name="down",
    )


def dact_body(place_ref, cot_ref, wd_ref, wd_sib, out_ref):
    out_ref[...] = nt(cot_ref[...], chosen(pl.program_id(0), wd_ref, wd_sib))


def hidden_upstream(place, cot, w_down, down_sib, after=()):
    rows, width = cot.shape
    units = 2 * down_sib.shape[0]
    tile = 512
    steps = units // tile
    return call(
        dact_body,
        jax.ShapeDtypeStruct((rows, units), F32),
        [place, cot, w_down, down_sib],
        [pl.BlockSpec((rows, width), lambda j, place: (0, 0))] + own_rows(width, tile, steps),
        2 * rows * width * units,
        2 * width * units + 4 * rows * units + 2 * rows * width,
        after=after,
        prefetch=1,
        grid=(steps,),
        out_specs=pl.BlockSpec((rows, tile), lambda j, place: (0, j)),
        name="hidden_upstream",
    )


def turn_body(n, aligned, offset_ref, order_ref, *refs):
    pieces, out_ref = refs[:n], refs[n]
    size = pieces[0].shape[0]
    for j in range(n):
        if aligned:
            out_ref[0, :, j * size : (j + 1) * size] = pieces[j][...].T
        else:
            at = pl.multiple_of(offset_ref[j] * size, size)
            out_ref[0, :, pl.ds(at, size)] = pieces[j][...].T


def turn(order, group, pieces, offsets=None, after=()):
    wide = pieces[0].shape[1]
    aligned = offsets is None
    if group % 128 != 0:
        pieces = [
            jnp.concatenate(
                [
                    lax.dynamic_slice_in_dim(piece, order[p] * group, group, 1)
                    for p in range(order.shape[0])
                ],
                axis=1,
            )
            for piece in pieces
        ]
        block = math.gcd(256, wide)
        order_in = jnp.arange(wide // block, dtype=jnp.int32)
    else:
        block = group
        order_in = order
    n = len(pieces)
    size = pieces[0].shape[0]
    tokens = n * size
    if aligned:
        offsets = jnp.arange(n, dtype=jnp.int32)
    return call(
        functools.partial(turn_body, n, aligned),
        jax.ShapeDtypeStruct((wide // block, block, tokens), BF16),
        [offsets, order_in, *pieces],
        [pl.BlockSpec((size, block), lambda p, f, o: (0, o[p]))] * n,
        0,
        4 * tokens * wide,
        after=after,
        prefetch=2,
        grid=(wide // block,),
        out_specs=pl.BlockSpec((1, block, tokens), lambda p, f, o: (p, 0, 0)),
        name="turn",
    ).reshape(wide, tokens)


def weight_body(added, left_ref, right_ref, *refs):
    total = nn(left_ref[...], right_ref[...])
    if added:
        total = total + refs[0][...].astype(F32)
    refs[-1][...] = total.astype(BF16)


def weight_grad(turned, part, right, width, column, add=None, after=()):
    wide, tokens = turned.shape
    wide = wide // 2
    if width % 256 == 0:
        high, tile = wide, 256
    else:
        high, tile = 256, width
    steps = (wide // high, width // tile)
    first = column * steps[1]
    operands = [turned, right]
    in_specs = [
        pl.BlockSpec((high, tokens), lambda i, j: (part * steps[0] + i, 0)),
        pl.BlockSpec((tokens, tile), lambda i, j: (0, first + j)),
    ]
    if add is not None:
        in_specs.append(pl.BlockSpec((high, tile), lambda i, j: (i, j)))
        operands.append(add)
    return call(
        functools.partial(weight_body, add is not None),
        jax.ShapeDtypeStruct((wide, width), BF16),
        operands,
        in_specs,
        2 * tokens * wide * width,
        2 * (tokens * wide + tokens * width + (1 + (add is not None)) * wide * width),
        after=after,
        grid=steps,
        out_specs=pl.BlockSpec((high, tile), lambda i, j: (i, j)),
        name="weight_grad",
    )


def merge_body(kept_ref, got_ref, low_ref, high_ref):
    total = kept_ref[...].astype(F32) + got_ref[...].astype(F32)
    low_ref[...] = total[0]
    high_ref[...] = total[1].astype(BF16)


def merge(kept, got, after=()):
    wide, width = kept.shape
    high = wide // 2
    tile = math.gcd(high, 128)
    operands = [kept.reshape(2, high, width), got.reshape(2, high, width)]
    block = pl.BlockSpec((2, tile, width), lambda i: (0, i, 0))
    out = pl.BlockSpec((tile, width), lambda i: (i, 0))
    return call(
        merge_body,
        (
            jax.ShapeDtypeStruct((high, width), F32),
            jax.ShapeDtypeStruct((high, width), BF16),
        ),
        operands,
        [block, block],
        wide * width,
        wide * width * 8,
        after=after,
        grid=(high // tile,),
        out_specs=(out, out),
        name="merge",
    )


def lay_body(turned, place_ref, own_ref, got_ref, out_ref):
    value = jnp.where(pl.program_id(0) == 0, own_ref[...], got_ref[...].astype(F32))
    out_ref[...] = value.T if turned else value


def lay(place, own, got, turned):
    rows, width = own.shape
    if turned:
        shape, block = (2 * width, rows), (width, rows)
        index = lambda i, place: (place[3] ^ i, 0)
    else:
        shape, block = (rows, 2 * width), (rows, width)
        index = lambda i, place: (0, place[3] ^ i)
    fixed = pl.BlockSpec((rows, width), lambda i, place: (0, 0))
    return call(
        functools.partial(lay_body, turned),
        jax.ShapeDtypeStruct(shape, F32),
        [place, own, got],
        [fixed, fixed],
        0,
        14 * rows * width,
        prefetch=1,
        grid=(2,),
        out_specs=pl.BlockSpec(block, index),
        name="lay",
    )


def rope_tables(position):
    middle = HD // 2
    frequency = THETA ** (-(jnp.arange(middle, dtype=F32) * 2.0 / HD))
    angles = position.astype(F32)[..., None] * frequency
    cosine = jnp.cos(angles)
    sine = jnp.sin(angles)
    return (
        jnp.concatenate([cosine, cosine], axis=-1),
        jnp.concatenate([-sine, sine], axis=-1),
    )


def rms_scale(values):
    return lax.rsqrt(jnp.mean(values * values, axis=-1, keepdims=True) + EPSILON)


def norm_back(values, scale, gain, upstream):
    normed = values * scale
    gain_grad = jnp.sum(upstream * normed, axis=0)
    weighted = upstream * gain
    return (
        gain_grad,
        scale * (weighted - normed * jnp.mean(weighted * normed, axis=-1, keepdims=True)),
    )


def in_order(own, other, bit, axis):
    return jnp.where(
        bit == 0,
        jnp.concatenate([own, other], axis=axis),
        jnp.concatenate([other, own], axis=axis),
    )


def untangle(values, index, axis):
    size = values.shape[axis]
    bits = size.bit_length() - 1
    shape = values.shape
    values = values.reshape(shape[:axis] + (2,) * bits + shape[axis + 1 :])
    for b in range(bits):
        at = axis + bits - 1 - b
        values = jnp.where((index >> b) & 1 == 1, jnp.flip(values, at), values)
    return values.reshape(shape)


def layer(
    n_seq,
    n_mp,
    mixed_in,
    w_query,
    w_key,
    w_value,
    w_out,
    gain_attn,
    w_gate,
    w_up,
    w_down,
    gain_mlp,
    doc_ends,
    cotangent,
):
    rows, width = mixed_in.shape
    nz = w_query.shape[1] // HD
    ring = n_seq // nz
    bits = n_seq.bit_length() - 1
    low_bits = ring.bit_length() - 1
    units = w_gate.shape[1]
    half_units = units // 2
    half_rows = rows // 2
    group = width // n_seq
    pair_bit = bits - 2
    pair = 1 << pair_bit

    s = lax.axis_index("seq")
    m = lax.axis_index("mp")
    z, r = s // ring, s % ring
    core = m % 2
    side = m // 2
    low = (s >> pair_bit) & 1

    def seq_swap(v, distance):
        return lax.ppermute(v, "seq", [(i, i ^ distance) for i in range(n_seq)])

    def mp_swap(v, distance):
        return lax.ppermute(v, "mp", [(i, i ^ distance) for i in range(n_mp)])

    sum_bits = list(range(pair_bit)) + [bits - 1]
    places = []
    for p in range(n_seq):
        e = 0
        for at, bit in enumerate(sum_bits + [pair_bit]):
            if (p >> (bits - 1 - at)) & 1:
                e |= 1 << bit
        places.append(e)
    order = s ^ jnp.array(places, dtype=jnp.int32)

    place = jnp.stack([z, r, m, low]).astype(jnp.int32)
    inputs = mixed_in.astype(F32)
    scale_attn = rms_scale(inputs)
    normed = (inputs * scale_attn * gain_attn).astype(BF16)
    quarter = rows // n_mp
    quarters = {0: lax.dynamic_slice_in_dim(normed, m * quarter, quarter, 0)}
    for b in reversed(range(nz.bit_length() - 1)):
        for d in list(quarters):
            quarters[d | (1 << b)] = seq_swap(quarters[d], ring << b)
    pieces_z = [None]
    for d in range(1, nz):
        got = quarters[d]
        both = jnp.stack([got, mp_swap(got, 2)])
        sib = mp_swap(both, 1)
        pieces_z.append([both[0], sib[0], both[1], sib[1]])

    w_heads = [
        jnp.concatenate(
            [lax.dynamic_slice_in_dim(w, (z ^ d) * HD, HD, 1) for w in (w_query, w_key, w_value)],
            axis=1,
        )
        for d in range(nz)
    ]
    w_out_heads = jnp.concatenate(
        [lax.dynamic_slice_in_dim(w_out, (z ^ d) * HD, HD, 0) for d in range(nz)], axis=0
    )
    gate_sib = mp_swap(lax.dynamic_slice_in_dim(w_gate, low * half_units, half_units, 1), 1)
    up_sib = mp_swap(lax.dynamic_slice_in_dim(w_up, low * half_units, half_units, 1), 1)
    down_sib = mp_swap(lax.dynamic_slice_in_dim(w_down, low * half_units, half_units, 0), 1)

    cot_half = lax.dynamic_slice_in_dim(cotangent, core * half_rows, half_rows, 0)
    cot_pair = seq_swap(cot_half, pair)
    cot = jnp.concatenate([cot_half, cot_pair], axis=0)
    dact = hidden_upstream(place, cot, w_down, down_sib)
    cot_turned = turn(order, group, [cot_half, cot_pair])

    blocks = (z ^ jnp.arange(nz, dtype=jnp.int32)) * ring + r
    token_index = blocks[:, None] * rows + jnp.arange(rows, dtype=jnp.int32)[None, :]
    ends_below = doc_ends[None, None, :] <= token_index[..., None]
    begin = jnp.max(jnp.where(ends_below, doc_ends, 0), axis=-1)
    cosine, signed = rope_tables(token_index - begin)
    queries, near = [], []
    for d in range(nz):
        x_d = [normed] if d == 0 else pieces_z[d]
        q_d, kv_d = project_qkv(place, x_d, w_heads[0], cosine[d], signed[d])
        queries.append(q_d)
        near.append(kv_d)
    keys_values = [near]
    for b in range(low_bits):
        keys_values = keys_values + [[seq_swap(kv, 1 << b) for kv in kvs] for kvs in keys_values]

    flat = [kv for kvs in keys_values for kv in kvs]
    outs = attend(place, doc_ends, queries, flat, nz, ring)
    heads_out = jnp.concatenate(
        [outs[0]] + [seq_swap(outs[d], d * ring) for d in range(1, nz)], axis=1
    )
    mine_at, sib_at = core * half_rows, (1 - core) * half_rows

    def over_mp(rows_of, weights, contract):
        sib = contract(rows_of(sib_at), weights).astype(BF16)
        mine = contract(rows_of(mine_at), weights)
        part = (mine + mp_swap(sib, 1).astype(F32)).astype(BF16)
        return part.astype(F32) + mp_swap(part, 2).astype(F32)

    def slicer(values):
        return lambda at: lax.dynamic_slice_in_dim(values, at, half_rows, 0)

    x_half = slicer(mixed_in)(mine_at).astype(F32)
    residual = x_half + over_mp(slicer(heads_out), w_out_heads, nn)
    scale_mlp = rms_scale(residual)
    normed_half = (residual * scale_mlp * gain_mlp).astype(BF16)
    normed_pair = seq_swap(normed_half, pair)
    normed_mlp = jnp.concatenate([normed_half, normed_pair], axis=0)

    act, dgate, dup, mine, theirs = feed(
        place, normed_mlp, w_gate, gate_sib, w_up, up_sib, dact
    )

    def over_pair(mine, theirs):
        part = (mine.astype(F32) + seq_swap(theirs, pair).astype(F32)).astype(BF16)
        return part.astype(F32) + mp_swap(part, 2).astype(F32)

    upstream = over_pair(mine, theirs)
    gain_mlp_grad, norm_part = norm_back(residual, scale_mlp, gain_mlp, upstream)
    residual_grad = cot_half.astype(F32) + norm_part
    branch_half = residual_grad.astype(BF16)
    branch_sib = mp_swap(branch_half, 1)
    branch = in_order(branch_half, branch_sib, core, 0)

    def halve(kept, sent):
        for bit in sum_bits:
            kept, sent = merge(kept, seq_swap(sent, 1 << bit))
        return kept, seq_swap(sent, pair)

    def hidden_grad(left, right, turned):
        made = []
        for part in (1, 0):
            sib = weight_grad(left, part, right, half_units, 1)
            made.append(weight_grad(left, part, right, half_units, 0, mp_swap(sib, 1)))
        own, got = halve(made[1], made[0])
        return lay(place, own, got, turned)

    down_share = hidden_grad(cot_turned, act, True)
    normed_turned = turn(order, group, [normed_half, normed_pair])
    gate_share = hidden_grad(normed_turned, dgate, False)
    up_share = hidden_grad(normed_turned, dup, False)

    down_mine, down_theirs = down(place, act, w_down, down_sib)
    out_half = (residual + over_pair(down_mine, down_theirs)).astype(BF16)
    mixed_out = in_order(out_half, mp_swap(out_half, 1), core, 0)

    dheads = nt(branch, w_out_heads).astype(BF16)
    out_grads = [dheads[:, :HD]] + [
        seq_swap(dheads[:, d * HD : (d + 1) * HD], d * ring) for d in range(1, nz)
    ]
    far = [kv for kvs in keys_values[1:] for kv in kvs]
    dq_far, *dkv_far = attend_back(
        place, doc_ends, queries, out_grads, far, None, nz, ring, 1, ring - 1, BF16
    )
    dq, dkv = attend_back(
        place, doc_ends, queries, out_grads, near, dq_far, nz, ring, 0, 1, F32
    )
    pieces = [None] + list(dkv_far)
    for b in reversed(range(low_bits)):
        bit = 1 << b
        for e in range(bit):
            got = seq_swap(pieces[e | bit], bit)
            pieces[e] = (
                got
                if pieces[e] is None
                else (pieces[e].astype(F32) + got.astype(F32)).astype(BF16)
            )
    grads = finish_grads(dq, dkv, pieces[0], cosine, signed)

    wide = nz * HD
    heads_placed = untangle(heads_out.reshape(rows, nz, HD), z, 1).reshape(rows, wide)
    branch_turned = turn(
        order, group, [branch_half, branch_sib], jnp.stack([core, 1 - core]).astype(jnp.int32)
    )
    out_sent = weight_grad(branch_turned, 1, heads_placed, wide, 0)
    out_kept = weight_grad(branch_turned, 0, heads_placed, wide, 0)
    own, got = halve(out_kept, out_sent)
    out_share = (own + got.astype(F32)).T

    own_grads = jnp.concatenate(
        [grads[0]] + [seq_swap(grads[d], d * ring) for d in range(1, nz)], axis=1
    )
    w_all = jnp.concatenate(w_heads, axis=1)
    attn_upstream = over_mp(slicer(own_grads), w_all, nt)
    scale_half = slicer(scale_attn)(mine_at)
    gain_attn_grad, attn_part = norm_back(x_half, scale_half, gain_attn, attn_upstream)
    grad_half = (residual_grad + attn_part).astype(BF16)
    input_grad = in_order(grad_half, mp_swap(grad_half, 1), core, 0)

    own_pieces = [
        lax.dynamic_slice_in_dim(normed, (m ^ j) * quarter, quarter, 0) for j in range(n_mp)
    ]
    spots = jnp.concatenate(
        [(m ^ jnp.arange(n_mp, dtype=jnp.int32)) + d * n_mp for d in range(nz)]
    ).astype(jnp.int32)
    all_turned = turn(
        order, group, own_pieces + [piece for d in range(1, nz) for piece in pieces_z[d]], spots
    )
    all_grads = jnp.concatenate(grads, axis=0)
    sent = weight_grad(all_turned, 1, all_grads, 3 * HD, 0)
    kept = weight_grad(all_turned, 0, all_grads, 3 * HD, 0)
    for bit in sum_bits[: pair_bit - 1]:
        kept, sent = merge(kept, seq_swap(sent, 1 << bit))
    total = kept.astype(F32) + seq_swap(sent, 1 << sum_bits[pair_bit - 1]).astype(F32)
    total = total.reshape(nz, group, 3 * HD)
    small = total.astype(BF16)
    heads = jnp.stack(
        [total[0]] + [seq_swap(small[d], d * ring).astype(F32) for d in range(1, nz)], axis=1
    )
    heads = untangle(heads, z, 1).reshape(group, nz, 3, HD)
    shares = [heads[:, :, i].reshape(group, wide) for i in range(3)]

    gains = jnp.stack([gain_attn_grad, gain_mlp_grad])
    gains = gains + mp_swap(gains, 1)
    for bit in range(bits):
        gains = gains + seq_swap(gains, 1 << bit)
    gains = lax.dynamic_slice_in_dim(gains, s * group, group, 1)

    return (
        mixed_out,
        input_grad,
        shares[0],
        shares[1],
        shares[2],
        out_share,
        gains[0],
        gate_share,
        up_share,
        down_share,
        gains[1],
    )


def solution(mesh):
    placed = (
        P("seq", None),
        P(None, "mp"),
        P(None, "mp"),
        P(None, "mp"),
        P("mp", None),
        P(),
        P(None, "mp"),
        P(None, "mp"),
        P("mp", None),
        P(),
        P(),
        P("seq", None),
    )
    return jax.shard_map(
        functools.partial(layer, mesh.shape["seq"], mesh.shape["mp"]),
        mesh=mesh,
        in_specs=placed,
        out_specs=(
            P("seq", None),
            P("seq", None),
            P("seq", "mp"),
            P("seq", "mp"),
            P("seq", "mp"),
            P("mp", "seq"),
            P("seq"),
            P("seq", "mp"),
            P("seq", "mp"),
            P("mp", "seq"),
            P("seq"),
        ),
        check_vma=False,
    )
```

```python
import functools
import math

import jax
import jax.numpy as jnp
from jax import lax
from jax.experimental import pallas as pl
from jax.experimental.pallas import tpu as pltpu
from jax.sharding import PartitionSpec as P

HD = 128
EPSILON = 1e-05
THETA = 10000.0
FACTOR = 1.0 / math.sqrt(HD)
CLAMP = 80.0
CHUNKS = 2
SHARE = 100
ORDER = []
VMEM_LIMIT = 56 * 1024 * 1024
F32 = jnp.float32
BF16 = jnp.bfloat16


def nn(left, right):
    return lax.dot_general(left, right, (((1,), (0,)), ((), ())), preferred_element_type=F32)


def nt(left, right):
    return lax.dot_general(left, right, (((1,), (1,)), ((), ())), preferred_element_type=F32)


def tn(left, right):
    return lax.dot_general(left, right, (((0,), (0,)), ((), ())), preferred_element_type=F32)


def call(body, out_shape, operands, in_specs, flops, moved, transcendentals=0, after=(), prefetch=0, **kwargs):
    n = prefetch + len(in_specs)
    after = list(after) + ORDER

    def kernel(*refs):
        body(*refs[:n], *refs[n + len(after) :])

    in_specs = list(in_specs) + [pl.BlockSpec(memory_space=pl.ANY)] * len(after)
    if prefetch:
        kwargs = {
            "name": kwargs.pop("name"),
            "grid_spec": pltpu.PrefetchScalarGridSpec(
                num_scalar_prefetch=prefetch, in_specs=in_specs, **kwargs
            ),
        }
    else:
        kwargs["in_specs"] = in_specs
    made = pl.pallas_call(
        kernel,
        out_shape=out_shape,
        compiler_params=pltpu.CompilerParams(vmem_limit_bytes=VMEM_LIMIT),
        cost_estimate=pl.CostEstimate(
            flops=int(flops / SHARE),
            bytes_accessed=int(moved / SHARE),
            transcendentals=int(transcendentals / SHARE),
        ),
        **kwargs,
    )(*operands, *after)
    ORDER[:] = [made[0] if isinstance(made, (tuple, list)) else made]
    return made


def hold_body(n, *refs):
    del n, refs


def hold(values, after=()):
    n = len(values)
    made = call(
        functools.partial(hold_body, n),
        tuple(jax.ShapeDtypeStruct(v.shape, v.dtype) for v in values),
        list(values),
        [pl.BlockSpec(memory_space=pl.ANY)] * n,
        0,
        0,
        after=after,
        out_specs=tuple(pl.BlockSpec(memory_space=pl.ANY) for _ in values),
        input_output_aliases={i: i for i in range(n)},
        name="hold",
    )
    return list(made)


def whole(memory):
    return pl.BlockSpec(memory_space=memory)


def rotated(values, cosine, signed):
    return values * cosine + pltpu.roll(values, HD // 2, 1) * signed


def unrotated(values, cosine, signed):
    return values * cosine - pltpu.roll(values, HD // 2, 1) * signed


def qkv_body(n, place_ref, *refs):
    pieces, refs = refs[:n], refs[n:]
    w_ref, cos_ref, sin_ref, q_ref, kv_ref, x_s = refs
    if n == 1:
        x = pieces[0][...]
    else:
        size = pieces[0].shape[0]
        for j in range(n):
            at = pl.multiple_of((place_ref[2] ^ j) * size, size)
            x_s[pl.ds(at, size), :] = pieces[j][...]
        x = x_s[...]
    made = nn(x, w_ref[...])
    cosine = cos_ref[...]
    signed = sin_ref[...]
    q_ref[...] = rotated(made[:, :HD], cosine, signed).astype(BF16)
    kv_ref[:, :HD] = rotated(made[:, HD : 2 * HD], cosine, signed).astype(BF16)
    kv_ref[:, HD:] = made[:, 2 * HD :].astype(BF16)


def project_qkv(place, pieces, weights, cosine, signed):
    n = len(pieces)
    width = pieces[0].shape[1]
    rows = n * pieces[0].shape[0]
    return call(
        functools.partial(qkv_body, n),
        (
            jax.ShapeDtypeStruct((rows, HD), BF16),
            jax.ShapeDtypeStruct((rows, 2 * HD), BF16),
        ),
        [place, *pieces, weights, cosine, signed],
        [whole(pltpu.SMEM)] + [whole(pltpu.VMEM)] * (n + 3),
        2 * rows * width * 3 * HD,
        2 * rows * width + 6 * width * HD + 14 * rows * HD,
        out_specs=(whole(pltpu.VMEM), whole(pltpu.VMEM)),
        scratch_shapes=[pltpu.VMEM((rows, width), BF16)],
        name="project_qkv",
    )


def begin_of(index, ends_ref, count):
    begin = jnp.zeros_like(index)
    for e in range(count):
        end = ends_ref[e]
        begin = jnp.where(end <= index, jnp.maximum(begin, end), begin)
    return begin


def finish_of(index, ends_ref, count):
    finish = jnp.zeros_like(index) + ends_ref[count - 1]
    for e in range(count):
        end = ends_ref[e]
        finish = jnp.where(end > index, jnp.minimum(finish, end), finish)
    return finish


def attend_body(nz, ring, count, place_ref, ends_ref, *refs):
    n_kv = nz * ring
    q_refs, refs = refs[:nz], refs[nz:]
    kv_refs, refs = refs[:n_kv], refs[n_kv:]
    o_refs, refs = refs[:nz], refs[nz:]
    q_s, k_s, v_s, o_s, acc = refs
    z, r = place_ref[0], place_ref[1]
    rows = q_s.shape[1]
    for d in range(nz):
        q_s[d] = q_refs[d][...]
    for i in range(n_kv):
        k_s[i] = kv_refs[i][:, :HD]
        v_s[i] = kv_refs[i][:, HD:]

    @pl.loop(0, nz)
    def per_query(d):
        q_block = (z ^ d) * ring + r
        q_start = q_block * rows
        q_index = q_start + lax.broadcasted_iota(jnp.int32, (rows, 1), 0)
        begin = begin_of(q_index, ends_ref, count)
        shift = jnp.log((finish_of(q_index, ends_ref, count) - begin).astype(F32))
        first_begin = begin_of(q_start, ends_ref, count)
        last_begin = begin_of(q_start + (rows - 1), ends_ref, count)
        acc[...] = jnp.zeros_like(acc)

        @pl.loop(0, n_kv)
        def per_key(i):
            k_block = (z ^ (i & (nz - 1))) * ring + (r ^ (i // nz))
            k_start = k_block * rows
            needed = (k_block <= q_block) & (k_start + rows > first_begin)
            full = (k_block < q_block) & (k_start >= last_begin)

            def tile(masked):
                half = rows // 2
                for part in range(2):
                    at = slice(part * half, (part + 1) * half)
                    scores = nt(q_s[d, at], k_s[i])
                    grown = jnp.exp(jnp.minimum(shift[at] - scores * FACTOR, CLAMP))
                    probs = pl.reciprocal(1.0 + grown, approx=True)
                    if masked:
                        k_index = k_start + lax.broadcasted_iota(jnp.int32, (1, rows), 1)
                        allowed = (k_index <= q_index[at]) & (k_index >= begin[at])
                        probs = jnp.where(allowed, probs, 0.0)
                    acc[at] += nn(probs.astype(BF16), v_s[i])

            pl.when(needed & full)(functools.partial(tile, False))
            pl.when(needed & jnp.logical_not(full))(functools.partial(tile, True))

        o_s[d] = acc[...].astype(BF16)

    for d in range(nz):
        o_refs[d][...] = o_s[d]


def attend(place, ends, queries, keys_values, nz, ring, after=()):
    rows = queries[0].shape[0]
    n_kv = nz * ring
    pairs = nz * n_kv / 2
    return call(
        functools.partial(attend_body, nz, ring, ends.shape[0]),
        tuple(jax.ShapeDtypeStruct((rows, HD), BF16) for _ in range(nz)),
        [place, ends, *queries, *keys_values],
        [whole(pltpu.SMEM)] * 2 + [whole(pltpu.VMEM)] * (nz + n_kv),
        pairs * 4 * rows * rows * HD * 2,
        2 * (2 * nz + 2 * n_kv) * rows * HD,
        pairs * 2 * rows * rows,
        after=after,
        out_specs=tuple(whole(pltpu.VMEM) for _ in range(nz)),
        scratch_shapes=[
            pltpu.VMEM((nz, rows, HD), BF16),
            pltpu.VMEM((n_kv, rows, HD), BF16),
            pltpu.VMEM((n_kv, rows, HD), BF16),
            pltpu.VMEM((nz, rows, HD), BF16),
            pltpu.VMEM((rows, HD), F32),
        ],
        name="attend",
    )


def attend_back_body(nz, ring, n_dr, first_dr, chained, count, place_ref, ends_ref, *refs):
    n_kv = nz * n_dr
    q_refs, refs = refs[:nz], refs[nz:]
    do_refs, refs = refs[:nz], refs[nz:]
    kv_refs, refs = refs[:n_kv], refs[n_kv:]
    if chained:
        before_ref, refs = refs[0], refs[1:]
    dq_ref, refs = refs[0], refs[1:]
    dkv_refs, refs = refs[:n_dr], refs[n_dr:]
    q_s, do_s, k_s, v_s, begin_s, shift_s, dkv_s, dk_acc, dv_acc = refs
    z, r = place_ref[0], place_ref[1]
    rows = q_s.shape[1]
    for d in range(nz):
        q_s[d] = q_refs[d][...]
        do_s[d] = do_refs[d][...]
    for i in range(n_kv):
        k_s[i] = kv_refs[i][:, :HD]
        v_s[i] = kv_refs[i][:, HD:]
    if chained:
        dq_ref[...] = before_ref[...]
    else:
        dq_ref[...] = jnp.zeros_like(dq_ref)

    @pl.loop(0, nz)
    def tables(d):
        q_index = ((z ^ d) * ring + r) * rows + lax.broadcasted_iota(jnp.int32, (1, rows), 1)
        begin = begin_of(q_index, ends_ref, count)
        begin_s[d] = begin
        shift_s[d] = jnp.log((finish_of(q_index, ends_ref, count) - begin).astype(F32))

    @pl.loop(0, n_kv)
    def per_key(i):
        k_block = (z ^ (i & (nz - 1))) * ring + (r ^ (first_dr + i // nz))
        k_start = k_block * rows
        dk_acc[...] = jnp.zeros_like(dk_acc)
        dv_acc[...] = jnp.zeros_like(dv_acc)

        @pl.loop(0, nz)
        def per_query(d):
            q_block = (z ^ d) * ring + r
            q_start = q_block * rows
            first_begin = begin_of(q_start, ends_ref, count)
            last_begin = begin_of(q_start + (rows - 1), ends_ref, count)
            needed = (k_block <= q_block) & (k_start + rows > first_begin)
            full = (k_block < q_block) & (k_start >= last_begin)

            def tile(masked):
                half = rows // 2
                for part in range(2):
                    at = slice(part * half, (part + 1) * half)
                    keys = k_s[i, at]
                    scores = nt(keys, q_s[d])
                    grown = jnp.exp(jnp.minimum(shift_s[d] - scores * FACTOR, CLAMP))
                    probs = pl.reciprocal(1.0 + grown, approx=True)
                    if masked:
                        k_index = (
                            k_start
                            + part * half
                            + lax.broadcasted_iota(jnp.int32, (half, 1), 0)
                        )
                        q_index = q_start + lax.broadcasted_iota(jnp.int32, (1, rows), 1)
                        allowed = (k_index <= q_index) & (k_index >= begin_s[d])
                        probs = jnp.where(allowed, probs, 0.0)
                    weight_grad = nt(v_s[i, at], do_s[d])
                    score_grad = (weight_grad * (probs * probs * grown)).astype(BF16)
                    dv_acc[at] += nn(probs.astype(BF16), do_s[d])
                    dk_acc[at] += nn(score_grad, q_s[d])
                    dq_ref[d] += tn(score_grad, keys)

            pl.when(needed & full)(functools.partial(tile, False))
            pl.when(needed & jnp.logical_not(full))(functools.partial(tile, True))

        dkv_s[i, :, :HD] = (dk_acc[...] * FACTOR).astype(dkv_s.dtype)
        dkv_s[i, :, HD:] = dv_acc[...].astype(dkv_s.dtype)

    for e in range(n_dr):
        for d in range(nz):
            dkv_refs[e][d] = dkv_s[e * nz + d]


def attend_back(
    place, ends, queries, out_grads, keys_values, before, nz, ring, first_dr, n_dr, kept, after=()
):
    rows = queries[0].shape[0]
    n_kv = nz * n_dr
    pairs = nz * n_kv / 2
    chained = before is not None
    return call(
        functools.partial(
            attend_back_body, nz, ring, n_dr, first_dr, chained, ends.shape[0]
        ),
        (jax.ShapeDtypeStruct((nz, rows, HD), F32),)
        + tuple(jax.ShapeDtypeStruct((nz, rows, 2 * HD), kept) for _ in range(n_dr)),
        [place, ends, *queries, *out_grads, *keys_values, *([before] if chained else [])],
        [whole(pltpu.SMEM)] * 2 + [whole(pltpu.VMEM)] * (2 * nz + n_kv + chained),
        pairs * 10 * rows * rows * HD * 2,
        2 * (2 * nz + 4 * n_kv) * rows * HD,
        pairs * 2 * rows * rows,
        after=after,
        out_specs=tuple(whole(pltpu.VMEM) for _ in range(1 + n_dr)),
        scratch_shapes=[
            pltpu.VMEM((nz, rows, HD), BF16),
            pltpu.VMEM((nz, rows, HD), BF16),
            pltpu.VMEM((n_kv, rows, HD), BF16),
            pltpu.VMEM((n_kv, rows, HD), BF16),
            pltpu.VMEM((nz, 1, rows), jnp.int32),
            pltpu.VMEM((nz, 1, rows), F32),
            pltpu.VMEM((n_kv, rows, 2 * HD), kept),
            pltpu.VMEM((rows, HD), F32),
            pltpu.VMEM((rows, HD), F32),
        ],
        name="attend_back",
    )


def finish_body(nz, dq_ref, dkv_ref, got_ref, cos_ref, sin_ref, *out_refs):
    for d in range(nz):
        cosine = cos_ref[d]
        signed = sin_ref[d]
        total = dkv_ref[d] + got_ref[d].astype(F32)
        out = out_refs[d]
        out[:, :HD] = unrotated(dq_ref[d] * FACTOR, cosine, signed).astype(BF16)
        out[:, HD : 2 * HD] = unrotated(total[:, :HD], cosine, signed).astype(BF16)
        out[:, 2 * HD :] = total[:, HD:].astype(BF16)


def finish_grads(dq, dkv, got, cosine, signed):
    nz, rows, _ = dq.shape
    return call(
        functools.partial(finish_body, nz),
        tuple(jax.ShapeDtypeStruct((rows, 3 * HD), BF16) for _ in range(nz)),
        [dq, dkv, got, cosine, signed],
        [whole(pltpu.VMEM)] * 5,
        12 * nz * rows * HD,
        nz * rows * HD * 30,
        out_specs=tuple(whole(pltpu.VMEM) for _ in range(nz)),
        name="finish_grads",
    )


def rows_at(place, width, height, tile_of):
    return pl.BlockSpec((height, width), lambda j, place: (tile_of(place), 0))


def place_rows(pieces, scratch, spot):
    size = pieces[0].shape[0]
    half = size * len(pieces)
    for i, piece in enumerate(pieces):
        at = pl.multiple_of(spot * half + i * size, size)
        scratch[pl.ds(at, size), :] = piece[...]


def upstream_body(place_ref, *refs):
    pieces, (w_ref, out_ref, x_s) = refs[:-3], refs[-3:]
    size = pieces[0].shape[0]

    @pl.when(pl.program_id(0) == 0)
    def _():
        for i, piece in enumerate(pieces):
            x_s[i * size : (i + 1) * size] = piece[...]

    out_ref[...] = nt(x_s[...], w_ref[...])


def hidden_upstream(place, pieces, weights, own, after=()):
    size, width = pieces[0].shape
    rows = size * len(pieces)
    units = weights.shape[0] // (2 if own else 1)
    tile = 256
    steps = units // tile
    first = (lambda place: place[3] * steps) if own else (lambda place: 0)
    return call(
        upstream_body,
        jax.ShapeDtypeStruct((rows, units), F32),
        [place, *pieces, weights],
        [pl.BlockSpec((size, width), lambda j, place: (0, 0))] * len(pieces)
        + [pl.BlockSpec((tile, width), lambda j, place: (first(place) + j, 0))],
        2 * rows * width * units,
        2 * width * units + 4 * rows * units + 2 * rows * width,
        after=after,
        prefetch=1,
        grid=(steps,),
        out_specs=pl.BlockSpec((rows, tile), lambda j, place: (0, j)),
        scratch_shapes=[pltpu.VMEM((rows, width), BF16)],
        name="hidden_upstream",
    )


def hidden_body(place_ref, *refs):
    pieces, refs = refs[:-8], refs[-8:]
    wg_ref, wu_ref, dact_ref, act_ref, dg_ref, du_ref, x_s, _ = refs
    size = pieces[0].shape[0]

    @pl.when(pl.program_id(0) == 0)
    def _():
        for i, piece in enumerate(pieces):
            x_s[i * size : (i + 1) * size] = piece[...]

    x = x_s[...]
    gate = nn(x, wg_ref[...])
    up = nn(x, wu_ref[...])
    dact = dact_ref[...]
    sig = jax.nn.sigmoid(gate)
    silu = gate * sig
    act_ref[...] = (silu * up).astype(BF16)
    dg_ref[...] = (dact * up * sig * (1.0 + gate * (1.0 - sig))).astype(BF16)
    du_ref[...] = (dact * silu).astype(BF16)


def hidden(place, pieces, w_gate, w_up, dact, own, after=()):
    size, width = pieces[0].shape
    rows = size * len(pieces)
    units = dact.shape[1]
    tile = 256
    steps = units // tile
    first = (lambda place: place[3] * steps) if own else (lambda place: 0)
    made = jax.ShapeDtypeStruct((rows, units), BF16)
    block = pl.BlockSpec((rows, tile), lambda j, place: (0, j))
    weight = pl.BlockSpec((width, tile), lambda j, place: (0, first(place) + j))
    return call(
        hidden_body,
        (made, made, made),
        [place, *pieces, w_gate, w_up, dact],
        [pl.BlockSpec((size, width), lambda j, place: (0, 0))] * len(pieces)
        + [weight, weight, block],
        4 * rows * width * units,
        4 * width * units + 10 * rows * units + 2 * rows * width,
        rows * units,
        after=after,
        prefetch=1,
        grid=(steps,),
        out_specs=(block, block, block),
        scratch_shapes=[pltpu.VMEM((rows, width), BF16), pltpu.VMEM((8, 128), F32)],
        name="hidden",
    )


def chunked(total, out_refs):
    size = out_refs[0].shape[0]
    for i, ref in enumerate(out_refs):
        ref[...] = total[i * size : (i + 1) * size].astype(ref.dtype)


def back_body(place_ref, dg_ref, dg_sib, du_ref, du_sib, wg_ref, wg_sib, wu_ref, wu_sib, *outs):
    chunked(
        nt(dg_ref[...], wg_ref[...])
        + nt(dg_sib[...], wg_sib[...])
        + nt(du_ref[...], wu_ref[...])
        + nt(du_sib[...], wu_sib[...]),
        outs,
    )


def hidden_back(place, dg, dg_sib, du, du_sib, w_gate, gate_sib, w_up, up_sib, chunks, after=()):
    rows, half = dg.shape
    width = w_gate.shape[0]
    tile = 256
    size = rows // chunks
    left = pl.BlockSpec((rows, half), lambda j, place: (0, 0))
    own = pl.BlockSpec((tile, half), lambda j, place: (j, place[3]))
    sib = pl.BlockSpec((tile, half), lambda j, place: (j, 0))
    return call(
        back_body,
        tuple(jax.ShapeDtypeStruct((size, width), BF16) for _ in range(chunks)),
        [place, dg, dg_sib, du, du_sib, w_gate, gate_sib, w_up, up_sib],
        [left] * 4 + [own, sib, own, sib],
        8 * rows * width * half,
        8 * width * half + 8 * rows * half + 2 * rows * width,
        after=after,
        prefetch=1,
        grid=(width // tile,),
        out_specs=tuple(pl.BlockSpec((size, tile), lambda j, place: (0, j)) for _ in range(chunks)),
        name="hidden_back",
    )


def down_body(place_ref, act_ref, act_sib, wd_ref, wd_sib, *outs):
    chunked(nn(act_ref[...], wd_ref[...]) + nn(act_sib[...], wd_sib[...]), outs)


def down(place, act, act_sib, w_down, down_sib, chunks, after=()):
    rows, half = act.shape
    width = w_down.shape[1]
    tile = 256
    size = rows // chunks
    left = pl.BlockSpec((rows, half), lambda j, place: (0, 0))
    return call(
        down_body,
        tuple(jax.ShapeDtypeStruct((size, width), BF16) for _ in range(chunks)),
        [place, act, act_sib, w_down, down_sib],
        [
            left,
            left,
            pl.BlockSpec((half, tile), lambda j, place: (place[3], j)),
            pl.BlockSpec((half, tile), lambda j, place: (0, j)),
        ],
        4 * rows * width * half,
        4 * width * half + 4 * rows * half + 2 * rows * width,
        after=after,
        prefetch=1,
        grid=(width // tile,),
        out_specs=tuple(pl.BlockSpec((size, tile), lambda j, place: (0, j)) for _ in range(chunks)),
        name="down",
    )


def heads_body(nz, contract, keep, place_ref, *refs):
    pieces, refs = refs[:nz], refs[nz:]
    w_ref, sib_ref, mine_ref = refs[:3]
    joined = refs[3]
    wide = pieces[0].shape[1]
    for d in range(nz):
        if keep:
            at = pl.multiple_of((place_ref[0] ^ d) * wide, wide)
            joined[:, pl.ds(at, wide)] = pieces[d][...]
        else:
            joined[:, d * wide : (d + 1) * wide] = pieces[d][...]
    half = sib_ref.shape[0]
    core = place_ref[2] & 1
    there = pl.multiple_of((1 - core) * half, half)
    here = pl.multiple_of(core * half, half)
    weights = w_ref[...]
    sib_ref[...] = contract(joined[pl.ds(there, half), :], weights).astype(BF16)
    mine_ref[...] = contract(joined[pl.ds(here, half), :], weights)


def heads_project(place, pieces, weights, contract, keep, after=()):
    nz = len(pieces)
    rows, wide = pieces[0].shape
    width = weights.shape[1] if contract is nn else weights.shape[0]
    half = rows // 2
    joined = (rows, nz * wide)
    out = (
        jax.ShapeDtypeStruct((half, width), BF16),
        jax.ShapeDtypeStruct((half, width), F32),
    ) + ((jax.ShapeDtypeStruct(joined, BF16),) if keep else ())
    return call(
        functools.partial(heads_body, nz, contract, keep),
        out,
        [place, *pieces, weights],
        [whole(pltpu.SMEM)] + [whole(pltpu.VMEM)] * (nz + 1),
        2 * rows * width * nz * wide,
        2 * width * nz * wide + 2 * rows * nz * wide + 3 * rows * width,
        after=after,
        out_specs=tuple(whole(pltpu.VMEM) for _ in out),
        scratch_shapes=() if keep else (pltpu.VMEM(joined, BF16),),
        name="heads_project",
    )


def dheads_body(nz, n, place_ref, *refs):
    mine, refs = refs[:n], refs[n:]
    sibs, refs = refs[:n], refs[n:]
    w_ref, outs, x_s = refs[0], refs[1:-1], refs[-1]
    core = place_ref[2] & 1
    place_rows(mine, x_s, core)
    place_rows(sibs, x_s, 1 - core)
    x = x_s[...]
    wide = outs[0].shape[1]
    for d in range(nz):
        at = pl.multiple_of((place_ref[0] ^ d) * wide, wide)
        outs[d][...] = nt(x, w_ref[pl.ds(at, wide), :]).astype(BF16)


def heads_upstream(place, mine, sibs, w_out, nz, after=()):
    n = len(mine)
    size, width = mine[0].shape
    rows = 2 * n * size
    wide = w_out.shape[0] // nz
    return call(
        functools.partial(dheads_body, nz, n),
        tuple(jax.ShapeDtypeStruct((rows, wide), BF16) for _ in range(nz)),
        [place, *mine, *sibs, w_out],
        [whole(pltpu.SMEM)] + [whole(pltpu.VMEM)] * (2 * n + 1),
        2 * rows * width * nz * wide,
        2 * width * nz * wide + 2 * rows * nz * wide + 2 * rows * width,
        after=after,
        out_specs=tuple(whole(pltpu.VMEM) for _ in range(nz)),
        scratch_shapes=[pltpu.VMEM((rows, width), BF16)],
        name="heads_upstream",
    )


def sum_body(mine_ref, got_ref, *outs):
    chunked(mine_ref[...].astype(F32) + got_ref[...].astype(F32), outs)


def row_sum(mine, got, chunks, after=()):
    rows, width = mine.shape
    size = rows // chunks
    return call(
        sum_body,
        tuple(jax.ShapeDtypeStruct((size, width), BF16) for _ in range(chunks)),
        [mine, got],
        [whole(pltpu.VMEM)] * 2,
        rows * width,
        8 * rows * width,
        after=after,
        out_specs=tuple(whole(pltpu.VMEM) for _ in range(chunks)),
        name="row_sum",
    )


def scale_of(values):
    return lax.rsqrt(jnp.mean(values * values, axis=-1, keepdims=True) + EPSILON)


def norm_body(part_ref, got_ref, x_ref, gain_ref, res_ref, normed_ref):
    residual = x_ref[...].astype(F32) + (part_ref[...].astype(F32) + got_ref[...].astype(F32))
    res_ref[...] = residual
    normed_ref[...] = (residual * scale_of(residual) * gain_ref[...]).astype(BF16)


def norm_rows(part, got, x, gain, after=()):
    rows, width = part.shape
    return call(
        norm_body,
        (
            jax.ShapeDtypeStruct((rows, width), F32),
            jax.ShapeDtypeStruct((rows, width), BF16),
        ),
        [part, got, x, gain],
        [whole(pltpu.VMEM)] * 4,
        8 * rows * width,
        12 * rows * width,
        after=after,
        out_specs=(whole(pltpu.VMEM), whole(pltpu.VMEM)),
        name="norm_rows",
    )


def norm_back_body(part_ref, got_ref, values_ref, add_ref, gain_ref, *outs):
    upstream = part_ref[...].astype(F32) + got_ref[...].astype(F32)
    values = values_ref[...].astype(F32)
    scale = scale_of(values)
    normed = values * scale
    outs[-1][...] = jnp.sum(upstream * normed, axis=0, keepdims=True)
    weighted = upstream * gain_ref[...]
    grad = scale * (weighted - normed * jnp.mean(weighted * normed, axis=-1, keepdims=True))
    total = add_ref[...].astype(F32) + grad
    for ref in outs[:-1]:
        ref[...] = total.astype(ref.dtype)


def norm_back(part, got, values, add, gain, kinds, after=()):
    rows, width = part.shape
    return call(
        norm_back_body,
        tuple(jax.ShapeDtypeStruct((rows, width), kind) for kind in kinds)
        + (jax.ShapeDtypeStruct((1, width), F32),),
        [part, got, values, add, gain],
        [whole(pltpu.VMEM)] * 5,
        16 * rows * width,
        16 * rows * width,
        after=after,
        out_specs=tuple(whole(pltpu.VMEM) for _ in range(len(kinds) + 1)),
        name="norm_back",
    )


def add_body(part_ref, got_ref, res_ref, out_ref):
    out_ref[...] = (
        res_ref[...] + (part_ref[...].astype(F32) + got_ref[...].astype(F32))
    ).astype(BF16)


def add_rows(part, got, residual, after=()):
    return call(
        add_body,
        jax.ShapeDtypeStruct(part.shape, BF16),
        [part, got, residual],
        [whole(pltpu.VMEM)] * 3,
        part.size,
        10 * part.size,
        after=after,
        out_specs=whole(pltpu.VMEM),
        name="add_rows",
    )


def join_body(n, place_ref, *refs):
    core = place_ref[2] & 1
    place_rows(refs[:n], refs[-1], core)
    place_rows(refs[n : 2 * n], refs[-1], 1 - core)


def join_rows(place, mine, sibs, after=()):
    n = len(mine)
    size, width = mine[0].shape
    return call(
        functools.partial(join_body, n),
        jax.ShapeDtypeStruct((2 * n * size, width), BF16),
        [place, *mine, *sibs],
        [whole(pltpu.SMEM)] + [whole(pltpu.VMEM)] * (2 * n),
        0,
        8 * n * size * width,
        after=after,
        out_specs=whole(pltpu.VMEM),
        name="join_rows",
    )


def turn_body(n, offset_ref, order_ref, *refs):
    pieces, out_ref = refs[:n], refs[n]
    size, block = pieces[0].shape
    unit = (
        lax.broadcasted_iota(jnp.int32, (block, block), 0)
        == lax.broadcasted_iota(jnp.int32, (block, block), 1)
    ).astype(F32).astype(BF16)
    for j in range(n):
        at = pl.multiple_of(offset_ref[j] * size, size)
        out_ref[0, :, pl.ds(at, size)] = nt(unit, pieces[j][...]).astype(BF16)


def turn(order, group, pieces, offsets=None, after=()):
    wide = pieces[0].shape[1]
    if group % 128 != 0:
        pieces = [
            jnp.concatenate(
                [
                    lax.dynamic_slice_in_dim(piece, order[p] * group, group, 1)
                    for p in range(order.shape[0])
                ],
                axis=1,
            )
            for piece in pieces
        ]
        block = math.gcd(256, wide)
        order_in = jnp.arange(wide // block, dtype=jnp.int32)
    else:
        block = group
        order_in = order
    n = len(pieces)
    size = pieces[0].shape[0]
    tokens = n * size
    if offsets is None:
        offsets = jnp.arange(n, dtype=jnp.int32)
    return call(
        functools.partial(turn_body, n),
        jax.ShapeDtypeStruct((wide // block, block, tokens), BF16),
        [offsets, order_in, *pieces],
        [pl.BlockSpec((size, block), lambda p, f, o: (0, o[p]))] * n,
        2 * tokens * wide * block,
        4 * tokens * wide,
        after=after,
        prefetch=2,
        grid=(wide // block,),
        out_specs=pl.BlockSpec((1, block, tokens), lambda p, f, o: (p, 0, 0)),
        name="turn",
    ).reshape(wide, tokens)


def weight_body(left_ref, right_ref, out_ref):
    out_ref[...] = nn(left_ref[...], right_ref[...]).astype(BF16)


def weight_grad(turned, right, after=()):
    wide, tokens = turned.shape
    width = right.shape[1]
    tile = wide // 4
    return call(
        weight_body,
        jax.ShapeDtypeStruct((wide, width), BF16),
        [turned, right],
        [
            pl.BlockSpec((tile, tokens), lambda i: (i, 0)),
            pl.BlockSpec((tokens, width), lambda i: (0, 0)),
        ],
        2 * tokens * wide * width,
        2 * (tokens * wide + tokens * width + wide * width),
        after=after,
        grid=(4,),
        out_specs=pl.BlockSpec((tile, width), lambda i: (i, 0)),
        name="weight_grad",
    )


def weight_parts_body(added, left_ref, right_ref, *refs):
    total = nn(left_ref[...], right_ref[...])
    if added:
        total = total + refs[0][...].astype(F32)
    for i, ref in enumerate(refs[-4:]):

        @pl.when(pl.program_id(0) == i)
        def _(ref=ref):
            ref[...] = total.astype(BF16)


def weight_parts(turned, right, add=None, after=()):
    wide, tokens = turned.shape
    width = right.shape[1]
    tile = wide // 4
    made = jax.ShapeDtypeStruct((tile, width), BF16)
    row = lambda i: (3 - i, 0)
    operands = [turned, right] + ([] if add is None else [add])
    return call(
        functools.partial(weight_parts_body, add is not None),
        (made,) * 4,
        operands,
        [pl.BlockSpec((tile, tokens), row), pl.BlockSpec((tokens, width), lambda i: (0, 0))]
        + [pl.BlockSpec((tile, width), row)] * (add is not None),
        2 * tokens * wide * width,
        2 * (tokens * wide + tokens * width + (1 + (add is not None)) * wide * width),
        after=after,
        grid=(4,),
        out_specs=(pl.BlockSpec((tile, width), lambda i: (0, 0)),) * 4,
        name="weight_parts",
    )


def sum3_body(n, *refs):
    total = refs[0][...].astype(F32)
    for ref in refs[1:n]:
        total = total + ref[...].astype(F32)
    low_ref, high_ref = refs[n:]
    low_ref[...] = total[0]
    high_ref[...] = total[1].astype(BF16)


def final_sum(terms, after=()):
    wide, width = terms[0].shape
    high = wide // 2
    tile = math.gcd(high, 128)
    block = pl.BlockSpec((2, tile, width), lambda i: (0, i, 0))
    out = pl.BlockSpec((tile, width), lambda i: (i, 0))
    return call(
        functools.partial(sum3_body, len(terms)),
        (
            jax.ShapeDtypeStruct((high, width), F32),
            jax.ShapeDtypeStruct((high, width), BF16),
        ),
        [term.reshape(2, high, width) for term in terms],
        [block] * len(terms),
        wide * width,
        wide * width * 8,
        after=after,
        grid=(high // tile,),
        out_specs=(out, out),
        name="final_sum",
    )


def merge_body(kept_ref, got_ref, low_ref, high_ref):
    total = kept_ref[...].astype(F32) + got_ref[...].astype(F32)
    low_ref[...] = total[0]
    high_ref[...] = total[1].astype(BF16)


def merge(kept, got, after=()):
    wide, width = kept.shape
    high = wide // 2
    tile = math.gcd(high, 128)
    operands = [kept.reshape(2, high, width), got.reshape(2, high, width)]
    block = pl.BlockSpec((2, tile, width), lambda i: (0, i, 0))
    out = pl.BlockSpec((tile, width), lambda i: (i, 0))
    return call(
        merge_body,
        (
            jax.ShapeDtypeStruct((high, width), F32),
            jax.ShapeDtypeStruct((high, width), BF16),
        ),
        operands,
        [block, block],
        wide * width,
        wide * width * 8,
        after=after,
        grid=(high // tile,),
        out_specs=(out, out),
        name="merge",
    )


def lay_body(turned, place_ref, own_ref, got_ref, out_ref):
    value = jnp.where(pl.program_id(0) == 0, own_ref[...], got_ref[...].astype(F32))
    out_ref[...] = value.T if turned else value


def lay(place, own, got, turned):
    rows, width = own.shape
    if turned:
        shape, block = (2 * width, rows), (width, rows)
        index = lambda i, place: (place[3] ^ i, 0)
    else:
        shape, block = (rows, 2 * width), (rows, width)
        index = lambda i, place: (0, place[3] ^ i)
    fixed = pl.BlockSpec((rows, width), lambda i, place: (0, 0))
    return call(
        functools.partial(lay_body, turned),
        jax.ShapeDtypeStruct(shape, F32),
        [place, own, got],
        [fixed, fixed],
        0,
        14 * rows * width,
        prefetch=1,
        grid=(2,),
        out_specs=pl.BlockSpec(block, index),
        name="lay",
    )


def rope_tables(position):
    middle = HD // 2
    frequency = THETA ** (-(jnp.arange(middle, dtype=F32) * 2.0 / HD))
    angles = position.astype(F32)[..., None] * frequency
    cosine = jnp.cos(angles)
    sine = jnp.sin(angles)
    return (
        jnp.concatenate([cosine, cosine], axis=-1),
        jnp.concatenate([-sine, sine], axis=-1),
    )


def rms_scale(values):
    return lax.rsqrt(jnp.mean(values * values, axis=-1, keepdims=True) + EPSILON)


def untangle(values, index, axis):
    size = values.shape[axis]
    bits = size.bit_length() - 1
    shape = values.shape
    values = values.reshape(shape[:axis] + (2,) * bits + shape[axis + 1 :])
    for b in range(bits):
        at = axis + bits - 1 - b
        values = jnp.where((index >> b) & 1 == 1, jnp.flip(values, at), values)
    return values.reshape(shape)


def layer(
    n_seq,
    n_mp,
    mixed_in,
    w_query,
    w_key,
    w_value,
    w_out,
    gain_attn,
    w_gate,
    w_up,
    w_down,
    gain_mlp,
    doc_ends,
    cotangent,
):
    rows, width = mixed_in.shape
    nz = w_query.shape[1] // HD
    ring = n_seq // nz
    bits = n_seq.bit_length() - 1
    low_bits = ring.bit_length() - 1
    units = w_gate.shape[1]
    half_units = units // 2
    half_rows = rows // 2
    group = width // n_seq
    pair_bit = bits - 2
    pair = 1 << pair_bit

    s = lax.axis_index("seq")
    m = lax.axis_index("mp")
    z, r = s // ring, s % ring
    core = m % 2
    side = m // 2
    low = (s >> pair_bit) & 1

    def seq_swap(v, distance):
        return lax.ppermute(v, "seq", [(i, i ^ distance) for i in range(n_seq)])

    def mp_swap(v, distance):
        return lax.ppermute(v, "mp", [(i, i ^ distance) for i in range(n_mp)])

    sum_bits = list(range(pair_bit)) + [bits - 1]
    places = []
    for p in range(n_seq):
        e = 0
        for at, bit in enumerate(sum_bits + [pair_bit]):
            if (p >> (bits - 1 - at)) & 1:
                e |= 1 << bit
        places.append(e)
    order = s ^ jnp.array(places, dtype=jnp.int32)

    ORDER.clear()

    place = jnp.stack([z, r, m, low]).astype(jnp.int32)
    inputs = mixed_in.astype(F32)
    scale_attn = rms_scale(inputs)
    normed = (inputs * scale_attn * gain_attn).astype(BF16)
    quarter = rows // n_mp
    quarters = {0: lax.dynamic_slice_in_dim(normed, m * quarter, quarter, 0)}
    for b in reversed(range(nz.bit_length() - 1)):
        for d in list(quarters):
            quarters[d | (1 << b)] = seq_swap(quarters[d], ring << b)
    pieces_z = [[normed]]
    for d in range(1, nz):
        across = mp_swap(quarters[d], 2)
        pieces_z.append([quarters[d], mp_swap(quarters[d], 1), across, mp_swap(across, 1)])

    w_heads = [
        jnp.concatenate(
            [lax.dynamic_slice_in_dim(w, (z ^ d) * HD, HD, 1) for w in (w_query, w_key, w_value)],
            axis=1,
        )
        for d in range(nz)
    ]
    halves = [
        lax.dynamic_slice_in_dim(w_gate, low * half_units, half_units, 1),
        lax.dynamic_slice_in_dim(w_up, low * half_units, half_units, 1),
        lax.dynamic_slice_in_dim(w_down, low * half_units, half_units, 0),
    ]
    cot_half = lax.dynamic_slice_in_dim(cotangent, core * half_rows, half_rows, 0)

    blocks = (z ^ jnp.arange(nz, dtype=jnp.int32)) * ring + r
    token_index = blocks[:, None] * rows + jnp.arange(rows, dtype=jnp.int32)[None, :]
    ends_below = doc_ends[None, None, :] <= token_index[..., None]
    begin = jnp.max(jnp.where(ends_below, doc_ends, 0), axis=-1)
    cosine, signed = rope_tables(token_index - begin)
    queries, near = [], []
    for d in range(nz):
        q_d, kv_d = project_qkv(place, pieces_z[d], w_heads[0], cosine[d], signed[d])
        queries.append(q_d)
        near.append(kv_d)
        if d == 1:
            (cot_half,) = hold([cot_half])
            cot_pair = seq_swap(cot_half, pair)
    keys_values = [near]
    for b in range(low_bits):
        keys_values = keys_values + [[seq_swap(kv, 1 << b) for kv in kvs] for kvs in keys_values]

    flat = [kv for kvs in keys_values for kv in kvs]
    gate_sib, up_sib, down_sib = [mp_swap(half, 1) for half in hold(halves)]
    outs = attend(place, doc_ends, queries, flat, nz, ring)
    heads = [outs[0]] + [seq_swap(outs[d], d * ring) for d in range(1, nz)]
    size = half_rows // CHUNKS

    def chunks_of(values):
        return [values[i * size : (i + 1) * size] for i in range(CHUNKS)]

    x_chunks = chunks_of(lax.dynamic_slice_in_dim(mixed_in, core * half_rows, half_rows, 0))
    cot_chunks = chunks_of(cot_half)
    cot_all = cot_chunks + chunks_of(cot_pair)
    cot_turned = turn(order, group, cot_all, after=[gate_sib, up_sib, down_sib])

    sib, mine, heads_placed = heads_project(place, heads, w_out, nn, True)
    parts = row_sum(mine, mp_swap(sib, 1), CHUNKS)
    gain_row = gain_mlp.reshape(1, width)
    residual, normed_own, dacts = [], [], []
    for i in range(CHUNKS):
        if i < 2:
            dacts.append(
                hidden_upstream(place, cot_all, (w_down, down_sib)[i], i == 0)
            )
        res, out = norm_rows(parts[i], mp_swap(parts[i], 2), x_chunks[i], gain_row)
        residual.append(res)
        normed_own.append(out)
    dact, dact_sib = dacts
    normed_all = normed_own + [seq_swap(part, pair) for part in normed_own]

    def first_sums(parts):
        sent_b, sent_a, kept_b, kept_a = parts
        for bit in sum_bits[: pair_bit - 1]:
            kept = jnp.concatenate([kept_a, kept_b], axis=0)
            sent = jnp.concatenate([sent_a, sent_b], axis=0)
            kept, sent = merge(kept, seq_swap(sent, 1 << bit))
            n = kept.shape[0] // 2
            sent_b, sent_a, kept_b, kept_a = sent[n:], sent[:n], kept[n:], kept[:n]
        return sent_b, sent_a, kept_b, kept_a

    last_low = 1 << sum_bits[pair_bit - 1]
    high = 1 << sum_bits[pair_bit]

    act_sib, dg_sib, du_sib = hidden(place, normed_all, gate_sib, up_sib, dact_sib, False)
    act, dg, du = hidden(place, normed_all, w_gate, w_up, dact, True)
    sib_down = mp_swap(weight_grad(cot_turned, act_sib), 1)
    made = hidden_back(
        place, dg, dg_sib, du, du_sib, w_gate, gate_sib, w_up, up_sib, 2 * CHUNKS
    )
    back_got = [seq_swap(made[CHUNKS + i], pair) for i in range(CHUNKS)]
    down_sent_b, down_sent_a, down_kept_b, down_kept_a = first_sums(
        weight_parts(cot_turned, act, sib_down)
    )
    down_b = seq_swap(down_sent_b, last_low)
    normed_turned = turn(order, group, normed_all)
    sib_gate = mp_swap(weight_grad(normed_turned, dg_sib), 1)
    back_parts, branch, residual_grad, gain_parts = [], [], [], []

    def upstream_of(i):
        back_parts.extend(row_sum(made[i], back_got[i], 1))
        return mp_swap(back_parts[i], 2)

    def through_norm(i, got):
        grad, low_grad, gain_part = norm_back(
            back_parts[i], got, residual[i], cot_chunks[i], gain_row, (F32, BF16)
        )
        residual_grad.append(grad)
        branch.append(low_grad)
        gain_parts.append(gain_part)

    got = [upstream_of(0)]
    gate_sent_b, gate_sent_a, gate_kept_b, gate_kept_a = first_sums(
        weight_parts(normed_turned, dg, sib_gate)
    )
    got += [upstream_of(i) for i in range(1, CHUNKS)]
    sib_up = mp_swap(weight_grad(normed_turned, du_sib), 1)
    through_norm(0, got[0])
    up_sent_b, up_sent_a, up_kept_b, up_kept_a = first_sums(
        weight_parts(normed_turned, du, sib_up)
    )
    (half_down,) = row_sum(down_kept_b, down_b, 1)
    down_high = seq_swap(half_down, high)
    (down_sent_a,) = hold([down_sent_a])
    down_a = seq_swap(down_sent_a, last_low)
    for i in range(1, CHUNKS):
        through_norm(i, got[i])
    gain_mlp_grad = sum(gain_parts)
    branch_sib = [mp_swap(part, 1) for part in branch]

    dheads = heads_upstream(place, branch, branch_sib, w_out, nz)
    out_grads = [dheads[0]] + [seq_swap(dheads[d], d * ring) for d in range(1, nz)]
    spots = jnp.concatenate(
        [core * CHUNKS + jnp.arange(CHUNKS), (1 - core) * CHUNKS + jnp.arange(CHUNKS)]
    ).astype(jnp.int32)
    branch_turned = turn(order, group, branch + branch_sib, spots)
    out_parts = weight_parts(branch_turned, heads_placed)
    down_mine, down_theirs = down(place, act, act_sib, w_down, down_sib, 2)
    gate_sent_b, down_theirs = hold([gate_sent_b, down_theirs], after=out_grads)
    gate_b = seq_swap(gate_sent_b, last_low)
    down_got = seq_swap(down_theirs, pair)
    far = [kv for kvs in keys_values[1:] for kv in kvs]
    dq_far, *dkv_far = attend_back(
        place, doc_ends, queries, out_grads, far, None, nz, ring, 1, ring - 1, BF16
    )
    pieces = [None] + list(dkv_far)
    for b in reversed(range(low_bits)):
        bit = 1 << b
        for e in range(bit):
            got = seq_swap(pieces[e | bit], bit)
            pieces[e] = (
                got
                if pieces[e] is None
                else (pieces[e].astype(F32) + got.astype(F32)).astype(BF16)
            )
    dq, dkv = attend_back(
        place, doc_ends, queries, out_grads, near, dq_far, nz, ring, 0, 1, F32
    )
    (down_part,) = row_sum(down_mine, down_got, 1)
    down_across = mp_swap(down_part, 2)
    own_down, pair_down = final_sum([down_kept_a, down_a, down_high])
    pair_down = seq_swap(pair_down, pair)
    (half_gate,) = row_sum(gate_kept_b, gate_b, 1)
    gate_high = seq_swap(half_gate, high)
    (gate_sent_a,) = hold([gate_sent_a])
    gate_a = seq_swap(gate_sent_a, last_low)
    down_share = lay(place, own_down, pair_down, True)
    grads = finish_grads(dq, dkv, pieces[0], cosine, signed)
    own_grads = [grads[0]] + [seq_swap(grads[d], d * ring) for d in range(1, nz)]

    spots = jnp.concatenate(
        [jnp.arange(n_mp, dtype=jnp.int32)]
        + [(m ^ jnp.arange(n_mp, dtype=jnp.int32)) + d * n_mp for d in range(1, nz)]
    ).astype(jnp.int32)
    own_pieces = [normed[i * quarter : (i + 1) * quarter] for i in range(n_mp)]
    all_turned = turn(
        order, group, own_pieces + [piece for d in range(1, nz) for piece in pieces_z[d]], spots
    )
    all_grads = jnp.concatenate(grads, axis=0)
    qkv_parts = weight_parts(all_turned, all_grads)
    (up_sent_b,) = hold([up_sent_b], after=[gate_a])
    up_b = seq_swap(up_sent_b, last_low)
    own_gate, pair_gate = final_sum([gate_kept_a, gate_a, gate_high])
    pair_gate = seq_swap(pair_gate, pair)
    (half_up,) = row_sum(up_kept_b, up_b, 1)
    up_high = seq_swap(half_up, high)
    (up_sent_a,) = hold([up_sent_a])
    up_a = seq_swap(up_sent_a, last_low)

    w_all = jnp.concatenate(w_heads, axis=1)
    sib, mine = heads_project(place, own_grads, w_all, nt, False)
    sib_got = mp_swap(sib, 1)
    gate_share = lay(place, own_gate, pair_gate, False)
    parts = row_sum(mine, sib_got, CHUNKS)
    across = [mp_swap(part, 2) for part in parts]
    out_rows = add_rows(down_part, down_across, jnp.concatenate(residual, axis=0))
    out_sent = jnp.concatenate([out_parts[1], out_parts[0]], axis=0)
    out_kept = jnp.concatenate([out_parts[3], out_parts[2]], axis=0)
    (out_sent,) = hold([out_sent])
    out_got = seq_swap(out_sent, 1 << sum_bits[0])
    gain_row = gain_attn.reshape(1, width)
    grad_rows, gain_parts = [], []
    for i in range(CHUNKS):
        low_grad, gain_part = norm_back(
            parts[i], across[i], x_chunks[i], residual_grad[i], gain_row, (BF16,)
        )
        grad_rows.append(low_grad)
        gain_parts.append(gain_part)
    gain_attn_grad = sum(gain_parts)
    grad_sib = [mp_swap(part, 1) for part in grad_rows]
    mixed_out = join_rows(place, [out_rows], [mp_swap(out_rows, 1)])
    input_grad = join_rows(place, grad_rows, grad_sib)

    def out_sums(kept, got):
        kept, sent = merge(kept, got)
        for bit in sum_bits[1:-1]:
            kept, sent = merge(kept, seq_swap(sent, 1 << bit))
        return kept, seq_swap(sent, high)

    out_kept, out_got = out_sums(out_kept, out_got)
    qkv_sent = jnp.concatenate([qkv_parts[1], qkv_parts[0]], axis=0)
    qkv_kept = jnp.concatenate([qkv_parts[3], qkv_parts[2]], axis=0)
    (qkv_sent,) = hold([qkv_sent])
    kept, sent = qkv_kept, qkv_sent
    for bit in sum_bits[: pair_bit - 1]:
        kept, sent = merge(kept, seq_swap(sent, 1 << bit))
    qkv_got = seq_swap(sent, last_low)

    own_up, pair_up = final_sum([up_kept_a, up_a, up_high])
    pair_up = seq_swap(pair_up, pair)

    total = (kept.astype(F32) + qkv_got.astype(F32)).reshape(nz, group, 3 * HD)
    small = total.astype(BF16)
    heads = jnp.stack(
        [total[0]] + [seq_swap(small[d], d * ring).astype(F32) for d in range(1, nz)], axis=1
    )
    heads = untangle(heads, z, 1).reshape(group, nz, 3, HD)
    shares = [heads[:, :, i].reshape(group, nz * HD) for i in range(3)]
    up_share = lay(place, own_up, pair_up, False)
    own_out, pair_out = final_sum([out_kept, out_got])
    out_share = (own_out + seq_swap(pair_out, pair).astype(F32)).T

    gains = jnp.concatenate([gain_attn_grad, gain_mlp_grad])
    gains = gains + mp_swap(gains, 1)
    for bit in range(bits):
        gains = gains + seq_swap(gains, 1 << bit)
    gains = lax.dynamic_slice_in_dim(gains, s * group, group, 1)

    return (
        mixed_out,
        input_grad,
        shares[0],
        shares[1],
        shares[2],
        out_share,
        gains[0],
        gate_share,
        up_share,
        down_share,
        gains[1],
    )


def solution(mesh):
    placed = (
        P("seq", None),
        P(None, "mp"),
        P(None, "mp"),
        P(None, "mp"),
        P("mp", None),
        P(),
        P(None, "mp"),
        P(None, "mp"),
        P("mp", None),
        P(),
        P(),
        P("seq", None),
    )
    return jax.shard_map(
        functools.partial(layer, mesh.shape["seq"], mesh.shape["mp"]),
        mesh=mesh,
        in_specs=placed,
        out_specs=(
            P("seq", None),
            P("seq", None),
            P("seq", "mp"),
            P("seq", "mp"),
            P("seq", "mp"),
            P("mp", "seq"),
            P("seq"),
            P("seq", "mp"),
            P("seq", "mp"),
            P("mp", "seq"),
            P("seq"),
        ),
        check_vma=False,
    )
```

```python
import functools
import math

import jax
import jax.numpy as jnp
from jax import lax
from jax.experimental import pallas as pl
from jax.experimental.pallas import tpu as pltpu
from jax.sharding import PartitionSpec as P

HD = 128
EPSILON = 1e-05
THETA = 10000.0
FACTOR = 1.0 / math.sqrt(HD)
CLAMP = 80.0
CHUNKS = 2
SHARE = 100
ORDER = []
MIB = 1024 * 1024
F32 = jnp.float32
BF16 = jnp.bfloat16


def nn(left, right):
    return lax.dot_general(left, right, (((1,), (0,)), ((), ())), preferred_element_type=F32)


def nt(left, right):
    return lax.dot_general(left, right, (((1,), (1,)), ((), ())), preferred_element_type=F32)


def tn(left, right):
    return lax.dot_general(left, right, (((0,), (0,)), ((), ())), preferred_element_type=F32)


def call(
    body,
    out_shape,
    operands,
    in_specs,
    flops,
    moved,
    transcendentals=0,
    after=(),
    prefetch=0,
    chain=True,
    vmem=20,
    **kwargs,
):
    n = prefetch + len(in_specs)
    after = list(after) + (ORDER if chain else [])

    def kernel(*refs):
        body(*refs[:n], *refs[n + len(after) :])

    in_specs = list(in_specs) + [pl.BlockSpec(memory_space=pl.ANY)] * len(after)
    if prefetch:
        kwargs = {
            "name": kwargs.pop("name"),
            "grid_spec": pltpu.PrefetchScalarGridSpec(
                num_scalar_prefetch=prefetch, in_specs=in_specs, **kwargs
            ),
        }
    else:
        kwargs["in_specs"] = in_specs
    made = pl.pallas_call(
        kernel,
        out_shape=out_shape,
        compiler_params=pltpu.CompilerParams(vmem_limit_bytes=vmem * MIB),
        cost_estimate=pl.CostEstimate(
            flops=int(flops / SHARE),
            bytes_accessed=int(moved / SHARE),
            transcendentals=int(transcendentals / SHARE),
        ),
        **kwargs,
    )(*operands, *after)
    if chain:
        ORDER[:] = [made[0] if isinstance(made, (tuple, list)) else made]
    return made


def hold_body(n, *refs):
    del n, refs


def hold(values, after=()):
    n = len(values)
    made = call(
        functools.partial(hold_body, n),
        tuple(jax.ShapeDtypeStruct(v.shape, v.dtype) for v in values),
        list(values),
        [pl.BlockSpec(memory_space=pl.ANY)] * n,
        0,
        0,
        after=after,
        out_specs=tuple(pl.BlockSpec(memory_space=pl.ANY) for _ in values),
        input_output_aliases={i: i for i in range(n)},
        name="hold",
    )
    return list(made)


def whole(memory):
    return pl.BlockSpec(memory_space=memory)


def rotated(values, cosine, signed):
    return values * cosine + pltpu.roll(values, HD // 2, 1) * signed


def unrotated(values, cosine, signed):
    return values * cosine - pltpu.roll(values, HD // 2, 1) * signed


def qkv_body(n, fresh, place_ref, *refs):
    if fresh:
        x_ref, gain_ref, refs = refs[0], refs[1], refs[2:]
    else:
        x_ref, refs = refs[0], refs[1:]
    wq_ref, wk_ref, wv_ref, cos_ref, sin_ref = refs[:5]
    outs, (w_s, x_s) = refs[5 : 5 + n], refs[-2:]
    step = pl.program_id(0)

    @pl.when(step == 0)
    def _():
        if fresh:
            x = x_ref[...].astype(F32)
            x_s[...] = (x * scale_of(x) * gain_ref[...]).astype(BF16)
            refs[5 + n][...] = x_s[...]
        else:
            x_s[...] = x_ref[...]

    w_s[:, :HD] = wq_ref[...]
    w_s[:, HD : 2 * HD] = wk_ref[...]
    w_s[:, 2 * HD :] = wv_ref[...]
    made = nn(x_s[...], w_s[...])
    cosine = cos_ref[...]
    signed = sin_ref[...]
    query = rotated(made[:, :HD], cosine, signed).astype(BF16)
    key = rotated(made[:, HD : 2 * HD], cosine, signed).astype(BF16)
    value = made[:, 2 * HD :].astype(BF16)
    for i in range(n):

        @pl.when(step == i)
        def _(i=i):
            outs[i][:, :HD] = query
            outs[i][:, HD : 2 * HD] = key
            outs[i][:, 2 * HD :] = value


def project_qkv(place, x, gain, weights, cosine, signed, spots):
    n = len(spots)
    rows, width = x.shape
    fresh = gain is not None
    fixed = pl.BlockSpec((rows, width), lambda i, place: (0, 0))
    table = pl.BlockSpec((rows, HD), lambda i, place: (0, 0))
    first = spots[0]
    assert list(spots) == [first ^ i for i in range(n)]
    weight = pl.BlockSpec((width, HD), lambda i, place: (0, place[0] ^ first ^ i))
    piece = jax.ShapeDtypeStruct((rows, 3 * HD), BF16)
    return call(
        functools.partial(qkv_body, n, fresh),
        (piece,) * n + ((jax.ShapeDtypeStruct(x.shape, BF16),) if fresh else ()),
        [place, x] + ([gain] if fresh else []) + [*weights, cosine, signed],
        [fixed]
        + ([pl.BlockSpec((1, width), lambda i, place: (0, 0))] if fresh else [])
        + [weight] * 3
        + [table] * 2,
        6 * n * rows * width * HD,
        4 * rows * width + 6 * n * width * HD + 6 * n * rows * HD,
        prefetch=1,
        grid=(n,),
        out_specs=(pl.BlockSpec((rows, 3 * HD), lambda i, place: (0, 0)),) * n
        + ((fixed,) if fresh else ()),
        scratch_shapes=[pltpu.VMEM((width, 3 * HD), BF16), pltpu.VMEM((rows, width), BF16)],
        vmem=32,
        name="project_qkv",
    )


def begin_of(index, ends_ref, count):
    begin = jnp.zeros_like(index)
    for e in range(count):
        end = ends_ref[e]
        begin = jnp.where(end <= index, jnp.maximum(begin, end), begin)
    return begin


def finish_of(index, ends_ref, count):
    finish = jnp.zeros_like(index) + ends_ref[count - 1]
    for e in range(count):
        end = ends_ref[e]
        finish = jnp.where(end > index, jnp.minimum(finish, end), finish)
    return finish


def attend_body(nz, ring, count, place_ref, ends_ref, *refs):
    n_kv = nz * ring
    q_refs, refs = refs[:nz], refs[nz:]
    kv_refs, refs = refs[:n_kv], refs[n_kv:]
    o_refs, refs = refs[:nz], refs[nz:]
    q_s, k_s, v_s, o_s, acc = refs
    z, r = place_ref[0], place_ref[1]
    rows = q_s.shape[1]
    for d in range(nz):
        q_s[d] = q_refs[d][:, :HD]
    for i in range(n_kv):
        first = kv_refs[i].shape[1] - 2 * HD
        k_s[i] = kv_refs[i][:, first : first + HD]
        v_s[i] = kv_refs[i][:, first + HD :]

    @pl.loop(0, nz)
    def per_query(d):
        q_block = (z ^ d) * ring + r
        q_start = q_block * rows
        q_index = q_start + lax.broadcasted_iota(jnp.int32, (rows, 1), 0)
        begin = begin_of(q_index, ends_ref, count)
        shift = jnp.log((finish_of(q_index, ends_ref, count) - begin).astype(F32))
        first_begin = begin_of(q_start, ends_ref, count)
        last_begin = begin_of(q_start + (rows - 1), ends_ref, count)
        acc[...] = jnp.zeros_like(acc)

        @pl.loop(0, n_kv)
        def per_key(i):
            k_block = (z ^ (i & (nz - 1))) * ring + (r ^ (i // nz))
            k_start = k_block * rows
            needed = (k_block <= q_block) & (k_start + rows > first_begin)
            full = (k_block < q_block) & (k_start >= last_begin)

            def tile(masked):
                half = rows // 2
                for part in range(2):
                    at = slice(part * half, (part + 1) * half)
                    scores = nt(q_s[d, at], k_s[i])
                    grown = jnp.exp(jnp.minimum(shift[at] - scores * FACTOR, CLAMP))
                    probs = pl.reciprocal(1.0 + grown, approx=True)
                    if masked:
                        k_index = k_start + lax.broadcasted_iota(jnp.int32, (1, rows), 1)
                        allowed = (k_index <= q_index[at]) & (k_index >= begin[at])
                        probs = jnp.where(allowed, probs, 0.0)
                    acc[at] += nn(probs.astype(BF16), v_s[i])

            pl.when(needed & full)(functools.partial(tile, False))
            pl.when(needed & jnp.logical_not(full))(functools.partial(tile, True))

        o_s[d] = acc[...].astype(BF16)

    for d in range(nz):
        o_refs[d][...] = o_s[d]


def attend(place, ends, queries, keys_values, nz, ring, after=()):
    rows = queries[0].shape[0]
    n_kv = nz * ring
    pairs = nz * n_kv / 2
    return call(
        functools.partial(attend_body, nz, ring, ends.shape[0]),
        tuple(jax.ShapeDtypeStruct((rows, HD), BF16) for _ in range(nz)),
        [place, ends, *queries, *keys_values],
        [whole(pltpu.SMEM)] * 2 + [whole(pltpu.VMEM)] * (nz + n_kv),
        pairs * 4 * rows * rows * HD * 2,
        2 * (2 * nz + 2 * n_kv) * rows * HD,
        pairs * 2 * rows * rows,
        after=after,
        out_specs=tuple(whole(pltpu.VMEM) for _ in range(nz)),
        scratch_shapes=[
            pltpu.VMEM((nz, rows, HD), BF16),
            pltpu.VMEM((n_kv, rows, HD), BF16),
            pltpu.VMEM((n_kv, rows, HD), BF16),
            pltpu.VMEM((nz, rows, HD), BF16),
            pltpu.VMEM((rows, HD), F32),
        ],
        vmem=12 + 2 * n_kv * rows * HD * 8 // MIB,
        name="attend",
    )


def attend_back_body(nz, ring, n_dr, first_dr, chained, count, place_ref, ends_ref, *refs):
    n_kv = nz * n_dr
    q_refs, refs = refs[:nz], refs[nz:]
    do_refs, refs = refs[:nz], refs[nz:]
    kv_refs, refs = refs[:n_kv], refs[n_kv:]
    if chained:
        before_ref, refs = refs[0], refs[1:]
    dq_ref, refs = refs[0], refs[1:]
    dkv_refs, refs = refs[:n_dr], refs[n_dr:]
    q_s, do_s, k_s, v_s, begin_s, shift_s, dkv_s, dk_acc, dv_acc = refs
    z, r = place_ref[0], place_ref[1]
    rows = q_s.shape[1]
    for d in range(nz):
        q_s[d] = q_refs[d][:, :HD]
        do_s[d] = do_refs[d][...]
    for i in range(n_kv):
        first = kv_refs[i].shape[1] - 2 * HD
        k_s[i] = kv_refs[i][:, first : first + HD]
        v_s[i] = kv_refs[i][:, first + HD :]
    if chained:
        dq_ref[...] = before_ref[...]
    else:
        dq_ref[...] = jnp.zeros_like(dq_ref)

    @pl.loop(0, nz)
    def tables(d):
        q_index = ((z ^ d) * ring + r) * rows + lax.broadcasted_iota(jnp.int32, (1, rows), 1)
        begin = begin_of(q_index, ends_ref, count)
        begin_s[d] = begin
        shift_s[d] = jnp.log((finish_of(q_index, ends_ref, count) - begin).astype(F32))

    @pl.loop(0, n_kv)
    def per_key(i):
        k_block = (z ^ (i & (nz - 1))) * ring + (r ^ (first_dr + i // nz))
        k_start = k_block * rows
        dk_acc[...] = jnp.zeros_like(dk_acc)
        dv_acc[...] = jnp.zeros_like(dv_acc)

        @pl.loop(0, nz)
        def per_query(d):
            q_block = (z ^ d) * ring + r
            q_start = q_block * rows
            first_begin = begin_of(q_start, ends_ref, count)
            last_begin = begin_of(q_start + (rows - 1), ends_ref, count)
            needed = (k_block <= q_block) & (k_start + rows > first_begin)
            full = (k_block < q_block) & (k_start >= last_begin)

            def tile(masked):
                half = rows // 2
                for part in range(2):
                    at = slice(part * half, (part + 1) * half)
                    keys = k_s[i, at]
                    scores = nt(keys, q_s[d])
                    grown = jnp.exp(jnp.minimum(shift_s[d] - scores * FACTOR, CLAMP))
                    probs = pl.reciprocal(1.0 + grown, approx=True)
                    if masked:
                        k_index = (
                            k_start
                            + part * half
                            + lax.broadcasted_iota(jnp.int32, (half, 1), 0)
                        )
                        q_index = q_start + lax.broadcasted_iota(jnp.int32, (1, rows), 1)
                        allowed = (k_index <= q_index) & (k_index >= begin_s[d])
                        probs = jnp.where(allowed, probs, 0.0)
                    weight_grad = nt(v_s[i, at], do_s[d])
                    score_grad = (weight_grad * (probs * probs * grown)).astype(BF16)
                    dv_acc[at] += nn(probs.astype(BF16), do_s[d])
                    dk_acc[at] += nn(score_grad, q_s[d])
                    dq_ref[d] += tn(score_grad, keys)

            pl.when(needed & full)(functools.partial(tile, False))
            pl.when(needed & jnp.logical_not(full))(functools.partial(tile, True))

        dkv_s[i, :, :HD] = (dk_acc[...] * FACTOR).astype(dkv_s.dtype)
        dkv_s[i, :, HD:] = dv_acc[...].astype(dkv_s.dtype)

    for e in range(n_dr):
        for d in range(nz):
            dkv_refs[e][d] = dkv_s[e * nz + d]


def attend_back(
    place, ends, queries, out_grads, keys_values, before, nz, ring, first_dr, n_dr, kept, after=()
):
    rows = queries[0].shape[0]
    n_kv = nz * n_dr
    pairs = nz * n_kv / 2
    chained = before is not None
    return call(
        functools.partial(
            attend_back_body, nz, ring, n_dr, first_dr, chained, ends.shape[0]
        ),
        (jax.ShapeDtypeStruct((nz, rows, HD), F32),)
        + tuple(jax.ShapeDtypeStruct((nz, rows, 2 * HD), kept) for _ in range(n_dr)),
        [place, ends, *queries, *out_grads, *keys_values, *([before] if chained else [])],
        [whole(pltpu.SMEM)] * 2 + [whole(pltpu.VMEM)] * (2 * nz + n_kv + chained),
        pairs * 10 * rows * rows * HD * 2,
        2 * (2 * nz + 4 * n_kv) * rows * HD,
        pairs * 2 * rows * rows,
        after=after,
        out_specs=tuple(whole(pltpu.VMEM) for _ in range(1 + n_dr)),
        scratch_shapes=[
            pltpu.VMEM((nz, rows, HD), BF16),
            pltpu.VMEM((nz, rows, HD), BF16),
            pltpu.VMEM((n_kv, rows, HD), BF16),
            pltpu.VMEM((n_kv, rows, HD), BF16),
            pltpu.VMEM((nz, 1, rows), jnp.int32),
            pltpu.VMEM((nz, 1, rows), F32),
            pltpu.VMEM((n_kv, rows, 2 * HD), kept),
            pltpu.VMEM((rows, HD), F32),
            pltpu.VMEM((rows, HD), F32),
        ],
        vmem=16 + 2 * n_kv * rows * HD * 14 // MIB,
        name="attend_back",
    )


def finish_body(nz, dq_ref, dkv_ref, got_ref, cos_ref, sin_ref, *out_refs):
    for d in range(nz):
        cosine = cos_ref[d]
        signed = sin_ref[d]
        total = dkv_ref[d] + got_ref[d].astype(F32)
        out = out_refs[d]
        out[:, :HD] = unrotated(dq_ref[d] * FACTOR, cosine, signed).astype(BF16)
        out[:, HD : 2 * HD] = unrotated(total[:, :HD], cosine, signed).astype(BF16)
        out[:, 2 * HD :] = total[:, HD:].astype(BF16)


def finish_grads(dq, dkv, got, cosine, signed):
    nz, rows, _ = dq.shape
    return call(
        functools.partial(finish_body, nz),
        tuple(jax.ShapeDtypeStruct((rows, 3 * HD), BF16) for _ in range(nz)),
        [dq, dkv, got, cosine, signed],
        [whole(pltpu.VMEM)] * 5,
        12 * nz * rows * HD,
        nz * rows * HD * 30,
        out_specs=tuple(whole(pltpu.VMEM) for _ in range(nz)),
        name="finish_grads",
    )


def rows_at(place, width, height, tile_of):
    return pl.BlockSpec((height, width), lambda j, place: (tile_of(place), 0))


def place_rows(pieces, scratch, spot):
    size = pieces[0].shape[0]
    half = size * len(pieces)
    for i, piece in enumerate(pieces):
        at = pl.multiple_of(spot * half + i * size, size)
        scratch[pl.ds(at, size), :] = piece[...]


def upstream_body(place_ref, *refs):
    pieces, (w_ref, out_ref, x_s) = refs[:-3], refs[-3:]
    size = pieces[0].shape[0]

    @pl.when(pl.program_id(0) == 0)
    def _():
        for i, piece in enumerate(pieces):
            x_s[i * size : (i + 1) * size] = piece[...]

    out_ref[...] = nt(x_s[...], w_ref[...]).astype(BF16)


def hidden_upstream(place, pieces, weights, own, after=()):
    size, width = pieces[0].shape
    rows = size * len(pieces)
    units = weights.shape[0] // (2 if own else 1)
    tile = 512
    steps = units // tile
    first = (lambda place: place[3] * steps) if own else (lambda place: 0)
    return call(
        upstream_body,
        jax.ShapeDtypeStruct((rows, units), BF16),
        [place, *pieces, weights],
        [pl.BlockSpec((size, width), lambda j, place: (0, 0))] * len(pieces)
        + [pl.BlockSpec((tile, width), lambda j, place: (first(place) + j, 0))],
        2 * rows * width * units,
        2 * width * units + 4 * rows * units + 2 * rows * width,
        after=after,
        prefetch=1,
        grid=(steps,),
        out_specs=pl.BlockSpec((rows, tile), lambda j, place: (0, j)),
        scratch_shapes=[pltpu.VMEM((rows, width), BF16)],
        vmem=28,
        name="hidden_upstream",
    )


def hidden_body(place_ref, *refs):
    pieces, refs = refs[:-7], refs[-7:]
    wg_ref, wu_ref, dact_ref, act_ref, dg_ref, du_ref, x_s = refs
    size = pieces[0].shape[0]

    @pl.when(pl.program_id(0) == 0)
    def _():
        for i, piece in enumerate(pieces):
            x_s[i * size : (i + 1) * size] = piece[...]

    x = x_s[...]
    for first in range(0, act_ref.shape[1], 256):
        at = slice(first, first + 256)
        gate = nn(x, wg_ref[:, at])
        up = nn(x, wu_ref[:, at])
        dact = dact_ref[:, at].astype(F32)
        sig = jax.nn.sigmoid(gate)
        silu = gate * sig
        act_ref[:, at] = (silu * up).astype(BF16)
        dg_ref[:, at] = (dact * up * sig * (1.0 + gate * (1.0 - sig))).astype(BF16)
        du_ref[:, at] = (dact * silu).astype(BF16)


def hidden(place, pieces, w_gate, w_up, dact, own, after=()):
    size, width = pieces[0].shape
    rows = size * len(pieces)
    units = dact.shape[1]
    tile = 512
    steps = units // tile
    first = (lambda place: place[3] * steps) if own else (lambda place: 0)
    made = jax.ShapeDtypeStruct((rows, units), BF16)
    block = pl.BlockSpec((rows, tile), lambda j, place: (0, j))
    weight = pl.BlockSpec((width, tile), lambda j, place: (0, first(place) + j))
    return call(
        hidden_body,
        (made, made, made),
        [place, *pieces, w_gate, w_up, dact],
        [pl.BlockSpec((size, width), lambda j, place: (0, 0))] * len(pieces)
        + [weight, weight, block],
        4 * rows * width * units,
        4 * width * units + 8 * rows * units + 2 * rows * width,
        rows * units,
        after=after,
        prefetch=1,
        grid=(steps,),
        out_specs=(block, block, block),
        scratch_shapes=[pltpu.VMEM((rows, width), BF16)],
        vmem=36,
        name="hidden",
    )


def chunked(total, out_refs):
    size = out_refs[0].shape[0]
    for i, ref in enumerate(out_refs):
        ref[...] = total[i * size : (i + 1) * size].astype(ref.dtype)


def back_body(place_ref, dg_ref, dg_sib, du_ref, du_sib, wg_ref, wg_sib, wu_ref, wu_sib, *outs):
    chunked(
        nt(dg_ref[...], wg_ref[...])
        + nt(dg_sib[...], wg_sib[...])
        + nt(du_ref[...], wu_ref[...])
        + nt(du_sib[...], wu_sib[...]),
        outs,
    )


def hidden_back(place, dg, dg_sib, du, du_sib, w_gate, gate_sib, w_up, up_sib, chunks, after=()):
    rows, half = dg.shape
    width = w_gate.shape[0]
    tile = 512
    size = rows // chunks
    left = pl.BlockSpec((rows, half), lambda j, place: (0, 0))
    own = pl.BlockSpec((tile, half), lambda j, place: (j, place[3]))
    sib = pl.BlockSpec((tile, half), lambda j, place: (j, 0))
    return call(
        back_body,
        tuple(jax.ShapeDtypeStruct((size, width), BF16) for _ in range(chunks)),
        [place, dg, dg_sib, du, du_sib, w_gate, gate_sib, w_up, up_sib],
        [left] * 4 + [own, sib, own, sib],
        8 * rows * width * half,
        8 * width * half + 8 * rows * half + 2 * rows * width,
        after=after,
        prefetch=1,
        grid=(width // tile,),
        out_specs=tuple(pl.BlockSpec((size, tile), lambda j, place: (0, j)) for _ in range(chunks)),
        vmem=32,
        name="hidden_back",
    )


def down_body(place_ref, act_ref, act_sib, wd_ref, wd_sib, *outs):
    chunked(nn(act_ref[...], wd_ref[...]) + nn(act_sib[...], wd_sib[...]), outs)


def down(place, act, act_sib, w_down, down_sib, chunks, after=()):
    rows, half = act.shape
    width = w_down.shape[1]
    tile = 512
    size = rows // chunks
    left = pl.BlockSpec((rows, half), lambda j, place: (0, 0))
    return call(
        down_body,
        tuple(jax.ShapeDtypeStruct((size, width), BF16) for _ in range(chunks)),
        [place, act, act_sib, w_down, down_sib],
        [
            left,
            left,
            pl.BlockSpec((half, tile), lambda j, place: (place[3], j)),
            pl.BlockSpec((half, tile), lambda j, place: (0, j)),
        ],
        4 * rows * width * half,
        4 * width * half + 4 * rows * half + 2 * rows * width,
        after=after,
        prefetch=1,
        grid=(width // tile,),
        out_specs=tuple(pl.BlockSpec((size, tile), lambda j, place: (0, j)) for _ in range(chunks)),
        vmem=24,
        name="down",
    )


def heads_body(nz, contract, keep, place_ref, *refs):
    n_w = 1 if keep else 3
    pieces, refs = refs[:nz], refs[nz:]
    w_refs, (sib_ref, mine_ref), refs = refs[:n_w], refs[n_w : n_w + 2], refs[n_w + 2 :]
    joined = refs[:n_w]
    for d in range(nz):
        at = pl.multiple_of((place_ref[0] ^ d) * HD, HD)
        for i in range(n_w):
            joined[i][:, pl.ds(at, HD)] = pieces[d][:, i * HD : (i + 1) * HD]
    half = sib_ref.shape[0]
    core = place_ref[2] & 1

    def rows_of(start):
        start = pl.multiple_of(start, half)
        total = contract(joined[0][pl.ds(start, half), :], w_refs[0][...])
        for i in range(1, n_w):
            total = total + contract(joined[i][pl.ds(start, half), :], w_refs[i][...])
        return total

    sib_ref[...] = rows_of((1 - core) * half).astype(BF16)
    mine_ref[...] = rows_of(core * half)


def heads_project(place, pieces, weights, contract, keep, after=()):
    nz = len(pieces)
    rows = pieces[0].shape[0]
    n_w = len(weights)
    width = weights[0].shape[1] if contract is nn else weights[0].shape[0]
    half = rows // 2
    joined = (rows, nz * HD)
    out = (
        jax.ShapeDtypeStruct((half, width), BF16),
        jax.ShapeDtypeStruct((half, width), F32),
    ) + ((jax.ShapeDtypeStruct(joined, BF16),) if keep else ())
    return call(
        functools.partial(heads_body, nz, contract, keep),
        out,
        [place, *pieces, *weights],
        [whole(pltpu.SMEM)] + [whole(pltpu.VMEM)] * (nz + n_w),
        2 * rows * width * nz * HD * n_w,
        2 * n_w * (width * nz * HD + rows * nz * HD) + 3 * rows * width,
        after=after,
        out_specs=tuple(whole(pltpu.VMEM) for _ in out),
        scratch_shapes=() if keep else (pltpu.VMEM(joined, BF16),) * n_w,
        vmem=24,
        name="heads_project",
    )


def dheads_body(nz, n, place_ref, *refs):
    mine, refs = refs[:n], refs[n:]
    sibs, refs = refs[:n], refs[n:]
    w_ref, outs, x_s = refs[0], refs[1:-1], refs[-1]
    core = place_ref[2] & 1
    place_rows(mine, x_s, core)
    place_rows(sibs, x_s, 1 - core)
    x = x_s[...]
    wide = outs[0].shape[1]
    for d in range(nz):
        at = pl.multiple_of((place_ref[0] ^ d) * wide, wide)
        outs[d][...] = nt(x, w_ref[pl.ds(at, wide), :]).astype(BF16)


def heads_upstream(place, mine, sibs, w_out, nz, after=()):
    n = len(mine)
    size, width = mine[0].shape
    rows = 2 * n * size
    wide = w_out.shape[0] // nz
    return call(
        functools.partial(dheads_body, nz, n),
        tuple(jax.ShapeDtypeStruct((rows, wide), BF16) for _ in range(nz)),
        [place, *mine, *sibs, w_out],
        [whole(pltpu.SMEM)] + [whole(pltpu.VMEM)] * (2 * n + 1),
        2 * rows * width * nz * wide,
        2 * width * nz * wide + 2 * rows * nz * wide + 2 * rows * width,
        after=after,
        out_specs=tuple(whole(pltpu.VMEM) for _ in range(nz)),
        scratch_shapes=[pltpu.VMEM((rows, width), BF16)],
        name="heads_upstream",
    )


def sum_body(mine_ref, got_ref, *outs):
    chunked(mine_ref[...].astype(F32) + got_ref[...].astype(F32), outs)


def row_sum(mine, got, chunks, after=()):
    rows, width = mine.shape
    size = rows // chunks
    return call(
        sum_body,
        tuple(jax.ShapeDtypeStruct((size, width), BF16) for _ in range(chunks)),
        [mine, got],
        [whole(pltpu.VMEM)] * 2,
        rows * width,
        8 * rows * width,
        after=after,
        out_specs=tuple(whole(pltpu.VMEM) for _ in range(chunks)),
        name="row_sum",
    )


def scale_of(values):
    return lax.rsqrt(jnp.mean(values * values, axis=-1, keepdims=True) + EPSILON)


def norm_body(part_ref, got_ref, x_ref, gain_ref, res_ref, normed_ref):
    residual = x_ref[...].astype(F32) + (part_ref[...].astype(F32) + got_ref[...].astype(F32))
    res_ref[...] = residual
    normed_ref[...] = (residual * scale_of(residual) * gain_ref[...]).astype(BF16)


def norm_rows(part, got, x, gain, after=()):
    rows, width = part.shape
    return call(
        norm_body,
        (
            jax.ShapeDtypeStruct((rows, width), F32),
            jax.ShapeDtypeStruct((rows, width), BF16),
        ),
        [part, got, x, gain],
        [whole(pltpu.VMEM)] * 4,
        8 * rows * width,
        12 * rows * width,
        after=after,
        out_specs=(whole(pltpu.VMEM), whole(pltpu.VMEM)),
        name="norm_rows",
    )


def norm_back_body(part_ref, got_ref, values_ref, add_ref, gain_ref, *outs):
    upstream = part_ref[...].astype(F32) + got_ref[...].astype(F32)
    values = values_ref[...].astype(F32)
    scale = scale_of(values)
    normed = values * scale
    outs[-1][...] = jnp.sum(upstream * normed, axis=0, keepdims=True)
    weighted = upstream * gain_ref[...]
    grad = scale * (weighted - normed * jnp.mean(weighted * normed, axis=-1, keepdims=True))
    total = add_ref[...].astype(F32) + grad
    for ref in outs[:-1]:
        ref[...] = total.astype(ref.dtype)


def norm_back(part, got, values, add, gain, kinds, after=()):
    rows, width = part.shape
    return call(
        norm_back_body,
        tuple(jax.ShapeDtypeStruct((rows, width), kind) for kind in kinds)
        + (jax.ShapeDtypeStruct((1, width), F32),),
        [part, got, values, add, gain],
        [whole(pltpu.VMEM)] * 5,
        16 * rows * width,
        16 * rows * width,
        after=after,
        out_specs=tuple(whole(pltpu.VMEM) for _ in range(len(kinds) + 1)),
        name="norm_back",
    )


def add_body(part_ref, got_ref, res_ref, out_ref):
    out_ref[...] = (
        res_ref[...] + (part_ref[...].astype(F32) + got_ref[...].astype(F32))
    ).astype(BF16)


def add_rows(part, got, residual, after=()):
    return call(
        add_body,
        jax.ShapeDtypeStruct(part.shape, BF16),
        [part, got, residual],
        [whole(pltpu.VMEM)] * 3,
        part.size,
        10 * part.size,
        after=after,
        out_specs=whole(pltpu.VMEM),
        name="add_rows",
    )


def join_body(n, place_ref, *refs):
    core = place_ref[2] & 1
    place_rows(refs[:n], refs[-1], core)
    place_rows(refs[n : 2 * n], refs[-1], 1 - core)


def join_rows(place, mine, sibs, after=()):
    n = len(mine)
    size, width = mine[0].shape
    return call(
        functools.partial(join_body, n),
        jax.ShapeDtypeStruct((2 * n * size, width), BF16),
        [place, *mine, *sibs],
        [whole(pltpu.SMEM)] + [whole(pltpu.VMEM)] * (2 * n),
        0,
        8 * n * size * width,
        after=after,
        out_specs=whole(pltpu.VMEM),
        name="join_rows",
    )


def turn_body(n, block, offset_ref, order_ref, *refs):
    pieces, out_ref = refs[:n], refs[n]
    size, wide = pieces[0].shape
    unit = (
        lax.broadcasted_iota(jnp.int32, (block, block), 0)
        == lax.broadcasted_iota(jnp.int32, (block, block), 1)
    ).astype(F32).astype(BF16)
    for p in range(wide // block):
        at = pl.multiple_of(order_ref[p] * block, block)
        for j in range(n):
            to = pl.multiple_of(offset_ref[j] * size, size)
            made = nt(unit, pieces[j][:, pl.ds(at, block)]).astype(BF16)
            out_ref[p * block : (p + 1) * block, pl.ds(to, size)] = made


def turn(order, group, pieces, offsets=None, after=()):
    wide = pieces[0].shape[1]
    if group % 128 != 0:
        pieces = [
            jnp.concatenate(
                [
                    lax.dynamic_slice_in_dim(piece, order[p] * group, group, 1)
                    for p in range(order.shape[0])
                ],
                axis=1,
            )
            for piece in pieces
        ]
        block = math.gcd(256, wide)
        order_in = jnp.arange(wide // block, dtype=jnp.int32)
    else:
        block = group
        order_in = order
    n = len(pieces)
    size = pieces[0].shape[0]
    tokens = n * size
    if offsets is None:
        offsets = jnp.arange(n, dtype=jnp.int32)
    return call(
        functools.partial(turn_body, n, block),
        jax.ShapeDtypeStruct((wide, tokens), BF16),
        [offsets, order_in, *pieces],
        [whole(pltpu.SMEM)] * 2 + [whole(pltpu.VMEM)] * n,
        2 * tokens * wide * block,
        4 * tokens * wide,
        after=after,
        out_specs=whole(pltpu.VMEM),
        vmem=8 + 4 * tokens * wide // MIB,
        name="turn",
    )


def turn_all_body(block, place_ref, order_ref, x_ref, out_ref):
    n_mp, _, size, wide = x_ref.shape
    unit = (
        lax.broadcasted_iota(jnp.int32, (block, block), 0)
        == lax.broadcasted_iota(jnp.int32, (block, block), 1)
    ).astype(F32).astype(BF16)
    for p in range(wide // block):
        at = pl.multiple_of(order_ref[p] * block, block)
        for j in range(n_mp):
            made = nt(unit, x_ref[j, 0, :, pl.ds(at, block)]).astype(BF16)
            out_ref[p * block : (p + 1) * block, j * size : (j + 1) * size] = made


def turn_all(order, group, gathered, z):
    n_mp, nz, size, wide = gathered.shape
    if group % 128 != 0:
        gathered = jnp.concatenate(
            [
                lax.dynamic_slice_in_dim(gathered, order[p] * group, group, 3)
                for p in range(order.shape[0])
            ],
            axis=3,
        )
        block = math.gcd(256, wide)
        order_in = jnp.arange(wide // block, dtype=jnp.int32)
    else:
        block = group
        order_in = order
    tokens = n_mp * size
    return call(
        functools.partial(turn_all_body, block),
        jax.ShapeDtypeStruct((wide, nz * tokens), BF16),
        [z.reshape(1).astype(jnp.int32), order_in, gathered],
        [pl.BlockSpec((n_mp, 1, size, wide), lambda d, place, order: (0, place[0] ^ d, 0, 0))],
        2 * nz * tokens * wide * block,
        4 * nz * tokens * wide,
        prefetch=2,
        grid=(nz,),
        out_specs=pl.BlockSpec((wide, tokens), lambda d, place, order: (0, d)),
        vmem=24,
        name="turn_all",
    )


def weight_body(n, *refs):
    lefts, refs = refs[:n], refs[n:]
    rights, (sent_ref, kept_ref) = refs[:n], refs[n:]
    total = nn(lefts[0][...], rights[0][...])
    for i in range(1, n):
        total = total + nn(lefts[i][...], rights[i][...])
    half = pl.num_programs(0) // 2

    @pl.when(pl.program_id(0) < half)
    def _():
        sent_ref[...] = total.astype(BF16)

    @pl.when(pl.program_id(0) >= half)
    def _():
        kept_ref[...] = total.astype(BF16)


def weight_grad(lefts, rights, after=()):
    wide = lefts[0].shape[0]
    width = rights[0].shape[1]
    tokens = sum(left.shape[1] for left in lefts)
    steps = 4
    tile = wide // steps
    half = steps // 2
    made = jax.ShapeDtypeStruct((wide // 2, width), BF16)
    return call(
        functools.partial(weight_body, len(lefts)),
        (made,) * 2,
        [*lefts, *rights],
        [
            pl.BlockSpec((tile, left.shape[1]), lambda i: ((i + half) % steps, 0))
            for left in lefts
        ]
        + [pl.BlockSpec(right.shape, lambda i: (0, 0)) for right in rights],
        2 * tokens * wide * width,
        2 * (tokens * wide + tokens * width + wide * width),
        after=after,
        grid=(steps,),
        out_specs=(
            pl.BlockSpec((tile, width), lambda i: (jnp.minimum(i, half - 1), 0)),
            pl.BlockSpec((tile, width), lambda i: (jnp.maximum(i - half, 0), 0)),
        ),
        vmem=28,
        name="weight_grad",
    )


def sum3_body(n, *refs):
    total = refs[0][...].astype(F32)
    for ref in refs[1:n]:
        total = total + ref[...].astype(F32)
    low_ref, high_ref = refs[n:]
    low_ref[...] = total[0]
    high_ref[...] = total[1].astype(BF16)


def final_sum(terms, after=()):
    wide, width = terms[0].shape
    high = wide // 2
    tile = math.gcd(high, 128)
    block = pl.BlockSpec((2, tile, width), lambda i: (0, i, 0))
    out = pl.BlockSpec((tile, width), lambda i: (i, 0))
    return call(
        functools.partial(sum3_body, len(terms)),
        (
            jax.ShapeDtypeStruct((high, width), F32),
            jax.ShapeDtypeStruct((high, width), BF16),
        ),
        [term.reshape(2, high, width) for term in terms],
        [block] * len(terms),
        wide * width,
        wide * width * 8,
        after=after,
        grid=(high // tile,),
        out_specs=(out, out),
        name="final_sum",
    )


def merge_body(kept_ref, got_ref, low_ref, high_ref):
    total = kept_ref[...].astype(F32) + got_ref[...].astype(F32)
    low_ref[...] = total[0]
    high_ref[...] = total[1].astype(BF16)


def merge(kept, got, after=()):
    wide, width = kept.shape
    high = wide // 2
    tile = math.gcd(high, 128)
    operands = [kept.reshape(2, high, width), got.reshape(2, high, width)]
    block = pl.BlockSpec((2, tile, width), lambda i: (0, i, 0))
    out = pl.BlockSpec((tile, width), lambda i: (i, 0))
    return call(
        merge_body,
        (
            jax.ShapeDtypeStruct((high, width), F32),
            jax.ShapeDtypeStruct((high, width), BF16),
        ),
        operands,
        [block, block],
        wide * width,
        wide * width * 8,
        after=after,
        grid=(high // tile,),
        out_specs=(out, out),
        name="merge",
    )


def lay_body(turned, place_ref, own_ref, got_ref, out_ref):
    value = jnp.where(pl.program_id(0) == 0, own_ref[...], got_ref[...].astype(F32))
    out_ref[...] = value.T if turned else value


def lay(place, own, got, turned):
    rows, width = own.shape
    if turned:
        shape, block = (2 * width, rows), (width, rows)
        index = lambda i, place: (place[3] ^ i, 0)
    else:
        shape, block = (rows, 2 * width), (rows, width)
        index = lambda i, place: (0, place[3] ^ i)
    fixed = pl.BlockSpec((rows, width), lambda i, place: (0, 0))
    return call(
        functools.partial(lay_body, turned),
        jax.ShapeDtypeStruct(shape, F32),
        [place, own, got],
        [fixed, fixed],
        0,
        14 * rows * width,
        prefetch=1,
        grid=(2,),
        out_specs=pl.BlockSpec(block, index),
        name="lay",
    )


def qkv_sum_body(kept_ref, got_ref, own_ref, *outs):
    size = own_ref.shape[0]
    total = kept_ref[...].astype(F32) + got_ref[...].astype(F32)
    own_ref[...] = total[:size]
    for i, ref in enumerate(outs):
        ref[...] = total[(i + 1) * size : (i + 2) * size].astype(BF16)


def split_sum(kept, got, n):
    rows, width = kept.shape
    size = rows // n
    return call(
        qkv_sum_body,
        (jax.ShapeDtypeStruct((size, width), F32),)
        + (jax.ShapeDtypeStruct((size, width), BF16),) * (n - 1),
        [kept, got],
        [whole(pltpu.VMEM)] * 2,
        rows * width,
        8 * rows * width,
        out_specs=(whole(pltpu.VMEM),) * n,
        name="split_sum",
    )


def place_heads_body(nz, place_ref, *refs):
    pieces, outs = refs[:nz], refs[nz:]
    for d in range(nz):
        at = pl.multiple_of((place_ref[0] ^ d) * HD, HD)
        for i, out in enumerate(outs):
            out[:, pl.ds(at, HD)] = pieces[d][:, i * HD : (i + 1) * HD].astype(F32)


def place_heads(place, pieces):
    nz = len(pieces)
    rows = pieces[0].shape[0]
    return call(
        functools.partial(place_heads_body, nz),
        (jax.ShapeDtypeStruct((rows, nz * HD), F32),) * 3,
        [place, *pieces],
        [whole(pltpu.SMEM)] + [whole(pltpu.VMEM)] * nz,
        0,
        20 * rows * nz * HD,
        out_specs=(whole(pltpu.VMEM),) * 3,
        name="place_heads",
    )


def rope_tables(position):
    middle = HD // 2
    frequency = THETA ** (-(jnp.arange(middle, dtype=F32) * 2.0 / HD))
    angles = position.astype(F32)[..., None] * frequency
    cosine = jnp.cos(angles)
    sine = jnp.sin(angles)
    return (
        jnp.concatenate([cosine, cosine], axis=-1),
        jnp.concatenate([-sine, sine], axis=-1),
    )


def rms_scale(values):
    return lax.rsqrt(jnp.mean(values * values, axis=-1, keepdims=True) + EPSILON)


def layer(
    n_seq,
    n_mp,
    mixed_in,
    w_query,
    w_key,
    w_value,
    w_out,
    gain_attn,
    w_gate,
    w_up,
    w_down,
    gain_mlp,
    doc_ends,
    cotangent,
):
    rows, width = mixed_in.shape
    nz = w_query.shape[1] // HD
    ring = n_seq // nz
    bits = n_seq.bit_length() - 1
    low_bits = ring.bit_length() - 1
    units = w_gate.shape[1]
    half_units = units // 2
    half_rows = rows // 2
    group = width // n_seq
    pair_bit = bits - 2
    pair = 1 << pair_bit

    s = lax.axis_index("seq")
    m = lax.axis_index("mp")
    z, r = s // ring, s % ring
    core = m % 2
    side = m // 2
    low = (s >> pair_bit) & 1

    def seq_swap(v, distance):
        return lax.ppermute(v, "seq", [(i, i ^ distance) for i in range(n_seq)])

    def mp_swap(v, distance):
        return lax.ppermute(v, "mp", [(i, i ^ distance) for i in range(n_mp)])

    sum_bits = list(range(pair_bit)) + [bits - 1]
    places = []
    for p in range(n_seq):
        e = 0
        for at, bit in enumerate(sum_bits + [pair_bit]):
            if (p >> (bits - 1 - at)) & 1:
                e |= 1 << bit
        places.append(e)
    order = s ^ jnp.array(places, dtype=jnp.int32)

    ORDER.clear()

    place = jnp.stack([z, r, m, low]).astype(jnp.int32)
    blocks = (z ^ jnp.arange(nz, dtype=jnp.int32)) * ring + r
    token_index = blocks[:, None] * rows + jnp.arange(rows, dtype=jnp.int32)[None, :]
    ends_below = doc_ends[None, None, :] <= token_index[..., None]
    begin = jnp.max(jnp.where(ends_below, doc_ends, 0), axis=-1)
    cos_own, sin_own = rope_tables(token_index[0] - begin[0])
    weights = [w_query, w_key, w_value]
    half_z = nz // 2
    made = project_qkv(
        place,
        mixed_in,
        gain_attn.reshape(1, width),
        weights,
        cos_own,
        sin_own,
        list(range(half_z, nz)),
    )
    normed = made[-1]
    pieces = {half_z + i: made[i] for i in range(half_z)}
    made = project_qkv(place, normed, None, weights, cos_own, sin_own, list(range(half_z)))
    pieces.update({i: made[i] for i in range(half_z)})
    pieces = [pieces[0]] + [seq_swap(pieces[d], d * ring) for d in range(1, nz)]
    near = pieces
    keys_values = [near, [seq_swap(piece[:, HD:], 1) for piece in pieces]]
    for b in range(1, low_bits):
        keys_values = keys_values + [
            [seq_swap(kv[:, -2 * HD :], 1 << b) for kv in kvs] for kvs in keys_values
        ]
    queries = pieces

    quarter = rows // n_mp
    over_z = [[j * ring + i for j in range(nz)] for i in range(ring)]
    gathered = lax.all_gather(
        lax.dynamic_slice_in_dim(normed, m * quarter, quarter, 0),
        "seq",
        axis_index_groups=over_z,
    )

    halves = [
        lax.dynamic_slice_in_dim(w_down, low * half_units, half_units, 0),
        lax.dynamic_slice_in_dim(w_gate, low * half_units, half_units, 1),
        lax.dynamic_slice_in_dim(w_up, low * half_units, half_units, 1),
    ]
    cot_half = lax.dynamic_slice_in_dim(cotangent, core * half_rows, half_rows, 0)

    flat = [kv for kvs in keys_values for kv in kvs]
    cot_half, *halves = hold([cot_half, *halves], after=[pieces[1]])
    cot_pair = seq_swap(cot_half, pair)
    outs = attend(place, doc_ends, queries, flat, nz, ring)
    heads = [outs[0]] + [seq_swap(outs[d], d * ring) for d in range(1, nz)]
    size = half_rows // CHUNKS

    def chunks_of(values):
        return [values[i * size : (i + 1) * size] for i in range(CHUNKS)]

    x_chunks = chunks_of(lax.dynamic_slice_in_dim(mixed_in, core * half_rows, half_rows, 0))
    cot_chunks = chunks_of(cot_half)
    cot_all = cot_chunks + chunks_of(cot_pair)
    sib, mine, heads_placed = heads_project(place, heads, [w_out], nn, True)
    parts = row_sum(mine, mp_swap(sib, 1), CHUNKS, after=[cot_pair])
    down_sib, gate_sib, up_sib = [mp_swap(half, 1) for half in hold(halves)]
    gain_row = gain_mlp.reshape(1, width)
    residual, normed_own = [], []
    across = [mp_swap(part, 2) for part in parts]
    dact = hidden_upstream(place, cot_all, w_down, True)
    for i in range(CHUNKS):
        res, out = norm_rows(parts[i], across[i], x_chunks[i], gain_row)
        residual.append(res)
        normed_own.append(out)
    normed_all = normed_own + [seq_swap(part, pair) for part in normed_own]
    dact_sib = hidden_upstream(place, cot_all, down_sib, False)
    cot_turned = turn(order, group, cot_all)
    cot_turned = [cot_turned, mp_swap(cot_turned, 1)]

    last_low = 1 << sum_bits[pair_bit - 1]
    high = 1 << sum_bits[pair_bit]

    def low_sums(sent, kept):
        for bit in sum_bits[: pair_bit - 1]:
            kept, sent = merge(kept, seq_swap(sent, 1 << bit))
        return kept, seq_swap(sent, last_low)

    act_sib, dg_sib, du_sib = hidden(place, normed_all, gate_sib, up_sib, dact_sib, False)
    act_got, dg_got, du_got = [mp_swap(part, 1) for part in (act_sib, dg_sib, du_sib)]
    act, dg, du = hidden(place, normed_all, w_gate, w_up, dact, True)
    sent_down, kept_down = weight_grad(cot_turned, [act, act_got])
    kept_down, got_down = low_sums(sent_down, kept_down)
    made = hidden_back(
        place, dg, dg_sib, du, du_sib, w_gate, gate_sib, w_up, up_sib, 2 * CHUNKS
    )
    back_got = [seq_swap(made[CHUNKS + i], pair) for i in range(CHUNKS)]
    normed_turned = turn(order, group, normed_all)
    normed_turned = [normed_turned, mp_swap(normed_turned, 1)]
    back_parts, branch, residual_grad, gain_parts = [], [], [], []

    def upstream_of(i):
        back_parts.extend(row_sum(made[i], back_got[i], 1))
        return mp_swap(back_parts[i], 2)

    def through_norm(i, got):
        grad, low_grad, gain_part = norm_back(
            back_parts[i], got, residual[i], cot_chunks[i], gain_row, (F32, BF16)
        )
        residual_grad.append(grad)
        branch.append(low_grad)
        gain_parts.append(gain_part)

    got = [upstream_of(0)]
    sent_gate, kept_gate = weight_grad(normed_turned, [dg, dg_got])
    kept_gate, got_gate = low_sums(sent_gate, kept_gate)
    got += [upstream_of(i) for i in range(1, CHUNKS)]
    through_norm(0, got[0])
    kept_down, sent_down = merge(kept_down, got_down)
    high_down = seq_swap(sent_down, high)
    for i in range(1, CHUNKS):
        through_norm(i, got[i])
    gain_mlp_grad = sum(gain_parts)
    branch_sib = [mp_swap(part, 1) for part in branch]

    (gathered,) = hold([gathered])
    gathered = lax.all_gather(gathered, "mp")
    dheads = heads_upstream(place, branch, branch_sib, w_out, nz)
    out_grads = [dheads[0]] + [seq_swap(dheads[d], d * ring) for d in range(1, nz)]
    sent_up, kept_up = weight_grad(normed_turned, [du, du_got])
    far = [kv for kvs in keys_values[1:] for kv in kvs]
    dq_far, *dkv_far = attend_back(
        place, doc_ends, queries, out_grads, far, None, nz, ring, 1, ring - 1, BF16
    )
    summed = [None] + list(dkv_far)
    for b in reversed(range(low_bits)):
        bit = 1 << b
        for e in range(bit):
            got = seq_swap(summed[e | bit], bit)
            summed[e] = (
                got
                if summed[e] is None
                else (summed[e].astype(F32) + got.astype(F32)).astype(BF16)
            )
    own_down, pair_down = final_sum([kept_down, high_down])
    kept_gate, sent_gate = merge(kept_gate, got_gate)
    high_gate = seq_swap(sent_gate, high)
    dq, dkv = attend_back(
        place, doc_ends, queries, out_grads, near, dq_far, nz, ring, 0, 1, F32
    )
    cosine, signed = rope_tables(token_index - begin)
    grads = finish_grads(dq, dkv, summed[0], cosine, signed)
    own_grads = [grads[0]] + [seq_swap(grads[d], d * ring) for d in range(1, nz)]
    (sent_up,) = hold([sent_up])
    kept_up, got_up = low_sums(sent_up, kept_up)
    own_gate, pair_gate = final_sum([kept_gate, high_gate])
    spots = jnp.concatenate(
        [core * CHUNKS + jnp.arange(CHUNKS), (1 - core) * CHUNKS + jnp.arange(CHUNKS)]
    ).astype(jnp.int32)
    branch_turned = turn(order, group, branch + branch_sib, spots)
    sent_out, kept_out = weight_grad([branch_turned], [heads_placed])
    all_turned = turn_all(order, group, gathered, z)
    sent_qkv, kept_qkv = weight_grad([all_turned], [jnp.concatenate(grads, axis=0)])
    down_mine, down_theirs = down(place, act, act_sib, w_down, down_sib, 2)
    kept_up, sent_up = merge(kept_up, got_up)
    high_up = seq_swap(sent_up, high)
    (sent_out,) = hold([sent_out])
    kept_out, got_out = low_sums(sent_out, kept_out)

    sib, mine = heads_project(place, own_grads, weights, nt, False)
    parts = row_sum(mine, mp_swap(sib, 1), CHUNKS)
    across = [mp_swap(part, 2) for part in parts]
    (pair_down,) = hold([pair_down])
    pair_down = seq_swap(pair_down, pair)
    gain_row = gain_attn.reshape(1, width)
    grad_rows, gain_parts = [], []
    for i in range(CHUNKS):
        low_grad, gain_part = norm_back(
            parts[i], across[i], x_chunks[i], residual_grad[i], gain_row, (BF16,)
        )
        grad_rows.append(low_grad)
        gain_parts.append(gain_part)
    gain_attn_grad = sum(gain_parts)
    grad_sib = [mp_swap(part, 1) for part in grad_rows]
    kept_out, sent_out = merge(kept_out, got_out)
    high_out = seq_swap(sent_out, high)
    (sent_qkv,) = hold([sent_qkv])
    kept_qkv, got_qkv = low_sums(sent_qkv, kept_qkv)
    down_share = lay(place, own_down, pair_down, True)
    (pair_gate, down_theirs) = hold([pair_gate, down_theirs])
    pair_gate = seq_swap(pair_gate, pair)
    down_got = seq_swap(down_theirs, pair)
    input_grad = join_rows(place, grad_rows, grad_sib)
    own_up, pair_up = final_sum([kept_up, high_up])
    pair_up = seq_swap(pair_up, pair)
    gate_share = lay(place, own_gate, pair_gate, False)
    (down_part,) = row_sum(down_mine, down_got, 1)
    down_across = mp_swap(down_part, 2)
    own_qkv, *sent_qkv = split_sum(kept_qkv, got_qkv, nz)
    heads = [own_qkv] + [seq_swap(sent_qkv[d - 1], d * ring) for d in range(1, nz)]
    own_out, pair_out = final_sum([kept_out, high_out])
    pair_out = seq_swap(pair_out, pair)
    up_share = lay(place, own_up, pair_up, False)
    out_rows = add_rows(down_part, down_across, jnp.concatenate(residual, axis=0))
    out_sib = mp_swap(out_rows, 1)
    shares = place_heads(place, heads)
    mixed_out = join_rows(place, [out_rows], [out_sib])
    out_share = (own_out + pair_out.astype(F32)).T

    gains = jnp.concatenate([gain_attn_grad, gain_mlp_grad])
    gains = gains + mp_swap(gains, 1)
    for bit in range(bits):
        gains = gains + seq_swap(gains, 1 << bit)
    gains = lax.dynamic_slice_in_dim(gains, s * group, group, 1)

    return (
        mixed_out,
        input_grad,
        shares[0],
        shares[1],
        shares[2],
        out_share,
        gains[0],
        gate_share,
        up_share,
        down_share,
        gains[1],
    )


def solution(mesh):
    placed = (
        P("seq", None),
        P(None, "mp"),
        P(None, "mp"),
        P(None, "mp"),
        P("mp", None),
        P(),
        P(None, "mp"),
        P(None, "mp"),
        P("mp", None),
        P(),
        P(),
        P("seq", None),
    )
    return jax.shard_map(
        functools.partial(layer, mesh.shape["seq"], mesh.shape["mp"]),
        mesh=mesh,
        in_specs=placed,
        out_specs=(
            P("seq", None),
            P("seq", None),
            P("seq", "mp"),
            P("seq", "mp"),
            P("seq", "mp"),
            P("mp", "seq"),
            P("seq"),
            P("seq", "mp"),
            P("seq", "mp"),
            P("mp", "seq"),
            P("seq"),
        ),
        check_vma=False,
    )
```

```python
import functools
import math
import types

import jax
import jax.numpy as jnp
from jax import lax
from jax.experimental import pallas as pl
from jax.experimental.pallas import tpu as pltpu
from jax.sharding import PartitionSpec as P

HD = 128
EPSILON = 1e-05
THETA = 10000.0
FACTOR = 1.0 / math.sqrt(HD)
CLAMP = 80.0
CHUNKS = 2
SHARE = 0.5
ORDER = []
MIB = 1024 * 1024
F32 = jnp.float32
BF16 = jnp.bfloat16


def nn(left, right):
    return lax.dot_general(left, right, (((1,), (0,)), ((), ())), preferred_element_type=F32)


def nt(left, right):
    return lax.dot_general(left, right, (((1,), (1,)), ((), ())), preferred_element_type=F32)


def tn(left, right):
    return lax.dot_general(left, right, (((0,), (0,)), ((), ())), preferred_element_type=F32)


def call(
    body,
    out_shape,
    operands,
    in_specs,
    flops,
    moved,
    transcendentals=0,
    after=(),
    prefetch=0,
    chain=True,
    vmem=20,
    **kwargs,
):
    n = prefetch + len(in_specs)
    after = list(after) + (ORDER if chain else [])

    def kernel(*refs):
        body(*refs[:n], *refs[n + len(after) :])

    in_specs = list(in_specs) + [pl.BlockSpec(memory_space=pl.ANY)] * len(after)
    if prefetch:
        kwargs = {
            "name": kwargs.pop("name"),
            "grid_spec": pltpu.PrefetchScalarGridSpec(
                num_scalar_prefetch=prefetch, in_specs=in_specs, **kwargs
            ),
        }
    else:
        kwargs["in_specs"] = in_specs
    made = pl.pallas_call(
        kernel,
        out_shape=out_shape,
        compiler_params=pltpu.CompilerParams(vmem_limit_bytes=vmem * MIB),
        cost_estimate=pl.CostEstimate(
            flops=int(flops / SHARE),
            bytes_accessed=int(moved / SHARE),
            transcendentals=int(transcendentals / SHARE),
        ),
        **kwargs,
    )(*operands, *after)
    if chain:
        ORDER[:] = [made[0] if isinstance(made, (tuple, list)) else made]
    return made


def hold(values, after=()):
    n = len(values)
    made = lax.optimization_barrier((*values, *ORDER, *after))
    ORDER[:] = made[n : n + len(ORDER)]
    return list(made[:n])


def whole(memory):
    return pl.BlockSpec(memory_space=memory)


def rotated(values, cosine, signed):
    return values * cosine + pltpu.roll(values, HD // 2, 1) * signed


def unrotated(values, cosine, signed):
    return values * cosine - pltpu.roll(values, HD // 2, 1) * signed


def qkv_body(n, fresh, place_ref, *refs):
    if fresh:
        x_ref, gain_ref, refs = refs[0], refs[1], refs[2:]
    else:
        x_ref, refs = refs[0], refs[1:]
    wq_ref, wk_ref, wv_ref, cos_ref, sin_ref = refs[:5]
    outs, (w_s, x_s) = refs[5 : 5 + n], refs[-2:]
    step = pl.program_id(0)

    @pl.when(step == 0)
    def _():
        if fresh:
            x = x_ref[...].astype(F32)
            x_s[...] = (x * scale_of(x) * gain_ref[...]).astype(BF16)
            refs[5 + n][...] = x_s[...]
        else:
            x_s[...] = x_ref[...]

    w_s[:, :HD] = wq_ref[...]
    w_s[:, HD : 2 * HD] = wk_ref[...]
    w_s[:, 2 * HD :] = wv_ref[...]
    made = nn(x_s[...], w_s[...])
    cosine = cos_ref[...]
    signed = sin_ref[...]
    query = rotated(made[:, :HD], cosine, signed).astype(BF16)
    key = rotated(made[:, HD : 2 * HD], cosine, signed).astype(BF16)
    value = made[:, 2 * HD :].astype(BF16)
    for i in range(n):

        @pl.when(step == i)
        def _(i=i):
            outs[i][:, :HD] = query
            outs[i][:, HD : 2 * HD] = key
            outs[i][:, 2 * HD :] = value


def project_qkv(place, x, gain, weights, cosine, signed, spots):
    n = len(spots)
    rows, width = x.shape
    fresh = gain is not None
    fixed = pl.BlockSpec((rows, width), lambda i, place: (0, 0))
    table = pl.BlockSpec((rows, HD), lambda i, place: (0, 0))
    first = spots[0]
    assert list(spots) == [first ^ i for i in range(n)]
    weight = pl.BlockSpec((width, HD), lambda i, place: (0, place[0] ^ first ^ i))
    piece = jax.ShapeDtypeStruct((rows, 3 * HD), BF16)
    return call(
        functools.partial(qkv_body, n, fresh),
        (piece,) * n + ((jax.ShapeDtypeStruct(x.shape, BF16),) if fresh else ()),
        [place, x] + ([gain] if fresh else []) + [*weights, cosine, signed],
        [fixed]
        + ([pl.BlockSpec((1, width), lambda i, place: (0, 0))] if fresh else [])
        + [weight] * 3
        + [table] * 2,
        6 * n * rows * width * HD,
        4 * rows * width + 6 * n * width * HD + 6 * n * rows * HD,
        prefetch=1,
        grid=(n,),
        out_specs=(pl.BlockSpec((rows, 3 * HD), lambda i, place: (0, 0)),) * n
        + ((fixed,) if fresh else ()),
        scratch_shapes=[pltpu.VMEM((width, 3 * HD), BF16), pltpu.VMEM((rows, width), BF16)],
        vmem=60,
        name="project_qkv",
    )


def begin_of(index, ends_ref, count):
    begin = jnp.zeros_like(index)
    for e in range(count):
        end = ends_ref[e]
        begin = jnp.where(end <= index, jnp.maximum(begin, end), begin)
    return begin


def finish_of(index, ends_ref, count):
    finish = jnp.zeros_like(index) + ends_ref[count - 1]
    for e in range(count):
        end = ends_ref[e]
        finish = jnp.where(end > index, jnp.minimum(finish, end), finish)
    return finish


def attend_body(nz, ring, count, place_ref, ends_ref, *refs):
    n_kv = nz * ring
    q_refs, refs = refs[:nz], refs[nz:]
    kv_refs, refs = refs[:n_kv], refs[n_kv:]
    o_refs, refs = refs[:nz], refs[nz:]
    q_s, k_s, v_s, o_s, acc = refs
    z, r = place_ref[0], place_ref[1]
    rows = q_s.shape[1]
    for d in range(nz):
        q_s[d] = q_refs[d][:, :HD]
    for i in range(n_kv):
        first = kv_refs[i].shape[1] - 2 * HD
        k_s[i] = kv_refs[i][:, first : first + HD]
        v_s[i] = kv_refs[i][:, first + HD :]

    @pl.loop(0, nz)
    def per_query(d):
        q_block = (z ^ d) * ring + r
        q_start = q_block * rows
        q_index = q_start + lax.broadcasted_iota(jnp.int32, (rows, 1), 0)
        begin = begin_of(q_index, ends_ref, count)
        shift = jnp.log((finish_of(q_index, ends_ref, count) - begin).astype(F32))
        first_begin = begin_of(q_start, ends_ref, count)
        last_begin = begin_of(q_start + (rows - 1), ends_ref, count)
        acc[...] = jnp.zeros_like(acc)

        @pl.loop(0, n_kv)
        def per_key(i):
            k_block = (z ^ (i & (nz - 1))) * ring + (r ^ (i // nz))
            k_start = k_block * rows
            needed = (k_block <= q_block) & (k_start + rows > first_begin)
            full = (k_block < q_block) & (k_start >= last_begin)

            def tile(masked):
                half = rows // 2
                for part in range(2):
                    at = slice(part * half, (part + 1) * half)
                    scores = nt(q_s[d, at], k_s[i])
                    grown = jnp.exp(jnp.minimum(shift[at] - scores * FACTOR, CLAMP))
                    probs = pl.reciprocal(1.0 + grown, approx=True)
                    if masked:
                        k_index = k_start + lax.broadcasted_iota(jnp.int32, (1, rows), 1)
                        allowed = (k_index <= q_index[at]) & (k_index >= begin[at])
                        probs = jnp.where(allowed, probs, 0.0)
                    acc[at] += nn(probs.astype(BF16), v_s[i])

            pl.when(needed & full)(functools.partial(tile, False))
            pl.when(needed & jnp.logical_not(full))(functools.partial(tile, True))

        o_s[d] = acc[...].astype(BF16)

    for d in range(nz):
        o_refs[d][...] = o_s[d]


def attend(place, ends, queries, keys_values, nz, ring, after=()):
    rows = queries[0].shape[0]
    n_kv = nz * ring
    pairs = nz * n_kv / 2
    return call(
        functools.partial(attend_body, nz, ring, ends.shape[0]),
        tuple(jax.ShapeDtypeStruct((rows, HD), BF16) for _ in range(nz)),
        [place, ends, *queries, *keys_values],
        [whole(pltpu.SMEM)] * 2 + [whole(pltpu.VMEM)] * (nz + n_kv),
        pairs * 4 * rows * rows * HD * 2,
        2 * (2 * nz + 2 * n_kv) * rows * HD,
        pairs * 2 * rows * rows,
        after=after,
        out_specs=tuple(whole(pltpu.VMEM) for _ in range(nz)),
        scratch_shapes=[
            pltpu.VMEM((nz, rows, HD), BF16),
            pltpu.VMEM((n_kv, rows, HD), BF16),
            pltpu.VMEM((n_kv, rows, HD), BF16),
            pltpu.VMEM((nz, rows, HD), BF16),
            pltpu.VMEM((rows, HD), F32),
        ],
        vmem=12 + 2 * n_kv * rows * HD * 8 // MIB,
        name="attend",
    )


def attend_back_body(nz, ring, n_dr, first_dr, chained, count, place_ref, ends_ref, *refs):
    n_kv = nz * n_dr
    q_refs, refs = refs[:nz], refs[nz:]
    do_refs, refs = refs[:nz], refs[nz:]
    kv_refs, refs = refs[:n_kv], refs[n_kv:]
    if chained:
        before_ref, refs = refs[0], refs[1:]
    dq_ref, refs = refs[0], refs[1:]
    dkv_refs, refs = refs[:n_dr], refs[n_dr:]
    q_s, do_s, k_s, v_s, begin_s, shift_s, dkv_s, dk_acc, dv_acc = refs
    z, r = place_ref[0], place_ref[1]
    rows = q_s.shape[1]
    for d in range(nz):
        q_s[d] = q_refs[d][:, :HD]
        do_s[d] = do_refs[d][...]
    for i in range(n_kv):
        first = kv_refs[i].shape[1] - 2 * HD
        k_s[i] = kv_refs[i][:, first : first + HD]
        v_s[i] = kv_refs[i][:, first + HD :]
    if chained:
        dq_ref[...] = before_ref[...]
    else:
        dq_ref[...] = jnp.zeros_like(dq_ref)

    @pl.loop(0, nz)
    def tables(d):
        q_index = ((z ^ d) * ring + r) * rows + lax.broadcasted_iota(jnp.int32, (1, rows), 1)
        begin = begin_of(q_index, ends_ref, count)
        begin_s[d] = begin
        shift_s[d] = jnp.log((finish_of(q_index, ends_ref, count) - begin).astype(F32))

    @pl.loop(0, n_kv)
    def per_key(i):
        k_block = (z ^ (i & (nz - 1))) * ring + (r ^ (first_dr + i // nz))
        k_start = k_block * rows
        dk_acc[...] = jnp.zeros_like(dk_acc)
        dv_acc[...] = jnp.zeros_like(dv_acc)

        @pl.loop(0, nz)
        def per_query(d):
            q_block = (z ^ d) * ring + r
            q_start = q_block * rows
            first_begin = begin_of(q_start, ends_ref, count)
            last_begin = begin_of(q_start + (rows - 1), ends_ref, count)
            needed = (k_block <= q_block) & (k_start + rows > first_begin)
            full = (k_block < q_block) & (k_start >= last_begin)

            def tile(masked):
                half = rows // 2
                for part in range(2):
                    at = slice(part * half, (part + 1) * half)
                    keys = k_s[i, at]
                    scores = nt(keys, q_s[d])
                    grown = jnp.exp(jnp.minimum(shift_s[d] - scores * FACTOR, CLAMP))
                    probs = pl.reciprocal(1.0 + grown, approx=True)
                    if masked:
                        k_index = (
                            k_start
                            + part * half
                            + lax.broadcasted_iota(jnp.int32, (half, 1), 0)
                        )
                        q_index = q_start + lax.broadcasted_iota(jnp.int32, (1, rows), 1)
                        allowed = (k_index <= q_index) & (k_index >= begin_s[d])
                        probs = jnp.where(allowed, probs, 0.0)
                    weight_grad = nt(v_s[i, at], do_s[d])
                    score_grad = (weight_grad * (probs * probs * grown)).astype(BF16)
                    dv_acc[at] += nn(probs.astype(BF16), do_s[d])
                    dk_acc[at] += nn(score_grad, q_s[d])
                    dq_ref[d] += tn(score_grad, keys)

            pl.when(needed & full)(functools.partial(tile, False))
            pl.when(needed & jnp.logical_not(full))(functools.partial(tile, True))

        dkv_s[i, :, :HD] = (dk_acc[...] * FACTOR).astype(dkv_s.dtype)
        dkv_s[i, :, HD:] = dv_acc[...].astype(dkv_s.dtype)

    for e in range(n_dr):
        for d in range(nz):
            dkv_refs[e][d] = dkv_s[e * nz + d]


def attend_back(
    place, ends, queries, out_grads, keys_values, before, nz, ring, first_dr, n_dr, kept, after=()
):
    rows = queries[0].shape[0]
    n_kv = nz * n_dr
    pairs = nz * n_kv / 2
    chained = before is not None
    return call(
        functools.partial(
            attend_back_body, nz, ring, n_dr, first_dr, chained, ends.shape[0]
        ),
        (jax.ShapeDtypeStruct((nz, rows, HD), F32),)
        + tuple(jax.ShapeDtypeStruct((nz, rows, 2 * HD), kept) for _ in range(n_dr)),
        [place, ends, *queries, *out_grads, *keys_values, *([before] if chained else [])],
        [whole(pltpu.SMEM)] * 2 + [whole(pltpu.VMEM)] * (2 * nz + n_kv + chained),
        pairs * 10 * rows * rows * HD * 2,
        2 * (2 * nz + 4 * n_kv) * rows * HD,
        pairs * 2 * rows * rows,
        after=after,
        out_specs=tuple(whole(pltpu.VMEM) for _ in range(1 + n_dr)),
        scratch_shapes=[
            pltpu.VMEM((nz, rows, HD), BF16),
            pltpu.VMEM((nz, rows, HD), BF16),
            pltpu.VMEM((n_kv, rows, HD), BF16),
            pltpu.VMEM((n_kv, rows, HD), BF16),
            pltpu.VMEM((nz, 1, rows), jnp.int32),
            pltpu.VMEM((nz, 1, rows), F32),
            pltpu.VMEM((n_kv, rows, 2 * HD), kept),
            pltpu.VMEM((rows, HD), F32),
            pltpu.VMEM((rows, HD), F32),
        ],
        vmem=16 + 2 * n_kv * rows * HD * 14 // MIB,
        name="attend_back",
    )


def finish_body(nz, dq_ref, dkv_ref, got_ref, cos_ref, sin_ref, *out_refs):
    for d in range(nz):
        cosine = cos_ref[d]
        signed = sin_ref[d]
        total = dkv_ref[d] + got_ref[d].astype(F32)
        out = out_refs[d]
        out[:, :HD] = unrotated(dq_ref[d] * FACTOR, cosine, signed).astype(BF16)
        out[:, HD : 2 * HD] = unrotated(total[:, :HD], cosine, signed).astype(BF16)
        out[:, 2 * HD :] = total[:, HD:].astype(BF16)


def finish_grads(dq, dkv, got, cosine, signed):
    nz, rows, _ = dq.shape
    return call(
        functools.partial(finish_body, nz),
        tuple(jax.ShapeDtypeStruct((rows, 3 * HD), BF16) for _ in range(nz)),
        [dq, dkv, got, cosine, signed],
        [whole(pltpu.VMEM)] * 5,
        12 * nz * rows * HD,
        nz * rows * HD * 30,
        out_specs=tuple(whole(pltpu.VMEM) for _ in range(nz)),
        name="finish_grads",
    )


def rows_at(place, width, height, tile_of):
    return pl.BlockSpec((height, width), lambda j, place: (tile_of(place), 0))


def place_rows(pieces, scratch, spot):
    size = pieces[0].shape[0]
    half = size * len(pieces)
    for i, piece in enumerate(pieces):
        at = pl.multiple_of(spot * half + i * size, size)
        scratch[pl.ds(at, size), :] = piece[...]


def upstream_body(place_ref, *refs):
    pieces, (w_ref, out_ref, x_s) = refs[:-3], refs[-3:]
    size = pieces[0].shape[0]

    @pl.when(pl.program_id(0) == 0)
    def _():
        for i, piece in enumerate(pieces):
            x_s[i * size : (i + 1) * size] = piece[...]

    out_ref[...] = nt(x_s[...], w_ref[...]).astype(BF16)


def hidden_upstream(place, pieces, weights, own, after=()):
    size, width = pieces[0].shape
    rows = size * len(pieces)
    units = weights.shape[0] // (2 if own else 1)
    tile = 512
    steps = units // tile
    first = (lambda place: place[3] * steps) if own else (lambda place: 0)
    return call(
        upstream_body,
        jax.ShapeDtypeStruct((rows, units), BF16),
        [place, *pieces, weights],
        [pl.BlockSpec((size, width), lambda j, place: (0, 0))] * len(pieces)
        + [pl.BlockSpec((tile, width), lambda j, place: (first(place) + j, 0))],
        2 * rows * width * units,
        2 * width * units + 4 * rows * units + 2 * rows * width,
        after=after,
        prefetch=1,
        grid=(steps,),
        out_specs=pl.BlockSpec((rows, tile), lambda j, place: (0, j)),
        scratch_shapes=[pltpu.VMEM((rows, width), BF16)],
        vmem=52,
        name="hidden_upstream",
    )


def hidden_body(place_ref, *refs):
    pieces, refs = refs[:-7], refs[-7:]
    wg_ref, wu_ref, dact_ref, act_ref, dg_ref, du_ref, x_s = refs
    size = pieces[0].shape[0]

    @pl.when(pl.program_id(0) == 0)
    def _():
        for i, piece in enumerate(pieces):
            x_s[i * size : (i + 1) * size] = piece[...]

    x = x_s[...]
    for first in range(0, act_ref.shape[1], 256):
        at = slice(first, first + 256)
        gate = nn(x, wg_ref[:, at])
        up = nn(x, wu_ref[:, at])
        dact = dact_ref[:, at].astype(F32)
        sig = jax.nn.sigmoid(gate)
        silu = gate * sig
        act_ref[:, at] = (silu * up).astype(BF16)
        dg_ref[:, at] = (dact * up * sig * (1.0 + gate * (1.0 - sig))).astype(BF16)
        du_ref[:, at] = (dact * silu).astype(BF16)


def hidden(place, pieces, w_gate, w_up, dact, own, after=()):
    size, width = pieces[0].shape
    rows = size * len(pieces)
    units = dact.shape[1]
    tile = 512
    steps = units // tile
    first = (lambda place: place[3] * steps) if own else (lambda place: 0)
    made = jax.ShapeDtypeStruct((rows, units), BF16)
    block = pl.BlockSpec((rows, tile), lambda j, place: (0, j))
    weight = pl.BlockSpec((width, tile), lambda j, place: (0, first(place) + j))
    return call(
        hidden_body,
        (made, made, made),
        [place, *pieces, w_gate, w_up, dact],
        [pl.BlockSpec((size, width), lambda j, place: (0, 0))] * len(pieces)
        + [weight, weight, block],
        4 * rows * width * units,
        4 * width * units + 8 * rows * units + 2 * rows * width,
        rows * units,
        after=after,
        prefetch=1,
        grid=(steps,),
        out_specs=(block, block, block),
        scratch_shapes=[pltpu.VMEM((rows, width), BF16)],
        vmem=52,
        name="hidden",
    )


def chunked(total, out_refs):
    size = out_refs[0].shape[0]
    for i, ref in enumerate(out_refs):
        ref[...] = total[i * size : (i + 1) * size].astype(ref.dtype)


def back_body(place_ref, dg_ref, dg_sib, du_ref, du_sib, wg_ref, wg_sib, wu_ref, wu_sib, *outs):
    chunked(
        nt(dg_ref[...], wg_ref[...])
        + nt(dg_sib[...], wg_sib[...])
        + nt(du_ref[...], wu_ref[...])
        + nt(du_sib[...], wu_sib[...]),
        outs,
    )


def hidden_back(place, dg, dg_sib, du, du_sib, w_gate, gate_sib, w_up, up_sib, chunks, after=()):
    rows, half = dg.shape
    width = w_gate.shape[0]
    tile = 512
    size = rows // chunks
    left = pl.BlockSpec((rows, half), lambda j, place: (0, 0))
    own = pl.BlockSpec((tile, half), lambda j, place: (j, place[3]))
    sib = pl.BlockSpec((tile, half), lambda j, place: (j, 0))
    return call(
        back_body,
        tuple(jax.ShapeDtypeStruct((size, width), BF16) for _ in range(chunks)),
        [place, dg, dg_sib, du, du_sib, w_gate, gate_sib, w_up, up_sib],
        [left] * 4 + [own, sib, own, sib],
        8 * rows * width * half,
        8 * width * half + 8 * rows * half + 2 * rows * width,
        after=after,
        prefetch=1,
        grid=(width // tile,),
        out_specs=tuple(pl.BlockSpec((size, tile), lambda j, place: (0, j)) for _ in range(chunks)),
        vmem=52,
        name="hidden_back",
    )


def down_body(place_ref, act_ref, act_sib, wd_ref, wd_sib, *outs):
    chunked(nn(act_ref[...], wd_ref[...]) + nn(act_sib[...], wd_sib[...]), outs)


def down(place, act, act_sib, w_down, down_sib, chunks, after=()):
    rows, half = act.shape
    width = w_down.shape[1]
    tile = 512
    size = rows // chunks
    left = pl.BlockSpec((rows, half), lambda j, place: (0, 0))
    return call(
        down_body,
        tuple(jax.ShapeDtypeStruct((size, width), BF16) for _ in range(chunks)),
        [place, act, act_sib, w_down, down_sib],
        [
            left,
            left,
            pl.BlockSpec((half, tile), lambda j, place: (place[3], j)),
            pl.BlockSpec((half, tile), lambda j, place: (0, j)),
        ],
        4 * rows * width * half,
        4 * width * half + 4 * rows * half + 2 * rows * width,
        after=after,
        prefetch=1,
        grid=(width // tile,),
        out_specs=tuple(pl.BlockSpec((size, tile), lambda j, place: (0, j)) for _ in range(chunks)),
        vmem=52,
        name="down",
    )


def heads_body(nz, contract, keep, place_ref, *refs):
    n_w = 1 if keep else 3
    pieces, refs = refs[:nz], refs[nz:]
    w_refs, (sib_ref, mine_ref), refs = refs[:n_w], refs[n_w : n_w + 2], refs[n_w + 2 :]
    joined = refs[:n_w]
    for d in range(nz):
        at = pl.multiple_of((place_ref[0] ^ d) * HD, HD)
        for i in range(n_w):
            joined[i][:, pl.ds(at, HD)] = pieces[d][:, i * HD : (i + 1) * HD]
    half = sib_ref.shape[0]
    core = place_ref[2] & 1

    def rows_of(start):
        start = pl.multiple_of(start, half)
        total = contract(joined[0][pl.ds(start, half), :], w_refs[0][...])
        for i in range(1, n_w):
            total = total + contract(joined[i][pl.ds(start, half), :], w_refs[i][...])
        return total

    sib_ref[...] = rows_of((1 - core) * half).astype(BF16)
    mine_ref[...] = rows_of(core * half)


def heads_project(place, pieces, weights, contract, keep, after=()):
    nz = len(pieces)
    rows = pieces[0].shape[0]
    n_w = len(weights)
    width = weights[0].shape[1] if contract is nn else weights[0].shape[0]
    half = rows // 2
    joined = (rows, nz * HD)
    out = (
        jax.ShapeDtypeStruct((half, width), BF16),
        jax.ShapeDtypeStruct((half, width), F32),
    ) + ((jax.ShapeDtypeStruct(joined, BF16),) if keep else ())
    return call(
        functools.partial(heads_body, nz, contract, keep),
        out,
        [place, *pieces, *weights],
        [whole(pltpu.SMEM)] + [whole(pltpu.VMEM)] * (nz + n_w),
        2 * rows * width * nz * HD * n_w,
        2 * n_w * (width * nz * HD + rows * nz * HD) + 3 * rows * width,
        after=after,
        out_specs=tuple(whole(pltpu.VMEM) for _ in out),
        scratch_shapes=() if keep else (pltpu.VMEM(joined, BF16),) * n_w,
        vmem=24,
        name="heads_project",
    )


def dheads_body(nz, n, place_ref, *refs):
    mine, refs = refs[:n], refs[n:]
    sibs, refs = refs[:n], refs[n:]
    w_ref, outs, x_s = refs[0], refs[1:-1], refs[-1]
    core = place_ref[2] & 1
    place_rows(mine, x_s, core)
    place_rows(sibs, x_s, 1 - core)
    x = x_s[...]
    wide = outs[0].shape[1]
    for d in range(nz):
        at = pl.multiple_of((place_ref[0] ^ d) * wide, wide)
        outs[d][...] = nt(x, w_ref[pl.ds(at, wide), :]).astype(BF16)


def heads_upstream(place, mine, sibs, w_out, nz, after=()):
    n = len(mine)
    size, width = mine[0].shape
    rows = 2 * n * size
    wide = w_out.shape[0] // nz
    return call(
        functools.partial(dheads_body, nz, n),
        tuple(jax.ShapeDtypeStruct((rows, wide), BF16) for _ in range(nz)),
        [place, *mine, *sibs, w_out],
        [whole(pltpu.SMEM)] + [whole(pltpu.VMEM)] * (2 * n + 1),
        2 * rows * width * nz * wide,
        2 * width * nz * wide + 2 * rows * nz * wide + 2 * rows * width,
        after=after,
        out_specs=tuple(whole(pltpu.VMEM) for _ in range(nz)),
        scratch_shapes=[pltpu.VMEM((rows, width), BF16)],
        name="heads_upstream",
    )


def sum_body(mine_ref, got_ref, *outs):
    chunked(mine_ref[...].astype(F32) + got_ref[...].astype(F32), outs)


def row_sum(mine, got, chunks, after=()):
    rows, width = mine.shape
    size = rows // chunks
    return call(
        sum_body,
        tuple(jax.ShapeDtypeStruct((size, width), BF16) for _ in range(chunks)),
        [mine, got],
        [whole(pltpu.VMEM)] * 2,
        rows * width,
        8 * rows * width,
        after=after,
        out_specs=tuple(whole(pltpu.VMEM) for _ in range(chunks)),
        name="row_sum",
    )


def scale_of(values):
    return lax.rsqrt(jnp.mean(values * values, axis=-1, keepdims=True) + EPSILON)


def norm_body(part_ref, got_ref, x_ref, gain_ref, res_ref, normed_ref):
    residual = x_ref[...].astype(F32) + (part_ref[...].astype(F32) + got_ref[...].astype(F32))
    res_ref[...] = residual
    normed_ref[...] = (residual * scale_of(residual) * gain_ref[...]).astype(BF16)


def norm_rows(part, got, x, gain, after=()):
    rows, width = part.shape
    return call(
        norm_body,
        (
            jax.ShapeDtypeStruct((rows, width), F32),
            jax.ShapeDtypeStruct((rows, width), BF16),
        ),
        [part, got, x, gain],
        [whole(pltpu.VMEM)] * 4,
        8 * rows * width,
        12 * rows * width,
        after=after,
        out_specs=(whole(pltpu.VMEM), whole(pltpu.VMEM)),
        name="norm_rows",
    )


def norm_back_body(part_ref, got_ref, values_ref, add_ref, gain_ref, *outs):
    upstream = part_ref[...].astype(F32) + got_ref[...].astype(F32)
    values = values_ref[...].astype(F32)
    scale = scale_of(values)
    normed = values * scale
    outs[-1][...] = jnp.sum(upstream * normed, axis=0, keepdims=True)
    weighted = upstream * gain_ref[...]
    grad = scale * (weighted - normed * jnp.mean(weighted * normed, axis=-1, keepdims=True))
    total = add_ref[...].astype(F32) + grad
    for ref in outs[:-1]:
        ref[...] = total.astype(ref.dtype)


def norm_back(part, got, values, add, gain, kinds, after=()):
    rows, width = part.shape
    return call(
        norm_back_body,
        tuple(jax.ShapeDtypeStruct((rows, width), kind) for kind in kinds)
        + (jax.ShapeDtypeStruct((1, width), F32),),
        [part, got, values, add, gain],
        [whole(pltpu.VMEM)] * 5,
        16 * rows * width,
        16 * rows * width,
        after=after,
        out_specs=tuple(whole(pltpu.VMEM) for _ in range(len(kinds) + 1)),
        name="norm_back",
    )


def add_body(part_ref, got_ref, res_ref, out_ref):
    out_ref[...] = (
        res_ref[...] + (part_ref[...].astype(F32) + got_ref[...].astype(F32))
    ).astype(BF16)


def add_rows(part, got, residual, after=()):
    return call(
        add_body,
        jax.ShapeDtypeStruct(part.shape, BF16),
        [part, got, residual],
        [whole(pltpu.VMEM)] * 3,
        part.size,
        10 * part.size,
        after=after,
        out_specs=whole(pltpu.VMEM),
        name="add_rows",
    )


def join_body(n, place_ref, *refs):
    core = place_ref[2] & 1
    place_rows(refs[:n], refs[-1], core)
    place_rows(refs[n : 2 * n], refs[-1], 1 - core)


def join_rows(place, mine, sibs, after=()):
    n = len(mine)
    size, width = mine[0].shape
    return call(
        functools.partial(join_body, n),
        jax.ShapeDtypeStruct((2 * n * size, width), BF16),
        [place, *mine, *sibs],
        [whole(pltpu.SMEM)] + [whole(pltpu.VMEM)] * (2 * n),
        0,
        8 * n * size * width,
        after=after,
        out_specs=whole(pltpu.VMEM),
        name="join_rows",
    )


def turn_body(n, block, offset_ref, order_ref, *refs):
    pieces, out_ref = refs[:n], refs[n]
    size, wide = pieces[0].shape
    unit = (
        lax.broadcasted_iota(jnp.int32, (block, block), 0)
        == lax.broadcasted_iota(jnp.int32, (block, block), 1)
    ).astype(F32).astype(BF16)
    for p in range(wide // block):
        at = pl.multiple_of(order_ref[p] * block, block)
        for j in range(n):
            to = pl.multiple_of(offset_ref[j] * size, size)
            made = nt(unit, pieces[j][:, pl.ds(at, block)]).astype(BF16)
            out_ref[p * block : (p + 1) * block, pl.ds(to, size)] = made


def turn(order, group, pieces, offsets=None, after=()):
    wide = pieces[0].shape[1]
    if group % 128 != 0:
        pieces = [
            jnp.concatenate(
                [
                    lax.dynamic_slice_in_dim(piece, order[p] * group, group, 1)
                    for p in range(order.shape[0])
                ],
                axis=1,
            )
            for piece in pieces
        ]
        block = math.gcd(256, wide)
        order_in = jnp.arange(wide // block, dtype=jnp.int32)
    else:
        block = group
        order_in = order
    n = len(pieces)
    size = pieces[0].shape[0]
    tokens = n * size
    if offsets is None:
        offsets = jnp.arange(n, dtype=jnp.int32)
    return call(
        functools.partial(turn_body, n, block),
        jax.ShapeDtypeStruct((wide, tokens), BF16),
        [offsets, order_in, *pieces],
        [whole(pltpu.SMEM)] * 2 + [whole(pltpu.VMEM)] * n,
        2 * tokens * wide * block,
        4 * tokens * wide,
        after=after,
        out_specs=whole(pltpu.VMEM),
        vmem=8 + 4 * tokens * wide // MIB,
        name="turn",
    )


def stack_body(*refs):
    for i, ref in enumerate(refs[:-1]):
        refs[-1][i] = ref[...]


def stack_rows(pieces):
    n = len(pieces)
    return call(
        stack_body,
        jax.ShapeDtypeStruct((n, *pieces[0].shape), BF16),
        list(pieces),
        [whole(pltpu.VMEM)] * n,
        0,
        4 * n * pieces[0].size,
        out_specs=whole(pltpu.VMEM),
        name="stack_rows",
    )


def turn_all_body(block, place_ref, order_ref, own_ref, *refs):
    parts, out_ref = refs[:-1], refs[-1]
    n = len(parts)
    size, wide = parts[0].shape[1:]
    unit = (
        lax.broadcasted_iota(jnp.int32, (block, block), 0)
        == lax.broadcasted_iota(jnp.int32, (block, block), 1)
    ).astype(F32).astype(BF16)

    @pl.when(pl.program_id(0) == 0)
    def _():
        for p in range(wide // block):
            at = pl.multiple_of(order_ref[p] * block, block)
            made = nt(unit, own_ref[:, pl.ds(at, block)]).astype(BF16)
            out_ref[p * block : (p + 1) * block, :] = made

    @pl.when(pl.program_id(0) > 0)
    def _():
        for p in range(wide // block):
            at = pl.multiple_of(order_ref[p] * block, block)
            for j in range(n):
                to = pl.multiple_of((place_ref[0] ^ j) * size, size)
                made = nt(unit, parts[j][0, :, pl.ds(at, block)]).astype(BF16)
                out_ref[p * block : (p + 1) * block, pl.ds(to, size)] = made


def turn_all(order, group, own, parts, m):
    tokens, wide = own.shape
    others, size, _ = parts[0].shape
    if group % 128 != 0:

        def ordered(values):
            axis = values.ndim - 1
            return jnp.concatenate(
                [
                    lax.dynamic_slice_in_dim(values, order[p] * group, group, axis)
                    for p in range(order.shape[0])
                ],
                axis=axis,
            )

        own = ordered(own)
        parts = [ordered(part) for part in parts]
        block = math.gcd(256, wide)
        order_in = jnp.arange(wide // block, dtype=jnp.int32)
    else:
        block = group
        order_in = order
    return call(
        functools.partial(turn_all_body, block),
        jax.ShapeDtypeStruct((wide, (others + 1) * tokens), BF16),
        [m.reshape(1).astype(jnp.int32), order_in, own, *parts],
        [pl.BlockSpec((tokens, wide), lambda d, place, order: (0, 0))]
        + [
            pl.BlockSpec((1, size, wide), lambda d, place, order: (jnp.maximum(d - 1, 0), 0, 0))
        ]
        * len(parts),
        2 * (others + 1) * tokens * wide * block,
        4 * (others + 1) * tokens * wide,
        prefetch=2,
        grid=(others + 1,),
        out_specs=pl.BlockSpec((wide, tokens), lambda d, place, order: (0, d)),
        vmem=52,
        name="turn_all",
    )


def weight_body(n, *refs):
    lefts, refs = refs[:n], refs[n:]
    rights, (sent_ref, kept_ref) = refs[:n], refs[n:]
    total = nn(lefts[0][...], rights[0][...])
    for i in range(1, n):
        total = total + nn(lefts[i][...], rights[i][...])
    half = pl.num_programs(0) // 2

    @pl.when(pl.program_id(0) < half)
    def _():
        sent_ref[...] = total.astype(BF16)

    @pl.when(pl.program_id(0) >= half)
    def _():
        kept_ref[...] = total.astype(BF16)


def weight_grad(lefts, rights, after=()):
    wide = lefts[0].shape[0]
    width = rights[0].shape[1]
    tokens = sum(left.shape[1] for left in lefts)
    steps = 4
    tile = wide // steps
    half = steps // 2
    made = jax.ShapeDtypeStruct((wide // 2, width), BF16)
    return call(
        functools.partial(weight_body, len(lefts)),
        (made,) * 2,
        [*lefts, *rights],
        [
            pl.BlockSpec((tile, left.shape[1]), lambda i: ((i + half) % steps, 0))
            for left in lefts
        ]
        + [pl.BlockSpec(right.shape, lambda i: (0, 0)) for right in rights],
        2 * tokens * wide * width,
        2 * (tokens * wide + tokens * width + wide * width),
        after=after,
        grid=(steps,),
        out_specs=(
            pl.BlockSpec((tile, width), lambda i: (jnp.minimum(i, half - 1), 0)),
            pl.BlockSpec((tile, width), lambda i: (jnp.maximum(i - half, 0), 0)),
        ),
        vmem=52,
        name="weight_grad",
    )


def sum3_body(n, *refs):
    total = refs[0][...].astype(F32)
    for ref in refs[1:n]:
        total = total + ref[...].astype(F32)
    low_ref, high_ref = refs[n:]
    low_ref[...] = total[0]
    high_ref[...] = total[1].astype(BF16)


def final_sum(terms, after=()):
    wide, width = terms[0].shape
    high = wide // 2
    tile = math.gcd(high, 128)
    block = pl.BlockSpec((2, tile, width), lambda i: (0, i, 0))
    out = pl.BlockSpec((tile, width), lambda i: (i, 0))
    return call(
        functools.partial(sum3_body, len(terms)),
        (
            jax.ShapeDtypeStruct((high, width), F32),
            jax.ShapeDtypeStruct((high, width), BF16),
        ),
        [term.reshape(2, high, width) for term in terms],
        [block] * len(terms),
        wide * width,
        wide * width * 8,
        after=after,
        grid=(high // tile,),
        out_specs=(out, out),
        name="final_sum",
    )


def merge_body(kept_ref, got_ref, low_ref, high_ref):
    total = kept_ref[...].astype(F32) + got_ref[...].astype(F32)
    low_ref[...] = total[0]
    high_ref[...] = total[1].astype(BF16)


def merge(kept, got, after=()):
    wide, width = kept.shape
    high = wide // 2
    tile = math.gcd(high, 128)
    operands = [kept.reshape(2, high, width), got.reshape(2, high, width)]
    block = pl.BlockSpec((2, tile, width), lambda i: (0, i, 0))
    out = pl.BlockSpec((tile, width), lambda i: (i, 0))
    return call(
        merge_body,
        (
            jax.ShapeDtypeStruct((high, width), F32),
            jax.ShapeDtypeStruct((high, width), BF16),
        ),
        operands,
        [block, block],
        wide * width,
        wide * width * 8,
        after=after,
        grid=(high // tile,),
        out_specs=(out, out),
        name="merge",
    )


def lay_body(turned, place_ref, own_ref, got_ref, out_ref):
    value = jnp.where(pl.program_id(0) == 0, own_ref[...], got_ref[...].astype(F32))
    out_ref[...] = value.T if turned else value


def lay(place, own, got, turned):
    rows, width = own.shape
    if turned:
        shape, block = (2 * width, rows), (width, rows)
        index = lambda i, place: (place[3] ^ i, 0)
    else:
        shape, block = (rows, 2 * width), (rows, width)
        index = lambda i, place: (0, place[3] ^ i)
    fixed = pl.BlockSpec((rows, width), lambda i, place: (0, 0))
    return call(
        functools.partial(lay_body, turned),
        jax.ShapeDtypeStruct(shape, F32),
        [place, own, got],
        [fixed, fixed],
        0,
        14 * rows * width,
        prefetch=1,
        grid=(2,),
        out_specs=pl.BlockSpec(block, index),
        name="lay",
    )


def qkv_sum_body(kept_ref, got_ref, own_ref, *outs):
    size = own_ref.shape[0]
    total = kept_ref[...].astype(F32) + got_ref[...].astype(F32)
    own_ref[...] = total[:size]
    for i, ref in enumerate(outs):
        ref[...] = total[(i + 1) * size : (i + 2) * size].astype(BF16)


def split_sum(kept, got, n):
    rows, width = kept.shape
    size = rows // n
    return call(
        qkv_sum_body,
        (jax.ShapeDtypeStruct((size, width), F32),)
        + (jax.ShapeDtypeStruct((size, width), BF16),) * (n - 1),
        [kept, got],
        [whole(pltpu.VMEM)] * 2,
        rows * width,
        8 * rows * width,
        out_specs=(whole(pltpu.VMEM),) * n,
        name="split_sum",
    )


def place_heads_body(nz, place_ref, *refs):
    pieces, outs = refs[:nz], refs[nz:]
    for d in range(nz):
        at = pl.multiple_of((place_ref[0] ^ d) * HD, HD)
        for i, out in enumerate(outs):
            out[:, pl.ds(at, HD)] = pieces[d][:, i * HD : (i + 1) * HD].astype(F32)


def place_heads(place, pieces):
    nz = len(pieces)
    rows = pieces[0].shape[0]
    return call(
        functools.partial(place_heads_body, nz),
        (jax.ShapeDtypeStruct((rows, nz * HD), F32),) * 3,
        [place, *pieces],
        [whole(pltpu.SMEM)] + [whole(pltpu.VMEM)] * nz,
        0,
        20 * rows * nz * HD,
        out_specs=(whole(pltpu.VMEM),) * 3,
        name="place_heads",
    )


def rope_tables(position):
    middle = HD // 2
    frequency = THETA ** (-(jnp.arange(middle, dtype=F32) * 2.0 / HD))
    angles = position.astype(F32)[..., None] * frequency
    cosine = jnp.cos(angles)
    sine = jnp.sin(angles)
    return (
        jnp.concatenate([cosine, cosine], axis=-1),
        jnp.concatenate([-sine, sine], axis=-1),
    )


def rms_scale(values):
    return lax.rsqrt(jnp.mean(values * values, axis=-1, keepdims=True) + EPSILON)


def layer(
    n_seq,
    n_mp,
    mixed_in,
    w_query,
    w_key,
    w_value,
    w_out,
    gain_attn,
    w_gate,
    w_up,
    w_down,
    gain_mlp,
    doc_ends,
    cotangent,
):
    rows, width = mixed_in.shape
    nz = w_query.shape[1] // HD
    ring = n_seq // nz
    bits = n_seq.bit_length() - 1
    low_bits = ring.bit_length() - 1
    units = w_gate.shape[1]
    half_units = units // 2
    half_rows = rows // 2
    group = width // n_seq
    pair_bit = bits - 2
    pair = 1 << pair_bit

    s = lax.axis_index("seq")
    m = lax.axis_index("mp")
    z, r = s // ring, s % ring
    core = m % 2
    side = m // 2
    low = (s >> pair_bit) & 1

    def seq_swap(v, distance):
        return lax.ppermute(v, "seq", [(i, i ^ distance) for i in range(n_seq)])

    def mp_swap(v, distance):
        return lax.ppermute(v, "mp", [(i, i ^ distance) for i in range(n_mp)])

    sum_bits = list(range(pair_bit)) + [bits - 1]
    places = []
    for p in range(n_seq):
        e = 0
        for at, bit in enumerate(sum_bits + [pair_bit]):
            if (p >> (bits - 1 - at)) & 1:
                e |= 1 << bit
        places.append(e)
    order = s ^ jnp.array(places, dtype=jnp.int32)

    ORDER.clear()

    place = jnp.stack([z, r, m, low]).astype(jnp.int32)
    blocks = (z ^ jnp.arange(nz, dtype=jnp.int32)) * ring + r
    token_index = blocks[:, None] * rows + jnp.arange(rows, dtype=jnp.int32)[None, :]
    ends_below = doc_ends[None, None, :] <= token_index[..., None]
    begin = jnp.max(jnp.where(ends_below, doc_ends, 0), axis=-1)
    cos_own, sin_own = rope_tables(token_index[0] - begin[0])
    weights = [w_query, w_key, w_value]
    half_z = nz // 2
    made = project_qkv(
        place,
        mixed_in,
        gain_attn.reshape(1, width),
        weights,
        cos_own,
        sin_own,
        list(range(half_z, nz)),
    )
    normed = made[-1]
    pieces = {half_z + i: made[i] for i in range(half_z)}
    made = project_qkv(place, normed, None, weights, cos_own, sin_own, list(range(half_z)))
    pieces.update({i: made[i] for i in range(half_z)})
    pieces = [pieces[0]] + [seq_swap(pieces[d], d * ring) for d in range(1, nz)]
    near = pieces
    keys_values = [near, [seq_swap(piece[:, HD:], 1) for piece in pieces]]
    for b in range(1, low_bits):
        keys_values = keys_values + [
            [seq_swap(kv[:, -2 * HD :], 1 << b) for kv in kvs] for kvs in keys_values
        ]
    queries = pieces

    quarter = rows // n_mp
    my_quarter = lax.dynamic_slice_in_dim(normed, m * quarter, quarter, 0)
    halves = [
        lax.dynamic_slice_in_dim(w_down, low * half_units, half_units, 0),
        lax.dynamic_slice_in_dim(w_gate, low * half_units, half_units, 1),
        lax.dynamic_slice_in_dim(w_up, low * half_units, half_units, 1),
    ]
    cot_half = lax.dynamic_slice_in_dim(cotangent, core * half_rows, half_rows, 0)

    flat = [kv for kvs in keys_values for kv in kvs]
    far = [kv for kvs in keys_values[1:] for kv in kvs]
    cot_half, *halves = hold([cot_half, *halves], after=pieces)
    cot_pair = seq_swap(cot_half, pair)
    outs = attend(place, doc_ends, queries, flat, nz, ring)
    heads = [outs[0]] + [seq_swap(outs[d], d * ring) for d in range(1, nz)]

    size = half_rows // CHUNKS
    last_low = 1 << sum_bits[pair_bit - 1]
    high = 1 << sum_bits[pair_bit]
    gain_mlp_row = gain_mlp.reshape(1, width)
    gain_attn_row = gain_attn.reshape(1, width)

    def chunks_of(values):
        return [values[i * size : (i + 1) * size] for i in range(CHUNKS)]

    def low_sums(sent, kept):
        for bit in sum_bits[: pair_bit - 1]:
            kept, sent = merge(kept, seq_swap(sent, 1 << bit))
        return kept, seq_swap(sent, last_low)

    x_chunks = chunks_of(lax.dynamic_slice_in_dim(mixed_in, core * half_rows, half_rows, 0))
    cot_chunks = chunks_of(cot_half)
    cot_all = cot_chunks + chunks_of(cot_pair)
    spots = jnp.concatenate(
        [core * CHUNKS + jnp.arange(CHUNKS), (1 - core) * CHUNKS + jnp.arange(CHUNKS)]
    ).astype(jnp.int32)
    v = types.SimpleNamespace(
        residual=[None] * CHUNKS,
        normed=[None] * (2 * CHUNKS),
        back=[None] * CHUNKS,
        back_across=[None] * CHUNKS,
        residual_grad=[None] * CHUNKS,
        branch=[None] * CHUNKS,
        branch_sib=[None] * CHUNKS,
        gain_mlp=[None] * CHUNKS,
        gain_attn=[None] * CHUNKS,
        grad_rows=[None] * CHUNKS,
        grad_sib=[None] * CHUNKS,
        quarters={0: my_quarter},
        out_grads=(),
    )
    def heads_out():
        sib, v.mine, v.heads_placed = heads_project(
            place, heads, [w_out], nn, True, after=[cot_pair]
        )
        v.sib = mp_swap(sib, 1)

    def out_sum():
        v.parts = row_sum(v.mine, v.sib, CHUNKS)
        v.across = [mp_swap(part, 2) for part in v.parts]

    def swap_weights():
        v.down_sib, v.gate_sib, v.up_sib = [mp_swap(half, 1) for half in hold(halves)]

    def dact_own():
        v.dact = hidden_upstream(place, cot_all, w_down, True)

    def dact_sib():
        v.dact_sib = hidden_upstream(place, cot_all, v.down_sib, False)

    def norm_chunk(i):
        v.residual[i], v.normed[i] = norm_rows(
            v.parts[i], v.across[i], x_chunks[i], gain_mlp_row
        )
        v.normed[CHUNKS + i] = seq_swap(v.normed[i], pair)

    def turn_cot():
        v.cot_turned = turn(order, group, cot_all)

    def swap_cot():
        (turned,) = hold([v.cot_turned])
        v.cot_both = [turned, mp_swap(turned, 1)]

    def hidden_sib():
        v.act_sib, dg_sib, du_sib = hidden(
            place, v.normed, v.gate_sib, v.up_sib, v.dact_sib, False
        )
        v.act_got = mp_swap(v.act_sib, 1)
        v.dg_sib, v.du_sib = dg_sib, du_sib

    def swap_dg():
        (part,) = hold([v.dg_sib])
        v.dg_got = mp_swap(part, 1)

    def swap_du():
        (part,) = hold([v.du_sib])
        v.du_got = mp_swap(part, 1)

    def hidden_own():
        v.act, v.dg, v.du = hidden(place, v.normed, w_gate, w_up, v.dact, True)

    def turn_normed():
        v.normed_turned = turn(order, group, v.normed)

    def swap_normed():
        (turned,) = hold([v.normed_turned])
        v.normed_both = [turned, mp_swap(turned, 1)]

    def grad_down():
        v.sent_down, v.part_down = weight_grad(v.cot_both, [v.act, v.act_got])

    def send_down():
        (sent,) = hold([v.sent_down])
        v.low_down = low_sums(sent, v.part_down)

    def hidden_in():
        v.made = hidden_back(
            place,
            v.dg,
            v.dg_sib,
            v.du,
            v.du_sib,
            w_gate,
            v.gate_sib,
            w_up,
            v.up_sib,
            2 * CHUNKS,
        )
        v.made_got = [seq_swap(v.made[CHUNKS + i], pair) for i in range(CHUNKS)]

    def back_chunk(i):
        (v.back[i],) = row_sum(v.made[i], v.made_got[i], 1)
        v.back_across[i] = mp_swap(v.back[i], 2)

    def norm_back_chunk(i):
        v.residual_grad[i], v.branch[i], v.gain_mlp[i] = norm_back(
            v.back[i], v.back_across[i], v.residual[i], cot_chunks[i], gain_mlp_row, (F32, BF16)
        )
        v.branch_sib[i] = mp_swap(v.branch[i], 1)

    def grad_gate():
        v.sent_gate, v.part_gate = weight_grad(v.normed_both, [v.dg, v.dg_got])

    def send_gate():
        (sent,) = hold([v.sent_gate])
        v.low_gate = low_sums(sent, v.part_gate)

    def grad_up():
        v.sent_up, v.part_up = weight_grad(v.normed_both, [v.du, v.du_got])

    def send_up():
        (sent,) = hold([v.sent_up])
        v.low_up = low_sums(sent, v.part_up)

    def merge_down():
        v.kept_down, v.high_down = merge(*v.low_down)

    def high_down():
        (sent,) = hold([v.high_down], after=v.out_grads)
        v.come_down = seq_swap(sent, high)

    def merge_gate():
        v.kept_gate, v.high_gate = merge(*v.low_gate)

    def high_gate():
        (sent,) = hold([v.high_gate])
        v.come_gate = seq_swap(sent, high)

    def merge_up():
        v.kept_up, v.high_up = merge(*v.low_up)

    def high_up():
        (sent,) = hold([v.high_up])
        v.come_up = seq_swap(sent, high)

    def sum_down():
        v.own_down, v.pair_down = final_sum([v.kept_down, v.come_down])

    def sum_gate():
        v.own_gate, v.pair_gate = final_sum([v.kept_gate, v.come_gate])

    def sum_up():
        v.own_up, v.pair_up = final_sum([v.kept_up, v.come_up])

    def pair_down():
        (sent,) = hold([v.pair_down])
        v.theirs_down = seq_swap(sent, pair)

    def pair_gate():
        (sent,) = hold([v.pair_gate])
        v.theirs_gate = seq_swap(sent, pair)

    def pair_up():
        (sent,) = hold([v.pair_up])
        v.theirs_up = seq_swap(sent, pair)

    def lay_down():
        v.down_share = lay(place, v.own_down, v.theirs_down, True)

    def lay_gate():
        v.gate_share = lay(place, v.own_gate, v.theirs_gate, False)

    def lay_up():
        v.up_share = lay(place, v.own_up, v.theirs_up, False)

    def gather_z(d):
        (part,) = hold([v.quarters[d & (d - 1)]])
        v.quarters[d] = seq_swap(part, ring * (d & -d))

    def gather_x():
        v.rows = stack_rows([v.quarters[d] for d in range(1, nz)])
        v.rows_x = mp_swap(v.rows, 2)

    def gather_core():
        v.rows_core = [mp_swap(part, 1) for part in hold([v.rows, v.rows_x])]

    def heads_in():
        made = heads_upstream(place, v.branch, v.branch_sib, w_out, nz)
        v.out_grads = [made[0]] + [seq_swap(made[d], d * ring) for d in range(1, nz)]

    def attend_far():
        v.dq_far, *summed = attend_back(
            place, doc_ends, queries, v.out_grads, far, None, nz, ring, 1, ring - 1, BF16
        )
        summed = [None] + summed
        for b in reversed(range(low_bits)):
            bit = 1 << b
            for e in range(bit):
                got = seq_swap(summed[e | bit], bit)
                summed[e] = (
                    got
                    if summed[e] is None
                    else (summed[e].astype(F32) + got.astype(F32)).astype(BF16)
                )
        v.dkv_got = summed[0]

    def attend_near():
        v.dq, v.dkv = attend_back(
            place, doc_ends, queries, v.out_grads, near, v.dq_far, nz, ring, 0, 1, F32
        )

    def head_grads():
        cosine, signed = rope_tables(token_index - begin)
        v.grads = finish_grads(v.dq, v.dkv, v.dkv_got, cosine, signed)
        v.own_grads = [v.grads[0]] + [
            seq_swap(v.grads[d], d * ring) for d in range(1, nz)
        ]

    def turn_branch():
        v.branch_turned = turn(order, group, v.branch + v.branch_sib, spots)

    def grad_out():
        v.sent_out, v.part_out = weight_grad([v.branch_turned], [v.heads_placed])

    def send_out():
        (sent,) = hold([v.sent_out])
        v.low_out = low_sums(sent, v.part_out)

    def merge_out():
        v.kept_out, v.high_out = merge(*v.low_out)

    def high_out():
        (sent,) = hold([v.high_out])
        v.come_out = seq_swap(sent, high)

    def sum_out():
        v.own_out, sent = final_sum([v.kept_out, v.come_out])
        v.pair_out = seq_swap(sent, pair)

    def turn_rows():
        v.all_turned = turn_all(
            order, group, normed, [v.rows, v.rows_core[0], v.rows_x, v.rows_core[1]], m
        )

    def grad_qkv():
        v.sent_qkv, v.part_qkv = weight_grad(
            [v.all_turned], [jnp.concatenate(v.grads, axis=0)]
        )

    def send_qkv():
        (sent,) = hold([v.sent_qkv])
        v.low_qkv = low_sums(sent, v.part_qkv)

    def split_qkv():
        own, *sent = split_sum(*v.low_qkv, nz)
        v.qkv_heads = [own] + [seq_swap(sent[d - 1], d * ring) for d in range(1, nz)]

    def lay_qkv():
        v.shares = place_heads(place, v.qkv_heads)

    def rows_in():
        sib, v.in_mine = heads_project(place, v.own_grads, weights, nt, False)
        v.in_sib = mp_swap(sib, 1)

    def in_sum():
        v.in_parts = row_sum(v.in_mine, v.in_sib, CHUNKS)
        v.in_across = [mp_swap(part, 2) for part in v.in_parts]

    def norm_in_chunk(i):
        v.grad_rows[i], v.gain_attn[i] = norm_back(
            v.in_parts[i], v.in_across[i], x_chunks[i], v.residual_grad[i], gain_attn_row, (BF16,)
        )
        v.grad_sib[i] = mp_swap(v.grad_rows[i], 1)

    def join_in():
        v.input_grad = join_rows(place, v.grad_rows, v.grad_sib)

    def down_rows():
        v.down_mine, v.down_theirs = down(place, v.act, v.act_sib, w_down, v.down_sib, 2)

    def pair_rows():
        (sent,) = hold([v.down_theirs])
        v.down_got = seq_swap(sent, pair)

    def sum_rows():
        (v.down_part,) = row_sum(v.down_mine, v.down_got, 1)
        v.down_across = mp_swap(v.down_part, 2)

    def add_out():
        v.out_rows = add_rows(
            v.down_part, v.down_across, jnp.concatenate(v.residual, axis=0)
        )
        v.out_sib = mp_swap(v.out_rows, 1)

    def join_out():
        v.mixed_out = join_rows(place, [v.out_rows], [v.out_sib])

    def gains_core():
        (v.gains,) = hold([jnp.concatenate([sum(v.gain_attn), sum(v.gain_mlp)])])
        v.gains = v.gains + mp_swap(v.gains, 1)

    def gains_seq(bit):
        (v.gains,) = hold([v.gains])
        v.gains = v.gains + seq_swap(v.gains, 1 << bit)

    heads_out()
    dact_own()
    out_sum()
    swap_weights()
    norm_chunk(1)
    dact_sib()
    norm_chunk(0)
    turn_cot()
    hidden_sib()
    gather_z(2)
    gather_z(1)
    swap_cot()
    swap_dg()
    swap_du()
    turn_normed()
    swap_normed()
    hidden_own()
    grad_down()
    hidden_in()
    send_down()
    gather_z(3)
    grad_gate()
    back_chunk(1)
    send_gate()
    back_chunk(0)
    norm_back_chunk(1)
    norm_back_chunk(0)
    gather_x()
    heads_in()
    merge_down()
    high_down()
    grad_up()
    turn_branch()
    attend_far()
    gather_core()
    send_up()
    attend_near()
    merge_gate()
    high_gate()
    sum_down()
    head_grads()
    pair_down()
    rows_in()
    grad_out()
    merge_up()
    high_up()
    in_sum()
    down_rows()
    send_out()
    norm_in_chunk(0)
    turn_rows()
    grad_qkv()
    lay_down()
    merge_out()
    high_out()
    norm_in_chunk(1)
    pair_rows()
    send_qkv()
    sum_gate()
    join_in()
    gains_core()
    gains_seq(0)
    pair_gate()
    split_qkv()
    sum_up()
    pair_up()
    sum_rows()
    lay_up()
    gains_seq(2)
    sum_out()
    add_out()
    lay_gate()
    join_out()
    gains_seq(1)
    lay_qkv()
    for bit in range(3, bits):
        gains_seq(bit)
    gains = lax.dynamic_slice_in_dim(v.gains, s * group, group, 1)

    return (
        v.mixed_out,
        v.input_grad,
        *v.shares,
        (v.own_out + v.pair_out.astype(F32)).T,
        gains[0],
        v.gate_share,
        v.up_share,
        v.down_share,
        gains[1],
    )


def solution(mesh):
    placed = (
        P("seq", None),
        P(None, "mp"),
        P(None, "mp"),
        P(None, "mp"),
        P("mp", None),
        P(),
        P(None, "mp"),
        P(None, "mp"),
        P("mp", None),
        P(),
        P(),
        P("seq", None),
    )
    return jax.shard_map(
        functools.partial(layer, mesh.shape["seq"], mesh.shape["mp"]),
        mesh=mesh,
        in_specs=placed,
        out_specs=(
            P("seq", None),
            P("seq", None),
            P("seq", "mp"),
            P("seq", "mp"),
            P("seq", "mp"),
            P("mp", "seq"),
            P("seq"),
            P("seq", "mp"),
            P("seq", "mp"),
            P("mp", "seq"),
            P("seq"),
        ),
        check_vma=False,
    )
```

```python
import functools
import math
import types

import jax
import jax.numpy as jnp
from jax import lax
from jax.experimental import pallas as pl
from jax.experimental.pallas import tpu as pltpu
from jax.sharding import PartitionSpec as P

HD = 128
EPSILON = 1e-05
THETA = 10000.0
FACTOR = 1.0 / math.sqrt(HD)
CLAMP = 80.0
CHUNKS = 2
SHARE = 0.5
ORDER = []
LOOSE = [False]
MIB = 1024 * 1024
F32 = jnp.float32
BF16 = jnp.bfloat16


def nn(left, right):
    return lax.dot_general(left, right, (((1,), (0,)), ((), ())), preferred_element_type=F32)


def nt(left, right):
    return lax.dot_general(left, right, (((1,), (1,)), ((), ())), preferred_element_type=F32)


def tn(left, right):
    return lax.dot_general(left, right, (((0,), (0,)), ((), ())), preferred_element_type=F32)


def call(
    body,
    out_shape,
    operands,
    in_specs,
    flops,
    moved,
    transcendentals=0,
    after=(),
    prefetch=0,
    chain=True,
    vmem=20,
    **kwargs,
):
    n = prefetch + len(in_specs)
    chain = chain and not LOOSE[0]
    after = list(after) + (ORDER if chain else [])

    def kernel(*refs):
        body(*refs[:n], *refs[n + len(after) :])

    in_specs = list(in_specs) + [pl.BlockSpec(memory_space=pl.ANY)] * len(after)
    if prefetch:
        kwargs = {
            "name": kwargs.pop("name"),
            "grid_spec": pltpu.PrefetchScalarGridSpec(
                num_scalar_prefetch=prefetch, in_specs=in_specs, **kwargs
            ),
        }
    else:
        kwargs["in_specs"] = in_specs
    made = pl.pallas_call(
        kernel,
        out_shape=out_shape,
        compiler_params=pltpu.CompilerParams(vmem_limit_bytes=vmem * MIB),
        cost_estimate=pl.CostEstimate(
            flops=int(flops / SHARE),
            bytes_accessed=int(moved / SHARE),
            transcendentals=int(transcendentals / SHARE),
        ),
        **kwargs,
    )(*operands, *after)
    if chain:
        ORDER[:] = [made[0] if isinstance(made, (tuple, list)) else made]
    return made


def hold(values, after=()):
    n = len(values)
    if LOOSE[0]:
        return list(lax.optimization_barrier((*values, *after))[:n])
    made = lax.optimization_barrier((*values, *ORDER, *after))
    ORDER[:] = made[n : n + len(ORDER)]
    return list(made[:n])


def loose(step, *args):
    LOOSE[0] = True
    step(*args)
    LOOSE[0] = False


def whole(memory):
    return pl.BlockSpec(memory_space=memory)


def rotated(values, cosine, signed):
    return values * cosine + pltpu.roll(values, HD // 2, 1) * signed


def unrotated(values, cosine, signed):
    return values * cosine - pltpu.roll(values, HD // 2, 1) * signed


def qkv_body(n, fresh, place_ref, *refs):
    if fresh:
        x_ref, gain_ref, refs = refs[0], refs[1], refs[2:]
    else:
        x_ref, refs = refs[0], refs[1:]
    wq_ref, wk_ref, wv_ref, cos_ref, sin_ref = refs[:5]
    outs, (w_s, x_s) = refs[5 : 5 + n], refs[-2:]
    step = pl.program_id(0)

    @pl.when(step == 0)
    def _():
        if fresh:
            x = x_ref[...].astype(F32)
            x_s[...] = (x * scale_of(x) * gain_ref[...]).astype(BF16)
            refs[5 + n][...] = x_s[...]
        else:
            x_s[...] = x_ref[...]

    w_s[:, :HD] = wq_ref[...]
    w_s[:, HD : 2 * HD] = wk_ref[...]
    w_s[:, 2 * HD :] = wv_ref[...]
    made = nn(x_s[...], w_s[...])
    cosine = cos_ref[...]
    signed = sin_ref[...]
    query = rotated(made[:, :HD], cosine, signed).astype(BF16)
    key = rotated(made[:, HD : 2 * HD], cosine, signed).astype(BF16)
    value = made[:, 2 * HD :].astype(BF16)
    for i in range(n):

        @pl.when(step == i)
        def _(i=i):
            outs[i][:, :HD] = query
            outs[i][:, HD : 2 * HD] = key
            outs[i][:, 2 * HD :] = value


def project_qkv(place, x, gain, weights, cosine, signed, spots):
    n = len(spots)
    rows, width = x.shape
    fresh = gain is not None
    fixed = pl.BlockSpec((rows, width), lambda i, place: (0, 0))
    table = pl.BlockSpec((rows, HD), lambda i, place: (0, 0))
    first = spots[0]
    assert list(spots) == [first ^ i for i in range(n)]
    weight = pl.BlockSpec((width, HD), lambda i, place: (0, place[0] ^ first ^ i))
    piece = jax.ShapeDtypeStruct((rows, 3 * HD), BF16)
    return call(
        functools.partial(qkv_body, n, fresh),
        (piece,) * n + ((jax.ShapeDtypeStruct(x.shape, BF16),) if fresh else ()),
        [place, x] + ([gain] if fresh else []) + [*weights, cosine, signed],
        [fixed]
        + ([pl.BlockSpec((1, width), lambda i, place: (0, 0))] if fresh else [])
        + [weight] * 3
        + [table] * 2,
        6 * n * rows * width * HD,
        4 * rows * width + 6 * n * width * HD + 6 * n * rows * HD,
        prefetch=1,
        grid=(n,),
        out_specs=(pl.BlockSpec((rows, 3 * HD), lambda i, place: (0, 0)),) * n
        + ((fixed,) if fresh else ()),
        scratch_shapes=[pltpu.VMEM((width, 3 * HD), BF16), pltpu.VMEM((rows, width), BF16)],
        vmem=60,
        name="project_qkv",
    )


def begin_of(index, ends_ref, count):
    begin = jnp.zeros_like(index)
    for e in range(count):
        end = ends_ref[e]
        begin = jnp.where(end <= index, jnp.maximum(begin, end), begin)
    return begin


def finish_of(index, ends_ref, count):
    finish = jnp.zeros_like(index) + ends_ref[count - 1]
    for e in range(count):
        end = ends_ref[e]
        finish = jnp.where(end > index, jnp.minimum(finish, end), finish)
    return finish


def attend_body(nz, ring, count, place_ref, ends_ref, *refs):
    n_kv = nz * ring
    q_refs, refs = refs[:nz], refs[nz:]
    kv_refs, refs = refs[:n_kv], refs[n_kv:]
    o_refs, refs = refs[:nz], refs[nz:]
    q_s, k_s, v_s, o_s, acc = refs
    z, r = place_ref[0], place_ref[1]
    rows = q_s.shape[1]
    for d in range(nz):
        q_s[d] = q_refs[d][:, :HD]
    for i in range(n_kv):
        first = kv_refs[i].shape[1] - 2 * HD
        k_s[i] = kv_refs[i][:, first : first + HD]
        v_s[i] = kv_refs[i][:, first + HD :]

    @pl.loop(0, nz)
    def per_query(d):
        q_block = (z ^ d) * ring + r
        q_start = q_block * rows
        q_index = q_start + lax.broadcasted_iota(jnp.int32, (rows, 1), 0)
        begin = begin_of(q_index, ends_ref, count)
        shift = jnp.log((finish_of(q_index, ends_ref, count) - begin).astype(F32))
        first_begin = begin_of(q_start, ends_ref, count)
        last_begin = begin_of(q_start + (rows - 1), ends_ref, count)
        acc[...] = jnp.zeros_like(acc)

        @pl.loop(0, n_kv)
        def per_key(i):
            k_block = (z ^ (i & (nz - 1))) * ring + (r ^ (i // nz))
            k_start = k_block * rows
            needed = (k_block <= q_block) & (k_start + rows > first_begin)
            full = (k_block < q_block) & (k_start >= last_begin)

            def tile(masked):
                half = rows // 2
                for part in range(2):
                    at = slice(part * half, (part + 1) * half)
                    scores = nt(q_s[d, at], k_s[i])
                    grown = jnp.exp(jnp.minimum(shift[at] - scores * FACTOR, CLAMP))
                    probs = pl.reciprocal(1.0 + grown, approx=True)
                    if masked:
                        k_index = k_start + lax.broadcasted_iota(jnp.int32, (1, rows), 1)
                        allowed = (k_index <= q_index[at]) & (k_index >= begin[at])
                        probs = jnp.where(allowed, probs, 0.0)
                    acc[at] += nn(probs.astype(BF16), v_s[i])

            pl.when(needed & full)(functools.partial(tile, False))
            pl.when(needed & jnp.logical_not(full))(functools.partial(tile, True))

        o_s[d] = acc[...].astype(BF16)

    for d in range(nz):
        o_refs[d][...] = o_s[d]


def attend(place, ends, queries, keys_values, nz, ring, after=()):
    rows = queries[0].shape[0]
    n_kv = nz * ring
    pairs = nz * n_kv / 2
    return call(
        functools.partial(attend_body, nz, ring, ends.shape[0]),
        tuple(jax.ShapeDtypeStruct((rows, HD), BF16) for _ in range(nz)),
        [place, ends, *queries, *keys_values],
        [whole(pltpu.SMEM)] * 2 + [whole(pltpu.VMEM)] * (nz + n_kv),
        pairs * 4 * rows * rows * HD * 2,
        2 * (2 * nz + 2 * n_kv) * rows * HD,
        pairs * 2 * rows * rows,
        after=after,
        out_specs=tuple(whole(pltpu.VMEM) for _ in range(nz)),
        scratch_shapes=[
            pltpu.VMEM((nz, rows, HD), BF16),
            pltpu.VMEM((n_kv, rows, HD), BF16),
            pltpu.VMEM((n_kv, rows, HD), BF16),
            pltpu.VMEM((nz, rows, HD), BF16),
            pltpu.VMEM((rows, HD), F32),
        ],
        vmem=12 + 2 * n_kv * rows * HD * 8 // MIB,
        name="attend",
    )


def attend_back_body(nz, ring, n_dr, first_dr, chained, count, place_ref, ends_ref, *refs):
    n_kv = nz * n_dr
    q_refs, refs = refs[:nz], refs[nz:]
    do_refs, refs = refs[:nz], refs[nz:]
    kv_refs, refs = refs[:n_kv], refs[n_kv:]
    if chained:
        before_ref, refs = refs[0], refs[1:]
    dq_ref, refs = refs[0], refs[1:]
    dkv_refs, refs = refs[:n_dr], refs[n_dr:]
    q_s, do_s, k_s, v_s, begin_s, shift_s, dkv_s, dk_acc, dv_acc = refs
    z, r = place_ref[0], place_ref[1]
    rows = q_s.shape[1]
    for d in range(nz):
        q_s[d] = q_refs[d][:, :HD]
        do_s[d] = do_refs[d][...]
    for i in range(n_kv):
        first = kv_refs[i].shape[1] - 2 * HD
        k_s[i] = kv_refs[i][:, first : first + HD]
        v_s[i] = kv_refs[i][:, first + HD :]
    if chained:
        dq_ref[...] = before_ref[...]
    else:
        dq_ref[...] = jnp.zeros_like(dq_ref)

    @pl.loop(0, nz)
    def tables(d):
        q_index = ((z ^ d) * ring + r) * rows + lax.broadcasted_iota(jnp.int32, (1, rows), 1)
        begin = begin_of(q_index, ends_ref, count)
        begin_s[d] = begin
        shift_s[d] = jnp.log((finish_of(q_index, ends_ref, count) - begin).astype(F32))

    @pl.loop(0, n_kv)
    def per_key(i):
        k_block = (z ^ (i & (nz - 1))) * ring + (r ^ (first_dr + i // nz))
        k_start = k_block * rows
        dk_acc[...] = jnp.zeros_like(dk_acc)
        dv_acc[...] = jnp.zeros_like(dv_acc)

        @pl.loop(0, nz)
        def per_query(d):
            q_block = (z ^ d) * ring + r
            q_start = q_block * rows
            first_begin = begin_of(q_start, ends_ref, count)
            last_begin = begin_of(q_start + (rows - 1), ends_ref, count)
            needed = (k_block <= q_block) & (k_start + rows > first_begin)
            full = (k_block < q_block) & (k_start >= last_begin)

            def tile(masked):
                half = rows // 2
                for part in range(2):
                    at = slice(part * half, (part + 1) * half)
                    keys = k_s[i, at]
                    scores = nt(keys, q_s[d])
                    grown = jnp.exp(jnp.minimum(shift_s[d] - scores * FACTOR, CLAMP))
                    probs = pl.reciprocal(1.0 + grown, approx=True)
                    if masked:
                        k_index = (
                            k_start
                            + part * half
                            + lax.broadcasted_iota(jnp.int32, (half, 1), 0)
                        )
                        q_index = q_start + lax.broadcasted_iota(jnp.int32, (1, rows), 1)
                        allowed = (k_index <= q_index) & (k_index >= begin_s[d])
                        probs = jnp.where(allowed, probs, 0.0)
                    weight_grad = nt(v_s[i, at], do_s[d])
                    score_grad = (weight_grad * (probs * probs * grown)).astype(BF16)
                    dv_acc[at] += nn(probs.astype(BF16), do_s[d])
                    dk_acc[at] += nn(score_grad, q_s[d])
                    dq_ref[d] += tn(score_grad, keys)

            pl.when(needed & full)(functools.partial(tile, False))
            pl.when(needed & jnp.logical_not(full))(functools.partial(tile, True))

        dkv_s[i, :, :HD] = (dk_acc[...] * FACTOR).astype(dkv_s.dtype)
        dkv_s[i, :, HD:] = dv_acc[...].astype(dkv_s.dtype)

    for e in range(n_dr):
        for d in range(nz):
            dkv_refs[e][d] = dkv_s[e * nz + d]


def attend_back(
    place, ends, queries, out_grads, keys_values, before, nz, ring, first_dr, n_dr, kept, after=()
):
    rows = queries[0].shape[0]
    n_kv = nz * n_dr
    pairs = nz * n_kv / 2
    chained = before is not None
    return call(
        functools.partial(
            attend_back_body, nz, ring, n_dr, first_dr, chained, ends.shape[0]
        ),
        (jax.ShapeDtypeStruct((nz, rows, HD), F32),)
        + tuple(jax.ShapeDtypeStruct((nz, rows, 2 * HD), kept) for _ in range(n_dr)),
        [place, ends, *queries, *out_grads, *keys_values, *([before] if chained else [])],
        [whole(pltpu.SMEM)] * 2 + [whole(pltpu.VMEM)] * (2 * nz + n_kv + chained),
        pairs * 10 * rows * rows * HD * 2,
        2 * (2 * nz + 4 * n_kv) * rows * HD,
        pairs * 2 * rows * rows,
        after=after,
        out_specs=tuple(whole(pltpu.VMEM) for _ in range(1 + n_dr)),
        scratch_shapes=[
            pltpu.VMEM((nz, rows, HD), BF16),
            pltpu.VMEM((nz, rows, HD), BF16),
            pltpu.VMEM((n_kv, rows, HD), BF16),
            pltpu.VMEM((n_kv, rows, HD), BF16),
            pltpu.VMEM((nz, 1, rows), jnp.int32),
            pltpu.VMEM((nz, 1, rows), F32),
            pltpu.VMEM((n_kv, rows, 2 * HD), kept),
            pltpu.VMEM((rows, HD), F32),
            pltpu.VMEM((rows, HD), F32),
        ],
        vmem=16 + 2 * n_kv * rows * HD * 14 // MIB,
        name="attend_back",
    )


def finish_body(nz, dq_ref, dkv_ref, got_ref, cos_ref, sin_ref, *out_refs):
    for d in range(nz):
        cosine = cos_ref[d]
        signed = sin_ref[d]
        total = dkv_ref[d] + got_ref[d].astype(F32)
        out = out_refs[d]
        out[:, :HD] = unrotated(dq_ref[d] * FACTOR, cosine, signed).astype(BF16)
        out[:, HD : 2 * HD] = unrotated(total[:, :HD], cosine, signed).astype(BF16)
        out[:, 2 * HD :] = total[:, HD:].astype(BF16)


def finish_grads(dq, dkv, got, cosine, signed):
    nz, rows, _ = dq.shape
    return call(
        functools.partial(finish_body, nz),
        tuple(jax.ShapeDtypeStruct((rows, 3 * HD), BF16) for _ in range(nz)),
        [dq, dkv, got, cosine, signed],
        [whole(pltpu.VMEM)] * 5,
        12 * nz * rows * HD,
        nz * rows * HD * 30,
        out_specs=tuple(whole(pltpu.VMEM) for _ in range(nz)),
        name="finish_grads",
    )


def rows_at(place, width, height, tile_of):
    return pl.BlockSpec((height, width), lambda j, place: (tile_of(place), 0))


def place_rows(pieces, scratch, spot):
    size = pieces[0].shape[0]
    half = size * len(pieces)
    for i, piece in enumerate(pieces):
        at = pl.multiple_of(spot * half + i * size, size)
        scratch[pl.ds(at, size), :] = piece[...]


def upstream_body(place_ref, *refs):
    pieces, (w_ref, out_ref, x_s) = refs[:-3], refs[-3:]
    size = pieces[0].shape[0]

    @pl.when(pl.program_id(0) == 0)
    def _():
        for i, piece in enumerate(pieces):
            x_s[i * size : (i + 1) * size] = piece[...]

    out_ref[...] = nt(x_s[...], w_ref[...]).astype(BF16)


def hidden_upstream(place, pieces, weights, own, after=()):
    size, width = pieces[0].shape
    rows = size * len(pieces)
    units = weights.shape[0] // (2 if own else 1)
    tile = 512
    steps = units // tile
    first = (lambda place: place[3] * steps) if own else (lambda place: 0)
    return call(
        upstream_body,
        jax.ShapeDtypeStruct((rows, units), BF16),
        [place, *pieces, weights],
        [pl.BlockSpec((size, width), lambda j, place: (0, 0))] * len(pieces)
        + [pl.BlockSpec((tile, width), lambda j, place: (first(place) + j, 0))],
        2 * rows * width * units,
        2 * width * units + 4 * rows * units + 2 * rows * width,
        after=after,
        prefetch=1,
        grid=(steps,),
        out_specs=pl.BlockSpec((rows, tile), lambda j, place: (0, j)),
        scratch_shapes=[pltpu.VMEM((rows, width), BF16)],
        vmem=28,
        name="hidden_upstream",
    )


def hidden_body(place_ref, *refs):
    pieces, refs = refs[:-7], refs[-7:]
    wg_ref, wu_ref, dact_ref, act_ref, dg_ref, du_ref, x_s = refs
    size = pieces[0].shape[0]

    @pl.when(pl.program_id(0) == 0)
    def _():
        for i, piece in enumerate(pieces):
            x_s[i * size : (i + 1) * size] = piece[...]

    x = x_s[...]
    for first in range(0, act_ref.shape[1], 256):
        at = slice(first, first + 256)
        gate = nn(x, wg_ref[:, at])
        up = nn(x, wu_ref[:, at])
        dact = dact_ref[:, at].astype(F32)
        sig = jax.nn.sigmoid(gate)
        silu = gate * sig
        act_ref[:, at] = (silu * up).astype(BF16)
        dg_ref[:, at] = (dact * up * sig * (1.0 + gate * (1.0 - sig))).astype(BF16)
        du_ref[:, at] = (dact * silu).astype(BF16)


def hidden(place, pieces, w_gate, w_up, dact, own, after=()):
    size, width = pieces[0].shape
    rows = size * len(pieces)
    units = dact.shape[1]
    tile = 512
    steps = units // tile
    first = (lambda place: place[3] * steps) if own else (lambda place: 0)
    made = jax.ShapeDtypeStruct((rows, units), BF16)
    block = pl.BlockSpec((rows, tile), lambda j, place: (0, j))
    weight = pl.BlockSpec((width, tile), lambda j, place: (0, first(place) + j))
    return call(
        hidden_body,
        (made, made, made),
        [place, *pieces, w_gate, w_up, dact],
        [pl.BlockSpec((size, width), lambda j, place: (0, 0))] * len(pieces)
        + [weight, weight, block],
        4 * rows * width * units,
        4 * width * units + 8 * rows * units + 2 * rows * width,
        rows * units,
        after=after,
        prefetch=1,
        grid=(steps,),
        out_specs=(block, block, block),
        scratch_shapes=[pltpu.VMEM((rows, width), BF16)],
        vmem=36,
        name="hidden",
    )


def chunked(total, out_refs):
    size = out_refs[0].shape[0]
    for i, ref in enumerate(out_refs):
        ref[...] = total[i * size : (i + 1) * size].astype(ref.dtype)


def back_body(place_ref, dg_ref, dg_sib, du_ref, du_sib, wg_ref, wg_sib, wu_ref, wu_sib, *outs):
    chunked(
        nt(dg_ref[...], wg_ref[...])
        + nt(dg_sib[...], wg_sib[...])
        + nt(du_ref[...], wu_ref[...])
        + nt(du_sib[...], wu_sib[...]),
        outs,
    )


def hidden_back(place, dg, dg_sib, du, du_sib, w_gate, gate_sib, w_up, up_sib, chunks, after=()):
    rows, half = dg.shape
    width = w_gate.shape[0]
    tile = 512
    size = rows // chunks
    left = pl.BlockSpec((rows, half), lambda j, place: (0, 0))
    own = pl.BlockSpec((tile, half), lambda j, place: (j, place[3]))
    sib = pl.BlockSpec((tile, half), lambda j, place: (j, 0))
    return call(
        back_body,
        tuple(jax.ShapeDtypeStruct((size, width), BF16) for _ in range(chunks)),
        [place, dg, dg_sib, du, du_sib, w_gate, gate_sib, w_up, up_sib],
        [left] * 4 + [own, sib, own, sib],
        8 * rows * width * half,
        8 * width * half + 8 * rows * half + 2 * rows * width,
        after=after,
        prefetch=1,
        grid=(width // tile,),
        out_specs=tuple(pl.BlockSpec((size, tile), lambda j, place: (0, j)) for _ in range(chunks)),
        vmem=52,
        name="hidden_back",
    )


def down_body(place_ref, act_ref, act_sib, wd_ref, wd_sib, *outs):
    chunked(nn(act_ref[...], wd_ref[...]) + nn(act_sib[...], wd_sib[...]), outs)


def down(place, act, act_sib, w_down, down_sib, chunks, after=()):
    rows, half = act.shape
    width = w_down.shape[1]
    tile = 512
    size = rows // chunks
    left = pl.BlockSpec((rows, half), lambda j, place: (0, 0))
    return call(
        down_body,
        tuple(jax.ShapeDtypeStruct((size, width), BF16) for _ in range(chunks)),
        [place, act, act_sib, w_down, down_sib],
        [
            left,
            left,
            pl.BlockSpec((half, tile), lambda j, place: (place[3], j)),
            pl.BlockSpec((half, tile), lambda j, place: (0, j)),
        ],
        4 * rows * width * half,
        4 * width * half + 4 * rows * half + 2 * rows * width,
        after=after,
        prefetch=1,
        grid=(width // tile,),
        out_specs=tuple(pl.BlockSpec((size, tile), lambda j, place: (0, j)) for _ in range(chunks)),
        vmem=24,
        name="down",
    )


def heads_body(nz, contract, keep, place_ref, *refs):
    n_w = 1 if keep else 3
    pieces, refs = refs[:nz], refs[nz:]
    w_refs, (sib_ref, mine_ref), refs = refs[:n_w], refs[n_w : n_w + 2], refs[n_w + 2 :]
    joined = refs[:n_w]
    for d in range(nz):
        at = pl.multiple_of((place_ref[0] ^ d) * HD, HD)
        for i in range(n_w):
            joined[i][:, pl.ds(at, HD)] = pieces[d][:, i * HD : (i + 1) * HD]
    half = sib_ref.shape[0]
    core = place_ref[2] & 1

    def rows_of(start):
        start = pl.multiple_of(start, half)
        total = contract(joined[0][pl.ds(start, half), :], w_refs[0][...])
        for i in range(1, n_w):
            total = total + contract(joined[i][pl.ds(start, half), :], w_refs[i][...])
        return total

    sib_ref[...] = rows_of((1 - core) * half).astype(BF16)
    mine_ref[...] = rows_of(core * half)


def heads_project(place, pieces, weights, contract, keep, after=()):
    nz = len(pieces)
    rows = pieces[0].shape[0]
    n_w = len(weights)
    width = weights[0].shape[1] if contract is nn else weights[0].shape[0]
    half = rows // 2
    joined = (rows, nz * HD)
    out = (
        jax.ShapeDtypeStruct((half, width), BF16),
        jax.ShapeDtypeStruct((half, width), F32),
    ) + ((jax.ShapeDtypeStruct(joined, BF16),) if keep else ())
    return call(
        functools.partial(heads_body, nz, contract, keep),
        out,
        [place, *pieces, *weights],
        [whole(pltpu.SMEM)] + [whole(pltpu.VMEM)] * (nz + n_w),
        2 * rows * width * nz * HD * n_w,
        2 * n_w * (width * nz * HD + rows * nz * HD) + 3 * rows * width,
        after=after,
        out_specs=tuple(whole(pltpu.VMEM) for _ in out),
        scratch_shapes=() if keep else (pltpu.VMEM(joined, BF16),) * n_w,
        vmem=24,
        name="heads_project",
    )


def dheads_body(nz, n, place_ref, *refs):
    mine, refs = refs[:n], refs[n:]
    sibs, refs = refs[:n], refs[n:]
    w_ref, outs, x_s = refs[0], refs[1:-1], refs[-1]
    core = place_ref[2] & 1
    place_rows(mine, x_s, core)
    place_rows(sibs, x_s, 1 - core)
    x = x_s[...]
    wide = outs[0].shape[1]
    for d in range(nz):
        at = pl.multiple_of((place_ref[0] ^ d) * wide, wide)
        outs[d][...] = nt(x, w_ref[pl.ds(at, wide), :]).astype(BF16)


def heads_upstream(place, mine, sibs, w_out, nz, after=()):
    n = len(mine)
    size, width = mine[0].shape
    rows = 2 * n * size
    wide = w_out.shape[0] // nz
    return call(
        functools.partial(dheads_body, nz, n),
        tuple(jax.ShapeDtypeStruct((rows, wide), BF16) for _ in range(nz)),
        [place, *mine, *sibs, w_out],
        [whole(pltpu.SMEM)] + [whole(pltpu.VMEM)] * (2 * n + 1),
        2 * rows * width * nz * wide,
        2 * width * nz * wide + 2 * rows * nz * wide + 2 * rows * width,
        after=after,
        out_specs=tuple(whole(pltpu.VMEM) for _ in range(nz)),
        scratch_shapes=[pltpu.VMEM((rows, width), BF16)],
        name="heads_upstream",
    )


def sum_body(mine_ref, got_ref, *outs):
    chunked(mine_ref[...].astype(F32) + got_ref[...].astype(F32), outs)


def row_sum(mine, got, chunks, after=()):
    rows, width = mine.shape
    size = rows // chunks
    return call(
        sum_body,
        tuple(jax.ShapeDtypeStruct((size, width), BF16) for _ in range(chunks)),
        [mine, got],
        [whole(pltpu.VMEM)] * 2,
        rows * width,
        8 * rows * width,
        after=after,
        out_specs=tuple(whole(pltpu.VMEM) for _ in range(chunks)),
        name="row_sum",
    )


def scale_of(values):
    return lax.rsqrt(jnp.mean(values * values, axis=-1, keepdims=True) + EPSILON)


def norm_body(part_ref, got_ref, x_ref, gain_ref, res_ref, normed_ref):
    residual = x_ref[...].astype(F32) + (part_ref[...].astype(F32) + got_ref[...].astype(F32))
    res_ref[...] = residual
    normed_ref[...] = (residual * scale_of(residual) * gain_ref[...]).astype(BF16)


def norm_rows(part, got, x, gain, after=()):
    rows, width = part.shape
    return call(
        norm_body,
        (
            jax.ShapeDtypeStruct((rows, width), F32),
            jax.ShapeDtypeStruct((rows, width), BF16),
        ),
        [part, got, x, gain],
        [whole(pltpu.VMEM)] * 4,
        8 * rows * width,
        12 * rows * width,
        after=after,
        out_specs=(whole(pltpu.VMEM), whole(pltpu.VMEM)),
        name="norm_rows",
    )


def norm_back_body(part_ref, got_ref, values_ref, add_ref, gain_ref, *outs):
    upstream = part_ref[...].astype(F32) + got_ref[...].astype(F32)
    values = values_ref[...].astype(F32)
    scale = scale_of(values)
    normed = values * scale
    outs[-1][...] = jnp.sum(upstream * normed, axis=0, keepdims=True)
    weighted = upstream * gain_ref[...]
    grad = scale * (weighted - normed * jnp.mean(weighted * normed, axis=-1, keepdims=True))
    total = add_ref[...].astype(F32) + grad
    for ref in outs[:-1]:
        ref[...] = total.astype(ref.dtype)


def norm_back(part, got, values, add, gain, kinds, after=()):
    rows, width = part.shape
    return call(
        norm_back_body,
        tuple(jax.ShapeDtypeStruct((rows, width), kind) for kind in kinds)
        + (jax.ShapeDtypeStruct((1, width), F32),),
        [part, got, values, add, gain],
        [whole(pltpu.VMEM)] * 5,
        16 * rows * width,
        16 * rows * width,
        after=after,
        out_specs=tuple(whole(pltpu.VMEM) for _ in range(len(kinds) + 1)),
        name="norm_back",
    )


def add_body(part_ref, got_ref, res_ref, out_ref):
    out_ref[...] = (
        res_ref[...] + (part_ref[...].astype(F32) + got_ref[...].astype(F32))
    ).astype(BF16)


def add_rows(part, got, residual, after=()):
    return call(
        add_body,
        jax.ShapeDtypeStruct(part.shape, BF16),
        [part, got, residual],
        [whole(pltpu.VMEM)] * 3,
        part.size,
        10 * part.size,
        after=after,
        out_specs=whole(pltpu.VMEM),
        name="add_rows",
    )


def join_body(n, place_ref, *refs):
    core = place_ref[2] & 1
    place_rows(refs[:n], refs[-1], core)
    place_rows(refs[n : 2 * n], refs[-1], 1 - core)


def join_rows(place, mine, sibs, after=()):
    n = len(mine)
    size, width = mine[0].shape
    return call(
        functools.partial(join_body, n),
        jax.ShapeDtypeStruct((2 * n * size, width), BF16),
        [place, *mine, *sibs],
        [whole(pltpu.SMEM)] + [whole(pltpu.VMEM)] * (2 * n),
        0,
        8 * n * size * width,
        after=after,
        out_specs=whole(pltpu.VMEM),
        name="join_rows",
    )


def turn_body(n, block, offset_ref, order_ref, *refs):
    pieces, out_ref = refs[:n], refs[n]
    size, wide = pieces[0].shape
    unit = (
        lax.broadcasted_iota(jnp.int32, (block, block), 0)
        == lax.broadcasted_iota(jnp.int32, (block, block), 1)
    ).astype(F32).astype(BF16)
    for p in range(wide // block):
        at = pl.multiple_of(order_ref[p] * block, block)
        for j in range(n):
            to = pl.multiple_of(offset_ref[j] * size, size)
            made = nt(unit, pieces[j][:, pl.ds(at, block)]).astype(BF16)
            out_ref[p * block : (p + 1) * block, pl.ds(to, size)] = made


def turn(order, group, pieces, offsets=None, after=()):
    wide = pieces[0].shape[1]
    if group % 128 != 0:
        pieces = [
            jnp.concatenate(
                [
                    lax.dynamic_slice_in_dim(piece, order[p] * group, group, 1)
                    for p in range(order.shape[0])
                ],
                axis=1,
            )
            for piece in pieces
        ]
        block = math.gcd(256, wide)
        order_in = jnp.arange(wide // block, dtype=jnp.int32)
    else:
        block = group
        order_in = order
    n = len(pieces)
    size = pieces[0].shape[0]
    tokens = n * size
    if offsets is None:
        offsets = jnp.arange(n, dtype=jnp.int32)
    return call(
        functools.partial(turn_body, n, block),
        jax.ShapeDtypeStruct((wide, tokens), BF16),
        [offsets, order_in, *pieces],
        [whole(pltpu.SMEM)] * 2 + [whole(pltpu.VMEM)] * n,
        2 * tokens * wide * block,
        4 * tokens * wide,
        after=after,
        out_specs=whole(pltpu.VMEM),
        vmem=8 + 4 * tokens * wide // MIB,
        name="turn",
    )


def stack_body(*refs):
    for i, ref in enumerate(refs[:-1]):
        refs[-1][i] = ref[...]


def stack_rows(pieces):
    n = len(pieces)
    return call(
        stack_body,
        jax.ShapeDtypeStruct((n, *pieces[0].shape), BF16),
        list(pieces),
        [whole(pltpu.VMEM)] * n,
        0,
        4 * n * pieces[0].size,
        out_specs=whole(pltpu.VMEM),
        name="stack_rows",
    )


def turn_all_body(block, place_ref, order_ref, own_ref, *refs):
    parts, out_ref = refs[:-1], refs[-1]
    n = len(parts)
    size, wide = parts[0].shape[1:]
    unit = (
        lax.broadcasted_iota(jnp.int32, (block, block), 0)
        == lax.broadcasted_iota(jnp.int32, (block, block), 1)
    ).astype(F32).astype(BF16)

    @pl.when(pl.program_id(0) == 0)
    def _():
        for p in range(wide // block):
            at = pl.multiple_of(order_ref[p] * block, block)
            made = nt(unit, own_ref[:, pl.ds(at, block)]).astype(BF16)
            out_ref[p * block : (p + 1) * block, :] = made

    @pl.when(pl.program_id(0) > 0)
    def _():
        for p in range(wide // block):
            at = pl.multiple_of(order_ref[p] * block, block)
            for j in range(n):
                to = pl.multiple_of((place_ref[0] ^ j) * size, size)
                made = nt(unit, parts[j][0, :, pl.ds(at, block)]).astype(BF16)
                out_ref[p * block : (p + 1) * block, pl.ds(to, size)] = made


def turn_all(order, group, own, parts, m):
    tokens, wide = own.shape
    others, size, _ = parts[0].shape
    if group % 128 != 0:

        def ordered(values):
            axis = values.ndim - 1
            return jnp.concatenate(
                [
                    lax.dynamic_slice_in_dim(values, order[p] * group, group, axis)
                    for p in range(order.shape[0])
                ],
                axis=axis,
            )

        own = ordered(own)
        parts = [ordered(part) for part in parts]
        block = math.gcd(256, wide)
        order_in = jnp.arange(wide // block, dtype=jnp.int32)
    else:
        block = group
        order_in = order
    return call(
        functools.partial(turn_all_body, block),
        jax.ShapeDtypeStruct((wide, (others + 1) * tokens), BF16),
        [m.reshape(1).astype(jnp.int32), order_in, own, *parts],
        [pl.BlockSpec((tokens, wide), lambda d, place, order: (0, 0))]
        + [
            pl.BlockSpec((1, size, wide), lambda d, place, order: (jnp.maximum(d - 1, 0), 0, 0))
        ]
        * len(parts),
        2 * (others + 1) * tokens * wide * block,
        4 * (others + 1) * tokens * wide,
        prefetch=2,
        grid=(others + 1,),
        out_specs=pl.BlockSpec((wide, tokens), lambda d, place, order: (0, d)),
        vmem=52,
        name="turn_all",
    )


def weight_body(sizes, *refs):
    n = sum(sizes)
    lefts, rights, (sent_ref, kept_ref) = refs[:n], refs[n : 2 * n], refs[2 * n :]
    half = pl.num_programs(0) // 2
    first, at = 0, 0
    for size in sizes:
        total = nn(lefts[first][...], rights[first][...])
        for i in range(first + 1, first + size):
            total = total + nn(lefts[i][...], rights[i][...])
        made = total.astype(BF16)
        columns = slice(at, at + total.shape[1])
        first, at = first + size, columns.stop

        @pl.when(pl.program_id(0) < half)
        def _(made=made, columns=columns):
            sent_ref[:, columns] = made

        @pl.when(pl.program_id(0) >= half)
        def _(made=made, columns=columns):
            kept_ref[:, columns] = made


def weight_grad(*groups):
    triples = [triple for group in groups for triple in group]
    wide = triples[0][0].shape[0]
    tokens = sum(right.shape[0] for _, right, _ in triples)
    width = sum(group[0][1].shape[1] for group in groups)
    steps = 4
    tile = wide // steps
    half = steps // 2
    made = jax.ShapeDtypeStruct((wide // 2, width), BF16)
    return call(
        functools.partial(weight_body, [len(group) for group in groups]),
        (made,) * 2,
        [left for left, _, _ in triples] + [right for _, right, _ in triples],
        [
            pl.BlockSpec((tile, right.shape[0]), lambda i, at=at: ((i + half) % steps, at))
            for _, right, at in triples
        ]
        + [pl.BlockSpec(right.shape, lambda i: (0, 0)) for _, right, _ in triples],
        sum(2 * wide * right.size for _, right, _ in triples),
        2 * (tokens * wide + sum(right.size for _, right, _ in triples) + wide * width),
        grid=(steps,),
        out_specs=(
            pl.BlockSpec((tile, width), lambda i: (jnp.minimum(i, half - 1), 0)),
            pl.BlockSpec((tile, width), lambda i: (jnp.maximum(i - half, 0), 0)),
        ),
        vmem=36,
        name="weight_grad",
    )


def sum3_body(n, *refs):
    total = refs[0][...].astype(F32)
    for ref in refs[1:n]:
        total = total + ref[...].astype(F32)
    low_ref, high_ref = refs[n:]
    low_ref[...] = total[0]
    high_ref[...] = total[1].astype(BF16)


def final_sum(terms, after=()):
    wide, width = terms[0].shape
    high = wide // 2
    tile = math.gcd(high, 128)
    block = pl.BlockSpec((2, tile, width), lambda i: (0, i, 0))
    out = pl.BlockSpec((tile, width), lambda i: (i, 0))
    return call(
        functools.partial(sum3_body, len(terms)),
        (
            jax.ShapeDtypeStruct((high, width), F32),
            jax.ShapeDtypeStruct((high, width), BF16),
        ),
        [term.reshape(2, high, width) for term in terms],
        [block] * len(terms),
        wide * width,
        wide * width * 8,
        after=after,
        grid=(high // tile,),
        out_specs=(out, out),
        name="final_sum",
    )


def merge_body(kept_ref, got_ref, low_ref, high_ref):
    total = kept_ref[...].astype(F32) + got_ref[...].astype(F32)
    low_ref[...] = total[0]
    high_ref[...] = total[1].astype(BF16)


def merge(kept, got, after=()):
    wide, width = kept.shape
    high = wide // 2
    tile = math.gcd(high, 128)
    operands = [kept.reshape(2, high, width), got.reshape(2, high, width)]
    block = pl.BlockSpec((2, tile, width), lambda i: (0, i, 0))
    out = pl.BlockSpec((tile, width), lambda i: (i, 0))
    return call(
        merge_body,
        (
            jax.ShapeDtypeStruct((high, width), F32),
            jax.ShapeDtypeStruct((high, width), BF16),
        ),
        operands,
        [block, block],
        wide * width,
        wide * width * 8,
        after=after,
        grid=(high // tile,),
        out_specs=(out, out),
        name="merge",
    )


def lay_body(turned, place_ref, own_ref, got_ref, out_ref):
    value = jnp.where(pl.program_id(0) == 0, own_ref[...], got_ref[...].astype(F32))
    out_ref[...] = value.T if turned else value


def lay(place, own, got, turned, width=None):
    rows = own.shape[0]
    width = width or own.shape[1]
    if turned:
        shape, block = (2 * width, rows), (width, rows)
        index = lambda i, place: (place[3] ^ i, 0)
    else:
        shape, block = (rows, 2 * width), (rows, width)
        index = lambda i, place: (0, place[3] ^ i)
    fixed = pl.BlockSpec((rows, width), lambda i, place: (0, 0))
    return call(
        functools.partial(lay_body, turned),
        jax.ShapeDtypeStruct(shape, F32),
        [place, own, got],
        [fixed, fixed],
        0,
        14 * rows * width,
        prefetch=1,
        grid=(2,),
        out_specs=pl.BlockSpec(block, index),
        name="lay",
    )


def qkv_sum_body(kept_ref, got_ref, own_ref, *outs):
    size = own_ref.shape[0]
    total = kept_ref[...].astype(F32) + got_ref[...].astype(F32)
    own_ref[...] = total[:size]
    for i, ref in enumerate(outs):
        ref[...] = total[(i + 1) * size : (i + 2) * size].astype(BF16)


def split_sum(kept, got, n):
    rows, width = kept.shape
    size = rows // n
    return call(
        qkv_sum_body,
        (jax.ShapeDtypeStruct((size, width), F32),)
        + (jax.ShapeDtypeStruct((size, width), BF16),) * (n - 1),
        [kept, got],
        [whole(pltpu.VMEM)] * 2,
        rows * width,
        8 * rows * width,
        out_specs=(whole(pltpu.VMEM),) * n,
        name="split_sum",
    )


def place_heads_body(nz, place_ref, *refs):
    pieces, outs = refs[:nz], refs[nz:]
    for d in range(nz):
        at = pl.multiple_of((place_ref[0] ^ d) * HD, HD)
        for i, out in enumerate(outs):
            out[:, pl.ds(at, HD)] = pieces[d][:, i * HD : (i + 1) * HD].astype(F32)


def place_heads(place, pieces):
    nz = len(pieces)
    rows = pieces[0].shape[0]
    return call(
        functools.partial(place_heads_body, nz),
        (jax.ShapeDtypeStruct((rows, nz * HD), F32),) * 3,
        [place, *pieces],
        [whole(pltpu.SMEM)] + [whole(pltpu.VMEM)] * nz,
        0,
        20 * rows * nz * HD,
        out_specs=(whole(pltpu.VMEM),) * 3,
        name="place_heads",
    )


def rope_tables(position):
    middle = HD // 2
    frequency = THETA ** (-(jnp.arange(middle, dtype=F32) * 2.0 / HD))
    angles = position.astype(F32)[..., None] * frequency
    cosine = jnp.cos(angles)
    sine = jnp.sin(angles)
    return (
        jnp.concatenate([cosine, cosine], axis=-1),
        jnp.concatenate([-sine, sine], axis=-1),
    )


def rms_scale(values):
    return lax.rsqrt(jnp.mean(values * values, axis=-1, keepdims=True) + EPSILON)


def layer(
    n_seq,
    n_mp,
    mixed_in,
    w_query,
    w_key,
    w_value,
    w_out,
    gain_attn,
    w_gate,
    w_up,
    w_down,
    gain_mlp,
    doc_ends,
    cotangent,
):
    rows, width = mixed_in.shape
    nz = w_query.shape[1] // HD
    ring = n_seq // nz
    bits = n_seq.bit_length() - 1
    low_bits = ring.bit_length() - 1
    units = w_gate.shape[1]
    half_units = units // 2
    half_rows = rows // 2
    group = width // n_seq
    pair_bit = bits - 2
    pair = 1 << pair_bit

    s = lax.axis_index("seq")
    m = lax.axis_index("mp")
    z, r = s // ring, s % ring
    core = m % 2
    side = m // 2
    low = (s >> pair_bit) & 1

    def seq_swap(v, distance):
        return lax.ppermute(v, "seq", [(i, i ^ distance) for i in range(n_seq)])

    def mp_swap(v, distance):
        return lax.ppermute(v, "mp", [(i, i ^ distance) for i in range(n_mp)])

    sum_bits = list(range(pair_bit)) + [bits - 1]
    places = []
    for p in range(n_seq):
        e = 0
        for at, bit in enumerate(sum_bits + [pair_bit]):
            if (p >> (bits - 1 - at)) & 1:
                e |= 1 << bit
        places.append(e)
    order = s ^ jnp.array(places, dtype=jnp.int32)

    ORDER.clear()

    place = jnp.stack([z, r, m, low]).astype(jnp.int32)
    blocks = (z ^ jnp.arange(nz, dtype=jnp.int32)) * ring + r
    token_index = blocks[:, None] * rows + jnp.arange(rows, dtype=jnp.int32)[None, :]
    ends_below = doc_ends[None, None, :] <= token_index[..., None]
    begin = jnp.max(jnp.where(ends_below, doc_ends, 0), axis=-1)
    cos_own, sin_own = rope_tables(token_index[0] - begin[0])
    cos_all, sin_all = rope_tables(token_index - begin)
    weights = [w_query, w_key, w_value]
    half_z = nz // 2
    made = project_qkv(
        place,
        mixed_in,
        gain_attn.reshape(1, width),
        weights,
        cos_own,
        sin_own,
        list(range(half_z, nz)),
    )
    normed = made[-1]
    pieces = {half_z + i: made[i] for i in range(half_z)}
    made = project_qkv(place, normed, None, weights, cos_own, sin_own, list(range(half_z)))
    pieces.update({i: made[i] for i in range(half_z)})
    pieces = [pieces[0]] + [seq_swap(pieces[d], d * ring) for d in range(1, nz)]
    near = pieces
    own_kv = [piece[:, HD:] for piece in pieces]
    for d in range(nz - 2, 0, -1):
        own_kv[d], own_kv[d + 1] = lax.optimization_barrier((own_kv[d], own_kv[d + 1]))
    keys_values = [near, [seq_swap(kv, 1) for kv in own_kv]]
    for b in range(1, low_bits):
        keys_values = keys_values + [
            [seq_swap(kv[:, -2 * HD :], 1 << b) for kv in kvs] for kvs in keys_values
        ]
    queries = pieces

    quarter = rows // n_mp
    my_quarter = lax.dynamic_slice_in_dim(normed, m * quarter, quarter, 0)
    halves = [
        lax.dynamic_slice_in_dim(w_down, low * half_units, half_units, 0),
        lax.dynamic_slice_in_dim(w_gate, low * half_units, half_units, 1),
        lax.dynamic_slice_in_dim(w_up, low * half_units, half_units, 1),
    ]
    cot_half = lax.dynamic_slice_in_dim(cotangent, core * half_rows, half_rows, 0)

    flat = [kv for kvs in keys_values for kv in kvs]
    far = [kv for kvs in keys_values[1:] for kv in kvs]
    cot_half, *halves = hold([cot_half, *halves], after=pieces)
    cot_pair = seq_swap(cot_half, pair)
    outs = attend(place, doc_ends, queries, flat, nz, ring, after=[cos_all, sin_all])
    heads = [outs[0]] + [seq_swap(outs[d], d * ring) for d in range(1, nz)]

    size = half_rows // CHUNKS
    last_low = 1 << sum_bits[pair_bit - 1]
    high = 1 << sum_bits[pair_bit]
    gain_mlp_row = gain_mlp.reshape(1, width)
    gain_attn_row = gain_attn.reshape(1, width)

    def chunks_of(values):
        return [values[i * size : (i + 1) * size] for i in range(CHUNKS)]

    def low_sums(sent, kept):
        for bit in sum_bits[: pair_bit - 1]:
            kept, sent = merge(kept, seq_swap(sent, 1 << bit))
        return kept, seq_swap(sent, last_low)

    x_chunks = chunks_of(lax.dynamic_slice_in_dim(mixed_in, core * half_rows, half_rows, 0))
    cot_chunks = chunks_of(cot_half)
    cot_all = cot_chunks + chunks_of(cot_pair)
    spots = jnp.concatenate(
        [core * CHUNKS + jnp.arange(CHUNKS), (1 - core) * CHUNKS + jnp.arange(CHUNKS)]
    ).astype(jnp.int32)
    v = types.SimpleNamespace(
        residual=[None] * CHUNKS,
        normed=[None] * (2 * CHUNKS),
        back=[None] * CHUNKS,
        back_across=[None] * CHUNKS,
        residual_grad=[None] * CHUNKS,
        branch=[None] * CHUNKS,
        branch_sib=[None] * CHUNKS,
        gain_mlp=[None] * CHUNKS,
        gain_attn=[None] * CHUNKS,
        grad_rows=[None] * CHUNKS,
        grad_sib=[None] * CHUNKS,
        quarters={0: my_quarter},
        out_grads=(),
    )
    def heads_out():
        sib, v.mine, v.heads_placed = heads_project(
            place, heads, [w_out], nn, True, after=[cot_pair]
        )
        v.sib = mp_swap(sib, 1)

    def out_sum():
        v.parts = row_sum(v.mine, v.sib, CHUNKS)
        v.across = [mp_swap(part, 2) for part in v.parts]

    def swap_weights():
        v.down_sib, v.gate_sib, v.up_sib = [mp_swap(half, 1) for half in hold(halves)]

    def dact_own():
        v.dact = hidden_upstream(place, cot_all, w_down, True)

    def dact_sib():
        v.dact_sib = hidden_upstream(place, cot_all, v.down_sib, False)

    def norm_chunk(i):
        v.residual[i], v.normed[i] = norm_rows(
            v.parts[i], v.across[i], x_chunks[i], gain_mlp_row
        )
        v.normed[CHUNKS + i] = seq_swap(v.normed[i], pair)

    def turn_cot():
        v.cot_turned = turn(order, group, cot_all)

    def swap_cot():
        (turned,) = hold([v.cot_turned])
        v.cot_both = [turned, mp_swap(turned, 1)]

    def hidden_sib():
        v.act_sib, dg_sib, du_sib = hidden(
            place, v.normed, v.gate_sib, v.up_sib, v.dact_sib, False
        )
        v.act_got = mp_swap(v.act_sib, 1)
        v.dg_sib, v.du_sib = dg_sib, du_sib

    def swap_dg():
        (part,) = hold([v.dg_sib])
        v.dg_got = mp_swap(part, 1)

    def swap_du():
        (part,) = hold([v.du_sib])
        v.du_got = mp_swap(part, 1)

    def hidden_own():
        v.act, v.dg, v.du = hidden(place, v.normed, w_gate, w_up, v.dact, True)

    def turn_normed():
        v.normed_turned = turn(order, group, v.normed)

    def swap_normed():
        (turned,) = hold([v.normed_turned])
        v.normed_both = [turned, mp_swap(turned, 1)]

    def grad_down():
        v.sent_down, v.part_down = weight_grad(
            [(v.cot_both[0], v.act, 0), (v.cot_both[1], v.act_got, 0)]
        )

    def send_down():
        (sent,) = hold([v.sent_down])
        v.low_down = low_sums(sent, v.part_down)

    def hidden_in():
        v.made = hidden_back(
            place,
            v.dg,
            v.dg_sib,
            v.du,
            v.du_sib,
            w_gate,
            v.gate_sib,
            w_up,
            v.up_sib,
            2 * CHUNKS,
        )
        v.made_got = [seq_swap(v.made[CHUNKS + i], pair) for i in range(CHUNKS)]

    def back_chunk(i):
        (v.back[i],) = row_sum(v.made[i], v.made_got[i], 1)
        v.back_across[i] = mp_swap(v.back[i], 2)

    def norm_back_chunk(i):
        v.residual_grad[i], v.branch[i], v.gain_mlp[i] = norm_back(
            v.back[i], v.back_across[i], v.residual[i], cot_chunks[i], gain_mlp_row, (F32, BF16)
        )
        v.branch_sib[i] = mp_swap(v.branch[i], 1)

    def grad_gate():
        v.sent_gate, v.part_gate = weight_grad(
            [(v.normed_both[0], v.dg, 0), (v.normed_both[1], v.dg_got, 0)]
        )

    def send_gate():
        (sent,) = hold([v.sent_gate])
        v.low_gate = low_sums(sent, v.part_gate)

    def grad_up():
        v.sent_up, v.part_up = weight_grad(
            [(v.normed_both[0], v.du, 0), (v.normed_both[1], v.du_got, 0)],
            [(v.branch_turned, v.heads_placed, 0)],
        )

    def send_up():
        (sent,) = hold([v.sent_up])
        v.low_up = low_sums(sent, v.part_up)

    def merge_down():
        v.kept_down, v.high_down = merge(*v.low_down)

    def high_down():
        (sent,) = hold([v.high_down], after=v.out_grads)
        v.come_down = seq_swap(sent, high)

    def merge_gate():
        v.kept_gate, v.high_gate = merge(*v.low_gate)

    def high_gate():
        (sent,) = hold([v.high_gate])
        v.come_gate = seq_swap(sent, high)

    def merge_up():
        v.kept_up, v.high_up = merge(*v.low_up)

    def high_up():
        (sent,) = hold([v.high_up])
        v.come_up = seq_swap(sent, high)

    def sum_down():
        v.own_down, v.pair_down = final_sum([v.kept_down, v.come_down])

    def sum_gate():
        v.own_gate, v.pair_gate = final_sum([v.kept_gate, v.come_gate])

    def sum_up():
        v.own_up, v.pair_up = final_sum([v.kept_up, v.come_up])

    def pair_down():
        (sent,) = hold([v.pair_down])
        v.theirs_down = seq_swap(sent, pair)

    def pair_gate():
        (sent,) = hold([v.pair_gate])
        v.theirs_gate = seq_swap(sent, pair)

    def pair_up():
        (sent,) = hold([v.pair_up])
        v.theirs_up = seq_swap(sent, pair)

    def lay_down():
        v.down_share = lay(place, v.own_down, v.theirs_down, True)

    def lay_gate():
        v.gate_share = lay(place, v.own_gate, v.theirs_gate, False)

    def lay_up():
        v.up_share = lay(place, v.own_up, v.theirs_up, False, half_units)

    def gather_z(d):
        (part,) = hold([v.quarters[d & (d - 1)]])
        v.quarters[d] = seq_swap(part, ring * (d & -d))

    def gather_x():
        v.rows = stack_rows([v.quarters[d] for d in range(1, nz)])
        v.rows_x = mp_swap(v.rows, 2)

    def gather_core():
        v.rows_core = [mp_swap(part, 1) for part in hold([v.rows, v.rows_x])]

    def heads_in():
        made = heads_upstream(place, v.branch, v.branch_sib, w_out, nz)
        v.out_grads = [made[0]] + [seq_swap(made[d], d * ring) for d in range(1, nz)]

    def attend_far():
        v.dq_far, *summed = attend_back(
            place, doc_ends, queries, v.out_grads, far, None, nz, ring, 1, ring - 1, BF16
        )
        summed = [None] + summed
        for b in reversed(range(low_bits)):
            bit = 1 << b
            for e in range(bit):
                got = seq_swap(summed[e | bit], bit)
                summed[e] = (
                    got
                    if summed[e] is None
                    else (summed[e].astype(F32) + got.astype(F32)).astype(BF16)
                )
        v.dkv_got = summed[0]

    def attend_near():
        v.dq, v.dkv = attend_back(
            place, doc_ends, queries, v.out_grads, near, v.dq_far, nz, ring, 0, 1, F32
        )

    def head_grads():
        v.grads = finish_grads(v.dq, v.dkv, v.dkv_got, cos_all, sin_all)
        v.own_grads = [v.grads[0]] + [
            seq_swap(v.grads[d], d * ring) for d in range(1, nz)
        ]

    def turn_branch():
        v.branch_turned = turn(order, group, v.branch + v.branch_sib, spots)

    def turn_rows():
        v.all_turned = turn_all(
            order, group, normed, [v.rows, v.rows_core[0], v.rows_x, v.rows_core[1]], m
        )

    def grad_qkv():
        v.sent_qkv, v.part_qkv = weight_grad(
            [(v.all_turned, v.grads[d], d) for d in range(nz)]
        )

    def send_qkv():
        (sent,) = hold([v.sent_qkv])
        v.low_qkv = low_sums(sent, v.part_qkv)

    def split_qkv():
        own, *sent = split_sum(*v.low_qkv, nz)
        v.qkv_heads = [own] + [seq_swap(sent[d - 1], d * ring) for d in range(1, nz)]

    def lay_qkv():
        v.shares = place_heads(place, v.qkv_heads)

    def rows_in():
        sib, v.in_mine = heads_project(place, v.own_grads, weights, nt, False)
        v.in_sib = mp_swap(sib, 1)

    def in_sum():
        v.in_parts = row_sum(v.in_mine, v.in_sib, CHUNKS)
        v.in_across = [mp_swap(part, 2) for part in v.in_parts]

    def norm_in_chunk(i):
        v.grad_rows[i], v.gain_attn[i] = norm_back(
            v.in_parts[i], v.in_across[i], x_chunks[i], v.residual_grad[i], gain_attn_row, (BF16,)
        )
        v.grad_sib[i] = mp_swap(v.grad_rows[i], 1)

    def join_in():
        v.input_grad = join_rows(place, v.grad_rows, v.grad_sib)

    def down_rows():
        v.down_mine, v.down_theirs = down(place, v.act, v.act_sib, w_down, v.down_sib, 2)

    def pair_rows():
        (sent,) = hold([v.down_theirs])
        v.down_got = seq_swap(sent, pair)

    def sum_rows():
        (v.down_part,) = row_sum(v.down_mine, v.down_got, 1)
        v.down_across = mp_swap(v.down_part, 2)

    def add_out():
        v.out_rows = add_rows(
            v.down_part, v.down_across, jnp.concatenate(v.residual, axis=0)
        )
        v.out_sib = mp_swap(v.out_rows, 1)

    def join_out():
        v.mixed_out = join_rows(place, [v.out_rows], [v.out_sib])

    def gains_core():
        (v.gains,) = hold([jnp.concatenate([sum(v.gain_attn), sum(v.gain_mlp)])])
        v.gains_sib = mp_swap(v.gains, 1)

    def gains_seq():
        (both,) = hold([v.gains + v.gains_sib])
        v.gains_all = lax.all_gather(both, "seq")

    def gains_sum():
        (every,) = hold([v.gains_all])
        v.gain_share = jnp.sum(lax.dynamic_slice_in_dim(every, s * group, group, 2), axis=0)

    gather_z(1)
    loose(turn_cot)
    dact_own()
    heads_out()
    out_sum()
    swap_weights()
    norm_chunk(1)
    dact_sib()
    norm_chunk(0)
    swap_cot()
    gather_z(2)
    hidden_sib()
    turn_normed()
    swap_dg()
    hidden_own()
    loose(swap_du)
    swap_normed()
    grad_down()
    hidden_in()
    send_down()
    grad_gate()
    send_gate()
    back_chunk(0)
    gather_z(3)
    back_chunk(1)
    norm_back_chunk(1)
    loose(norm_back_chunk, 0)
    gather_x()
    heads_in()
    merge_down()
    high_down()
    loose(gather_core)
    attend_far()
    attend_near()
    turn_branch()
    grad_up()
    send_up()
    merge_gate()
    high_gate()
    sum_down()
    head_grads()
    pair_down()
    rows_in()
    merge_up()
    high_up()
    in_sum()
    down_rows()
    turn_rows()
    loose(norm_in_chunk, 0)
    grad_qkv()
    lay_down()
    norm_in_chunk(1)
    loose(sum_gate)
    pair_rows()
    send_qkv()
    gains_core()
    gains_seq()
    pair_gate()
    sum_rows()
    split_qkv()
    sum_up()
    pair_up()
    join_in()
    lay_gate()
    lay_up()
    add_out()
    join_out()
    gains_sum()
    lay_qkv()
    return (
        v.mixed_out,
        v.input_grad,
        *v.shares,
        (v.own_up[:, half_units:] + v.theirs_up[:, half_units:].astype(F32)).T,
        v.gain_share[0],
        v.gate_share,
        v.up_share,
        v.down_share,
        v.gain_share[1],
    )


def solution(mesh):
    placed = (
        P("seq", None),
        P(None, "mp"),
        P(None, "mp"),
        P(None, "mp"),
        P("mp", None),
        P(),
        P(None, "mp"),
        P(None, "mp"),
        P("mp", None),
        P(),
        P(),
        P("seq", None),
    )
    return jax.shard_map(
        functools.partial(layer, mesh.shape["seq"], mesh.shape["mp"]),
        mesh=mesh,
        in_specs=placed,
        out_specs=(
            P("seq", None),
            P("seq", None),
            P("seq", "mp"),
            P("seq", "mp"),
            P("seq", "mp"),
            P("mp", "seq"),
            P("seq"),
            P("seq", "mp"),
            P("seq", "mp"),
            P("mp", "seq"),
            P("seq"),
        ),
        check_vma=False,
    )
```

```python
import functools
import math
import types

import jax
import jax.numpy as jnp
from jax import lax
from jax.experimental import pallas as pl
from jax.experimental.pallas import tpu as pltpu
from jax.sharding import PartitionSpec as P

HD = 128
EPSILON = 1e-05
THETA = 10000.0
FACTOR = 1.0 / math.sqrt(HD)
CLAMP = 80.0
CHUNKS = 2
SHARE = 0.5
ORDER = []
LOOSE = [False]
MIB = 1024 * 1024
F32 = jnp.float32
BF16 = jnp.bfloat16


def nn(left, right):
    return lax.dot_general(left, right, (((1,), (0,)), ((), ())), preferred_element_type=F32)


def nt(left, right):
    return lax.dot_general(left, right, (((1,), (1,)), ((), ())), preferred_element_type=F32)


def tn(left, right):
    return lax.dot_general(left, right, (((0,), (0,)), ((), ())), preferred_element_type=F32)


def call(
    body,
    out_shape,
    operands,
    in_specs,
    flops,
    moved,
    transcendentals=0,
    after=(),
    prefetch=0,
    chain=True,
    vmem=20,
    **kwargs,
):
    n = prefetch + len(in_specs)
    chain = chain and not LOOSE[0]
    after = list(after) + (ORDER if chain else [])

    def kernel(*refs):
        body(*refs[:n], *refs[n + len(after) :])

    in_specs = list(in_specs) + [pl.BlockSpec(memory_space=pl.ANY)] * len(after)
    if prefetch:
        kwargs = {
            "name": kwargs.pop("name"),
            "grid_spec": pltpu.PrefetchScalarGridSpec(
                num_scalar_prefetch=prefetch, in_specs=in_specs, **kwargs
            ),
        }
    else:
        kwargs["in_specs"] = in_specs
    made = pl.pallas_call(
        kernel,
        out_shape=out_shape,
        compiler_params=pltpu.CompilerParams(vmem_limit_bytes=vmem * MIB),
        cost_estimate=pl.CostEstimate(
            flops=int(flops / SHARE),
            bytes_accessed=int(moved / SHARE),
            transcendentals=int(transcendentals / SHARE),
        ),
        **kwargs,
    )(*operands, *after)
    if chain:
        ORDER[:] = [made[0] if isinstance(made, (tuple, list)) else made]
    return made


def hold(values, after=()):
    n = len(values)
    if LOOSE[0]:
        return list(lax.optimization_barrier((*values, *after))[:n])
    made = lax.optimization_barrier((*values, *ORDER, *after))
    ORDER[:] = made[n : n + len(ORDER)]
    return list(made[:n])


def loose(step, *args):
    LOOSE[0] = True
    step(*args)
    LOOSE[0] = False


def whole(memory):
    return pl.BlockSpec(memory_space=memory)


def rotated(values, cosine, signed):
    return values * cosine + pltpu.roll(values, HD // 2, 1) * signed


def unrotated(values, cosine, signed):
    return values * cosine - pltpu.roll(values, HD // 2, 1) * signed


def qkv_body(n, fresh, place_ref, *refs):
    if fresh:
        x_ref, gain_ref, refs = refs[0], refs[1], refs[2:]
    else:
        x_ref, refs = refs[0], refs[1:]
    wq_ref, wk_ref, wv_ref, cos_ref, sin_ref = refs[:5]
    outs, (w_s, x_s) = refs[5 : 5 + n], refs[-2:]
    step = pl.program_id(0)

    @pl.when(step == 0)
    def _():
        if fresh:
            x = x_ref[...].astype(F32)
            x_s[...] = (x * scale_of(x) * gain_ref[...]).astype(BF16)
            refs[5 + n][...] = x_s[...]
        else:
            x_s[...] = x_ref[...]

    w_s[:, :HD] = wq_ref[...]
    w_s[:, HD : 2 * HD] = wk_ref[...]
    w_s[:, 2 * HD :] = wv_ref[...]
    made = nn(x_s[...], w_s[...])
    cosine = cos_ref[...]
    signed = sin_ref[...]
    query = rotated(made[:, :HD], cosine, signed).astype(BF16)
    key = rotated(made[:, HD : 2 * HD], cosine, signed).astype(BF16)
    value = made[:, 2 * HD :].astype(BF16)
    for i in range(n):

        @pl.when(step == i)
        def _(i=i):
            outs[i][:, :HD] = query
            outs[i][:, HD : 2 * HD] = key
            outs[i][:, 2 * HD :] = value


def project_qkv(place, x, gain, weights, cosine, signed, spots):
    n = len(spots)
    rows, width = x.shape
    fresh = gain is not None
    fixed = pl.BlockSpec((rows, width), lambda i, place: (0, 0))
    table = pl.BlockSpec((rows, HD), lambda i, place: (0, 0))
    first = spots[0]
    assert list(spots) == [first ^ i for i in range(n)]
    weight = pl.BlockSpec((width, HD), lambda i, place: (0, place[0] ^ first ^ i))
    piece = jax.ShapeDtypeStruct((rows, 3 * HD), BF16)
    return call(
        functools.partial(qkv_body, n, fresh),
        (piece,) * n + ((jax.ShapeDtypeStruct(x.shape, BF16),) if fresh else ()),
        [place, x] + ([gain] if fresh else []) + [*weights, cosine, signed],
        [fixed]
        + ([pl.BlockSpec((1, width), lambda i, place: (0, 0))] if fresh else [])
        + [weight] * 3
        + [table] * 2,
        6 * n * rows * width * HD,
        4 * rows * width + 6 * n * width * HD + 6 * n * rows * HD,
        prefetch=1,
        grid=(n,),
        out_specs=(pl.BlockSpec((rows, 3 * HD), lambda i, place: (0, 0)),) * n
        + ((fixed,) if fresh else ()),
        scratch_shapes=[pltpu.VMEM((width, 3 * HD), BF16), pltpu.VMEM((rows, width), BF16)],
        vmem=60,
        name="project_qkv",
    )


def begin_of(index, ends_ref, count):
    begin = jnp.zeros_like(index)
    for e in range(count):
        end = ends_ref[e]
        begin = jnp.where(end <= index, jnp.maximum(begin, end), begin)
    return begin


def finish_of(index, ends_ref, count):
    finish = jnp.zeros_like(index) + ends_ref[count - 1]
    for e in range(count):
        end = ends_ref[e]
        finish = jnp.where(end > index, jnp.minimum(finish, end), finish)
    return finish


def attend_body(nz, ring, count, place_ref, ends_ref, *refs):
    n_kv = nz * ring
    q_refs, refs = refs[:nz], refs[nz:]
    kv_refs, refs = refs[:n_kv], refs[n_kv:]
    o_refs, refs = refs[:nz], refs[nz:]
    q_s, k_s, v_s, o_s, acc = refs
    z, r = place_ref[0], place_ref[1]
    rows = q_s.shape[1]
    for d in range(nz):
        q_s[d] = q_refs[d][:, :HD]
    for i in range(n_kv):
        first = kv_refs[i].shape[1] - 2 * HD
        k_s[i] = kv_refs[i][:, first : first + HD]
        v_s[i] = kv_refs[i][:, first + HD :]

    @pl.loop(0, nz)
    def per_query(d):
        q_block = (z ^ d) * ring + r
        q_start = q_block * rows
        q_index = q_start + lax.broadcasted_iota(jnp.int32, (rows, 1), 0)
        begin = begin_of(q_index, ends_ref, count)
        shift = jnp.log((finish_of(q_index, ends_ref, count) - begin).astype(F32))
        first_begin = begin_of(q_start, ends_ref, count)
        last_begin = begin_of(q_start + (rows - 1), ends_ref, count)
        acc[...] = jnp.zeros_like(acc)

        @pl.loop(0, n_kv)
        def per_key(i):
            k_block = (z ^ (i & (nz - 1))) * ring + (r ^ (i // nz))
            k_start = k_block * rows
            needed = (k_block <= q_block) & (k_start + rows > first_begin)
            full = (k_block < q_block) & (k_start >= last_begin)

            def tile(masked):
                half = rows // 2
                for part in range(2):
                    at = slice(part * half, (part + 1) * half)
                    scores = nt(q_s[d, at], k_s[i])
                    grown = jnp.exp(jnp.minimum(shift[at] - scores * FACTOR, CLAMP))
                    probs = pl.reciprocal(1.0 + grown, approx=True)
                    if masked:
                        k_index = k_start + lax.broadcasted_iota(jnp.int32, (1, rows), 1)
                        allowed = (k_index <= q_index[at]) & (k_index >= begin[at])
                        probs = jnp.where(allowed, probs, 0.0)
                    acc[at] += nn(probs.astype(BF16), v_s[i])

            pl.when(needed & full)(functools.partial(tile, False))
            pl.when(needed & jnp.logical_not(full))(functools.partial(tile, True))

        o_s[d] = acc[...].astype(BF16)

    for d in range(nz):
        o_refs[d][...] = o_s[d]


def attend(place, ends, queries, keys_values, nz, ring, after=()):
    rows = queries[0].shape[0]
    n_kv = nz * ring
    pairs = nz * n_kv / 2
    return call(
        functools.partial(attend_body, nz, ring, ends.shape[0]),
        tuple(jax.ShapeDtypeStruct((rows, HD), BF16) for _ in range(nz)),
        [place, ends, *queries, *keys_values],
        [whole(pltpu.SMEM)] * 2 + [whole(pltpu.VMEM)] * (nz + n_kv),
        pairs * 4 * rows * rows * HD * 2,
        2 * (2 * nz + 2 * n_kv) * rows * HD,
        pairs * 2 * rows * rows,
        after=after,
        out_specs=tuple(whole(pltpu.VMEM) for _ in range(nz)),
        scratch_shapes=[
            pltpu.VMEM((nz, rows, HD), BF16),
            pltpu.VMEM((n_kv, rows, HD), BF16),
            pltpu.VMEM((n_kv, rows, HD), BF16),
            pltpu.VMEM((nz, rows, HD), BF16),
            pltpu.VMEM((rows, HD), F32),
        ],
        vmem=12 + 2 * n_kv * rows * HD * 8 // MIB,
        name="attend",
    )


def attend_back_body(nz, ring, n_dr, first_dr, chained, count, place_ref, ends_ref, *refs):
    n_kv = nz * n_dr
    q_refs, refs = refs[:nz], refs[nz:]
    do_refs, refs = refs[:nz], refs[nz:]
    kv_refs, refs = refs[:n_kv], refs[n_kv:]
    if chained:
        before_ref, refs = refs[0], refs[1:]
    dq_ref, refs = refs[0], refs[1:]
    dkv_refs, refs = refs[:n_dr], refs[n_dr:]
    q_s, do_s, k_s, v_s, begin_s, shift_s, dkv_s, dk_acc, dv_acc = refs
    z, r = place_ref[0], place_ref[1]
    rows = q_s.shape[1]
    for d in range(nz):
        q_s[d] = q_refs[d][:, :HD]
        do_s[d] = do_refs[d][...]
    for i in range(n_kv):
        first = kv_refs[i].shape[1] - 2 * HD
        k_s[i] = kv_refs[i][:, first : first + HD]
        v_s[i] = kv_refs[i][:, first + HD :]
    if chained:
        dq_ref[...] = before_ref[...]
    else:
        dq_ref[...] = jnp.zeros_like(dq_ref)

    @pl.loop(0, nz)
    def tables(d):
        q_index = ((z ^ d) * ring + r) * rows + lax.broadcasted_iota(jnp.int32, (1, rows), 1)
        begin = begin_of(q_index, ends_ref, count)
        begin_s[d] = begin
        shift_s[d] = jnp.log((finish_of(q_index, ends_ref, count) - begin).astype(F32))

    @pl.loop(0, n_kv)
    def per_key(i):
        k_block = (z ^ (i & (nz - 1))) * ring + (r ^ (first_dr + i // nz))
        k_start = k_block * rows
        dk_acc[...] = jnp.zeros_like(dk_acc)
        dv_acc[...] = jnp.zeros_like(dv_acc)

        @pl.loop(0, nz)
        def per_query(d):
            q_block = (z ^ d) * ring + r
            q_start = q_block * rows
            first_begin = begin_of(q_start, ends_ref, count)
            last_begin = begin_of(q_start + (rows - 1), ends_ref, count)
            needed = (k_block <= q_block) & (k_start + rows > first_begin)
            full = (k_block < q_block) & (k_start >= last_begin)

            def tile(masked):
                half = rows // 2
                for part in range(2):
                    at = slice(part * half, (part + 1) * half)
                    keys = k_s[i, at]
                    scores = nt(keys, q_s[d])
                    grown = jnp.exp(jnp.minimum(shift_s[d] - scores * FACTOR, CLAMP))
                    probs = pl.reciprocal(1.0 + grown, approx=True)
                    if masked:
                        k_index = (
                            k_start
                            + part * half
                            + lax.broadcasted_iota(jnp.int32, (half, 1), 0)
                        )
                        q_index = q_start + lax.broadcasted_iota(jnp.int32, (1, rows), 1)
                        allowed = (k_index <= q_index) & (k_index >= begin_s[d])
                        probs = jnp.where(allowed, probs, 0.0)
                    weight_grad = nt(v_s[i, at], do_s[d])
                    score_grad = (weight_grad * (probs * probs * grown)).astype(BF16)
                    dv_acc[at] += nn(probs.astype(BF16), do_s[d])
                    dk_acc[at] += nn(score_grad, q_s[d])
                    dq_ref[d] += tn(score_grad, keys)

            pl.when(needed & full)(functools.partial(tile, False))
            pl.when(needed & jnp.logical_not(full))(functools.partial(tile, True))

        dkv_s[i, :, :HD] = (dk_acc[...] * FACTOR).astype(dkv_s.dtype)
        dkv_s[i, :, HD:] = dv_acc[...].astype(dkv_s.dtype)

    for e in range(n_dr):
        for d in range(nz):
            dkv_refs[e][d] = dkv_s[e * nz + d]


def attend_back(
    place, ends, queries, out_grads, keys_values, before, nz, ring, first_dr, n_dr, kept, after=()
):
    rows = queries[0].shape[0]
    n_kv = nz * n_dr
    pairs = nz * n_kv / 2
    chained = before is not None
    return call(
        functools.partial(
            attend_back_body, nz, ring, n_dr, first_dr, chained, ends.shape[0]
        ),
        (jax.ShapeDtypeStruct((nz, rows, HD), F32),)
        + tuple(jax.ShapeDtypeStruct((nz, rows, 2 * HD), kept) for _ in range(n_dr)),
        [place, ends, *queries, *out_grads, *keys_values, *([before] if chained else [])],
        [whole(pltpu.SMEM)] * 2 + [whole(pltpu.VMEM)] * (2 * nz + n_kv + chained),
        pairs * 10 * rows * rows * HD * 2,
        2 * (2 * nz + 4 * n_kv) * rows * HD,
        pairs * 2 * rows * rows,
        after=after,
        out_specs=tuple(whole(pltpu.VMEM) for _ in range(1 + n_dr)),
        scratch_shapes=[
            pltpu.VMEM((nz, rows, HD), BF16),
            pltpu.VMEM((nz, rows, HD), BF16),
            pltpu.VMEM((n_kv, rows, HD), BF16),
            pltpu.VMEM((n_kv, rows, HD), BF16),
            pltpu.VMEM((nz, 1, rows), jnp.int32),
            pltpu.VMEM((nz, 1, rows), F32),
            pltpu.VMEM((n_kv, rows, 2 * HD), kept),
            pltpu.VMEM((rows, HD), F32),
            pltpu.VMEM((rows, HD), F32),
        ],
        vmem=16 + 2 * n_kv * rows * HD * 14 // MIB,
        name="attend_back",
    )


def finish_body(nz, dq_ref, dkv_ref, got_ref, cos_ref, sin_ref, *out_refs):
    for d in range(nz):
        cosine = cos_ref[d]
        signed = sin_ref[d]
        total = dkv_ref[d] + got_ref[d].astype(F32)
        out = out_refs[d]
        out[:, :HD] = unrotated(dq_ref[d] * FACTOR, cosine, signed).astype(BF16)
        out[:, HD : 2 * HD] = unrotated(total[:, :HD], cosine, signed).astype(BF16)
        out[:, 2 * HD :] = total[:, HD:].astype(BF16)


def finish_grads(dq, dkv, got, cosine, signed):
    nz, rows, _ = dq.shape
    return call(
        functools.partial(finish_body, nz),
        tuple(jax.ShapeDtypeStruct((rows, 3 * HD), BF16) for _ in range(nz)),
        [dq, dkv, got, cosine, signed],
        [whole(pltpu.VMEM)] * 5,
        12 * nz * rows * HD,
        nz * rows * HD * 30,
        out_specs=tuple(whole(pltpu.VMEM) for _ in range(nz)),
        name="finish_grads",
    )


def rows_at(place, width, height, tile_of):
    return pl.BlockSpec((height, width), lambda j, place: (tile_of(place), 0))


def place_rows(pieces, scratch, spot):
    size = pieces[0].shape[0]
    half = size * len(pieces)
    for i, piece in enumerate(pieces):
        at = pl.multiple_of(spot * half + i * size, size)
        scratch[pl.ds(at, size), :] = piece[...]


def upstream_body(place_ref, *refs):
    pieces, (w_ref, out_ref, x_s) = refs[:-3], refs[-3:]
    size = pieces[0].shape[0]

    @pl.when(pl.program_id(0) == 0)
    def _():
        for i, piece in enumerate(pieces):
            x_s[i * size : (i + 1) * size] = piece[...]

    out_ref[...] = nt(x_s[...], w_ref[...]).astype(BF16)


def hidden_upstream(place, pieces, weights, own, after=()):
    size, width = pieces[0].shape
    rows = size * len(pieces)
    units = weights.shape[0] // (2 if own else 1)
    tile = 512
    steps = units // tile
    first = (lambda place: place[3] * steps) if own else (lambda place: 0)
    return call(
        upstream_body,
        jax.ShapeDtypeStruct((rows, units), BF16),
        [place, *pieces, weights],
        [pl.BlockSpec((size, width), lambda j, place: (0, 0))] * len(pieces)
        + [pl.BlockSpec((tile, width), lambda j, place: (first(place) + j, 0))],
        2 * rows * width * units,
        2 * width * units + 4 * rows * units + 2 * rows * width,
        after=after,
        prefetch=1,
        grid=(steps,),
        out_specs=pl.BlockSpec((rows, tile), lambda j, place: (0, j)),
        scratch_shapes=[pltpu.VMEM((rows, width), BF16)],
        vmem=28,
        name="hidden_upstream",
    )


def hidden_body(place_ref, *refs):
    pieces, refs = refs[:-7], refs[-7:]
    wg_ref, wu_ref, dact_ref, act_ref, dg_ref, du_ref, x_s = refs
    size = pieces[0].shape[0]

    @pl.when(pl.program_id(0) == 0)
    def _():
        for i, piece in enumerate(pieces):
            x_s[i * size : (i + 1) * size] = piece[...]

    x = x_s[...]
    for first in range(0, act_ref.shape[1], 256):
        at = slice(first, first + 256)
        gate = nn(x, wg_ref[:, at])
        up = nn(x, wu_ref[:, at])
        dact = dact_ref[:, at].astype(F32)
        sig = jax.nn.sigmoid(gate)
        silu = gate * sig
        act_ref[:, at] = (silu * up).astype(BF16)
        dg_ref[:, at] = (dact * up * sig * (1.0 + gate * (1.0 - sig))).astype(BF16)
        du_ref[:, at] = (dact * silu).astype(BF16)


def hidden(place, pieces, w_gate, w_up, dact, own, after=()):
    size, width = pieces[0].shape
    rows = size * len(pieces)
    units = dact.shape[1]
    tile = 512
    steps = units // tile
    first = (lambda place: place[3] * steps) if own else (lambda place: 0)
    made = jax.ShapeDtypeStruct((rows, units), BF16)
    block = pl.BlockSpec((rows, tile), lambda j, place: (0, j))
    weight = pl.BlockSpec((width, tile), lambda j, place: (0, first(place) + j))
    return call(
        hidden_body,
        (made, made, made),
        [place, *pieces, w_gate, w_up, dact],
        [pl.BlockSpec((size, width), lambda j, place: (0, 0))] * len(pieces)
        + [weight, weight, block],
        4 * rows * width * units,
        4 * width * units + 8 * rows * units + 2 * rows * width,
        rows * units,
        after=after,
        prefetch=1,
        grid=(steps,),
        out_specs=(block, block, block),
        scratch_shapes=[pltpu.VMEM((rows, width), BF16)],
        vmem=36,
        name="hidden",
    )


def chunked(total, out_refs):
    size = out_refs[0].shape[0]
    for i, ref in enumerate(out_refs):
        ref[...] = total[i * size : (i + 1) * size].astype(ref.dtype)


def back_body(place_ref, dg_ref, dg_sib, du_ref, du_sib, wg_ref, wg_sib, wu_ref, wu_sib, *outs):
    chunked(
        nt(dg_ref[...], wg_ref[...])
        + nt(dg_sib[...], wg_sib[...])
        + nt(du_ref[...], wu_ref[...])
        + nt(du_sib[...], wu_sib[...]),
        outs,
    )


def hidden_back(place, dg, dg_sib, du, du_sib, w_gate, gate_sib, w_up, up_sib, chunks, after=()):
    rows, half = dg.shape
    width = w_gate.shape[0]
    tile = 512
    size = rows // chunks
    left = pl.BlockSpec((rows, half), lambda j, place: (0, 0))
    own = pl.BlockSpec((tile, half), lambda j, place: (j, place[3]))
    sib = pl.BlockSpec((tile, half), lambda j, place: (j, 0))
    return call(
        back_body,
        tuple(jax.ShapeDtypeStruct((size, width), BF16) for _ in range(chunks)),
        [place, dg, dg_sib, du, du_sib, w_gate, gate_sib, w_up, up_sib],
        [left] * 4 + [own, sib, own, sib],
        8 * rows * width * half,
        8 * width * half + 8 * rows * half + 2 * rows * width,
        after=after,
        prefetch=1,
        grid=(width // tile,),
        out_specs=tuple(pl.BlockSpec((size, tile), lambda j, place: (0, j)) for _ in range(chunks)),
        vmem=52,
        name="hidden_back",
    )


def down_body(place_ref, act_ref, act_sib, wd_ref, wd_sib, *outs):
    chunked(nn(act_ref[...], wd_ref[...]) + nn(act_sib[...], wd_sib[...]), outs)


def down(place, act, act_sib, w_down, down_sib, chunks, after=()):
    rows, half = act.shape
    width = w_down.shape[1]
    tile = 512
    size = rows // chunks
    left = pl.BlockSpec((rows, half), lambda j, place: (0, 0))
    return call(
        down_body,
        tuple(jax.ShapeDtypeStruct((size, width), BF16) for _ in range(chunks)),
        [place, act, act_sib, w_down, down_sib],
        [
            left,
            left,
            pl.BlockSpec((half, tile), lambda j, place: (place[3], j)),
            pl.BlockSpec((half, tile), lambda j, place: (0, j)),
        ],
        4 * rows * width * half,
        4 * width * half + 4 * rows * half + 2 * rows * width,
        after=after,
        prefetch=1,
        grid=(width // tile,),
        out_specs=tuple(pl.BlockSpec((size, tile), lambda j, place: (0, j)) for _ in range(chunks)),
        vmem=24,
        name="down",
    )


def heads_body(nz, contract, keep, place_ref, *refs):
    n_w = 1 if keep else 3
    pieces, refs = refs[:nz], refs[nz:]
    w_refs, (sib_ref, mine_ref), refs = refs[:n_w], refs[n_w : n_w + 2], refs[n_w + 2 :]
    joined = refs[:n_w]
    for d in range(nz):
        at = pl.multiple_of((place_ref[0] ^ d) * HD, HD)
        for i in range(n_w):
            joined[i][:, pl.ds(at, HD)] = pieces[d][:, i * HD : (i + 1) * HD]
    half = sib_ref.shape[0]
    core = place_ref[2] & 1

    def rows_of(start):
        start = pl.multiple_of(start, half)
        total = contract(joined[0][pl.ds(start, half), :], w_refs[0][...])
        for i in range(1, n_w):
            total = total + contract(joined[i][pl.ds(start, half), :], w_refs[i][...])
        return total

    sib_ref[...] = rows_of((1 - core) * half).astype(BF16)
    mine_ref[...] = rows_of(core * half)


def heads_project(place, pieces, weights, contract, keep, after=()):
    nz = len(pieces)
    rows = pieces[0].shape[0]
    n_w = len(weights)
    width = weights[0].shape[1] if contract is nn else weights[0].shape[0]
    half = rows // 2
    joined = (rows, nz * HD)
    out = (
        jax.ShapeDtypeStruct((half, width), BF16),
        jax.ShapeDtypeStruct((half, width), F32),
    ) + ((jax.ShapeDtypeStruct(joined, BF16),) if keep else ())
    return call(
        functools.partial(heads_body, nz, contract, keep),
        out,
        [place, *pieces, *weights],
        [whole(pltpu.SMEM)] + [whole(pltpu.VMEM)] * (nz + n_w),
        2 * rows * width * nz * HD * n_w,
        2 * n_w * (width * nz * HD + rows * nz * HD) + 3 * rows * width,
        after=after,
        out_specs=tuple(whole(pltpu.VMEM) for _ in out),
        scratch_shapes=() if keep else (pltpu.VMEM(joined, BF16),) * n_w,
        vmem=24,
        name="heads_project",
    )


def dheads_body(nz, n, place_ref, *refs):
    mine, refs = refs[:n], refs[n:]
    sibs, refs = refs[:n], refs[n:]
    w_ref, outs, x_s = refs[0], refs[1:-1], refs[-1]
    core = place_ref[2] & 1
    place_rows(mine, x_s, core)
    place_rows(sibs, x_s, 1 - core)
    x = x_s[...]
    wide = outs[0].shape[1]
    for d in range(nz):
        at = pl.multiple_of((place_ref[0] ^ d) * wide, wide)
        outs[d][...] = nt(x, w_ref[pl.ds(at, wide), :]).astype(BF16)


def heads_upstream(place, mine, sibs, w_out, nz, after=()):
    n = len(mine)
    size, width = mine[0].shape
    rows = 2 * n * size
    wide = w_out.shape[0] // nz
    return call(
        functools.partial(dheads_body, nz, n),
        tuple(jax.ShapeDtypeStruct((rows, wide), BF16) for _ in range(nz)),
        [place, *mine, *sibs, w_out],
        [whole(pltpu.SMEM)] + [whole(pltpu.VMEM)] * (2 * n + 1),
        2 * rows * width * nz * wide,
        2 * width * nz * wide + 2 * rows * nz * wide + 2 * rows * width,
        after=after,
        out_specs=tuple(whole(pltpu.VMEM) for _ in range(nz)),
        scratch_shapes=[pltpu.VMEM((rows, width), BF16)],
        name="heads_upstream",
    )


def sum_body(mine_ref, got_ref, *outs):
    chunked(mine_ref[...].astype(F32) + got_ref[...].astype(F32), outs)


def row_sum(mine, got, chunks, after=()):
    rows, width = mine.shape
    size = rows // chunks
    return call(
        sum_body,
        tuple(jax.ShapeDtypeStruct((size, width), BF16) for _ in range(chunks)),
        [mine, got],
        [whole(pltpu.VMEM)] * 2,
        rows * width,
        8 * rows * width,
        after=after,
        out_specs=tuple(whole(pltpu.VMEM) for _ in range(chunks)),
        name="row_sum",
    )


def scale_of(values):
    return lax.rsqrt(jnp.mean(values * values, axis=-1, keepdims=True) + EPSILON)


def norm_body(part_ref, got_ref, x_ref, gain_ref, res_ref, normed_ref):
    residual = x_ref[...].astype(F32) + (part_ref[...].astype(F32) + got_ref[...].astype(F32))
    res_ref[...] = residual
    normed_ref[...] = (residual * scale_of(residual) * gain_ref[...]).astype(BF16)


def norm_rows(part, got, x, gain, after=()):
    rows, width = part.shape
    return call(
        norm_body,
        (
            jax.ShapeDtypeStruct((rows, width), F32),
            jax.ShapeDtypeStruct((rows, width), BF16),
        ),
        [part, got, x, gain],
        [whole(pltpu.VMEM)] * 4,
        8 * rows * width,
        12 * rows * width,
        after=after,
        out_specs=(whole(pltpu.VMEM), whole(pltpu.VMEM)),
        name="norm_rows",
    )


def norm_back_body(part_ref, got_ref, values_ref, add_ref, gain_ref, *outs):
    upstream = part_ref[...].astype(F32) + got_ref[...].astype(F32)
    values = values_ref[...].astype(F32)
    scale = scale_of(values)
    normed = values * scale
    outs[-1][...] = jnp.sum(upstream * normed, axis=0, keepdims=True)
    weighted = upstream * gain_ref[...]
    grad = scale * (weighted - normed * jnp.mean(weighted * normed, axis=-1, keepdims=True))
    total = add_ref[...].astype(F32) + grad
    for ref in outs[:-1]:
        ref[...] = total.astype(ref.dtype)


def norm_back(part, got, values, add, gain, kinds, after=()):
    rows, width = part.shape
    return call(
        norm_back_body,
        tuple(jax.ShapeDtypeStruct((rows, width), kind) for kind in kinds)
        + (jax.ShapeDtypeStruct((1, width), F32),),
        [part, got, values, add, gain],
        [whole(pltpu.VMEM)] * 5,
        16 * rows * width,
        16 * rows * width,
        after=after,
        out_specs=tuple(whole(pltpu.VMEM) for _ in range(len(kinds) + 1)),
        name="norm_back",
    )


def add_body(part_ref, got_ref, res_ref, out_ref):
    out_ref[...] = (
        res_ref[...] + (part_ref[...].astype(F32) + got_ref[...].astype(F32))
    ).astype(BF16)


def add_rows(part, got, residual, after=()):
    return call(
        add_body,
        jax.ShapeDtypeStruct(part.shape, BF16),
        [part, got, residual],
        [whole(pltpu.VMEM)] * 3,
        part.size,
        10 * part.size,
        after=after,
        out_specs=whole(pltpu.VMEM),
        name="add_rows",
    )


def join_body(n, place_ref, *refs):
    core = place_ref[2] & 1
    place_rows(refs[:n], refs[-1], core)
    place_rows(refs[n : 2 * n], refs[-1], 1 - core)


def join_rows(place, mine, sibs, after=()):
    n = len(mine)
    size, width = mine[0].shape
    return call(
        functools.partial(join_body, n),
        jax.ShapeDtypeStruct((2 * n * size, width), BF16),
        [place, *mine, *sibs],
        [whole(pltpu.SMEM)] + [whole(pltpu.VMEM)] * (2 * n),
        0,
        8 * n * size * width,
        after=after,
        out_specs=whole(pltpu.VMEM),
        name="join_rows",
    )


def turn_body(n, block, offset_ref, order_ref, *refs):
    pieces, out_ref = refs[:n], refs[n]
    size, wide = pieces[0].shape
    unit = (
        lax.broadcasted_iota(jnp.int32, (block, block), 0)
        == lax.broadcasted_iota(jnp.int32, (block, block), 1)
    ).astype(F32).astype(BF16)
    for p in range(wide // block):
        at = pl.multiple_of(order_ref[p] * block, block)
        for j in range(n):
            to = pl.multiple_of(offset_ref[j] * size, size)
            made = nt(unit, pieces[j][:, pl.ds(at, block)]).astype(BF16)
            out_ref[p * block : (p + 1) * block, pl.ds(to, size)] = made


def turn(order, group, pieces, offsets=None, after=()):
    wide = pieces[0].shape[1]
    if group % 128 != 0:
        pieces = [
            jnp.concatenate(
                [
                    lax.dynamic_slice_in_dim(piece, order[p] * group, group, 1)
                    for p in range(order.shape[0])
                ],
                axis=1,
            )
            for piece in pieces
        ]
        block = math.gcd(256, wide)
        order_in = jnp.arange(wide // block, dtype=jnp.int32)
    else:
        block = group
        order_in = order
    n = len(pieces)
    size = pieces[0].shape[0]
    tokens = n * size
    if offsets is None:
        offsets = jnp.arange(n, dtype=jnp.int32)
    return call(
        functools.partial(turn_body, n, block),
        jax.ShapeDtypeStruct((wide, tokens), BF16),
        [offsets, order_in, *pieces],
        [whole(pltpu.SMEM)] * 2 + [whole(pltpu.VMEM)] * n,
        2 * tokens * wide * block,
        4 * tokens * wide,
        after=after,
        out_specs=whole(pltpu.VMEM),
        vmem=8 + 4 * tokens * wide // MIB,
        name="turn",
    )


def stack_body(*refs):
    for i, ref in enumerate(refs[:-1]):
        refs[-1][i] = ref[...]


def stack_rows(pieces):
    n = len(pieces)
    return call(
        stack_body,
        jax.ShapeDtypeStruct((n, *pieces[0].shape), BF16),
        list(pieces),
        [whole(pltpu.VMEM)] * n,
        0,
        4 * n * pieces[0].size,
        out_specs=whole(pltpu.VMEM),
        name="stack_rows",
    )


def turn_all_body(block, place_ref, order_ref, own_ref, *refs):
    parts, out_ref = refs[:-1], refs[-1]
    n = len(parts)
    size, wide = parts[0].shape[1:]
    unit = (
        lax.broadcasted_iota(jnp.int32, (block, block), 0)
        == lax.broadcasted_iota(jnp.int32, (block, block), 1)
    ).astype(F32).astype(BF16)

    @pl.when(pl.program_id(0) == 0)
    def _():
        for p in range(wide // block):
            at = pl.multiple_of(order_ref[p] * block, block)
            made = nt(unit, own_ref[:, pl.ds(at, block)]).astype(BF16)
            out_ref[p * block : (p + 1) * block, :] = made

    @pl.when(pl.program_id(0) > 0)
    def _():
        for p in range(wide // block):
            at = pl.multiple_of(order_ref[p] * block, block)
            for j in range(n):
                to = pl.multiple_of((place_ref[0] ^ j) * size, size)
                made = nt(unit, parts[j][0, :, pl.ds(at, block)]).astype(BF16)
                out_ref[p * block : (p + 1) * block, pl.ds(to, size)] = made


def turn_all(order, group, own, parts, m):
    tokens, wide = own.shape
    others, size, _ = parts[0].shape
    if group % 128 != 0:

        def ordered(values):
            axis = values.ndim - 1
            return jnp.concatenate(
                [
                    lax.dynamic_slice_in_dim(values, order[p] * group, group, axis)
                    for p in range(order.shape[0])
                ],
                axis=axis,
            )

        own = ordered(own)
        parts = [ordered(part) for part in parts]
        block = math.gcd(256, wide)
        order_in = jnp.arange(wide // block, dtype=jnp.int32)
    else:
        block = group
        order_in = order
    return call(
        functools.partial(turn_all_body, block),
        jax.ShapeDtypeStruct((wide, (others + 1) * tokens), BF16),
        [m.reshape(1).astype(jnp.int32), order_in, own, *parts],
        [pl.BlockSpec((tokens, wide), lambda d, place, order: (0, 0))]
        + [
            pl.BlockSpec((1, size, wide), lambda d, place, order: (jnp.maximum(d - 1, 0), 0, 0))
        ]
        * len(parts),
        2 * (others + 1) * tokens * wide * block,
        4 * (others + 1) * tokens * wide,
        prefetch=2,
        grid=(others + 1,),
        out_specs=pl.BlockSpec((wide, tokens), lambda d, place, order: (0, d)),
        vmem=52,
        name="turn_all",
    )


def weight_body(sizes, *refs):
    n = sum(sizes)
    lefts, rights, (sent_ref, kept_ref) = refs[:n], refs[n : 2 * n], refs[2 * n :]
    half = pl.num_programs(0) // 2
    first, at = 0, 0
    for size in sizes:
        total = nn(lefts[first][...], rights[first][...])
        for i in range(first + 1, first + size):
            total = total + nn(lefts[i][...], rights[i][...])
        made = total.astype(BF16)
        columns = slice(at, at + total.shape[1])
        first, at = first + size, columns.stop

        @pl.when(pl.program_id(0) < half)
        def _(made=made, columns=columns):
            sent_ref[:, columns] = made

        @pl.when(pl.program_id(0) >= half)
        def _(made=made, columns=columns):
            kept_ref[:, columns] = made


def weight_grad(*groups):
    triples = [triple for group in groups for triple in group]
    wide = triples[0][0].shape[0]
    tokens = sum(right.shape[0] for _, right, _ in triples)
    width = sum(group[0][1].shape[1] for group in groups)
    steps = 4
    tile = wide // steps
    half = steps // 2
    made = jax.ShapeDtypeStruct((wide // 2, width), BF16)
    return call(
        functools.partial(weight_body, [len(group) for group in groups]),
        (made,) * 2,
        [left for left, _, _ in triples] + [right for _, right, _ in triples],
        [
            pl.BlockSpec((tile, right.shape[0]), lambda i, at=at: ((i + half) % steps, at))
            for _, right, at in triples
        ]
        + [pl.BlockSpec(right.shape, lambda i: (0, 0)) for _, right, _ in triples],
        sum(2 * wide * right.size for _, right, _ in triples),
        2 * (tokens * wide + sum(right.size for _, right, _ in triples) + wide * width),
        grid=(steps,),
        out_specs=(
            pl.BlockSpec((tile, width), lambda i: (jnp.minimum(i, half - 1), 0)),
            pl.BlockSpec((tile, width), lambda i: (jnp.maximum(i - half, 0), 0)),
        ),
        vmem=36,
        name="weight_grad",
    )


def sum3_body(n, *refs):
    total = refs[0][...].astype(F32)
    for ref in refs[1:n]:
        total = total + ref[...].astype(F32)
    low_ref, high_ref = refs[n:]
    low_ref[...] = total[0]
    high_ref[...] = total[1].astype(BF16)


def final_sum(terms, after=()):
    wide, width = terms[0].shape
    high = wide // 2
    tile = math.gcd(high, 128)
    block = pl.BlockSpec((2, tile, width), lambda i: (0, i, 0))
    out = pl.BlockSpec((tile, width), lambda i: (i, 0))
    return call(
        functools.partial(sum3_body, len(terms)),
        (
            jax.ShapeDtypeStruct((high, width), F32),
            jax.ShapeDtypeStruct((high, width), BF16),
        ),
        [term.reshape(2, high, width) for term in terms],
        [block] * len(terms),
        wide * width,
        wide * width * 8,
        after=after,
        grid=(high // tile,),
        out_specs=(out, out),
        name="final_sum",
    )


def merge_body(kept_ref, got_ref, low_ref, high_ref):
    total = kept_ref[...].astype(F32) + got_ref[...].astype(F32)
    low_ref[...] = total[0]
    high_ref[...] = total[1].astype(BF16)


def merge(kept, got, after=()):
    wide, width = kept.shape
    high = wide // 2
    tile = math.gcd(high, 128)
    operands = [kept.reshape(2, high, width), got.reshape(2, high, width)]
    block = pl.BlockSpec((2, tile, width), lambda i: (0, i, 0))
    out = pl.BlockSpec((tile, width), lambda i: (i, 0))
    return call(
        merge_body,
        (
            jax.ShapeDtypeStruct((high, width), F32),
            jax.ShapeDtypeStruct((high, width), BF16),
        ),
        operands,
        [block, block],
        wide * width,
        wide * width * 8,
        after=after,
        grid=(high // tile,),
        out_specs=(out, out),
        name="merge",
    )


def lay_body(turned, place_ref, own_ref, got_ref, out_ref):
    value = jnp.where(pl.program_id(0) == 0, own_ref[...], got_ref[...].astype(F32))
    out_ref[...] = value.T if turned else value


def lay(place, own, got, turned, width=None):
    rows = own.shape[0]
    width = width or own.shape[1]
    if turned:
        shape, block = (2 * width, rows), (width, rows)
        index = lambda i, place: (place[3] ^ i, 0)
    else:
        shape, block = (rows, 2 * width), (rows, width)
        index = lambda i, place: (0, place[3] ^ i)
    fixed = pl.BlockSpec((rows, width), lambda i, place: (0, 0))
    return call(
        functools.partial(lay_body, turned),
        jax.ShapeDtypeStruct(shape, F32),
        [place, own, got],
        [fixed, fixed],
        0,
        14 * rows * width,
        prefetch=1,
        grid=(2,),
        out_specs=pl.BlockSpec(block, index),
        name="lay",
    )


def qkv_sum_body(kept_ref, got_ref, own_ref, *outs):
    size = own_ref.shape[0]
    total = kept_ref[...].astype(F32) + got_ref[...].astype(F32)
    own_ref[...] = total[:size]
    for i, ref in enumerate(outs):
        ref[...] = total[(i + 1) * size : (i + 2) * size].astype(BF16)


def split_sum(kept, got, n):
    rows, width = kept.shape
    size = rows // n
    return call(
        qkv_sum_body,
        (jax.ShapeDtypeStruct((size, width), F32),)
        + (jax.ShapeDtypeStruct((size, width), BF16),) * (n - 1),
        [kept, got],
        [whole(pltpu.VMEM)] * 2,
        rows * width,
        8 * rows * width,
        out_specs=(whole(pltpu.VMEM),) * n,
        name="split_sum",
    )


def place_heads_body(nz, place_ref, *refs):
    pieces, outs = refs[:nz], refs[nz:]
    for d in range(nz):
        at = pl.multiple_of((place_ref[0] ^ d) * HD, HD)
        for i, out in enumerate(outs):
            out[:, pl.ds(at, HD)] = pieces[d][:, i * HD : (i + 1) * HD].astype(F32)


def place_heads(place, pieces):
    nz = len(pieces)
    rows = pieces[0].shape[0]
    return call(
        functools.partial(place_heads_body, nz),
        (jax.ShapeDtypeStruct((rows, nz * HD), F32),) * 3,
        [place, *pieces],
        [whole(pltpu.SMEM)] + [whole(pltpu.VMEM)] * nz,
        0,
        20 * rows * nz * HD,
        out_specs=(whole(pltpu.VMEM),) * 3,
        name="place_heads",
    )


def rope_tables(position):
    middle = HD // 2
    frequency = THETA ** (-(jnp.arange(middle, dtype=F32) * 2.0 / HD))
    angles = position.astype(F32)[..., None] * frequency
    cosine = jnp.cos(angles)
    sine = jnp.sin(angles)
    return (
        jnp.concatenate([cosine, cosine], axis=-1),
        jnp.concatenate([-sine, sine], axis=-1),
    )


def rms_scale(values):
    return lax.rsqrt(jnp.mean(values * values, axis=-1, keepdims=True) + EPSILON)


def layer(
    n_seq,
    n_mp,
    mixed_in,
    w_query,
    w_key,
    w_value,
    w_out,
    gain_attn,
    w_gate,
    w_up,
    w_down,
    gain_mlp,
    doc_ends,
    cotangent,
):
    rows, width = mixed_in.shape
    nz = w_query.shape[1] // HD
    ring = n_seq // nz
    bits = n_seq.bit_length() - 1
    low_bits = ring.bit_length() - 1
    units = w_gate.shape[1]
    half_units = units // 2
    half_rows = rows // 2
    group = width // n_seq
    pair_bit = bits - 2
    pair = 1 << pair_bit

    s = lax.axis_index("seq")
    m = lax.axis_index("mp")
    z, r = s // ring, s % ring
    core = m % 2
    side = m // 2
    low = (s >> pair_bit) & 1

    def seq_swap(v, distance):
        return lax.ppermute(v, "seq", [(i, i ^ distance) for i in range(n_seq)])

    def mp_swap(v, distance):
        return lax.ppermute(v, "mp", [(i, i ^ distance) for i in range(n_mp)])

    sum_bits = list(range(pair_bit)) + [bits - 1]
    places = []
    for p in range(n_seq):
        e = 0
        for at, bit in enumerate(sum_bits + [pair_bit]):
            if (p >> (bits - 1 - at)) & 1:
                e |= 1 << bit
        places.append(e)
    order = s ^ jnp.array(places, dtype=jnp.int32)

    ORDER.clear()

    place = jnp.stack([z, r, m, low]).astype(jnp.int32)
    blocks = (z ^ jnp.arange(nz, dtype=jnp.int32)) * ring + r
    token_index = blocks[:, None] * rows + jnp.arange(rows, dtype=jnp.int32)[None, :]
    ends_below = doc_ends[None, None, :] <= token_index[..., None]
    begin = jnp.max(jnp.where(ends_below, doc_ends, 0), axis=-1)
    cos_own, sin_own = rope_tables(token_index[0] - begin[0])
    cos_all, sin_all = rope_tables(token_index - begin)
    weights = [w_query, w_key, w_value]
    half_z = nz // 2
    made = project_qkv(
        place,
        mixed_in,
        gain_attn.reshape(1, width),
        weights,
        cos_own,
        sin_own,
        list(range(half_z, nz)),
    )
    normed = made[-1]
    pieces = {half_z + i: made[i] for i in range(half_z)}
    made = project_qkv(place, normed, None, weights, cos_own, sin_own, list(range(half_z)))
    pieces.update({i: made[i] for i in range(half_z)})
    pieces = [pieces[0]] + [seq_swap(pieces[d], d * ring) for d in range(1, nz)]
    near = pieces
    own_kv = [piece[:, HD:] for piece in pieces]
    for d in range(nz - 2, 0, -1):
        own_kv[d], own_kv[d + 1] = lax.optimization_barrier((own_kv[d], own_kv[d + 1]))
    keys_values = [near, [seq_swap(kv, 1) for kv in own_kv]]
    for b in range(1, low_bits):
        keys_values = keys_values + [
            [seq_swap(kv[:, -2 * HD :], 1 << b) for kv in kvs] for kvs in keys_values
        ]
    queries = pieces

    quarter = rows // n_mp
    my_quarter = lax.dynamic_slice_in_dim(normed, m * quarter, quarter, 0)
    halves = [
        lax.dynamic_slice_in_dim(w_down, low * half_units, half_units, 0),
        lax.dynamic_slice_in_dim(w_gate, low * half_units, half_units, 1),
        lax.dynamic_slice_in_dim(w_up, low * half_units, half_units, 1),
    ]
    cot_half = lax.dynamic_slice_in_dim(cotangent, core * half_rows, half_rows, 0)

    flat = [kv for kvs in keys_values for kv in kvs]
    far = [kv for kvs in keys_values[1:] for kv in kvs]
    cot_half, *halves = hold([cot_half, *halves], after=pieces)
    cot_pair = seq_swap(cot_half, pair)
    outs = attend(place, doc_ends, queries, flat, nz, ring, after=[cos_all, sin_all])
    heads = [outs[0]] + [seq_swap(outs[d], d * ring) for d in range(1, nz)]

    size = half_rows // CHUNKS
    last_low = 1 << sum_bits[pair_bit - 1]
    high = 1 << sum_bits[pair_bit]
    gain_mlp_row = gain_mlp.reshape(1, width)
    gain_attn_row = gain_attn.reshape(1, width)

    def chunks_of(values):
        return [values[i * size : (i + 1) * size] for i in range(CHUNKS)]

    def low_sums(sent, kept):
        for bit in sum_bits[: pair_bit - 1]:
            kept, sent = merge(kept, seq_swap(sent, 1 << bit))
        return kept, seq_swap(sent, last_low)

    x_chunks = chunks_of(lax.dynamic_slice_in_dim(mixed_in, core * half_rows, half_rows, 0))
    cot_chunks = chunks_of(cot_half)
    cot_all = cot_chunks + chunks_of(cot_pair)
    spots = jnp.concatenate(
        [core * CHUNKS + jnp.arange(CHUNKS), (1 - core) * CHUNKS + jnp.arange(CHUNKS)]
    ).astype(jnp.int32)
    v = types.SimpleNamespace(
        residual=[None] * CHUNKS,
        normed=[None] * (2 * CHUNKS),
        back=[None] * CHUNKS,
        back_across=[None] * CHUNKS,
        residual_grad=[None] * CHUNKS,
        branch=[None] * CHUNKS,
        branch_sib=[None] * CHUNKS,
        gain_mlp=[None] * CHUNKS,
        gain_attn=[None] * CHUNKS,
        grad_rows=[None] * CHUNKS,
        grad_sib=[None] * CHUNKS,
        quarters={0: my_quarter},
        out_grads=(),
    )
    def heads_out():
        sib, v.mine, v.heads_placed = heads_project(
            place, heads, [w_out], nn, True, after=[cot_pair]
        )
        v.sib = mp_swap(sib, 1)

    def out_sum():
        v.parts = row_sum(v.mine, v.sib, CHUNKS)
        v.across = [mp_swap(part, 2) for part in v.parts]

    def swap_weights():
        v.down_sib, v.gate_sib, v.up_sib = [mp_swap(half, 1) for half in hold(halves)]

    def dact_own():
        v.dact = hidden_upstream(place, cot_all, w_down, True)

    def dact_sib():
        v.dact_sib = hidden_upstream(place, cot_all, v.down_sib, False)

    def norm_chunk(i):
        v.residual[i], v.normed[i] = norm_rows(
            v.parts[i], v.across[i], x_chunks[i], gain_mlp_row
        )
        v.normed[CHUNKS + i] = seq_swap(v.normed[i], pair)

    def turn_cot():
        v.cot_turned = turn(order, group, cot_all)

    def swap_cot():
        (turned,) = hold([v.cot_turned])
        v.cot_both = [turned, mp_swap(turned, 1)]

    def hidden_sib():
        v.act_sib, dg_sib, du_sib = hidden(
            place, v.normed, v.gate_sib, v.up_sib, v.dact_sib, False
        )
        v.act_got = mp_swap(v.act_sib, 1)
        v.dg_sib, v.du_sib = dg_sib, du_sib

    def swap_dg():
        (part,) = hold([v.dg_sib])
        v.dg_got = mp_swap(part, 1)

    def swap_du():
        (part,) = hold([v.du_sib])
        v.du_got = mp_swap(part, 1)

    def hidden_own():
        v.act, v.dg, v.du = hidden(place, v.normed, w_gate, w_up, v.dact, True)

    def turn_normed():
        v.normed_turned = turn(order, group, v.normed)

    def swap_normed():
        (turned,) = hold([v.normed_turned])
        v.normed_both = [turned, mp_swap(turned, 1)]

    def grad_down():
        v.sent_down, v.part_down = weight_grad(
            [(v.cot_both[0], v.act, 0), (v.cot_both[1], v.act_got, 0)]
        )

    def send_down():
        (sent,) = hold([v.sent_down])
        v.low_down = low_sums(sent, v.part_down)

    def hidden_in():
        v.made = hidden_back(
            place,
            v.dg,
            v.dg_sib,
            v.du,
            v.du_sib,
            w_gate,
            v.gate_sib,
            w_up,
            v.up_sib,
            2 * CHUNKS,
        )
        v.made_got = [seq_swap(v.made[CHUNKS + i], pair) for i in range(CHUNKS)]

    def back_chunk(i):
        (v.back[i],) = row_sum(v.made[i], v.made_got[i], 1)
        v.back_across[i] = mp_swap(v.back[i], 2)

    def norm_back_chunk(i):
        v.residual_grad[i], v.branch[i], v.gain_mlp[i] = norm_back(
            v.back[i], v.back_across[i], v.residual[i], cot_chunks[i], gain_mlp_row, (F32, BF16)
        )
        v.branch_sib[i] = mp_swap(v.branch[i], 1)

    def grad_gate():
        v.sent_gate, v.part_gate = weight_grad(
            [(v.normed_both[0], v.dg, 0), (v.normed_both[1], v.dg_got, 0)]
        )

    def send_gate():
        (sent,) = hold([v.sent_gate])
        v.low_gate = low_sums(sent, v.part_gate)

    def grad_up():
        v.sent_up, v.part_up = weight_grad(
            [(v.normed_both[0], v.du, 0), (v.normed_both[1], v.du_got, 0)],
            [(v.branch_turned, v.heads_placed, 0)],
        )

    def send_up():
        (sent,) = hold([v.sent_up])
        v.low_up = low_sums(sent, v.part_up)

    def merge_down():
        v.kept_down, v.high_down = merge(*v.low_down)

    def high_down():
        (sent,) = hold([v.high_down], after=v.out_grads)
        v.come_down = seq_swap(sent, high)

    def merge_gate():
        v.kept_gate, v.high_gate = merge(*v.low_gate)

    def high_gate():
        (sent,) = hold([v.high_gate])
        v.come_gate = seq_swap(sent, high)

    def merge_up():
        v.kept_up, v.high_up = merge(*v.low_up)

    def high_up():
        (sent,) = hold([v.high_up])
        v.come_up = seq_swap(sent, high)

    def sum_down():
        v.own_down, v.pair_down = final_sum([v.kept_down, v.come_down])

    def sum_gate():
        v.own_gate, v.pair_gate = final_sum([v.kept_gate, v.come_gate])

    def sum_up():
        v.own_up, v.pair_up = final_sum([v.kept_up, v.come_up])

    def pair_down():
        (sent,) = hold([v.pair_down])
        v.theirs_down = seq_swap(sent, pair)

    def pair_gate():
        (sent,) = hold([v.pair_gate])
        v.theirs_gate = seq_swap(sent, pair)

    def pair_up():
        (sent,) = hold([v.pair_up])
        v.theirs_up = seq_swap(sent, pair)

    def lay_down():
        v.down_share = lay(place, v.own_down, v.theirs_down, True)

    def lay_gate():
        v.gate_share = lay(place, v.own_gate, v.theirs_gate, False)

    def lay_up():
        v.up_share = lay(place, v.own_up, v.theirs_up, False, half_units)

    def gather_z(d):
        (part,) = hold([v.quarters[d & (d - 1)]])
        v.quarters[d] = seq_swap(part, ring * (d & -d))

    def gather_x():
        v.rows = stack_rows([v.quarters[d] for d in range(1, nz)])
        v.rows_x = mp_swap(v.rows, 2)

    def gather_core():
        v.rows_core = [mp_swap(part, 1) for part in hold([v.rows, v.rows_x])]

    def heads_in():
        made = heads_upstream(place, v.branch, v.branch_sib, w_out, nz)
        v.out_grads = [made[0]] + [seq_swap(made[d], d * ring) for d in range(1, nz)]

    def attend_far():
        v.dq_far, *summed = attend_back(
            place, doc_ends, queries, v.out_grads, far, None, nz, ring, 1, ring - 1, BF16
        )
        summed = [None] + summed
        for b in reversed(range(low_bits)):
            bit = 1 << b
            for e in range(bit):
                got = seq_swap(summed[e | bit], bit)
                summed[e] = (
                    got
                    if summed[e] is None
                    else (summed[e].astype(F32) + got.astype(F32)).astype(BF16)
                )
        v.dkv_got = summed[0]

    def attend_near():
        v.dq, v.dkv = attend_back(
            place, doc_ends, queries, v.out_grads, near, v.dq_far, nz, ring, 0, 1, F32
        )

    def head_grads():
        v.grads = finish_grads(v.dq, v.dkv, v.dkv_got, cos_all, sin_all)
        v.own_grads = [v.grads[0]] + [
            seq_swap(v.grads[d], d * ring) for d in range(1, nz)
        ]

    def turn_branch():
        v.branch_turned = turn(order, group, v.branch + v.branch_sib, spots)

    def turn_rows():
        v.all_turned = turn_all(
            order, group, normed, [v.rows, v.rows_core[0], v.rows_x, v.rows_core[1]], m
        )

    def grad_qkv():
        v.sent_qkv, v.part_qkv = weight_grad(
            [(v.all_turned, v.grads[d], d) for d in range(nz)]
        )

    def send_qkv():
        (sent,) = hold([v.sent_qkv])
        v.low_qkv = low_sums(sent, v.part_qkv)

    def split_qkv():
        own, *sent = split_sum(*v.low_qkv, nz)
        v.qkv_heads = [own] + [seq_swap(sent[d - 1], d * ring) for d in range(1, nz)]

    def lay_qkv():
        v.shares = place_heads(place, v.qkv_heads)

    def rows_in():
        sib, v.in_mine = heads_project(place, v.own_grads, weights, nt, False)
        v.in_sib = mp_swap(sib, 1)

    def in_sum():
        v.in_parts = row_sum(v.in_mine, v.in_sib, CHUNKS)
        v.in_across = [mp_swap(part, 2) for part in v.in_parts]

    def norm_in_chunk(i):
        v.grad_rows[i], v.gain_attn[i] = norm_back(
            v.in_parts[i], v.in_across[i], x_chunks[i], v.residual_grad[i], gain_attn_row, (BF16,)
        )
        v.grad_sib[i] = mp_swap(v.grad_rows[i], 1)

    def join_in():
        v.input_grad = join_rows(place, v.grad_rows, v.grad_sib)

    def down_rows():
        v.down_mine, v.down_theirs = down(place, v.act, v.act_sib, w_down, v.down_sib, 2)

    def pair_rows():
        (sent,) = hold([v.down_theirs])
        v.down_got = seq_swap(sent, pair)

    def sum_rows():
        (v.down_part,) = row_sum(v.down_mine, v.down_got, 1)
        v.down_across = mp_swap(v.down_part, 2)

    def add_out():
        v.out_rows = add_rows(
            v.down_part, v.down_across, jnp.concatenate(v.residual, axis=0)
        )
        v.out_sib = mp_swap(v.out_rows, 1)

    def join_out():
        v.mixed_out = join_rows(place, [v.out_rows], [v.out_sib])

    def gains_core():
        (v.gains,) = hold([jnp.concatenate([sum(v.gain_attn), sum(v.gain_mlp)])])
        v.gains_sib = mp_swap(v.gains, 1)

    def gains_seq():
        (both,) = hold([v.gains + v.gains_sib])
        v.gains_all = lax.all_gather(both, "seq")

    def gains_sum():
        (every,) = hold([v.gains_all])
        v.gain_share = jnp.sum(lax.dynamic_slice_in_dim(every, s * group, group, 2), axis=0)

    dact_own()
    turn_cot()
    gather_z(1)
    swap_cot()
    heads_out()
    out_sum()
    swap_weights()
    norm_chunk(1)
    dact_sib()
    norm_chunk(0)
    gather_z(2)
    hidden_sib()
    turn_normed()
    swap_dg()
    swap_normed()
    hidden_own()
    grad_down()
    hidden_in()
    send_down()
    grad_gate()
    gather_z(3)
    send_gate()
    gather_x()
    back_chunk(1)
    loose(back_chunk, 0)
    loose(norm_back_chunk, 0)
    loose(swap_du)
    merge_down()
    loose(norm_back_chunk, 1)
    high_down()
    loose(heads_in)
    loose(gather_core)
    attend_far()
    merge_gate()
    turn_branch()
    grad_up()
    loose(attend_near)
    send_up()
    head_grads()
    high_gate()
    sum_down()
    rows_in()
    loose(merge_up)
    loose(in_sum)
    pair_down()
    down_rows()
    loose(norm_in_chunk, 0)
    loose(turn_rows)
    high_up()
    grad_qkv()
    loose(sum_gate)
    lay_down()
    pair_rows()
    loose(norm_in_chunk, 1)
    send_qkv()
    gains_core()
    loose(split_qkv)
    gains_seq()
    pair_gate()
    sum_rows()
    lay_gate()
    sum_up()
    pair_up()
    loose(add_out)
    join_out()
    lay_up()
    gains_sum()
    lay_qkv()
    loose(join_in)
    return (
        v.mixed_out,
        v.input_grad,
        *v.shares,
        (v.own_up[:, half_units:] + v.theirs_up[:, half_units:].astype(F32)).T,
        v.gain_share[0],
        v.gate_share,
        v.up_share,
        v.down_share,
        v.gain_share[1],
    )


def solution(mesh):
    placed = (
        P("seq", None),
        P(None, "mp"),
        P(None, "mp"),
        P(None, "mp"),
        P("mp", None),
        P(),
        P(None, "mp"),
        P(None, "mp"),
        P("mp", None),
        P(),
        P(),
        P("seq", None),
    )
    return jax.shard_map(
        functools.partial(layer, mesh.shape["seq"], mesh.shape["mp"]),
        mesh=mesh,
        in_specs=placed,
        out_specs=(
            P("seq", None),
            P("seq", None),
            P("seq", "mp"),
            P("seq", "mp"),
            P("seq", "mp"),
            P("mp", "seq"),
            P("seq"),
            P("seq", "mp"),
            P("seq", "mp"),
            P("mp", "seq"),
            P("seq"),
        ),
        check_vma=False,
    )
```

```python
import functools
import math
import types

import jax
import jax.numpy as jnp
from jax import lax
from jax.experimental import pallas as pl
from jax.experimental.pallas import tpu as pltpu
from jax.sharding import PartitionSpec as P

HD = 128
EPSILON = 1e-05
THETA = 10000.0
FACTOR = 1.0 / math.sqrt(HD)
CLAMP = 80.0
CHUNKS = 2
SHARE = 0.5
ORDER = []
LOOSE = [False]
MIB = 1024 * 1024
F32 = jnp.float32
BF16 = jnp.bfloat16


def nn(left, right):
    return lax.dot_general(left, right, (((1,), (0,)), ((), ())), preferred_element_type=F32)


def nt(left, right):
    return lax.dot_general(left, right, (((1,), (1,)), ((), ())), preferred_element_type=F32)


def tn(left, right):
    return lax.dot_general(left, right, (((0,), (0,)), ((), ())), preferred_element_type=F32)


def call(
    body,
    out_shape,
    operands,
    in_specs,
    flops,
    moved,
    transcendentals=0,
    after=(),
    prefetch=0,
    chain=True,
    vmem=20,
    **kwargs,
):
    n = prefetch + len(in_specs)
    chain = chain and not LOOSE[0]
    after = list(after) + (ORDER if chain else [])

    def kernel(*refs):
        body(*refs[:n], *refs[n + len(after) :])

    in_specs = list(in_specs) + [pl.BlockSpec(memory_space=pl.ANY)] * len(after)
    if prefetch:
        kwargs = {
            "name": kwargs.pop("name"),
            "grid_spec": pltpu.PrefetchScalarGridSpec(
                num_scalar_prefetch=prefetch, in_specs=in_specs, **kwargs
            ),
        }
    else:
        kwargs["in_specs"] = in_specs
    made = pl.pallas_call(
        kernel,
        out_shape=out_shape,
        compiler_params=pltpu.CompilerParams(vmem_limit_bytes=vmem * MIB),
        cost_estimate=pl.CostEstimate(
            flops=int(flops / SHARE),
            bytes_accessed=int(moved / SHARE),
            transcendentals=int(transcendentals / SHARE),
        ),
        **kwargs,
    )(*operands, *after)
    if chain:
        ORDER[:] = [made[0] if isinstance(made, (tuple, list)) else made]
    return made


def hold(values, after=()):
    n = len(values)
    if LOOSE[0]:
        return list(lax.optimization_barrier((*values, *after))[:n])
    made = lax.optimization_barrier((*values, *ORDER, *after))
    ORDER[:] = made[n : n + len(ORDER)]
    return list(made[:n])


def loose(step, *args):
    LOOSE[0] = True
    step(*args)
    LOOSE[0] = False


def whole(memory):
    return pl.BlockSpec(memory_space=memory)


def rotated(values, cosine, signed):
    return values * cosine + pltpu.roll(values, HD // 2, 1) * signed


def unrotated(values, cosine, signed):
    return values * cosine - pltpu.roll(values, HD // 2, 1) * signed


def qkv_body(n, fresh, place_ref, *refs):
    if fresh:
        x_ref, gain_ref, refs = refs[0], refs[1], refs[2:]
    else:
        x_ref, refs = refs[0], refs[1:]
    wq_ref, wk_ref, wv_ref, cos_ref, sin_ref = refs[:5]
    outs, (w_s, x_s) = refs[5 : 5 + n], refs[-2:]
    step = pl.program_id(0)

    @pl.when(step == 0)
    def _():
        if fresh:
            x = x_ref[...].astype(F32)
            x_s[...] = (x * scale_of(x) * gain_ref[...]).astype(BF16)
            refs[5 + n][...] = x_s[...]
        else:
            x_s[...] = x_ref[...]

    w_s[:, :HD] = wq_ref[...]
    w_s[:, HD : 2 * HD] = wk_ref[...]
    w_s[:, 2 * HD :] = wv_ref[...]
    made = nn(x_s[...], w_s[...])
    cosine = cos_ref[...]
    signed = sin_ref[...]
    query = rotated(made[:, :HD], cosine, signed).astype(BF16)
    key = rotated(made[:, HD : 2 * HD], cosine, signed).astype(BF16)
    value = made[:, 2 * HD :].astype(BF16)
    for i in range(n):

        @pl.when(step == i)
        def _(i=i):
            outs[i][:, :HD] = query
            outs[i][:, HD : 2 * HD] = key
            outs[i][:, 2 * HD :] = value


def project_qkv(place, x, gain, weights, cosine, signed, spots):
    n = len(spots)
    rows, width = x.shape
    fresh = gain is not None
    fixed = pl.BlockSpec((rows, width), lambda i, place: (0, 0))
    table = pl.BlockSpec((rows, HD), lambda i, place: (0, 0))
    first = spots[0]
    assert list(spots) == [first ^ i for i in range(n)]
    weight = pl.BlockSpec((width, HD), lambda i, place: (0, place[0] ^ first ^ i))
    piece = jax.ShapeDtypeStruct((rows, 3 * HD), BF16)
    return call(
        functools.partial(qkv_body, n, fresh),
        (piece,) * n + ((jax.ShapeDtypeStruct(x.shape, BF16),) if fresh else ()),
        [place, x] + ([gain] if fresh else []) + [*weights, cosine, signed],
        [fixed]
        + ([pl.BlockSpec((1, width), lambda i, place: (0, 0))] if fresh else [])
        + [weight] * 3
        + [table] * 2,
        6 * n * rows * width * HD,
        4 * rows * width + 6 * n * width * HD + 6 * n * rows * HD,
        prefetch=1,
        grid=(n,),
        out_specs=(pl.BlockSpec((rows, 3 * HD), lambda i, place: (0, 0)),) * n
        + ((fixed,) if fresh else ()),
        scratch_shapes=[pltpu.VMEM((width, 3 * HD), BF16), pltpu.VMEM((rows, width), BF16)],
        vmem=60,
        name="project_qkv",
    )


def begin_of(index, ends_ref, count):
    begin = jnp.zeros_like(index)
    for e in range(count):
        end = ends_ref[e]
        begin = jnp.where(end <= index, jnp.maximum(begin, end), begin)
    return begin


def finish_of(index, ends_ref, count):
    finish = jnp.zeros_like(index) + ends_ref[count - 1]
    for e in range(count):
        end = ends_ref[e]
        finish = jnp.where(end > index, jnp.minimum(finish, end), finish)
    return finish


def attend_body(nz, ring, count, place_ref, ends_ref, *refs):
    n_kv = nz * ring
    q_refs, refs = refs[:nz], refs[nz:]
    kv_refs, refs = refs[:n_kv], refs[n_kv:]
    o_refs, refs = refs[:nz], refs[nz:]
    q_s, k_s, v_s, o_s, acc = refs
    z, r = place_ref[0], place_ref[1]
    rows = q_s.shape[1]
    for d in range(nz):
        q_s[d] = q_refs[d][:, :HD]
    for i in range(n_kv):
        first = kv_refs[i].shape[1] - 2 * HD
        k_s[i] = kv_refs[i][:, first : first + HD]
        v_s[i] = kv_refs[i][:, first + HD :]

    @pl.loop(0, nz)
    def per_query(d):
        q_block = (z ^ d) * ring + r
        q_start = q_block * rows
        q_index = q_start + lax.broadcasted_iota(jnp.int32, (rows, 1), 0)
        begin = begin_of(q_index, ends_ref, count)
        shift = jnp.log((finish_of(q_index, ends_ref, count) - begin).astype(F32))
        first_begin = begin_of(q_start, ends_ref, count)
        last_begin = begin_of(q_start + (rows - 1), ends_ref, count)
        acc[...] = jnp.zeros_like(acc)

        @pl.loop(0, n_kv)
        def per_key(i):
            k_block = (z ^ (i & (nz - 1))) * ring + (r ^ (i // nz))
            k_start = k_block * rows
            needed = (k_block <= q_block) & (k_start + rows > first_begin)
            full = (k_block < q_block) & (k_start >= last_begin)

            def tile(masked):
                half = rows // 2
                for part in range(2):
                    at = slice(part * half, (part + 1) * half)
                    scores = nt(q_s[d, at], k_s[i])
                    grown = jnp.exp(jnp.minimum(shift[at] - scores * FACTOR, CLAMP))
                    probs = pl.reciprocal(1.0 + grown, approx=True)
                    if masked:
                        k_index = k_start + lax.broadcasted_iota(jnp.int32, (1, rows), 1)
                        allowed = (k_index <= q_index[at]) & (k_index >= begin[at])
                        probs = jnp.where(allowed, probs, 0.0)
                    acc[at] += nn(probs.astype(BF16), v_s[i])

            pl.when(needed & full)(functools.partial(tile, False))
            pl.when(needed & jnp.logical_not(full))(functools.partial(tile, True))

        o_s[d] = acc[...].astype(BF16)

    for d in range(nz):
        o_refs[d][...] = o_s[d]


def attend(place, ends, queries, keys_values, nz, ring, after=()):
    rows = queries[0].shape[0]
    n_kv = nz * ring
    pairs = nz * n_kv / 2
    return call(
        functools.partial(attend_body, nz, ring, ends.shape[0]),
        tuple(jax.ShapeDtypeStruct((rows, HD), BF16) for _ in range(nz)),
        [place, ends, *queries, *keys_values],
        [whole(pltpu.SMEM)] * 2 + [whole(pltpu.VMEM)] * (nz + n_kv),
        pairs * 4 * rows * rows * HD * 2,
        2 * (2 * nz + 2 * n_kv) * rows * HD,
        pairs * 2 * rows * rows,
        after=after,
        out_specs=tuple(whole(pltpu.VMEM) for _ in range(nz)),
        scratch_shapes=[
            pltpu.VMEM((nz, rows, HD), BF16),
            pltpu.VMEM((n_kv, rows, HD), BF16),
            pltpu.VMEM((n_kv, rows, HD), BF16),
            pltpu.VMEM((nz, rows, HD), BF16),
            pltpu.VMEM((rows, HD), F32),
        ],
        vmem=12 + 2 * n_kv * rows * HD * 8 // MIB,
        name="attend",
    )


def attend_back_body(nz, ring, n_dr, first_dr, chained, count, place_ref, ends_ref, *refs):
    n_kv = nz * n_dr
    q_refs, refs = refs[:nz], refs[nz:]
    do_refs, refs = refs[:nz], refs[nz:]
    kv_refs, refs = refs[:n_kv], refs[n_kv:]
    if chained:
        before_ref, refs = refs[0], refs[1:]
    dq_ref, refs = refs[0], refs[1:]
    dkv_refs, refs = refs[:n_dr], refs[n_dr:]
    q_s, do_s, k_s, v_s, begin_s, shift_s, dkv_s, dk_acc, dv_acc = refs
    z, r = place_ref[0], place_ref[1]
    rows = q_s.shape[1]
    for d in range(nz):
        q_s[d] = q_refs[d][:, :HD]
        do_s[d] = do_refs[d][...]
    for i in range(n_kv):
        first = kv_refs[i].shape[1] - 2 * HD
        k_s[i] = kv_refs[i][:, first : first + HD]
        v_s[i] = kv_refs[i][:, first + HD :]
    if chained:
        dq_ref[...] = before_ref[...]
    else:
        dq_ref[...] = jnp.zeros_like(dq_ref)

    @pl.loop(0, nz)
    def tables(d):
        q_index = ((z ^ d) * ring + r) * rows + lax.broadcasted_iota(jnp.int32, (1, rows), 1)
        begin = begin_of(q_index, ends_ref, count)
        begin_s[d] = begin
        shift_s[d] = jnp.log((finish_of(q_index, ends_ref, count) - begin).astype(F32))

    @pl.loop(0, n_kv)
    def per_key(i):
        k_block = (z ^ (i & (nz - 1))) * ring + (r ^ (first_dr + i // nz))
        k_start = k_block * rows
        dk_acc[...] = jnp.zeros_like(dk_acc)
        dv_acc[...] = jnp.zeros_like(dv_acc)

        @pl.loop(0, nz)
        def per_query(d):
            q_block = (z ^ d) * ring + r
            q_start = q_block * rows
            first_begin = begin_of(q_start, ends_ref, count)
            last_begin = begin_of(q_start + (rows - 1), ends_ref, count)
            needed = (k_block <= q_block) & (k_start + rows > first_begin)
            full = (k_block < q_block) & (k_start >= last_begin)

            def tile(masked):
                half = rows // 2
                for part in range(2):
                    at = slice(part * half, (part + 1) * half)
                    keys = k_s[i, at]
                    scores = nt(keys, q_s[d])
                    grown = jnp.exp(jnp.minimum(shift_s[d] - scores * FACTOR, CLAMP))
                    probs = pl.reciprocal(1.0 + grown, approx=True)
                    if masked:
                        k_index = (
                            k_start
                            + part * half
                            + lax.broadcasted_iota(jnp.int32, (half, 1), 0)
                        )
                        q_index = q_start + lax.broadcasted_iota(jnp.int32, (1, rows), 1)
                        allowed = (k_index <= q_index) & (k_index >= begin_s[d])
                        probs = jnp.where(allowed, probs, 0.0)
                    weight_grad = nt(v_s[i, at], do_s[d])
                    score_grad = (weight_grad * (probs * probs * grown)).astype(BF16)
                    dv_acc[at] += nn(probs.astype(BF16), do_s[d])
                    dk_acc[at] += nn(score_grad, q_s[d])
                    dq_ref[d] += tn(score_grad, keys)

            pl.when(needed & full)(functools.partial(tile, False))
            pl.when(needed & jnp.logical_not(full))(functools.partial(tile, True))

        dkv_s[i, :, :HD] = (dk_acc[...] * FACTOR).astype(dkv_s.dtype)
        dkv_s[i, :, HD:] = dv_acc[...].astype(dkv_s.dtype)

    for e in range(n_dr):
        for d in range(nz):
            dkv_refs[e][d] = dkv_s[e * nz + d]


def attend_back(
    place, ends, queries, out_grads, keys_values, before, nz, ring, first_dr, n_dr, kept, after=()
):
    rows = queries[0].shape[0]
    n_kv = nz * n_dr
    pairs = nz * n_kv / 2
    chained = before is not None
    return call(
        functools.partial(
            attend_back_body, nz, ring, n_dr, first_dr, chained, ends.shape[0]
        ),
        (jax.ShapeDtypeStruct((nz, rows, HD), F32),)
        + tuple(jax.ShapeDtypeStruct((nz, rows, 2 * HD), kept) for _ in range(n_dr)),
        [place, ends, *queries, *out_grads, *keys_values, *([before] if chained else [])],
        [whole(pltpu.SMEM)] * 2 + [whole(pltpu.VMEM)] * (2 * nz + n_kv + chained),
        pairs * 10 * rows * rows * HD * 2,
        2 * (2 * nz + 4 * n_kv) * rows * HD,
        pairs * 2 * rows * rows,
        after=after,
        out_specs=tuple(whole(pltpu.VMEM) for _ in range(1 + n_dr)),
        scratch_shapes=[
            pltpu.VMEM((nz, rows, HD), BF16),
            pltpu.VMEM((nz, rows, HD), BF16),
            pltpu.VMEM((n_kv, rows, HD), BF16),
            pltpu.VMEM((n_kv, rows, HD), BF16),
            pltpu.VMEM((nz, 1, rows), jnp.int32),
            pltpu.VMEM((nz, 1, rows), F32),
            pltpu.VMEM((n_kv, rows, 2 * HD), kept),
            pltpu.VMEM((rows, HD), F32),
            pltpu.VMEM((rows, HD), F32),
        ],
        vmem=16 + 2 * n_kv * rows * HD * 14 // MIB,
        name="attend_back",
    )


def finish_body(nz, dq_ref, dkv_ref, got_ref, cos_ref, sin_ref, *out_refs):
    for d in range(nz):
        cosine = cos_ref[d]
        signed = sin_ref[d]
        total = dkv_ref[d] + got_ref[d].astype(F32)
        out = out_refs[d]
        out[:, :HD] = unrotated(dq_ref[d] * FACTOR, cosine, signed).astype(BF16)
        out[:, HD : 2 * HD] = unrotated(total[:, :HD], cosine, signed).astype(BF16)
        out[:, 2 * HD :] = total[:, HD:].astype(BF16)


def finish_grads(dq, dkv, got, cosine, signed):
    nz, rows, _ = dq.shape
    return call(
        functools.partial(finish_body, nz),
        tuple(jax.ShapeDtypeStruct((rows, 3 * HD), BF16) for _ in range(nz)),
        [dq, dkv, got, cosine, signed],
        [whole(pltpu.VMEM)] * 5,
        12 * nz * rows * HD,
        nz * rows * HD * 30,
        out_specs=tuple(whole(pltpu.VMEM) for _ in range(nz)),
        name="finish_grads",
    )


def rows_at(place, width, height, tile_of):
    return pl.BlockSpec((height, width), lambda j, place: (tile_of(place), 0))


def place_rows(pieces, scratch, spot):
    size = pieces[0].shape[0]
    half = size * len(pieces)
    for i, piece in enumerate(pieces):
        at = pl.multiple_of(spot * half + i * size, size)
        scratch[pl.ds(at, size), :] = piece[...]


def upstream_body(place_ref, *refs):
    pieces, (w_ref, out_ref, x_s) = refs[:-3], refs[-3:]
    size = pieces[0].shape[0]

    @pl.when(pl.program_id(0) == 0)
    def _():
        for i, piece in enumerate(pieces):
            x_s[i * size : (i + 1) * size] = piece[...]

    out_ref[...] = nt(x_s[...], w_ref[...]).astype(BF16)


def hidden_upstream(place, pieces, weights, own, after=()):
    size, width = pieces[0].shape
    rows = size * len(pieces)
    units = weights.shape[0] // (2 if own else 1)
    tile = 512
    steps = units // tile
    first = (lambda place: place[3] * steps) if own else (lambda place: 0)
    return call(
        upstream_body,
        jax.ShapeDtypeStruct((rows, units), BF16),
        [place, *pieces, weights],
        [pl.BlockSpec((size, width), lambda j, place: (0, 0))] * len(pieces)
        + [pl.BlockSpec((tile, width), lambda j, place: (first(place) + j, 0))],
        2 * rows * width * units,
        2 * width * units + 4 * rows * units + 2 * rows * width,
        after=after,
        prefetch=1,
        grid=(steps,),
        out_specs=pl.BlockSpec((rows, tile), lambda j, place: (0, j)),
        scratch_shapes=[pltpu.VMEM((rows, width), BF16)],
        vmem=52,
        name="hidden_upstream",
    )


def hidden_body(place_ref, *refs):
    pieces, refs = refs[:-7], refs[-7:]
    wg_ref, wu_ref, dact_ref, act_ref, dg_ref, du_ref, x_s = refs
    size = pieces[0].shape[0]

    @pl.when(pl.program_id(0) == 0)
    def _():
        for i, piece in enumerate(pieces):
            x_s[i * size : (i + 1) * size] = piece[...]

    x = x_s[...]
    for first in range(0, act_ref.shape[1], 256):
        at = slice(first, first + 256)
        gate = nn(x, wg_ref[:, at])
        up = nn(x, wu_ref[:, at])
        dact = dact_ref[:, at].astype(F32)
        sig = jax.nn.sigmoid(gate)
        silu = gate * sig
        act_ref[:, at] = (silu * up).astype(BF16)
        dg_ref[:, at] = (dact * up * sig * (1.0 + gate * (1.0 - sig))).astype(BF16)
        du_ref[:, at] = (dact * silu).astype(BF16)


def hidden(place, pieces, w_gate, w_up, dact, own, after=()):
    size, width = pieces[0].shape
    rows = size * len(pieces)
    units = dact.shape[1]
    tile = 512
    steps = units // tile
    first = (lambda place: place[3] * steps) if own else (lambda place: 0)
    made = jax.ShapeDtypeStruct((rows, units), BF16)
    block = pl.BlockSpec((rows, tile), lambda j, place: (0, j))
    weight = pl.BlockSpec((width, tile), lambda j, place: (0, first(place) + j))
    return call(
        hidden_body,
        (made, made, made),
        [place, *pieces, w_gate, w_up, dact],
        [pl.BlockSpec((size, width), lambda j, place: (0, 0))] * len(pieces)
        + [weight, weight, block],
        4 * rows * width * units,
        4 * width * units + 8 * rows * units + 2 * rows * width,
        rows * units,
        after=after,
        prefetch=1,
        grid=(steps,),
        out_specs=(block, block, block),
        scratch_shapes=[pltpu.VMEM((rows, width), BF16)],
        vmem=52,
        name="hidden",
    )


def chunked(total, out_refs):
    size = out_refs[0].shape[0]
    for i, ref in enumerate(out_refs):
        ref[...] = total[i * size : (i + 1) * size].astype(ref.dtype)


def back_body(place_ref, dg_ref, dg_sib, du_ref, du_sib, wg_ref, wg_sib, wu_ref, wu_sib, *outs):
    chunked(
        nt(dg_ref[...], wg_ref[...])
        + nt(dg_sib[...], wg_sib[...])
        + nt(du_ref[...], wu_ref[...])
        + nt(du_sib[...], wu_sib[...]),
        outs,
    )


def hidden_back(place, dg, dg_sib, du, du_sib, w_gate, gate_sib, w_up, up_sib, chunks, after=()):
    rows, half = dg.shape
    width = w_gate.shape[0]
    tile = 512
    size = rows // chunks
    left = pl.BlockSpec((rows, half), lambda j, place: (0, 0))
    own = pl.BlockSpec((tile, half), lambda j, place: (j, place[3]))
    sib = pl.BlockSpec((tile, half), lambda j, place: (j, 0))
    return call(
        back_body,
        tuple(jax.ShapeDtypeStruct((size, width), BF16) for _ in range(chunks)),
        [place, dg, dg_sib, du, du_sib, w_gate, gate_sib, w_up, up_sib],
        [left] * 4 + [own, sib, own, sib],
        8 * rows * width * half,
        8 * width * half + 8 * rows * half + 2 * rows * width,
        after=after,
        prefetch=1,
        grid=(width // tile,),
        out_specs=tuple(pl.BlockSpec((size, tile), lambda j, place: (0, j)) for _ in range(chunks)),
        vmem=52,
        name="hidden_back",
    )


def down_body(place_ref, act_ref, act_sib, wd_ref, wd_sib, *outs):
    chunked(nn(act_ref[...], wd_ref[...]) + nn(act_sib[...], wd_sib[...]), outs)


def down(place, act, act_sib, w_down, down_sib, chunks, after=()):
    rows, half = act.shape
    width = w_down.shape[1]
    tile = 512
    size = rows // chunks
    left = pl.BlockSpec((rows, half), lambda j, place: (0, 0))
    return call(
        down_body,
        tuple(jax.ShapeDtypeStruct((size, width), BF16) for _ in range(chunks)),
        [place, act, act_sib, w_down, down_sib],
        [
            left,
            left,
            pl.BlockSpec((half, tile), lambda j, place: (place[3], j)),
            pl.BlockSpec((half, tile), lambda j, place: (0, j)),
        ],
        4 * rows * width * half,
        4 * width * half + 4 * rows * half + 2 * rows * width,
        after=after,
        prefetch=1,
        grid=(width // tile,),
        out_specs=tuple(pl.BlockSpec((size, tile), lambda j, place: (0, j)) for _ in range(chunks)),
        vmem=52,
        name="down",
    )


def heads_body(nz, contract, keep, place_ref, *refs):
    n_w = 1 if keep else 3
    pieces, refs = refs[:nz], refs[nz:]
    w_refs, (sib_ref, mine_ref), refs = refs[:n_w], refs[n_w : n_w + 2], refs[n_w + 2 :]
    joined = refs[:n_w]
    for d in range(nz):
        at = pl.multiple_of((place_ref[0] ^ d) * HD, HD)
        for i in range(n_w):
            joined[i][:, pl.ds(at, HD)] = pieces[d][:, i * HD : (i + 1) * HD]
    half = sib_ref.shape[0]
    core = place_ref[2] & 1

    def rows_of(start):
        start = pl.multiple_of(start, half)
        total = contract(joined[0][pl.ds(start, half), :], w_refs[0][...])
        for i in range(1, n_w):
            total = total + contract(joined[i][pl.ds(start, half), :], w_refs[i][...])
        return total

    sib_ref[...] = rows_of((1 - core) * half).astype(BF16)
    mine_ref[...] = rows_of(core * half)


def heads_project(place, pieces, weights, contract, keep, after=()):
    nz = len(pieces)
    rows = pieces[0].shape[0]
    n_w = len(weights)
    width = weights[0].shape[1] if contract is nn else weights[0].shape[0]
    half = rows // 2
    joined = (rows, nz * HD)
    out = (
        jax.ShapeDtypeStruct((half, width), BF16),
        jax.ShapeDtypeStruct((half, width), F32),
    ) + ((jax.ShapeDtypeStruct(joined, BF16),) if keep else ())
    return call(
        functools.partial(heads_body, nz, contract, keep),
        out,
        [place, *pieces, *weights],
        [whole(pltpu.SMEM)] + [whole(pltpu.VMEM)] * (nz + n_w),
        2 * rows * width * nz * HD * n_w,
        2 * n_w * (width * nz * HD + rows * nz * HD) + 3 * rows * width,
        after=after,
        out_specs=tuple(whole(pltpu.VMEM) for _ in out),
        scratch_shapes=() if keep else (pltpu.VMEM(joined, BF16),) * n_w,
        vmem=24,
        name="heads_project",
    )


def dheads_body(nz, n, place_ref, *refs):
    mine, refs = refs[:n], refs[n:]
    sibs, refs = refs[:n], refs[n:]
    w_ref, outs, x_s = refs[0], refs[1:-1], refs[-1]
    core = place_ref[2] & 1
    place_rows(mine, x_s, core)
    place_rows(sibs, x_s, 1 - core)
    x = x_s[...]
    wide = outs[0].shape[1]
    for d in range(nz):
        at = pl.multiple_of((place_ref[0] ^ d) * wide, wide)
        outs[d][...] = nt(x, w_ref[pl.ds(at, wide), :]).astype(BF16)


def heads_upstream(place, mine, sibs, w_out, nz, after=()):
    n = len(mine)
    size, width = mine[0].shape
    rows = 2 * n * size
    wide = w_out.shape[0] // nz
    return call(
        functools.partial(dheads_body, nz, n),
        tuple(jax.ShapeDtypeStruct((rows, wide), BF16) for _ in range(nz)),
        [place, *mine, *sibs, w_out],
        [whole(pltpu.SMEM)] + [whole(pltpu.VMEM)] * (2 * n + 1),
        2 * rows * width * nz * wide,
        2 * width * nz * wide + 2 * rows * nz * wide + 2 * rows * width,
        after=after,
        out_specs=tuple(whole(pltpu.VMEM) for _ in range(nz)),
        scratch_shapes=[pltpu.VMEM((rows, width), BF16)],
        name="heads_upstream",
    )


def sum_body(mine_ref, got_ref, *outs):
    chunked(mine_ref[...].astype(F32) + got_ref[...].astype(F32), outs)


def row_sum(mine, got, chunks, after=()):
    rows, width = mine.shape
    size = rows // chunks
    return call(
        sum_body,
        tuple(jax.ShapeDtypeStruct((size, width), BF16) for _ in range(chunks)),
        [mine, got],
        [whole(pltpu.VMEM)] * 2,
        rows * width,
        8 * rows * width,
        after=after,
        out_specs=tuple(whole(pltpu.VMEM) for _ in range(chunks)),
        name="row_sum",
    )


def scale_of(values):
    return lax.rsqrt(jnp.mean(values * values, axis=-1, keepdims=True) + EPSILON)


def norm_body(part_ref, got_ref, x_ref, gain_ref, res_ref, normed_ref):
    residual = x_ref[...].astype(F32) + (part_ref[...].astype(F32) + got_ref[...].astype(F32))
    res_ref[...] = residual
    normed_ref[...] = (residual * scale_of(residual) * gain_ref[...]).astype(BF16)


def norm_rows(part, got, x, gain, after=()):
    rows, width = part.shape
    return call(
        norm_body,
        (
            jax.ShapeDtypeStruct((rows, width), F32),
            jax.ShapeDtypeStruct((rows, width), BF16),
        ),
        [part, got, x, gain],
        [whole(pltpu.VMEM)] * 4,
        8 * rows * width,
        12 * rows * width,
        after=after,
        out_specs=(whole(pltpu.VMEM), whole(pltpu.VMEM)),
        name="norm_rows",
    )


def norm_back_body(part_ref, got_ref, values_ref, add_ref, gain_ref, *outs):
    upstream = part_ref[...].astype(F32) + got_ref[...].astype(F32)
    values = values_ref[...].astype(F32)
    scale = scale_of(values)
    normed = values * scale
    outs[-1][...] = jnp.sum(upstream * normed, axis=0, keepdims=True)
    weighted = upstream * gain_ref[...]
    grad = scale * (weighted - normed * jnp.mean(weighted * normed, axis=-1, keepdims=True))
    total = add_ref[...].astype(F32) + grad
    for ref in outs[:-1]:
        ref[...] = total.astype(ref.dtype)


def norm_back(part, got, values, add, gain, kinds, after=()):
    rows, width = part.shape
    return call(
        norm_back_body,
        tuple(jax.ShapeDtypeStruct((rows, width), kind) for kind in kinds)
        + (jax.ShapeDtypeStruct((1, width), F32),),
        [part, got, values, add, gain],
        [whole(pltpu.VMEM)] * 5,
        16 * rows * width,
        16 * rows * width,
        after=after,
        out_specs=tuple(whole(pltpu.VMEM) for _ in range(len(kinds) + 1)),
        name="norm_back",
    )


def add_body(part_ref, got_ref, res_ref, out_ref):
    out_ref[...] = (
        res_ref[...] + (part_ref[...].astype(F32) + got_ref[...].astype(F32))
    ).astype(BF16)


def add_rows(part, got, residual, after=()):
    return call(
        add_body,
        jax.ShapeDtypeStruct(part.shape, BF16),
        [part, got, residual],
        [whole(pltpu.VMEM)] * 3,
        part.size,
        10 * part.size,
        after=after,
        out_specs=whole(pltpu.VMEM),
        name="add_rows",
    )


def join_body(n, place_ref, *refs):
    core = place_ref[2] & 1
    place_rows(refs[:n], refs[-1], core)
    place_rows(refs[n : 2 * n], refs[-1], 1 - core)


def join_rows(place, mine, sibs, after=()):
    n = len(mine)
    size, width = mine[0].shape
    return call(
        functools.partial(join_body, n),
        jax.ShapeDtypeStruct((2 * n * size, width), BF16),
        [place, *mine, *sibs],
        [whole(pltpu.SMEM)] + [whole(pltpu.VMEM)] * (2 * n),
        0,
        8 * n * size * width,
        after=after,
        out_specs=whole(pltpu.VMEM),
        name="join_rows",
    )


def turn_body(n, block, offset_ref, order_ref, *refs):
    pieces, out_ref = refs[:n], refs[n]
    size, wide = pieces[0].shape
    unit = (
        lax.broadcasted_iota(jnp.int32, (block, block), 0)
        == lax.broadcasted_iota(jnp.int32, (block, block), 1)
    ).astype(F32).astype(BF16)
    for p in range(wide // block):
        at = pl.multiple_of(order_ref[p] * block, block)
        for j in range(n):
            to = pl.multiple_of(offset_ref[j] * size, size)
            made = nt(unit, pieces[j][:, pl.ds(at, block)]).astype(BF16)
            out_ref[p * block : (p + 1) * block, pl.ds(to, size)] = made


def turn(order, group, pieces, offsets=None, after=()):
    wide = pieces[0].shape[1]
    if group % 128 != 0:
        pieces = [
            jnp.concatenate(
                [
                    lax.dynamic_slice_in_dim(piece, order[p] * group, group, 1)
                    for p in range(order.shape[0])
                ],
                axis=1,
            )
            for piece in pieces
        ]
        block = math.gcd(256, wide)
        order_in = jnp.arange(wide // block, dtype=jnp.int32)
    else:
        block = group
        order_in = order
    n = len(pieces)
    size = pieces[0].shape[0]
    tokens = n * size
    if offsets is None:
        offsets = jnp.arange(n, dtype=jnp.int32)
    return call(
        functools.partial(turn_body, n, block),
        jax.ShapeDtypeStruct((wide, tokens), BF16),
        [offsets, order_in, *pieces],
        [whole(pltpu.SMEM)] * 2 + [whole(pltpu.VMEM)] * n,
        2 * tokens * wide * block,
        4 * tokens * wide,
        after=after,
        out_specs=whole(pltpu.VMEM),
        vmem=8 + 4 * tokens * wide // MIB,
        name="turn",
    )


def stack_body(*refs):
    for i, ref in enumerate(refs[:-1]):
        refs[-1][i] = ref[...]


def stack_rows(pieces):
    n = len(pieces)
    return call(
        stack_body,
        jax.ShapeDtypeStruct((n, *pieces[0].shape), BF16),
        list(pieces),
        [whole(pltpu.VMEM)] * n,
        0,
        4 * n * pieces[0].size,
        out_specs=whole(pltpu.VMEM),
        name="stack_rows",
    )


def turn_all_body(block, place_ref, order_ref, own_ref, *refs):
    parts, out_ref = refs[:-1], refs[-1]
    n = len(parts)
    size, wide = parts[0].shape[1:]
    unit = (
        lax.broadcasted_iota(jnp.int32, (block, block), 0)
        == lax.broadcasted_iota(jnp.int32, (block, block), 1)
    ).astype(F32).astype(BF16)

    @pl.when(pl.program_id(0) == 0)
    def _():
        for p in range(wide // block):
            at = pl.multiple_of(order_ref[p] * block, block)
            made = nt(unit, own_ref[:, pl.ds(at, block)]).astype(BF16)
            out_ref[p * block : (p + 1) * block, :] = made

    @pl.when(pl.program_id(0) > 0)
    def _():
        for p in range(wide // block):
            at = pl.multiple_of(order_ref[p] * block, block)
            for j in range(n):
                to = pl.multiple_of((place_ref[0] ^ j) * size, size)
                made = nt(unit, parts[j][0, :, pl.ds(at, block)]).astype(BF16)
                out_ref[p * block : (p + 1) * block, pl.ds(to, size)] = made


def turn_all(order, group, own, parts, m):
    tokens, wide = own.shape
    others, size, _ = parts[0].shape
    if group % 128 != 0:

        def ordered(values):
            axis = values.ndim - 1
            return jnp.concatenate(
                [
                    lax.dynamic_slice_in_dim(values, order[p] * group, group, axis)
                    for p in range(order.shape[0])
                ],
                axis=axis,
            )

        own = ordered(own)
        parts = [ordered(part) for part in parts]
        block = math.gcd(256, wide)
        order_in = jnp.arange(wide // block, dtype=jnp.int32)
    else:
        block = group
        order_in = order
    return call(
        functools.partial(turn_all_body, block),
        jax.ShapeDtypeStruct((wide, (others + 1) * tokens), BF16),
        [m.reshape(1).astype(jnp.int32), order_in, own, *parts],
        [pl.BlockSpec((tokens, wide), lambda d, place, order: (0, 0))]
        + [
            pl.BlockSpec((1, size, wide), lambda d, place, order: (jnp.maximum(d - 1, 0), 0, 0))
        ]
        * len(parts),
        2 * (others + 1) * tokens * wide * block,
        4 * (others + 1) * tokens * wide,
        prefetch=2,
        grid=(others + 1,),
        out_specs=pl.BlockSpec((wide, tokens), lambda d, place, order: (0, d)),
        vmem=52,
        name="turn_all",
    )


def weight_body(n, *refs):
    lefts, refs = refs[:n], refs[n:]
    rights, (sent_ref, kept_ref) = refs[:n], refs[n:]
    total = nn(lefts[0][...], rights[0][...])
    for i in range(1, n):
        total = total + nn(lefts[i][...], rights[i][...])
    half = pl.num_programs(0) // 2

    @pl.when(pl.program_id(0) < half)
    def _():
        sent_ref[...] = total.astype(BF16)

    @pl.when(pl.program_id(0) >= half)
    def _():
        kept_ref[...] = total.astype(BF16)


def weight_grad(lefts, rights, after=()):
    wide = lefts[0].shape[0]
    width = rights[0].shape[1]
    tokens = sum(left.shape[1] for left in lefts)
    steps = 4
    tile = wide // steps
    half = steps // 2
    made = jax.ShapeDtypeStruct((wide // 2, width), BF16)
    return call(
        functools.partial(weight_body, len(lefts)),
        (made,) * 2,
        [*lefts, *rights],
        [
            pl.BlockSpec((tile, left.shape[1]), lambda i: ((i + half) % steps, 0))
            for left in lefts
        ]
        + [pl.BlockSpec(right.shape, lambda i: (0, 0)) for right in rights],
        2 * tokens * wide * width,
        2 * (tokens * wide + tokens * width + wide * width),
        after=after,
        grid=(steps,),
        out_specs=(
            pl.BlockSpec((tile, width), lambda i: (jnp.minimum(i, half - 1), 0)),
            pl.BlockSpec((tile, width), lambda i: (jnp.maximum(i - half, 0), 0)),
        ),
        vmem=52,
        name="weight_grad",
    )


def sum3_body(n, *refs):
    total = refs[0][...].astype(F32)
    for ref in refs[1:n]:
        total = total + ref[...].astype(F32)
    low_ref, high_ref = refs[n:]
    low_ref[...] = total[0]
    high_ref[...] = total[1].astype(BF16)


def final_sum(terms, after=()):
    wide, width = terms[0].shape
    high = wide // 2
    tile = math.gcd(high, 128)
    block = pl.BlockSpec((2, tile, width), lambda i: (0, i, 0))
    out = pl.BlockSpec((tile, width), lambda i: (i, 0))
    return call(
        functools.partial(sum3_body, len(terms)),
        (
            jax.ShapeDtypeStruct((high, width), F32),
            jax.ShapeDtypeStruct((high, width), BF16),
        ),
        [term.reshape(2, high, width) for term in terms],
        [block] * len(terms),
        wide * width,
        wide * width * 8,
        after=after,
        grid=(high // tile,),
        out_specs=(out, out),
        name="final_sum",
    )


def merge_body(kept_ref, got_ref, low_ref, high_ref):
    total = kept_ref[...].astype(F32) + got_ref[...].astype(F32)
    low_ref[...] = total[0]
    high_ref[...] = total[1].astype(BF16)


def merge(kept, got, after=()):
    wide, width = kept.shape
    high = wide // 2
    tile = math.gcd(high, 128)
    operands = [kept.reshape(2, high, width), got.reshape(2, high, width)]
    block = pl.BlockSpec((2, tile, width), lambda i: (0, i, 0))
    out = pl.BlockSpec((tile, width), lambda i: (i, 0))
    return call(
        merge_body,
        (
            jax.ShapeDtypeStruct((high, width), F32),
            jax.ShapeDtypeStruct((high, width), BF16),
        ),
        operands,
        [block, block],
        wide * width,
        wide * width * 8,
        after=after,
        grid=(high // tile,),
        out_specs=(out, out),
        name="merge",
    )


def lay_body(turned, place_ref, own_ref, got_ref, out_ref):
    value = jnp.where(pl.program_id(0) == 0, own_ref[...], got_ref[...].astype(F32))
    out_ref[...] = value.T if turned else value


def lay(place, own, got, turned):
    rows, width = own.shape
    if turned:
        shape, block = (2 * width, rows), (width, rows)
        index = lambda i, place: (place[3] ^ i, 0)
    else:
        shape, block = (rows, 2 * width), (rows, width)
        index = lambda i, place: (0, place[3] ^ i)
    fixed = pl.BlockSpec((rows, width), lambda i, place: (0, 0))
    return call(
        functools.partial(lay_body, turned),
        jax.ShapeDtypeStruct(shape, F32),
        [place, own, got],
        [fixed, fixed],
        0,
        14 * rows * width,
        prefetch=1,
        grid=(2,),
        out_specs=pl.BlockSpec(block, index),
        name="lay",
    )


def qkv_sum_body(kept_ref, got_ref, own_ref, *outs):
    size = own_ref.shape[0]
    total = kept_ref[...].astype(F32) + got_ref[...].astype(F32)
    own_ref[...] = total[:size]
    for i, ref in enumerate(outs):
        ref[...] = total[(i + 1) * size : (i + 2) * size].astype(BF16)


def split_sum(kept, got, n):
    rows, width = kept.shape
    size = rows // n
    return call(
        qkv_sum_body,
        (jax.ShapeDtypeStruct((size, width), F32),)
        + (jax.ShapeDtypeStruct((size, width), BF16),) * (n - 1),
        [kept, got],
        [whole(pltpu.VMEM)] * 2,
        rows * width,
        8 * rows * width,
        out_specs=(whole(pltpu.VMEM),) * n,
        name="split_sum",
    )


def place_heads_body(nz, place_ref, *refs):
    pieces, outs = refs[:nz], refs[nz:]
    for d in range(nz):
        at = pl.multiple_of((place_ref[0] ^ d) * HD, HD)
        for i, out in enumerate(outs):
            out[:, pl.ds(at, HD)] = pieces[d][:, i * HD : (i + 1) * HD].astype(F32)


def place_heads(place, pieces):
    nz = len(pieces)
    rows = pieces[0].shape[0]
    return call(
        functools.partial(place_heads_body, nz),
        (jax.ShapeDtypeStruct((rows, nz * HD), F32),) * 3,
        [place, *pieces],
        [whole(pltpu.SMEM)] + [whole(pltpu.VMEM)] * nz,
        0,
        20 * rows * nz * HD,
        out_specs=(whole(pltpu.VMEM),) * 3,
        name="place_heads",
    )


def rope_tables(position):
    middle = HD // 2
    frequency = THETA ** (-(jnp.arange(middle, dtype=F32) * 2.0 / HD))
    angles = position.astype(F32)[..., None] * frequency
    cosine = jnp.cos(angles)
    sine = jnp.sin(angles)
    return (
        jnp.concatenate([cosine, cosine], axis=-1),
        jnp.concatenate([-sine, sine], axis=-1),
    )


def rms_scale(values):
    return lax.rsqrt(jnp.mean(values * values, axis=-1, keepdims=True) + EPSILON)


def layer(
    n_seq,
    n_mp,
    mixed_in,
    w_query,
    w_key,
    w_value,
    w_out,
    gain_attn,
    w_gate,
    w_up,
    w_down,
    gain_mlp,
    doc_ends,
    cotangent,
):
    rows, width = mixed_in.shape
    nz = w_query.shape[1] // HD
    ring = n_seq // nz
    bits = n_seq.bit_length() - 1
    low_bits = ring.bit_length() - 1
    units = w_gate.shape[1]
    half_units = units // 2
    half_rows = rows // 2
    group = width // n_seq
    pair_bit = bits - 2
    pair = 1 << pair_bit

    s = lax.axis_index("seq")
    m = lax.axis_index("mp")
    z, r = s // ring, s % ring
    core = m % 2
    side = m // 2
    low = (s >> pair_bit) & 1

    def seq_swap(v, distance):
        return lax.ppermute(v, "seq", [(i, i ^ distance) for i in range(n_seq)])

    def mp_swap(v, distance):
        return lax.ppermute(v, "mp", [(i, i ^ distance) for i in range(n_mp)])

    sum_bits = list(range(pair_bit)) + [bits - 1]
    places = []
    for p in range(n_seq):
        e = 0
        for at, bit in enumerate(sum_bits + [pair_bit]):
            if (p >> (bits - 1 - at)) & 1:
                e |= 1 << bit
        places.append(e)
    order = s ^ jnp.array(places, dtype=jnp.int32)

    ORDER.clear()

    place = jnp.stack([z, r, m, low]).astype(jnp.int32)
    blocks = (z ^ jnp.arange(nz, dtype=jnp.int32)) * ring + r
    token_index = blocks[:, None] * rows + jnp.arange(rows, dtype=jnp.int32)[None, :]
    ends_below = doc_ends[None, None, :] <= token_index[..., None]
    begin = jnp.max(jnp.where(ends_below, doc_ends, 0), axis=-1)
    cos_own, sin_own = rope_tables(token_index[0] - begin[0])
    weights = [w_query, w_key, w_value]
    half_z = nz // 2
    made = project_qkv(
        place,
        mixed_in,
        gain_attn.reshape(1, width),
        weights,
        cos_own,
        sin_own,
        list(range(half_z, nz)),
    )
    normed = made[-1]
    pieces = {half_z + i: made[i] for i in range(half_z)}
    made = project_qkv(place, normed, None, weights, cos_own, sin_own, list(range(half_z)))
    pieces.update({i: made[i] for i in range(half_z)})
    pieces = [pieces[0]] + [seq_swap(pieces[d], d * ring) for d in range(1, nz)]
    near = pieces
    keys_values = [near, [seq_swap(piece[:, HD:], 1) for piece in pieces]]
    for b in range(1, low_bits):
        keys_values = keys_values + [
            [seq_swap(kv[:, -2 * HD :], 1 << b) for kv in kvs] for kvs in keys_values
        ]
    queries = pieces

    quarter = rows // n_mp
    my_quarter = lax.dynamic_slice_in_dim(normed, m * quarter, quarter, 0)
    halves = [
        lax.dynamic_slice_in_dim(w_down, low * half_units, half_units, 0),
        lax.dynamic_slice_in_dim(w_gate, low * half_units, half_units, 1),
        lax.dynamic_slice_in_dim(w_up, low * half_units, half_units, 1),
    ]
    cot_half = lax.dynamic_slice_in_dim(cotangent, core * half_rows, half_rows, 0)

    flat = [kv for kvs in keys_values for kv in kvs]
    far = [kv for kvs in keys_values[1:] for kv in kvs]
    cot_half, *halves = hold([cot_half, *halves], after=pieces)
    cot_pair = seq_swap(cot_half, pair)
    outs = attend(place, doc_ends, queries, flat, nz, ring)
    heads = [outs[0]] + [seq_swap(outs[d], d * ring) for d in range(1, nz)]

    size = half_rows // CHUNKS
    last_low = 1 << sum_bits[pair_bit - 1]
    high = 1 << sum_bits[pair_bit]
    gain_mlp_row = gain_mlp.reshape(1, width)
    gain_attn_row = gain_attn.reshape(1, width)

    def chunks_of(values):
        return [values[i * size : (i + 1) * size] for i in range(CHUNKS)]

    def low_sums(sent, kept):
        for bit in sum_bits[: pair_bit - 1]:
            kept, sent = merge(kept, seq_swap(sent, 1 << bit))
        return kept, seq_swap(sent, last_low)

    x_chunks = chunks_of(lax.dynamic_slice_in_dim(mixed_in, core * half_rows, half_rows, 0))
    cot_chunks = chunks_of(cot_half)
    cot_all = cot_chunks + chunks_of(cot_pair)
    spots = jnp.concatenate(
        [core * CHUNKS + jnp.arange(CHUNKS), (1 - core) * CHUNKS + jnp.arange(CHUNKS)]
    ).astype(jnp.int32)
    v = types.SimpleNamespace(
        residual=[None] * CHUNKS,
        normed=[None] * (2 * CHUNKS),
        back=[None] * CHUNKS,
        back_across=[None] * CHUNKS,
        residual_grad=[None] * CHUNKS,
        branch=[None] * CHUNKS,
        branch_sib=[None] * CHUNKS,
        gain_mlp=[None] * CHUNKS,
        gain_attn=[None] * CHUNKS,
        grad_rows=[None] * CHUNKS,
        grad_sib=[None] * CHUNKS,
        quarters={0: my_quarter},
        out_grads=(),
    )
    def heads_out():
        sib, v.mine, v.heads_placed = heads_project(
            place, heads, [w_out], nn, True, after=[cot_pair]
        )
        v.sib = mp_swap(sib, 1)

    def out_sum():
        v.parts = row_sum(v.mine, v.sib, CHUNKS)
        v.across = [mp_swap(part, 2) for part in v.parts]

    def swap_weights():
        v.down_sib, v.gate_sib, v.up_sib = [mp_swap(half, 1) for half in hold(halves)]

    def dact_own():
        v.dact = hidden_upstream(place, cot_all, w_down, True)

    def dact_sib():
        v.dact_sib = hidden_upstream(place, cot_all, v.down_sib, False)

    def norm_chunk(i):
        v.residual[i], v.normed[i] = norm_rows(
            v.parts[i], v.across[i], x_chunks[i], gain_mlp_row
        )
        v.normed[CHUNKS + i] = seq_swap(v.normed[i], pair)

    def turn_cot():
        v.cot_turned = turn(order, group, cot_all)

    def swap_cot():
        (turned,) = hold([v.cot_turned])
        v.cot_both = [turned, mp_swap(turned, 1)]

    def hidden_sib():
        v.act_sib, dg_sib, du_sib = hidden(
            place, v.normed, v.gate_sib, v.up_sib, v.dact_sib, False
        )
        v.act_got = mp_swap(v.act_sib, 1)
        v.dg_sib, v.du_sib = dg_sib, du_sib

    def swap_dg():
        (part,) = hold([v.dg_sib])
        v.dg_got = mp_swap(part, 1)

    def swap_du():
        (part,) = hold([v.du_sib])
        v.du_got = mp_swap(part, 1)

    def hidden_own():
        v.act, v.dg, v.du = hidden(place, v.normed, w_gate, w_up, v.dact, True)

    def turn_normed():
        v.normed_turned = turn(order, group, v.normed)

    def swap_normed():
        (turned,) = hold([v.normed_turned])
        v.normed_both = [turned, mp_swap(turned, 1)]

    def grad_down():
        v.sent_down, v.part_down = weight_grad(v.cot_both, [v.act, v.act_got])

    def send_down():
        (sent,) = hold([v.sent_down])
        v.low_down = low_sums(sent, v.part_down)

    def hidden_in():
        v.made = hidden_back(
            place,
            v.dg,
            v.dg_sib,
            v.du,
            v.du_sib,
            w_gate,
            v.gate_sib,
            w_up,
            v.up_sib,
            2 * CHUNKS,
        )
        v.made_got = [seq_swap(v.made[CHUNKS + i], pair) for i in range(CHUNKS)]

    def back_chunk(i):
        (v.back[i],) = row_sum(v.made[i], v.made_got[i], 1)
        v.back_across[i] = mp_swap(v.back[i], 2)

    def norm_back_chunk(i):
        v.residual_grad[i], v.branch[i], v.gain_mlp[i] = norm_back(
            v.back[i], v.back_across[i], v.residual[i], cot_chunks[i], gain_mlp_row, (F32, BF16)
        )
        v.branch_sib[i] = mp_swap(v.branch[i], 1)

    def grad_gate():
        v.sent_gate, v.part_gate = weight_grad(v.normed_both, [v.dg, v.dg_got])

    def send_gate():
        (sent,) = hold([v.sent_gate])
        v.low_gate = low_sums(sent, v.part_gate)

    def grad_up():
        v.sent_up, v.part_up = weight_grad(v.normed_both, [v.du, v.du_got])

    def send_up():
        (sent,) = hold([v.sent_up])
        v.low_up = low_sums(sent, v.part_up)

    def merge_down():
        v.kept_down, v.high_down = merge(*v.low_down)

    def high_down():
        (sent,) = hold([v.high_down], after=v.out_grads)
        v.come_down = seq_swap(sent, high)

    def merge_gate():
        v.kept_gate, v.high_gate = merge(*v.low_gate)

    def high_gate():
        (sent,) = hold([v.high_gate])
        v.come_gate = seq_swap(sent, high)

    def merge_up():
        v.kept_up, v.high_up = merge(*v.low_up)

    def high_up():
        (sent,) = hold([v.high_up])
        v.come_up = seq_swap(sent, high)

    def sum_down():
        v.own_down, v.pair_down = final_sum([v.kept_down, v.come_down])

    def sum_gate():
        v.own_gate, v.pair_gate = final_sum([v.kept_gate, v.come_gate])

    def sum_up():
        v.own_up, v.pair_up = final_sum([v.kept_up, v.come_up])

    def pair_down():
        (sent,) = hold([v.pair_down])
        v.theirs_down = seq_swap(sent, pair)

    def pair_gate():
        (sent,) = hold([v.pair_gate])
        v.theirs_gate = seq_swap(sent, pair)

    def pair_up():
        (sent,) = hold([v.pair_up])
        v.theirs_up = seq_swap(sent, pair)

    def lay_down():
        v.down_share = lay(place, v.own_down, v.theirs_down, True)

    def lay_gate():
        v.gate_share = lay(place, v.own_gate, v.theirs_gate, False)

    def lay_up():
        v.up_share = lay(place, v.own_up, v.theirs_up, False)

    def gather_z(d):
        (part,) = hold([v.quarters[d & (d - 1)]])
        v.quarters[d] = seq_swap(part, ring * (d & -d))

    def gather_x():
        v.rows = stack_rows([v.quarters[d] for d in range(1, nz)])
        v.rows_x = mp_swap(v.rows, 2)

    def gather_core():
        v.rows_core = [mp_swap(part, 1) for part in hold([v.rows, v.rows_x])]

    def heads_in():
        made = heads_upstream(place, v.branch, v.branch_sib, w_out, nz)
        v.out_grads = [made[0]] + [seq_swap(made[d], d * ring) for d in range(1, nz)]

    def attend_far():
        v.dq_far, *summed = attend_back(
            place, doc_ends, queries, v.out_grads, far, None, nz, ring, 1, ring - 1, BF16
        )
        summed = [None] + summed
        for b in reversed(range(low_bits)):
            bit = 1 << b
            for e in range(bit):
                got = seq_swap(summed[e | bit], bit)
                summed[e] = (
                    got
                    if summed[e] is None
                    else (summed[e].astype(F32) + got.astype(F32)).astype(BF16)
                )
        v.dkv_got = summed[0]

    def attend_near():
        v.dq, v.dkv = attend_back(
            place, doc_ends, queries, v.out_grads, near, v.dq_far, nz, ring, 0, 1, F32
        )

    def head_grads():
        cosine, signed = rope_tables(token_index - begin)
        v.grads = finish_grads(v.dq, v.dkv, v.dkv_got, cosine, signed)
        v.own_grads = [v.grads[0]] + [
            seq_swap(v.grads[d], d * ring) for d in range(1, nz)
        ]

    def turn_branch():
        v.branch_turned = turn(order, group, v.branch + v.branch_sib, spots)

    def grad_out():
        v.sent_out, v.part_out = weight_grad([v.branch_turned], [v.heads_placed])

    def send_out():
        (sent,) = hold([v.sent_out])
        v.low_out = low_sums(sent, v.part_out)

    def merge_out():
        v.kept_out, v.high_out = merge(*v.low_out)

    def high_out():
        (sent,) = hold([v.high_out])
        v.come_out = seq_swap(sent, high)

    def sum_out():
        v.own_out, sent = final_sum([v.kept_out, v.come_out])
        v.pair_out = seq_swap(sent, pair)

    def turn_rows():
        v.all_turned = turn_all(
            order, group, normed, [v.rows, v.rows_core[0], v.rows_x, v.rows_core[1]], m
        )

    def grad_qkv():
        v.sent_qkv, v.part_qkv = weight_grad(
            [v.all_turned], [jnp.concatenate(v.grads, axis=0)]
        )

    def send_qkv():
        (sent,) = hold([v.sent_qkv])
        v.low_qkv = low_sums(sent, v.part_qkv)

    def split_qkv():
        own, *sent = split_sum(*v.low_qkv, nz)
        v.qkv_heads = [own] + [seq_swap(sent[d - 1], d * ring) for d in range(1, nz)]

    def lay_qkv():
        v.shares = place_heads(place, v.qkv_heads)

    def rows_in():
        sib, v.in_mine = heads_project(place, v.own_grads, weights, nt, False)
        v.in_sib = mp_swap(sib, 1)

    def in_sum():
        v.in_parts = row_sum(v.in_mine, v.in_sib, CHUNKS)
        v.in_across = [mp_swap(part, 2) for part in v.in_parts]

    def norm_in_chunk(i):
        v.grad_rows[i], v.gain_attn[i] = norm_back(
            v.in_parts[i], v.in_across[i], x_chunks[i], v.residual_grad[i], gain_attn_row, (BF16,)
        )
        v.grad_sib[i] = mp_swap(v.grad_rows[i], 1)

    def join_in():
        v.input_grad = join_rows(place, v.grad_rows, v.grad_sib)

    def down_rows():
        v.down_mine, v.down_theirs = down(place, v.act, v.act_sib, w_down, v.down_sib, 2)

    def pair_rows():
        (sent,) = hold([v.down_theirs])
        v.down_got = seq_swap(sent, pair)

    def sum_rows():
        (v.down_part,) = row_sum(v.down_mine, v.down_got, 1)
        v.down_across = mp_swap(v.down_part, 2)

    def add_out():
        v.out_rows = add_rows(
            v.down_part, v.down_across, jnp.concatenate(v.residual, axis=0)
        )
        v.out_sib = mp_swap(v.out_rows, 1)

    def join_out():
        v.mixed_out = join_rows(place, [v.out_rows], [v.out_sib])

    def gains_core():
        (v.gains,) = hold([jnp.concatenate([sum(v.gain_attn), sum(v.gain_mlp)])])
        v.gains = v.gains + mp_swap(v.gains, 1)

    def gains_seq(bit):
        (v.gains,) = hold([v.gains])
        v.gains = v.gains + seq_swap(v.gains, 1 << bit)

    heads_out()
    dact_own()
    gather_z(1)
    out_sum()
    swap_weights()
    norm_chunk(1)
    dact_sib()
    norm_chunk(0)
    turn_cot()
    swap_cot()
    gather_z(2)
    hidden_sib()
    swap_dg()
    hidden_own()
    turn_normed()
    swap_du()
    swap_normed()
    grad_down()
    hidden_in()
    send_down()
    grad_gate()
    gather_z(3)
    back_chunk(1)
    send_gate()
    back_chunk(0)
    gather_x()
    norm_back_chunk(1)
    norm_back_chunk(0)
    heads_in()
    merge_down()
    turn_branch()
    high_down()
    grad_up()
    attend_far()
    send_up()
    gather_core()
    attend_near()
    merge_gate()
    high_gate()
    sum_down()
    head_grads()
    pair_down()
    rows_in()
    merge_up()
    grad_out()
    loose(high_up)
    in_sum()
    down_rows()
    norm_in_chunk(0)
    send_out()
    turn_rows()
    lay_down()
    grad_qkv()
    merge_out()
    high_out()
    norm_in_chunk(1)
    pair_rows()
    send_qkv()
    sum_gate()
    gains_core()
    gains_seq(0)
    pair_gate()
    join_in()
    split_qkv()
    sum_up()
    sum_rows()
    gains_seq(2)
    pair_up()
    sum_out()
    lay_gate()
    loose(add_out)
    lay_up()
    gains_seq(1)
    join_out()
    lay_qkv()
    for bit in range(3, bits):
        gains_seq(bit)
    gains = lax.dynamic_slice_in_dim(v.gains, s * group, group, 1)

    return (
        v.mixed_out,
        v.input_grad,
        *v.shares,
        (v.own_out + v.pair_out.astype(F32)).T,
        gains[0],
        v.gate_share,
        v.up_share,
        v.down_share,
        gains[1],
    )


def solution(mesh):
    placed = (
        P("seq", None),
        P(None, "mp"),
        P(None, "mp"),
        P(None, "mp"),
        P("mp", None),
        P(),
        P(None, "mp"),
        P(None, "mp"),
        P("mp", None),
        P(),
        P(),
        P("seq", None),
    )
    return jax.shard_map(
        functools.partial(layer, mesh.shape["seq"], mesh.shape["mp"]),
        mesh=mesh,
        in_specs=placed,
        out_specs=(
            P("seq", None),
            P("seq", None),
            P("seq", "mp"),
            P("seq", "mp"),
            P("seq", "mp"),
            P("mp", "seq"),
            P("seq"),
            P("seq", "mp"),
            P("seq", "mp"),
            P("mp", "seq"),
            P("seq"),
        ),
        check_vma=False,
    )
```

```python
import functools
import math
import types

import jax
import jax.numpy as jnp
from jax import lax
from jax.experimental import pallas as pl
from jax.experimental.pallas import tpu as pltpu
from jax.sharding import PartitionSpec as P

HD = 128
EPSILON = 1e-05
THETA = 10000.0
FACTOR = 1.0 / math.sqrt(HD)
CLAMP = 80.0
CHUNKS = 2
SHARE = 0.5
ORDER = []
LOOSE = [False]
MIB = 1024 * 1024
F32 = jnp.float32
BF16 = jnp.bfloat16


def nn(left, right):
    return lax.dot_general(left, right, (((1,), (0,)), ((), ())), preferred_element_type=F32)


def nt(left, right):
    return lax.dot_general(left, right, (((1,), (1,)), ((), ())), preferred_element_type=F32)


def tn(left, right):
    return lax.dot_general(left, right, (((0,), (0,)), ((), ())), preferred_element_type=F32)


def call(
    body,
    out_shape,
    operands,
    in_specs,
    flops,
    moved,
    transcendentals=0,
    after=(),
    prefetch=0,
    chain=True,
    vmem=20,
    **kwargs,
):
    n = prefetch + len(in_specs)
    chain = chain and not LOOSE[0]
    after = list(after) + (ORDER if chain else [])

    def kernel(*refs):
        body(*refs[:n], *refs[n + len(after) :])

    in_specs = list(in_specs) + [pl.BlockSpec(memory_space=pl.ANY)] * len(after)
    if prefetch:
        kwargs = {
            "name": kwargs.pop("name"),
            "grid_spec": pltpu.PrefetchScalarGridSpec(
                num_scalar_prefetch=prefetch, in_specs=in_specs, **kwargs
            ),
        }
    else:
        kwargs["in_specs"] = in_specs
    made = pl.pallas_call(
        kernel,
        out_shape=out_shape,
        compiler_params=pltpu.CompilerParams(vmem_limit_bytes=vmem * MIB),
        cost_estimate=pl.CostEstimate(
            flops=int(flops / SHARE),
            bytes_accessed=int(moved / SHARE),
            transcendentals=int(transcendentals / SHARE),
        ),
        **kwargs,
    )(*operands, *after)
    if chain:
        ORDER[:] = [made[0] if isinstance(made, (tuple, list)) else made]
    return made


def hold(values, after=()):
    n = len(values)
    if LOOSE[0]:
        return list(lax.optimization_barrier((*values, *after))[:n])
    made = lax.optimization_barrier((*values, *ORDER, *after))
    ORDER[:] = made[n : n + len(ORDER)]
    return list(made[:n])


def loose(step, *args):
    LOOSE[0] = True
    step(*args)
    LOOSE[0] = False


def whole(memory):
    return pl.BlockSpec(memory_space=memory)


def rotated(values, cosine, signed):
    return values * cosine + pltpu.roll(values, HD // 2, 1) * signed


def unrotated(values, cosine, signed):
    return values * cosine - pltpu.roll(values, HD // 2, 1) * signed


def qkv_body(n, fresh, place_ref, *refs):
    if fresh:
        x_ref, gain_ref, refs = refs[0], refs[1], refs[2:]
    else:
        x_ref, refs = refs[0], refs[1:]
    wq_ref, wk_ref, wv_ref, cos_ref, sin_ref = refs[:5]
    outs, (w_s, x_s) = refs[5 : 5 + n], refs[-2:]
    step = pl.program_id(0)

    @pl.when(step == 0)
    def _():
        if fresh:
            x = x_ref[...].astype(F32)
            x_s[...] = (x * scale_of(x) * gain_ref[...]).astype(BF16)
            refs[5 + n][...] = x_s[...]
        else:
            x_s[...] = x_ref[...]

    w_s[:, :HD] = wq_ref[...]
    w_s[:, HD : 2 * HD] = wk_ref[...]
    w_s[:, 2 * HD :] = wv_ref[...]
    made = nn(x_s[...], w_s[...])
    cosine = cos_ref[...]
    signed = sin_ref[...]
    query = rotated(made[:, :HD], cosine, signed).astype(BF16)
    key = rotated(made[:, HD : 2 * HD], cosine, signed).astype(BF16)
    value = made[:, 2 * HD :].astype(BF16)
    for i in range(n):

        @pl.when(step == i)
        def _(i=i):
            outs[i][:, :HD] = query
            outs[i][:, HD : 2 * HD] = key
            outs[i][:, 2 * HD :] = value


def project_qkv(place, x, gain, weights, cosine, signed, spots):
    n = len(spots)
    rows, width = x.shape
    fresh = gain is not None
    fixed = pl.BlockSpec((rows, width), lambda i, place: (0, 0))
    table = pl.BlockSpec((rows, HD), lambda i, place: (0, 0))
    first = spots[0]
    assert list(spots) == [first ^ i for i in range(n)]
    weight = pl.BlockSpec((width, HD), lambda i, place: (0, place[0] ^ first ^ i))
    piece = jax.ShapeDtypeStruct((rows, 3 * HD), BF16)
    return call(
        functools.partial(qkv_body, n, fresh),
        (piece,) * n + ((jax.ShapeDtypeStruct(x.shape, BF16),) if fresh else ()),
        [place, x] + ([gain] if fresh else []) + [*weights, cosine, signed],
        [fixed]
        + ([pl.BlockSpec((1, width), lambda i, place: (0, 0))] if fresh else [])
        + [weight] * 3
        + [table] * 2,
        6 * n * rows * width * HD,
        4 * rows * width + 6 * n * width * HD + 6 * n * rows * HD,
        prefetch=1,
        grid=(n,),
        out_specs=(pl.BlockSpec((rows, 3 * HD), lambda i, place: (0, 0)),) * n
        + ((fixed,) if fresh else ()),
        scratch_shapes=[pltpu.VMEM((width, 3 * HD), BF16), pltpu.VMEM((rows, width), BF16)],
        vmem=60,
        name="project_qkv",
    )


def begin_of(index, ends_ref, count):
    begin = jnp.zeros_like(index)
    for e in range(count):
        end = ends_ref[e]
        begin = jnp.where(end <= index, jnp.maximum(begin, end), begin)
    return begin


def finish_of(index, ends_ref, count):
    finish = jnp.zeros_like(index) + ends_ref[count - 1]
    for e in range(count):
        end = ends_ref[e]
        finish = jnp.where(end > index, jnp.minimum(finish, end), finish)
    return finish


def attend_body(nz, ring, count, place_ref, ends_ref, *refs):
    n_kv = nz * ring
    q_refs, refs = refs[:nz], refs[nz:]
    kv_refs, refs = refs[:n_kv], refs[n_kv:]
    o_refs, refs = refs[:nz], refs[nz:]
    q_s, k_s, v_s, o_s, acc = refs
    z, r = place_ref[0], place_ref[1]
    rows = q_s.shape[1]
    for d in range(nz):
        q_s[d] = q_refs[d][:, :HD]
    for i in range(n_kv):
        first = kv_refs[i].shape[1] - 2 * HD
        k_s[i] = kv_refs[i][:, first : first + HD]
        v_s[i] = kv_refs[i][:, first + HD :]

    @pl.loop(0, nz)
    def per_query(d):
        q_block = (z ^ d) * ring + r
        q_start = q_block * rows
        q_index = q_start + lax.broadcasted_iota(jnp.int32, (rows, 1), 0)
        begin = begin_of(q_index, ends_ref, count)
        shift = jnp.log((finish_of(q_index, ends_ref, count) - begin).astype(F32))
        first_begin = begin_of(q_start, ends_ref, count)
        last_begin = begin_of(q_start + (rows - 1), ends_ref, count)
        acc[...] = jnp.zeros_like(acc)

        @pl.loop(0, n_kv)
        def per_key(i):
            k_block = (z ^ (i & (nz - 1))) * ring + (r ^ (i // nz))
            k_start = k_block * rows
            needed = (k_block <= q_block) & (k_start + rows > first_begin)
            full = (k_block < q_block) & (k_start >= last_begin)

            def tile(masked):
                half = rows // 2
                for part in range(2):
                    at = slice(part * half, (part + 1) * half)
                    scores = nt(q_s[d, at], k_s[i])
                    grown = jnp.exp(jnp.minimum(shift[at] - scores * FACTOR, CLAMP))
                    probs = pl.reciprocal(1.0 + grown, approx=True)
                    if masked:
                        k_index = k_start + lax.broadcasted_iota(jnp.int32, (1, rows), 1)
                        allowed = (k_index <= q_index[at]) & (k_index >= begin[at])
                        probs = jnp.where(allowed, probs, 0.0)
                    acc[at] += nn(probs.astype(BF16), v_s[i])

            pl.when(needed & full)(functools.partial(tile, False))
            pl.when(needed & jnp.logical_not(full))(functools.partial(tile, True))

        o_s[d] = acc[...].astype(BF16)

    for d in range(nz):
        o_refs[d][...] = o_s[d]


def attend(place, ends, queries, keys_values, nz, ring, after=()):
    rows = queries[0].shape[0]
    n_kv = nz * ring
    pairs = nz * n_kv / 2
    return call(
        functools.partial(attend_body, nz, ring, ends.shape[0]),
        tuple(jax.ShapeDtypeStruct((rows, HD), BF16) for _ in range(nz)),
        [place, ends, *queries, *keys_values],
        [whole(pltpu.SMEM)] * 2 + [whole(pltpu.VMEM)] * (nz + n_kv),
        pairs * 4 * rows * rows * HD * 2,
        2 * (2 * nz + 2 * n_kv) * rows * HD,
        pairs * 2 * rows * rows,
        after=after,
        out_specs=tuple(whole(pltpu.VMEM) for _ in range(nz)),
        scratch_shapes=[
            pltpu.VMEM((nz, rows, HD), BF16),
            pltpu.VMEM((n_kv, rows, HD), BF16),
            pltpu.VMEM((n_kv, rows, HD), BF16),
            pltpu.VMEM((nz, rows, HD), BF16),
            pltpu.VMEM((rows, HD), F32),
        ],
        vmem=12 + 2 * n_kv * rows * HD * 8 // MIB,
        name="attend",
    )


def attend_back_body(nz, ring, n_dr, first_dr, chained, count, place_ref, ends_ref, *refs):
    n_kv = nz * n_dr
    q_refs, refs = refs[:nz], refs[nz:]
    do_refs, refs = refs[:nz], refs[nz:]
    kv_refs, refs = refs[:n_kv], refs[n_kv:]
    if chained:
        before_ref, refs = refs[0], refs[1:]
    dq_ref, refs = refs[0], refs[1:]
    dkv_refs, refs = refs[:n_dr], refs[n_dr:]
    q_s, do_s, k_s, v_s, begin_s, shift_s, dkv_s, dk_acc, dv_acc = refs
    z, r = place_ref[0], place_ref[1]
    rows = q_s.shape[1]
    for d in range(nz):
        q_s[d] = q_refs[d][:, :HD]
        do_s[d] = do_refs[d][...]
    for i in range(n_kv):
        first = kv_refs[i].shape[1] - 2 * HD
        k_s[i] = kv_refs[i][:, first : first + HD]
        v_s[i] = kv_refs[i][:, first + HD :]
    if chained:
        dq_ref[...] = before_ref[...]
    else:
        dq_ref[...] = jnp.zeros_like(dq_ref)

    @pl.loop(0, nz)
    def tables(d):
        q_index = ((z ^ d) * ring + r) * rows + lax.broadcasted_iota(jnp.int32, (1, rows), 1)
        begin = begin_of(q_index, ends_ref, count)
        begin_s[d] = begin
        shift_s[d] = jnp.log((finish_of(q_index, ends_ref, count) - begin).astype(F32))

    @pl.loop(0, n_kv)
    def per_key(i):
        k_block = (z ^ (i & (nz - 1))) * ring + (r ^ (first_dr + i // nz))
        k_start = k_block * rows
        dk_acc[...] = jnp.zeros_like(dk_acc)
        dv_acc[...] = jnp.zeros_like(dv_acc)

        @pl.loop(0, nz)
        def per_query(d):
            q_block = (z ^ d) * ring + r
            q_start = q_block * rows
            first_begin = begin_of(q_start, ends_ref, count)
            last_begin = begin_of(q_start + (rows - 1), ends_ref, count)
            needed = (k_block <= q_block) & (k_start + rows > first_begin)
            full = (k_block < q_block) & (k_start >= last_begin)

            def tile(masked):
                half = rows // 2
                for part in range(2):
                    at = slice(part * half, (part + 1) * half)
                    keys = k_s[i, at]
                    scores = nt(keys, q_s[d])
                    grown = jnp.exp(jnp.minimum(shift_s[d] - scores * FACTOR, CLAMP))
                    probs = pl.reciprocal(1.0 + grown, approx=True)
                    if masked:
                        k_index = (
                            k_start
                            + part * half
                            + lax.broadcasted_iota(jnp.int32, (half, 1), 0)
                        )
                        q_index = q_start + lax.broadcasted_iota(jnp.int32, (1, rows), 1)
                        allowed = (k_index <= q_index) & (k_index >= begin_s[d])
                        probs = jnp.where(allowed, probs, 0.0)
                    weight_grad = nt(v_s[i, at], do_s[d])
                    score_grad = (weight_grad * (probs * probs * grown)).astype(BF16)
                    dv_acc[at] += nn(probs.astype(BF16), do_s[d])
                    dk_acc[at] += nn(score_grad, q_s[d])
                    dq_ref[d] += tn(score_grad, keys)

            pl.when(needed & full)(functools.partial(tile, False))
            pl.when(needed & jnp.logical_not(full))(functools.partial(tile, True))

        dkv_s[i, :, :HD] = (dk_acc[...] * FACTOR).astype(dkv_s.dtype)
        dkv_s[i, :, HD:] = dv_acc[...].astype(dkv_s.dtype)

    for e in range(n_dr):
        for d in range(nz):
            dkv_refs[e][d] = dkv_s[e * nz + d]


def attend_back(
    place, ends, queries, out_grads, keys_values, before, nz, ring, first_dr, n_dr, kept, after=()
):
    rows = queries[0].shape[0]
    n_kv = nz * n_dr
    pairs = nz * n_kv / 2
    chained = before is not None
    return call(
        functools.partial(
            attend_back_body, nz, ring, n_dr, first_dr, chained, ends.shape[0]
        ),
        (jax.ShapeDtypeStruct((nz, rows, HD), F32),)
        + tuple(jax.ShapeDtypeStruct((nz, rows, 2 * HD), kept) for _ in range(n_dr)),
        [place, ends, *queries, *out_grads, *keys_values, *([before] if chained else [])],
        [whole(pltpu.SMEM)] * 2 + [whole(pltpu.VMEM)] * (2 * nz + n_kv + chained),
        pairs * 10 * rows * rows * HD * 2,
        2 * (2 * nz + 4 * n_kv) * rows * HD,
        pairs * 2 * rows * rows,
        after=after,
        out_specs=tuple(whole(pltpu.VMEM) for _ in range(1 + n_dr)),
        scratch_shapes=[
            pltpu.VMEM((nz, rows, HD), BF16),
            pltpu.VMEM((nz, rows, HD), BF16),
            pltpu.VMEM((n_kv, rows, HD), BF16),
            pltpu.VMEM((n_kv, rows, HD), BF16),
            pltpu.VMEM((nz, 1, rows), jnp.int32),
            pltpu.VMEM((nz, 1, rows), F32),
            pltpu.VMEM((n_kv, rows, 2 * HD), kept),
            pltpu.VMEM((rows, HD), F32),
            pltpu.VMEM((rows, HD), F32),
        ],
        vmem=16 + 2 * n_kv * rows * HD * 14 // MIB,
        name="attend_back",
    )


def finish_body(nz, dq_ref, dkv_ref, got_ref, cos_ref, sin_ref, *out_refs):
    for d in range(nz):
        cosine = cos_ref[d]
        signed = sin_ref[d]
        total = dkv_ref[d] + got_ref[d].astype(F32)
        out = out_refs[d]
        out[:, :HD] = unrotated(dq_ref[d] * FACTOR, cosine, signed).astype(BF16)
        out[:, HD : 2 * HD] = unrotated(total[:, :HD], cosine, signed).astype(BF16)
        out[:, 2 * HD :] = total[:, HD:].astype(BF16)


def finish_grads(dq, dkv, got, cosine, signed):
    nz, rows, _ = dq.shape
    return call(
        functools.partial(finish_body, nz),
        tuple(jax.ShapeDtypeStruct((rows, 3 * HD), BF16) for _ in range(nz)),
        [dq, dkv, got, cosine, signed],
        [whole(pltpu.VMEM)] * 5,
        12 * nz * rows * HD,
        nz * rows * HD * 30,
        out_specs=tuple(whole(pltpu.VMEM) for _ in range(nz)),
        name="finish_grads",
    )


def rows_at(place, width, height, tile_of):
    return pl.BlockSpec((height, width), lambda j, place: (tile_of(place), 0))


def place_rows(pieces, scratch, spot):
    size = pieces[0].shape[0]
    half = size * len(pieces)
    for i, piece in enumerate(pieces):
        at = pl.multiple_of(spot * half + i * size, size)
        scratch[pl.ds(at, size), :] = piece[...]


def upstream_body(place_ref, *refs):
    pieces, (w_ref, out_ref, x_s) = refs[:-3], refs[-3:]
    size = pieces[0].shape[0]

    @pl.when(pl.program_id(0) == 0)
    def _():
        for i, piece in enumerate(pieces):
            x_s[i * size : (i + 1) * size] = piece[...]

    out_ref[...] = nt(x_s[...], w_ref[...]).astype(BF16)


def hidden_upstream(place, pieces, weights, own, after=()):
    size, width = pieces[0].shape
    rows = size * len(pieces)
    units = weights.shape[0] // (2 if own else 1)
    tile = 512
    steps = units // tile
    first = (lambda place: place[3] * steps) if own else (lambda place: 0)
    return call(
        upstream_body,
        jax.ShapeDtypeStruct((rows, units), BF16),
        [place, *pieces, weights],
        [pl.BlockSpec((size, width), lambda j, place: (0, 0))] * len(pieces)
        + [pl.BlockSpec((tile, width), lambda j, place: (first(place) + j, 0))],
        2 * rows * width * units,
        2 * width * units + 4 * rows * units + 2 * rows * width,
        after=after,
        prefetch=1,
        grid=(steps,),
        out_specs=pl.BlockSpec((rows, tile), lambda j, place: (0, j)),
        scratch_shapes=[pltpu.VMEM((rows, width), BF16)],
        vmem=52,
        name="hidden_upstream",
    )


def hidden_body(place_ref, *refs):
    pieces, refs = refs[:-7], refs[-7:]
    wg_ref, wu_ref, dact_ref, act_ref, dg_ref, du_ref, x_s = refs
    size = pieces[0].shape[0]

    @pl.when(pl.program_id(0) == 0)
    def _():
        for i, piece in enumerate(pieces):
            x_s[i * size : (i + 1) * size] = piece[...]

    x = x_s[...]
    for first in range(0, act_ref.shape[1], 256):
        at = slice(first, first + 256)
        gate = nn(x, wg_ref[:, at])
        up = nn(x, wu_ref[:, at])
        dact = dact_ref[:, at].astype(F32)
        sig = jax.nn.sigmoid(gate)
        silu = gate * sig
        act_ref[:, at] = (silu * up).astype(BF16)
        dg_ref[:, at] = (dact * up * sig * (1.0 + gate * (1.0 - sig))).astype(BF16)
        du_ref[:, at] = (dact * silu).astype(BF16)


def hidden(place, pieces, w_gate, w_up, dact, own, after=()):
    size, width = pieces[0].shape
    rows = size * len(pieces)
    units = dact.shape[1]
    tile = 512
    steps = units // tile
    first = (lambda place: place[3] * steps) if own else (lambda place: 0)
    made = jax.ShapeDtypeStruct((rows, units), BF16)
    block = pl.BlockSpec((rows, tile), lambda j, place: (0, j))
    weight = pl.BlockSpec((width, tile), lambda j, place: (0, first(place) + j))
    return call(
        hidden_body,
        (made, made, made),
        [place, *pieces, w_gate, w_up, dact],
        [pl.BlockSpec((size, width), lambda j, place: (0, 0))] * len(pieces)
        + [weight, weight, block],
        4 * rows * width * units,
        4 * width * units + 8 * rows * units + 2 * rows * width,
        rows * units,
        after=after,
        prefetch=1,
        grid=(steps,),
        out_specs=(block, block, block),
        scratch_shapes=[pltpu.VMEM((rows, width), BF16)],
        vmem=52,
        name="hidden",
    )


def chunked(total, out_refs):
    size = out_refs[0].shape[0]
    for i, ref in enumerate(out_refs):
        ref[...] = total[i * size : (i + 1) * size].astype(ref.dtype)


def back_body(place_ref, dg_ref, dg_sib, du_ref, du_sib, wg_ref, wg_sib, wu_ref, wu_sib, *outs):
    chunked(
        nt(dg_ref[...], wg_ref[...])
        + nt(dg_sib[...], wg_sib[...])
        + nt(du_ref[...], wu_ref[...])
        + nt(du_sib[...], wu_sib[...]),
        outs,
    )


def hidden_back(place, dg, dg_sib, du, du_sib, w_gate, gate_sib, w_up, up_sib, chunks, after=()):
    rows, half = dg.shape
    width = w_gate.shape[0]
    tile = 512
    size = rows // chunks
    left = pl.BlockSpec((rows, half), lambda j, place: (0, 0))
    own = pl.BlockSpec((tile, half), lambda j, place: (j, place[3]))
    sib = pl.BlockSpec((tile, half), lambda j, place: (j, 0))
    return call(
        back_body,
        tuple(jax.ShapeDtypeStruct((size, width), BF16) for _ in range(chunks)),
        [place, dg, dg_sib, du, du_sib, w_gate, gate_sib, w_up, up_sib],
        [left] * 4 + [own, sib, own, sib],
        8 * rows * width * half,
        8 * width * half + 8 * rows * half + 2 * rows * width,
        after=after,
        prefetch=1,
        grid=(width // tile,),
        out_specs=tuple(pl.BlockSpec((size, tile), lambda j, place: (0, j)) for _ in range(chunks)),
        vmem=52,
        name="hidden_back",
    )


def down_body(place_ref, act_ref, act_sib, wd_ref, wd_sib, *outs):
    chunked(nn(act_ref[...], wd_ref[...]) + nn(act_sib[...], wd_sib[...]), outs)


def down(place, act, act_sib, w_down, down_sib, chunks, after=()):
    rows, half = act.shape
    width = w_down.shape[1]
    tile = 512
    size = rows // chunks
    left = pl.BlockSpec((rows, half), lambda j, place: (0, 0))
    return call(
        down_body,
        tuple(jax.ShapeDtypeStruct((size, width), BF16) for _ in range(chunks)),
        [place, act, act_sib, w_down, down_sib],
        [
            left,
            left,
            pl.BlockSpec((half, tile), lambda j, place: (place[3], j)),
            pl.BlockSpec((half, tile), lambda j, place: (0, j)),
        ],
        4 * rows * width * half,
        4 * width * half + 4 * rows * half + 2 * rows * width,
        after=after,
        prefetch=1,
        grid=(width // tile,),
        out_specs=tuple(pl.BlockSpec((size, tile), lambda j, place: (0, j)) for _ in range(chunks)),
        vmem=52,
        name="down",
    )


def heads_body(nz, contract, keep, place_ref, *refs):
    n_w = 1 if keep else 3
    pieces, refs = refs[:nz], refs[nz:]
    w_refs, (sib_ref, mine_ref), refs = refs[:n_w], refs[n_w : n_w + 2], refs[n_w + 2 :]
    joined = refs[:n_w]
    for d in range(nz):
        at = pl.multiple_of((place_ref[0] ^ d) * HD, HD)
        for i in range(n_w):
            joined[i][:, pl.ds(at, HD)] = pieces[d][:, i * HD : (i + 1) * HD]
    half = sib_ref.shape[0]
    core = place_ref[2] & 1

    def rows_of(start):
        start = pl.multiple_of(start, half)
        total = contract(joined[0][pl.ds(start, half), :], w_refs[0][...])
        for i in range(1, n_w):
            total = total + contract(joined[i][pl.ds(start, half), :], w_refs[i][...])
        return total

    sib_ref[...] = rows_of((1 - core) * half).astype(BF16)
    mine_ref[...] = rows_of(core * half)


def heads_project(place, pieces, weights, contract, keep, after=()):
    nz = len(pieces)
    rows = pieces[0].shape[0]
    n_w = len(weights)
    width = weights[0].shape[1] if contract is nn else weights[0].shape[0]
    half = rows // 2
    joined = (rows, nz * HD)
    out = (
        jax.ShapeDtypeStruct((half, width), BF16),
        jax.ShapeDtypeStruct((half, width), F32),
    ) + ((jax.ShapeDtypeStruct(joined, BF16),) if keep else ())
    return call(
        functools.partial(heads_body, nz, contract, keep),
        out,
        [place, *pieces, *weights],
        [whole(pltpu.SMEM)] + [whole(pltpu.VMEM)] * (nz + n_w),
        2 * rows * width * nz * HD * n_w,
        2 * n_w * (width * nz * HD + rows * nz * HD) + 3 * rows * width,
        after=after,
        out_specs=tuple(whole(pltpu.VMEM) for _ in out),
        scratch_shapes=() if keep else (pltpu.VMEM(joined, BF16),) * n_w,
        vmem=24,
        name="heads_project",
    )


def dheads_body(nz, n, place_ref, *refs):
    mine, refs = refs[:n], refs[n:]
    sibs, refs = refs[:n], refs[n:]
    w_ref, outs, x_s = refs[0], refs[1:-1], refs[-1]
    core = place_ref[2] & 1
    place_rows(mine, x_s, core)
    place_rows(sibs, x_s, 1 - core)
    x = x_s[...]
    wide = outs[0].shape[1]
    for d in range(nz):
        at = pl.multiple_of((place_ref[0] ^ d) * wide, wide)
        outs[d][...] = nt(x, w_ref[pl.ds(at, wide), :]).astype(BF16)


def heads_upstream(place, mine, sibs, w_out, nz, after=()):
    n = len(mine)
    size, width = mine[0].shape
    rows = 2 * n * size
    wide = w_out.shape[0] // nz
    return call(
        functools.partial(dheads_body, nz, n),
        tuple(jax.ShapeDtypeStruct((rows, wide), BF16) for _ in range(nz)),
        [place, *mine, *sibs, w_out],
        [whole(pltpu.SMEM)] + [whole(pltpu.VMEM)] * (2 * n + 1),
        2 * rows * width * nz * wide,
        2 * width * nz * wide + 2 * rows * nz * wide + 2 * rows * width,
        after=after,
        out_specs=tuple(whole(pltpu.VMEM) for _ in range(nz)),
        scratch_shapes=[pltpu.VMEM((rows, width), BF16)],
        name="heads_upstream",
    )


def sum_body(mine_ref, got_ref, *outs):
    chunked(mine_ref[...].astype(F32) + got_ref[...].astype(F32), outs)


def row_sum(mine, got, chunks, after=()):
    rows, width = mine.shape
    size = rows // chunks
    return call(
        sum_body,
        tuple(jax.ShapeDtypeStruct((size, width), BF16) for _ in range(chunks)),
        [mine, got],
        [whole(pltpu.VMEM)] * 2,
        rows * width,
        8 * rows * width,
        after=after,
        out_specs=tuple(whole(pltpu.VMEM) for _ in range(chunks)),
        name="row_sum",
    )


def scale_of(values):
    return lax.rsqrt(jnp.mean(values * values, axis=-1, keepdims=True) + EPSILON)


def norm_body(part_ref, got_ref, x_ref, gain_ref, res_ref, normed_ref):
    residual = x_ref[...].astype(F32) + (part_ref[...].astype(F32) + got_ref[...].astype(F32))
    res_ref[...] = residual
    normed_ref[...] = (residual * scale_of(residual) * gain_ref[...]).astype(BF16)


def norm_rows(part, got, x, gain, after=()):
    rows, width = part.shape
    return call(
        norm_body,
        (
            jax.ShapeDtypeStruct((rows, width), F32),
            jax.ShapeDtypeStruct((rows, width), BF16),
        ),
        [part, got, x, gain],
        [whole(pltpu.VMEM)] * 4,
        8 * rows * width,
        12 * rows * width,
        after=after,
        out_specs=(whole(pltpu.VMEM), whole(pltpu.VMEM)),
        name="norm_rows",
    )


def norm_back_body(part_ref, got_ref, values_ref, add_ref, gain_ref, *outs):
    upstream = part_ref[...].astype(F32) + got_ref[...].astype(F32)
    values = values_ref[...].astype(F32)
    scale = scale_of(values)
    normed = values * scale
    outs[-1][...] = jnp.sum(upstream * normed, axis=0, keepdims=True)
    weighted = upstream * gain_ref[...]
    grad = scale * (weighted - normed * jnp.mean(weighted * normed, axis=-1, keepdims=True))
    total = add_ref[...].astype(F32) + grad
    for ref in outs[:-1]:
        ref[...] = total.astype(ref.dtype)


def norm_back(part, got, values, add, gain, kinds, after=()):
    rows, width = part.shape
    return call(
        norm_back_body,
        tuple(jax.ShapeDtypeStruct((rows, width), kind) for kind in kinds)
        + (jax.ShapeDtypeStruct((1, width), F32),),
        [part, got, values, add, gain],
        [whole(pltpu.VMEM)] * 5,
        16 * rows * width,
        16 * rows * width,
        after=after,
        out_specs=tuple(whole(pltpu.VMEM) for _ in range(len(kinds) + 1)),
        name="norm_back",
    )


def add_body(part_ref, got_ref, res_ref, out_ref):
    out_ref[...] = (
        res_ref[...] + (part_ref[...].astype(F32) + got_ref[...].astype(F32))
    ).astype(BF16)


def add_rows(part, got, residual, after=()):
    return call(
        add_body,
        jax.ShapeDtypeStruct(part.shape, BF16),
        [part, got, residual],
        [whole(pltpu.VMEM)] * 3,
        part.size,
        10 * part.size,
        after=after,
        out_specs=whole(pltpu.VMEM),
        name="add_rows",
    )


def join_body(n, place_ref, *refs):
    core = place_ref[2] & 1
    place_rows(refs[:n], refs[-1], core)
    place_rows(refs[n : 2 * n], refs[-1], 1 - core)


def join_rows(place, mine, sibs, after=()):
    n = len(mine)
    size, width = mine[0].shape
    return call(
        functools.partial(join_body, n),
        jax.ShapeDtypeStruct((2 * n * size, width), BF16),
        [place, *mine, *sibs],
        [whole(pltpu.SMEM)] + [whole(pltpu.VMEM)] * (2 * n),
        0,
        8 * n * size * width,
        after=after,
        out_specs=whole(pltpu.VMEM),
        name="join_rows",
    )


def turn_body(n, block, offset_ref, order_ref, *refs):
    pieces, out_ref = refs[:n], refs[n]
    size, wide = pieces[0].shape
    unit = (
        lax.broadcasted_iota(jnp.int32, (block, block), 0)
        == lax.broadcasted_iota(jnp.int32, (block, block), 1)
    ).astype(F32).astype(BF16)
    for p in range(wide // block):
        at = pl.multiple_of(order_ref[p] * block, block)
        for j in range(n):
            to = pl.multiple_of(offset_ref[j] * size, size)
            made = nt(unit, pieces[j][:, pl.ds(at, block)]).astype(BF16)
            out_ref[p * block : (p + 1) * block, pl.ds(to, size)] = made


def turn(order, group, pieces, offsets=None, after=()):
    wide = pieces[0].shape[1]
    if group % 128 != 0:
        pieces = [
            jnp.concatenate(
                [
                    lax.dynamic_slice_in_dim(piece, order[p] * group, group, 1)
                    for p in range(order.shape[0])
                ],
                axis=1,
            )
            for piece in pieces
        ]
        block = math.gcd(256, wide)
        order_in = jnp.arange(wide // block, dtype=jnp.int32)
    else:
        block = group
        order_in = order
    n = len(pieces)
    size = pieces[0].shape[0]
    tokens = n * size
    if offsets is None:
        offsets = jnp.arange(n, dtype=jnp.int32)
    return call(
        functools.partial(turn_body, n, block),
        jax.ShapeDtypeStruct((wide, tokens), BF16),
        [offsets, order_in, *pieces],
        [whole(pltpu.SMEM)] * 2 + [whole(pltpu.VMEM)] * n,
        2 * tokens * wide * block,
        4 * tokens * wide,
        after=after,
        out_specs=whole(pltpu.VMEM),
        vmem=8 + 4 * tokens * wide // MIB,
        name="turn",
    )


def stack_body(*refs):
    for i, ref in enumerate(refs[:-1]):
        refs[-1][i] = ref[...]


def stack_rows(pieces):
    n = len(pieces)
    return call(
        stack_body,
        jax.ShapeDtypeStruct((n, *pieces[0].shape), BF16),
        list(pieces),
        [whole(pltpu.VMEM)] * n,
        0,
        4 * n * pieces[0].size,
        out_specs=whole(pltpu.VMEM),
        name="stack_rows",
    )


def turn_all_body(block, place_ref, order_ref, own_ref, *refs):
    parts, out_ref = refs[:-1], refs[-1]
    n = len(parts)
    size, wide = parts[0].shape[1:]
    unit = (
        lax.broadcasted_iota(jnp.int32, (block, block), 0)
        == lax.broadcasted_iota(jnp.int32, (block, block), 1)
    ).astype(F32).astype(BF16)

    @pl.when(pl.program_id(0) == 0)
    def _():
        for p in range(wide // block):
            at = pl.multiple_of(order_ref[p] * block, block)
            made = nt(unit, own_ref[:, pl.ds(at, block)]).astype(BF16)
            out_ref[p * block : (p + 1) * block, :] = made

    @pl.when(pl.program_id(0) > 0)
    def _():
        for p in range(wide // block):
            at = pl.multiple_of(order_ref[p] * block, block)
            for j in range(n):
                to = pl.multiple_of((place_ref[0] ^ j) * size, size)
                made = nt(unit, parts[j][0, :, pl.ds(at, block)]).astype(BF16)
                out_ref[p * block : (p + 1) * block, pl.ds(to, size)] = made


def turn_all(order, group, own, parts, m):
    tokens, wide = own.shape
    others, size, _ = parts[0].shape
    if group % 128 != 0:

        def ordered(values):
            axis = values.ndim - 1
            return jnp.concatenate(
                [
                    lax.dynamic_slice_in_dim(values, order[p] * group, group, axis)
                    for p in range(order.shape[0])
                ],
                axis=axis,
            )

        own = ordered(own)
        parts = [ordered(part) for part in parts]
        block = math.gcd(256, wide)
        order_in = jnp.arange(wide // block, dtype=jnp.int32)
    else:
        block = group
        order_in = order
    return call(
        functools.partial(turn_all_body, block),
        jax.ShapeDtypeStruct((wide, (others + 1) * tokens), BF16),
        [m.reshape(1).astype(jnp.int32), order_in, own, *parts],
        [pl.BlockSpec((tokens, wide), lambda d, place, order: (0, 0))]
        + [
            pl.BlockSpec((1, size, wide), lambda d, place, order: (jnp.maximum(d - 1, 0), 0, 0))
        ]
        * len(parts),
        2 * (others + 1) * tokens * wide * block,
        4 * (others + 1) * tokens * wide,
        prefetch=2,
        grid=(others + 1,),
        out_specs=pl.BlockSpec((wide, tokens), lambda d, place, order: (0, d)),
        vmem=52,
        name="turn_all",
    )


def weight_body(n, *refs):
    lefts, refs = refs[:n], refs[n:]
    rights, (sent_ref, kept_ref) = refs[:n], refs[n:]
    total = nn(lefts[0][...], rights[0][...])
    for i in range(1, n):
        total = total + nn(lefts[i][...], rights[i][...])
    half = pl.num_programs(0) // 2

    @pl.when(pl.program_id(0) < half)
    def _():
        sent_ref[...] = total.astype(BF16)

    @pl.when(pl.program_id(0) >= half)
    def _():
        kept_ref[...] = total.astype(BF16)


def weight_grad(lefts, rights, after=()):
    wide = lefts[0].shape[0]
    width = rights[0].shape[1]
    tokens = sum(left.shape[1] for left in lefts)
    steps = 4
    tile = wide // steps
    half = steps // 2
    made = jax.ShapeDtypeStruct((wide // 2, width), BF16)
    return call(
        functools.partial(weight_body, len(lefts)),
        (made,) * 2,
        [*lefts, *rights],
        [
            pl.BlockSpec((tile, left.shape[1]), lambda i: ((i + half) % steps, 0))
            for left in lefts
        ]
        + [pl.BlockSpec(right.shape, lambda i: (0, 0)) for right in rights],
        2 * tokens * wide * width,
        2 * (tokens * wide + tokens * width + wide * width),
        after=after,
        grid=(steps,),
        out_specs=(
            pl.BlockSpec((tile, width), lambda i: (jnp.minimum(i, half - 1), 0)),
            pl.BlockSpec((tile, width), lambda i: (jnp.maximum(i - half, 0), 0)),
        ),
        vmem=52,
        name="weight_grad",
    )


def sum3_body(n, *refs):
    total = refs[0][...].astype(F32)
    for ref in refs[1:n]:
        total = total + ref[...].astype(F32)
    low_ref, high_ref = refs[n:]
    low_ref[...] = total[0]
    high_ref[...] = total[1].astype(BF16)


def final_sum(terms, after=()):
    wide, width = terms[0].shape
    high = wide // 2
    tile = math.gcd(high, 128)
    block = pl.BlockSpec((2, tile, width), lambda i: (0, i, 0))
    out = pl.BlockSpec((tile, width), lambda i: (i, 0))
    return call(
        functools.partial(sum3_body, len(terms)),
        (
            jax.ShapeDtypeStruct((high, width), F32),
            jax.ShapeDtypeStruct((high, width), BF16),
        ),
        [term.reshape(2, high, width) for term in terms],
        [block] * len(terms),
        wide * width,
        wide * width * 8,
        after=after,
        grid=(high // tile,),
        out_specs=(out, out),
        name="final_sum",
    )


def merge_body(kept_ref, got_ref, low_ref, high_ref):
    total = kept_ref[...].astype(F32) + got_ref[...].astype(F32)
    low_ref[...] = total[0]
    high_ref[...] = total[1].astype(BF16)


def merge(kept, got, after=()):
    wide, width = kept.shape
    high = wide // 2
    tile = math.gcd(high, 128)
    operands = [kept.reshape(2, high, width), got.reshape(2, high, width)]
    block = pl.BlockSpec((2, tile, width), lambda i: (0, i, 0))
    out = pl.BlockSpec((tile, width), lambda i: (i, 0))
    return call(
        merge_body,
        (
            jax.ShapeDtypeStruct((high, width), F32),
            jax.ShapeDtypeStruct((high, width), BF16),
        ),
        operands,
        [block, block],
        wide * width,
        wide * width * 8,
        after=after,
        grid=(high // tile,),
        out_specs=(out, out),
        name="merge",
    )


def lay_body(turned, place_ref, own_ref, got_ref, out_ref):
    value = jnp.where(pl.program_id(0) == 0, own_ref[...], got_ref[...].astype(F32))
    out_ref[...] = value.T if turned else value


def lay(place, own, got, turned):
    rows, width = own.shape
    if turned:
        shape, block = (2 * width, rows), (width, rows)
        index = lambda i, place: (place[3] ^ i, 0)
    else:
        shape, block = (rows, 2 * width), (rows, width)
        index = lambda i, place: (0, place[3] ^ i)
    fixed = pl.BlockSpec((rows, width), lambda i, place: (0, 0))
    return call(
        functools.partial(lay_body, turned),
        jax.ShapeDtypeStruct(shape, F32),
        [place, own, got],
        [fixed, fixed],
        0,
        14 * rows * width,
        prefetch=1,
        grid=(2,),
        out_specs=pl.BlockSpec(block, index),
        name="lay",
    )


def qkv_sum_body(kept_ref, got_ref, own_ref, *outs):
    size = own_ref.shape[0]
    total = kept_ref[...].astype(F32) + got_ref[...].astype(F32)
    own_ref[...] = total[:size]
    for i, ref in enumerate(outs):
        ref[...] = total[(i + 1) * size : (i + 2) * size].astype(BF16)


def split_sum(kept, got, n):
    rows, width = kept.shape
    size = rows // n
    return call(
        qkv_sum_body,
        (jax.ShapeDtypeStruct((size, width), F32),)
        + (jax.ShapeDtypeStruct((size, width), BF16),) * (n - 1),
        [kept, got],
        [whole(pltpu.VMEM)] * 2,
        rows * width,
        8 * rows * width,
        out_specs=(whole(pltpu.VMEM),) * n,
        name="split_sum",
    )


def place_heads_body(nz, place_ref, *refs):
    pieces, outs = refs[:nz], refs[nz:]
    for d in range(nz):
        at = pl.multiple_of((place_ref[0] ^ d) * HD, HD)
        for i, out in enumerate(outs):
            out[:, pl.ds(at, HD)] = pieces[d][:, i * HD : (i + 1) * HD].astype(F32)


def place_heads(place, pieces):
    nz = len(pieces)
    rows = pieces[0].shape[0]
    return call(
        functools.partial(place_heads_body, nz),
        (jax.ShapeDtypeStruct((rows, nz * HD), F32),) * 3,
        [place, *pieces],
        [whole(pltpu.SMEM)] + [whole(pltpu.VMEM)] * nz,
        0,
        20 * rows * nz * HD,
        out_specs=(whole(pltpu.VMEM),) * 3,
        name="place_heads",
    )


def rope_tables(position):
    middle = HD // 2
    frequency = THETA ** (-(jnp.arange(middle, dtype=F32) * 2.0 / HD))
    angles = position.astype(F32)[..., None] * frequency
    cosine = jnp.cos(angles)
    sine = jnp.sin(angles)
    return (
        jnp.concatenate([cosine, cosine], axis=-1),
        jnp.concatenate([-sine, sine], axis=-1),
    )


def rms_scale(values):
    return lax.rsqrt(jnp.mean(values * values, axis=-1, keepdims=True) + EPSILON)


def layer(
    n_seq,
    n_mp,
    mixed_in,
    w_query,
    w_key,
    w_value,
    w_out,
    gain_attn,
    w_gate,
    w_up,
    w_down,
    gain_mlp,
    doc_ends,
    cotangent,
):
    rows, width = mixed_in.shape
    nz = w_query.shape[1] // HD
    ring = n_seq // nz
    bits = n_seq.bit_length() - 1
    low_bits = ring.bit_length() - 1
    units = w_gate.shape[1]
    half_units = units // 2
    half_rows = rows // 2
    group = width // n_seq
    pair_bit = bits - 2
    pair = 1 << pair_bit

    s = lax.axis_index("seq")
    m = lax.axis_index("mp")
    z, r = s // ring, s % ring
    core = m % 2
    side = m // 2
    low = (s >> pair_bit) & 1

    def seq_swap(v, distance):
        return lax.ppermute(v, "seq", [(i, i ^ distance) for i in range(n_seq)])

    def mp_swap(v, distance):
        return lax.ppermute(v, "mp", [(i, i ^ distance) for i in range(n_mp)])

    sum_bits = list(range(pair_bit)) + [bits - 1]
    places = []
    for p in range(n_seq):
        e = 0
        for at, bit in enumerate(sum_bits + [pair_bit]):
            if (p >> (bits - 1 - at)) & 1:
                e |= 1 << bit
        places.append(e)
    order = s ^ jnp.array(places, dtype=jnp.int32)

    ORDER.clear()

    place = jnp.stack([z, r, m, low]).astype(jnp.int32)
    blocks = (z ^ jnp.arange(nz, dtype=jnp.int32)) * ring + r
    token_index = blocks[:, None] * rows + jnp.arange(rows, dtype=jnp.int32)[None, :]
    ends_below = doc_ends[None, None, :] <= token_index[..., None]
    begin = jnp.max(jnp.where(ends_below, doc_ends, 0), axis=-1)
    cos_own, sin_own = rope_tables(token_index[0] - begin[0])
    cos_all, sin_all = rope_tables(token_index - begin)
    weights = [w_query, w_key, w_value]
    half_z = nz // 2
    made = project_qkv(
        place,
        mixed_in,
        gain_attn.reshape(1, width),
        weights,
        cos_own,
        sin_own,
        list(range(half_z, nz)),
    )
    normed = made[-1]
    pieces = {half_z + i: made[i] for i in range(half_z)}
    made = project_qkv(place, normed, None, weights, cos_own, sin_own, list(range(half_z)))
    pieces.update({i: made[i] for i in range(half_z)})
    pieces = [pieces[0]] + [seq_swap(pieces[d], d * ring) for d in range(1, nz)]
    near = pieces
    keys_values = [near, [seq_swap(piece[:, HD:], 1) for piece in pieces]]
    for b in range(1, low_bits):
        keys_values = keys_values + [
            [seq_swap(kv[:, -2 * HD :], 1 << b) for kv in kvs] for kvs in keys_values
        ]
    queries = pieces

    quarter = rows // n_mp
    my_quarter = lax.dynamic_slice_in_dim(normed, m * quarter, quarter, 0)
    halves = [
        lax.dynamic_slice_in_dim(w_down, low * half_units, half_units, 0),
        lax.dynamic_slice_in_dim(w_gate, low * half_units, half_units, 1),
        lax.dynamic_slice_in_dim(w_up, low * half_units, half_units, 1),
    ]
    cot_half = lax.dynamic_slice_in_dim(cotangent, core * half_rows, half_rows, 0)

    flat = [kv for kvs in keys_values for kv in kvs]
    far = [kv for kvs in keys_values[1:] for kv in kvs]
    cot_half, *halves = hold([cot_half, *halves], after=pieces)
    cot_pair = seq_swap(cot_half, pair)
    outs = attend(place, doc_ends, queries, flat, nz, ring, after=[cos_all, sin_all])
    heads = [outs[0]] + [seq_swap(outs[d], d * ring) for d in range(1, nz)]

    size = half_rows // CHUNKS
    last_low = 1 << sum_bits[pair_bit - 1]
    high = 1 << sum_bits[pair_bit]
    gain_mlp_row = gain_mlp.reshape(1, width)
    gain_attn_row = gain_attn.reshape(1, width)

    def chunks_of(values):
        return [values[i * size : (i + 1) * size] for i in range(CHUNKS)]

    def low_sums(sent, kept):
        for bit in sum_bits[: pair_bit - 1]:
            kept, sent = merge(kept, seq_swap(sent, 1 << bit))
        return kept, seq_swap(sent, last_low)

    x_chunks = chunks_of(lax.dynamic_slice_in_dim(mixed_in, core * half_rows, half_rows, 0))
    cot_chunks = chunks_of(cot_half)
    cot_all = cot_chunks + chunks_of(cot_pair)
    spots = jnp.concatenate(
        [core * CHUNKS + jnp.arange(CHUNKS), (1 - core) * CHUNKS + jnp.arange(CHUNKS)]
    ).astype(jnp.int32)
    v = types.SimpleNamespace(
        residual=[None] * CHUNKS,
        normed=[None] * (2 * CHUNKS),
        back=[None] * CHUNKS,
        back_across=[None] * CHUNKS,
        residual_grad=[None] * CHUNKS,
        branch=[None] * CHUNKS,
        branch_sib=[None] * CHUNKS,
        gain_mlp=[None] * CHUNKS,
        gain_attn=[None] * CHUNKS,
        grad_rows=[None] * CHUNKS,
        grad_sib=[None] * CHUNKS,
        quarters={0: my_quarter},
        out_grads=(),
    )
    def heads_out():
        sib, v.mine, v.heads_placed = heads_project(
            place, heads, [w_out], nn, True, after=[cot_pair]
        )
        v.sib = mp_swap(sib, 1)

    def out_sum():
        v.parts = row_sum(v.mine, v.sib, CHUNKS)
        v.across = [mp_swap(part, 2) for part in v.parts]

    def swap_weights():
        v.down_sib, v.gate_sib, v.up_sib = [mp_swap(half, 1) for half in hold(halves)]

    def dact_own():
        v.dact = hidden_upstream(place, cot_all, w_down, True)

    def dact_sib():
        v.dact_sib = hidden_upstream(place, cot_all, v.down_sib, False)

    def norm_chunk(i):
        v.residual[i], v.normed[i] = norm_rows(
            v.parts[i], v.across[i], x_chunks[i], gain_mlp_row
        )
        v.normed[CHUNKS + i] = seq_swap(v.normed[i], pair)

    def turn_cot():
        v.cot_turned = turn(order, group, cot_all)

    def swap_cot():
        (turned,) = hold([v.cot_turned])
        v.cot_both = [turned, mp_swap(turned, 1)]

    def hidden_sib():
        v.act_sib, dg_sib, du_sib = hidden(
            place, v.normed, v.gate_sib, v.up_sib, v.dact_sib, False
        )
        v.act_got = mp_swap(v.act_sib, 1)
        v.dg_sib, v.du_sib = dg_sib, du_sib

    def swap_dg():
        (part,) = hold([v.dg_sib])
        v.dg_got = mp_swap(part, 1)

    def swap_du():
        (part,) = hold([v.du_sib])
        v.du_got = mp_swap(part, 1)

    def hidden_own():
        v.act, v.dg, v.du = hidden(place, v.normed, w_gate, w_up, v.dact, True)

    def turn_normed():
        v.normed_turned = turn(order, group, v.normed)

    def swap_normed():
        (turned,) = hold([v.normed_turned])
        v.normed_both = [turned, mp_swap(turned, 1)]

    def grad_down():
        v.sent_down, v.part_down = weight_grad(v.cot_both, [v.act, v.act_got])

    def send_down():
        (sent,) = hold([v.sent_down])
        v.low_down = low_sums(sent, v.part_down)

    def hidden_in():
        v.made = hidden_back(
            place,
            v.dg,
            v.dg_sib,
            v.du,
            v.du_sib,
            w_gate,
            v.gate_sib,
            w_up,
            v.up_sib,
            2 * CHUNKS,
        )
        v.made_got = [seq_swap(v.made[CHUNKS + i], pair) for i in range(CHUNKS)]

    def back_chunk(i):
        (v.back[i],) = row_sum(v.made[i], v.made_got[i], 1)
        v.back_across[i] = mp_swap(v.back[i], 2)

    def norm_back_chunk(i):
        v.residual_grad[i], v.branch[i], v.gain_mlp[i] = norm_back(
            v.back[i], v.back_across[i], v.residual[i], cot_chunks[i], gain_mlp_row, (F32, BF16)
        )
        v.branch_sib[i] = mp_swap(v.branch[i], 1)

    def grad_gate():
        v.sent_gate, v.part_gate = weight_grad(v.normed_both, [v.dg, v.dg_got])

    def send_gate():
        (sent,) = hold([v.sent_gate])
        v.low_gate = low_sums(sent, v.part_gate)

    def grad_up():
        v.sent_up, v.part_up = weight_grad(v.normed_both, [v.du, v.du_got])

    def send_up():
        (sent,) = hold([v.sent_up])
        v.low_up = low_sums(sent, v.part_up)

    def merge_down():
        v.kept_down, v.high_down = merge(*v.low_down)

    def high_down():
        (sent,) = hold([v.high_down], after=v.out_grads)
        v.come_down = seq_swap(sent, high)

    def merge_gate():
        v.kept_gate, v.high_gate = merge(*v.low_gate)

    def high_gate():
        (sent,) = hold([v.high_gate])
        v.come_gate = seq_swap(sent, high)

    def merge_up():
        v.kept_up, v.high_up = merge(*v.low_up)

    def high_up():
        (sent,) = hold([v.high_up])
        v.come_up = seq_swap(sent, high)

    def sum_down():
        v.own_down, v.pair_down = final_sum([v.kept_down, v.come_down])

    def sum_gate():
        v.own_gate, v.pair_gate = final_sum([v.kept_gate, v.come_gate])

    def sum_up():
        v.own_up, v.pair_up = final_sum([v.kept_up, v.come_up])

    def pair_down():
        (sent,) = hold([v.pair_down])
        v.theirs_down = seq_swap(sent, pair)

    def pair_gate():
        (sent,) = hold([v.pair_gate])
        v.theirs_gate = seq_swap(sent, pair)

    def pair_up():
        (sent,) = hold([v.pair_up])
        v.theirs_up = seq_swap(sent, pair)

    def lay_down():
        v.down_share = lay(place, v.own_down, v.theirs_down, True)

    def lay_gate():
        v.gate_share = lay(place, v.own_gate, v.theirs_gate, False)

    def lay_up():
        v.up_share = lay(place, v.own_up, v.theirs_up, False)

    def gather_z(d):
        (part,) = hold([v.quarters[d & (d - 1)]])
        v.quarters[d] = seq_swap(part, ring * (d & -d))

    def gather_x():
        v.rows = stack_rows([v.quarters[d] for d in range(1, nz)])
        v.rows_x = mp_swap(v.rows, 2)

    def gather_core():
        v.rows_core = [mp_swap(part, 1) for part in hold([v.rows, v.rows_x])]

    def heads_in():
        made = heads_upstream(place, v.branch, v.branch_sib, w_out, nz)
        v.out_grads = [made[0]] + [seq_swap(made[d], d * ring) for d in range(1, nz)]

    def attend_far():
        v.dq_far, *summed = attend_back(
            place, doc_ends, queries, v.out_grads, far, None, nz, ring, 1, ring - 1, BF16
        )
        summed = [None] + summed
        for b in reversed(range(low_bits)):
            bit = 1 << b
            for e in range(bit):
                got = seq_swap(summed[e | bit], bit)
                summed[e] = (
                    got
                    if summed[e] is None
                    else (summed[e].astype(F32) + got.astype(F32)).astype(BF16)
                )
        v.dkv_got = summed[0]

    def attend_near():
        v.dq, v.dkv = attend_back(
            place, doc_ends, queries, v.out_grads, near, v.dq_far, nz, ring, 0, 1, F32
        )

    def head_grads():
        v.grads = finish_grads(v.dq, v.dkv, v.dkv_got, cos_all, sin_all)
        v.own_grads = [v.grads[0]] + [
            seq_swap(v.grads[d], d * ring) for d in range(1, nz)
        ]

    def turn_branch():
        v.branch_turned = turn(order, group, v.branch + v.branch_sib, spots)

    def grad_out():
        v.sent_out, v.part_out = weight_grad([v.branch_turned], [v.heads_placed])

    def send_out():
        (sent,) = hold([v.sent_out])
        v.low_out = low_sums(sent, v.part_out)

    def merge_out():
        v.kept_out, v.high_out = merge(*v.low_out)

    def high_out():
        (sent,) = hold([v.high_out])
        v.come_out = seq_swap(sent, high)

    def sum_out():
        v.own_out, sent = final_sum([v.kept_out, v.come_out])
        v.pair_out = seq_swap(sent, pair)

    def turn_rows():
        v.all_turned = turn_all(
            order, group, normed, [v.rows, v.rows_core[0], v.rows_x, v.rows_core[1]], m
        )

    def grad_qkv():
        v.sent_qkv, v.part_qkv = weight_grad(
            [v.all_turned], [jnp.concatenate(v.grads, axis=0)]
        )

    def send_qkv():
        (sent,) = hold([v.sent_qkv])
        v.low_qkv = low_sums(sent, v.part_qkv)

    def split_qkv():
        own, *sent = split_sum(*v.low_qkv, nz)
        v.qkv_heads = [own] + [seq_swap(sent[d - 1], d * ring) for d in range(1, nz)]

    def lay_qkv():
        v.shares = place_heads(place, v.qkv_heads)

    def rows_in():
        sib, v.in_mine = heads_project(place, v.own_grads, weights, nt, False)
        v.in_sib = mp_swap(sib, 1)

    def in_sum():
        v.in_parts = row_sum(v.in_mine, v.in_sib, CHUNKS)
        v.in_across = [mp_swap(part, 2) for part in v.in_parts]

    def norm_in_chunk(i):
        v.grad_rows[i], v.gain_attn[i] = norm_back(
            v.in_parts[i], v.in_across[i], x_chunks[i], v.residual_grad[i], gain_attn_row, (BF16,)
        )
        v.grad_sib[i] = mp_swap(v.grad_rows[i], 1)

    def join_in():
        v.input_grad = join_rows(place, v.grad_rows, v.grad_sib)

    def down_rows():
        v.down_mine, v.down_theirs = down(place, v.act, v.act_sib, w_down, v.down_sib, 2)

    def pair_rows():
        (sent,) = hold([v.down_theirs])
        v.down_got = seq_swap(sent, pair)

    def sum_rows():
        (v.down_part,) = row_sum(v.down_mine, v.down_got, 1)
        v.down_across = mp_swap(v.down_part, 2)

    def add_out():
        v.out_rows = add_rows(
            v.down_part, v.down_across, jnp.concatenate(v.residual, axis=0)
        )
        v.out_sib = mp_swap(v.out_rows, 1)

    def join_out():
        v.mixed_out = join_rows(place, [v.out_rows], [v.out_sib])

    def gains_core():
        (v.gains,) = hold([jnp.concatenate([sum(v.gain_attn), sum(v.gain_mlp)])])
        v.gains = v.gains + mp_swap(v.gains, 1)

    def gains_seq(bit):
        (v.gains,) = hold([v.gains])
        v.gains = v.gains + seq_swap(v.gains, 1 << bit)

    loose(heads_out)
    dact_own()
    gather_z(1)
    out_sum()
    swap_weights()
    norm_chunk(1)
    dact_sib()
    norm_chunk(0)
    turn_cot()
    swap_cot()
    gather_z(2)
    hidden_sib()
    swap_dg()
    hidden_own()
    swap_du()
    turn_normed()
    swap_normed()
    grad_down()
    hidden_in()
    send_down()
    grad_gate()
    gather_z(3)
    back_chunk(1)
    back_chunk(0)
    send_gate()
    gather_x()
    norm_back_chunk(1)
    norm_back_chunk(0)
    heads_in()
    merge_down()
    turn_branch()
    high_down()
    attend_far()
    grad_up()
    send_up()
    gather_core()
    merge_gate()
    attend_near()
    high_gate()
    sum_down()
    head_grads()
    pair_down()
    rows_in()
    merge_up()
    grad_out()
    loose(high_up)
    in_sum()
    down_rows()
    pair_rows()
    norm_in_chunk(0)
    send_out()
    turn_rows()
    lay_down()
    grad_qkv()
    merge_out()
    high_out()
    norm_in_chunk(1)
    send_qkv()
    sum_gate()
    gains_core()
    gains_seq(0)
    loose(pair_gate)
    sum_rows()
    join_in()
    gains_seq(2)
    split_qkv()
    sum_up()
    pair_up()
    sum_out()
    lay_gate()
    loose(add_out)
    lay_up()
    gains_seq(1)
    join_out()
    lay_qkv()
    for bit in range(3, bits):
        gains_seq(bit)
    gains = lax.dynamic_slice_in_dim(v.gains, s * group, group, 1)

    return (
        v.mixed_out,
        v.input_grad,
        *v.shares,
        (v.own_out + v.pair_out.astype(F32)).T,
        gains[0],
        v.gate_share,
        v.up_share,
        v.down_share,
        gains[1],
    )


def solution(mesh):
    placed = (
        P("seq", None),
        P(None, "mp"),
        P(None, "mp"),
        P(None, "mp"),
        P("mp", None),
        P(),
        P(None, "mp"),
        P(None, "mp"),
        P("mp", None),
        P(),
        P(),
        P("seq", None),
    )
    return jax.shard_map(
        functools.partial(layer, mesh.shape["seq"], mesh.shape["mp"]),
        mesh=mesh,
        in_specs=placed,
        out_specs=(
            P("seq", None),
            P("seq", None),
            P("seq", "mp"),
            P("seq", "mp"),
            P("seq", "mp"),
            P("mp", "seq"),
            P("seq"),
            P("seq", "mp"),
            P("seq", "mp"),
            P("mp", "seq"),
            P("seq"),
        ),
        check_vma=False,
    )
```

```python
import functools
import math
import types

import jax
import jax.numpy as jnp
from jax import lax
from jax.experimental import pallas as pl
from jax.experimental.pallas import tpu as pltpu
from jax.sharding import PartitionSpec as P

HD = 128
EPSILON = 1e-05
THETA = 10000.0
FACTOR = 1.0 / math.sqrt(HD)
CLAMP = 80.0
CHUNKS = 2
SHARE = 0.5
ORDER = []
LOOSE = [False]
MIB = 1024 * 1024
F32 = jnp.float32
BF16 = jnp.bfloat16


def nn(left, right):
    return lax.dot_general(left, right, (((1,), (0,)), ((), ())), preferred_element_type=F32)


def nt(left, right):
    return lax.dot_general(left, right, (((1,), (1,)), ((), ())), preferred_element_type=F32)


def tn(left, right):
    return lax.dot_general(left, right, (((0,), (0,)), ((), ())), preferred_element_type=F32)


def call(
    body,
    out_shape,
    operands,
    in_specs,
    flops,
    moved,
    transcendentals=0,
    after=(),
    prefetch=0,
    chain=True,
    vmem=20,
    **kwargs,
):
    n = prefetch + len(in_specs)
    chain = chain and not LOOSE[0]
    after = list(after) + (ORDER if chain else [])

    def kernel(*refs):
        body(*refs[:n], *refs[n + len(after) :])

    in_specs = list(in_specs) + [pl.BlockSpec(memory_space=pl.ANY)] * len(after)
    if prefetch:
        kwargs = {
            "name": kwargs.pop("name"),
            "grid_spec": pltpu.PrefetchScalarGridSpec(
                num_scalar_prefetch=prefetch, in_specs=in_specs, **kwargs
            ),
        }
    else:
        kwargs["in_specs"] = in_specs
    made = pl.pallas_call(
        kernel,
        out_shape=out_shape,
        compiler_params=pltpu.CompilerParams(vmem_limit_bytes=vmem * MIB),
        cost_estimate=pl.CostEstimate(
            flops=int(flops / SHARE),
            bytes_accessed=int(moved / SHARE),
            transcendentals=int(transcendentals / SHARE),
        ),
        **kwargs,
    )(*operands, *after)
    if chain:
        ORDER[:] = [made[0] if isinstance(made, (tuple, list)) else made]
    return made


def hold(values, after=()):
    n = len(values)
    if LOOSE[0]:
        return list(lax.optimization_barrier((*values, *after))[:n])
    made = lax.optimization_barrier((*values, *ORDER, *after))
    ORDER[:] = made[n : n + len(ORDER)]
    return list(made[:n])


def loose(step, *args):
    LOOSE[0] = True
    step(*args)
    LOOSE[0] = False


def whole(memory):
    return pl.BlockSpec(memory_space=memory)


def rotated(values, cosine, signed):
    return values * cosine + pltpu.roll(values, HD // 2, 1) * signed


def unrotated(values, cosine, signed):
    return values * cosine - pltpu.roll(values, HD // 2, 1) * signed


def qkv_body(n, fresh, place_ref, *refs):
    if fresh:
        x_ref, gain_ref, refs = refs[0], refs[1], refs[2:]
    else:
        x_ref, refs = refs[0], refs[1:]
    wq_ref, wk_ref, wv_ref, cos_ref, sin_ref = refs[:5]
    outs, (w_s, x_s) = refs[5 : 5 + n], refs[-2:]
    step = pl.program_id(0)

    @pl.when(step == 0)
    def _():
        if fresh:
            x = x_ref[...].astype(F32)
            x_s[...] = (x * scale_of(x) * gain_ref[...]).astype(BF16)
            refs[5 + n][...] = x_s[...]
        else:
            x_s[...] = x_ref[...]

    w_s[:, :HD] = wq_ref[...]
    w_s[:, HD : 2 * HD] = wk_ref[...]
    w_s[:, 2 * HD :] = wv_ref[...]
    made = nn(x_s[...], w_s[...])
    cosine = cos_ref[...]
    signed = sin_ref[...]
    query = rotated(made[:, :HD], cosine, signed).astype(BF16)
    key = rotated(made[:, HD : 2 * HD], cosine, signed).astype(BF16)
    value = made[:, 2 * HD :].astype(BF16)
    for i in range(n):

        @pl.when(step == i)
        def _(i=i):
            outs[i][:, :HD] = query
            outs[i][:, HD : 2 * HD] = key
            outs[i][:, 2 * HD :] = value


def project_qkv(place, x, gain, weights, cosine, signed, spots):
    n = len(spots)
    rows, width = x.shape
    fresh = gain is not None
    fixed = pl.BlockSpec((rows, width), lambda i, place: (0, 0))
    table = pl.BlockSpec((rows, HD), lambda i, place: (0, 0))
    first = spots[0]
    assert list(spots) == [first ^ i for i in range(n)]
    weight = pl.BlockSpec((width, HD), lambda i, place: (0, place[0] ^ first ^ i))
    piece = jax.ShapeDtypeStruct((rows, 3 * HD), BF16)
    return call(
        functools.partial(qkv_body, n, fresh),
        (piece,) * n + ((jax.ShapeDtypeStruct(x.shape, BF16),) if fresh else ()),
        [place, x] + ([gain] if fresh else []) + [*weights, cosine, signed],
        [fixed]
        + ([pl.BlockSpec((1, width), lambda i, place: (0, 0))] if fresh else [])
        + [weight] * 3
        + [table] * 2,
        6 * n * rows * width * HD,
        4 * rows * width + 6 * n * width * HD + 6 * n * rows * HD,
        prefetch=1,
        grid=(n,),
        out_specs=(pl.BlockSpec((rows, 3 * HD), lambda i, place: (0, 0)),) * n
        + ((fixed,) if fresh else ()),
        scratch_shapes=[pltpu.VMEM((width, 3 * HD), BF16), pltpu.VMEM((rows, width), BF16)],
        vmem=60,
        name="project_qkv",
    )


def begin_of(index, ends_ref, count):
    begin = jnp.zeros_like(index)
    for e in range(count):
        end = ends_ref[e]
        begin = jnp.where(end <= index, jnp.maximum(begin, end), begin)
    return begin


def finish_of(index, ends_ref, count):
    finish = jnp.zeros_like(index) + ends_ref[count - 1]
    for e in range(count):
        end = ends_ref[e]
        finish = jnp.where(end > index, jnp.minimum(finish, end), finish)
    return finish


def attend_body(nz, ring, count, place_ref, ends_ref, *refs):
    n_kv = nz * ring
    q_refs, refs = refs[:nz], refs[nz:]
    kv_refs, refs = refs[:n_kv], refs[n_kv:]
    o_refs, refs = refs[:nz], refs[nz:]
    q_s, k_s, v_s, o_s, acc = refs
    z, r = place_ref[0], place_ref[1]
    rows = q_s.shape[1]
    for d in range(nz):
        q_s[d] = q_refs[d][:, :HD]
    for i in range(n_kv):
        first = kv_refs[i].shape[1] - 2 * HD
        k_s[i] = kv_refs[i][:, first : first + HD]
        v_s[i] = kv_refs[i][:, first + HD :]

    @pl.loop(0, nz)
    def per_query(d):
        q_block = (z ^ d) * ring + r
        q_start = q_block * rows
        q_index = q_start + lax.broadcasted_iota(jnp.int32, (rows, 1), 0)
        begin = begin_of(q_index, ends_ref, count)
        shift = jnp.log((finish_of(q_index, ends_ref, count) - begin).astype(F32))
        first_begin = begin_of(q_start, ends_ref, count)
        last_begin = begin_of(q_start + (rows - 1), ends_ref, count)
        acc[...] = jnp.zeros_like(acc)

        @pl.loop(0, n_kv)
        def per_key(i):
            k_block = (z ^ (i & (nz - 1))) * ring + (r ^ (i // nz))
            k_start = k_block * rows
            needed = (k_block <= q_block) & (k_start + rows > first_begin)
            full = (k_block < q_block) & (k_start >= last_begin)

            def tile(masked):
                half = rows // 2
                for part in range(2):
                    at = slice(part * half, (part + 1) * half)
                    scores = nt(q_s[d, at], k_s[i])
                    grown = jnp.exp(jnp.minimum(shift[at] - scores * FACTOR, CLAMP))
                    probs = pl.reciprocal(1.0 + grown, approx=True)
                    if masked:
                        k_index = k_start + lax.broadcasted_iota(jnp.int32, (1, rows), 1)
                        allowed = (k_index <= q_index[at]) & (k_index >= begin[at])
                        probs = jnp.where(allowed, probs, 0.0)
                    acc[at] += nn(probs.astype(BF16), v_s[i])

            pl.when(needed & full)(functools.partial(tile, False))
            pl.when(needed & jnp.logical_not(full))(functools.partial(tile, True))

        o_s[d] = acc[...].astype(BF16)

    for d in range(nz):
        o_refs[d][...] = o_s[d]


def attend(place, ends, queries, keys_values, nz, ring, after=()):
    rows = queries[0].shape[0]
    n_kv = nz * ring
    pairs = nz * n_kv / 2
    return call(
        functools.partial(attend_body, nz, ring, ends.shape[0]),
        tuple(jax.ShapeDtypeStruct((rows, HD), BF16) for _ in range(nz)),
        [place, ends, *queries, *keys_values],
        [whole(pltpu.SMEM)] * 2 + [whole(pltpu.VMEM)] * (nz + n_kv),
        pairs * 4 * rows * rows * HD * 2,
        2 * (2 * nz + 2 * n_kv) * rows * HD,
        pairs * 2 * rows * rows,
        after=after,
        out_specs=tuple(whole(pltpu.VMEM) for _ in range(nz)),
        scratch_shapes=[
            pltpu.VMEM((nz, rows, HD), BF16),
            pltpu.VMEM((n_kv, rows, HD), BF16),
            pltpu.VMEM((n_kv, rows, HD), BF16),
            pltpu.VMEM((nz, rows, HD), BF16),
            pltpu.VMEM((rows, HD), F32),
        ],
        vmem=12 + 2 * n_kv * rows * HD * 8 // MIB,
        name="attend",
    )


def attend_back_body(nz, ring, n_dr, first_dr, chained, count, place_ref, ends_ref, *refs):
    n_kv = nz * n_dr
    q_refs, refs = refs[:nz], refs[nz:]
    do_refs, refs = refs[:nz], refs[nz:]
    kv_refs, refs = refs[:n_kv], refs[n_kv:]
    if chained:
        before_ref, refs = refs[0], refs[1:]
    dq_ref, refs = refs[0], refs[1:]
    dkv_refs, refs = refs[:n_dr], refs[n_dr:]
    q_s, do_s, k_s, v_s, begin_s, shift_s, dkv_s, dk_acc, dv_acc = refs
    z, r = place_ref[0], place_ref[1]
    rows = q_s.shape[1]
    for d in range(nz):
        q_s[d] = q_refs[d][:, :HD]
        do_s[d] = do_refs[d][...]
    for i in range(n_kv):
        first = kv_refs[i].shape[1] - 2 * HD
        k_s[i] = kv_refs[i][:, first : first + HD]
        v_s[i] = kv_refs[i][:, first + HD :]
    if chained:
        dq_ref[...] = before_ref[...]
    else:
        dq_ref[...] = jnp.zeros_like(dq_ref)

    @pl.loop(0, nz)
    def tables(d):
        q_index = ((z ^ d) * ring + r) * rows + lax.broadcasted_iota(jnp.int32, (1, rows), 1)
        begin = begin_of(q_index, ends_ref, count)
        begin_s[d] = begin
        shift_s[d] = jnp.log((finish_of(q_index, ends_ref, count) - begin).astype(F32))

    @pl.loop(0, n_kv)
    def per_key(i):
        k_block = (z ^ (i & (nz - 1))) * ring + (r ^ (first_dr + i // nz))
        k_start = k_block * rows
        dk_acc[...] = jnp.zeros_like(dk_acc)
        dv_acc[...] = jnp.zeros_like(dv_acc)

        @pl.loop(0, nz)
        def per_query(d):
            q_block = (z ^ d) * ring + r
            q_start = q_block * rows
            first_begin = begin_of(q_start, ends_ref, count)
            last_begin = begin_of(q_start + (rows - 1), ends_ref, count)
            needed = (k_block <= q_block) & (k_start + rows > first_begin)
            full = (k_block < q_block) & (k_start >= last_begin)

            def tile(masked):
                half = rows // 2
                for part in range(2):
                    at = slice(part * half, (part + 1) * half)
                    keys = k_s[i, at]
                    scores = nt(keys, q_s[d])
                    grown = jnp.exp(jnp.minimum(shift_s[d] - scores * FACTOR, CLAMP))
                    probs = pl.reciprocal(1.0 + grown, approx=True)
                    if masked:
                        k_index = (
                            k_start
                            + part * half
                            + lax.broadcasted_iota(jnp.int32, (half, 1), 0)
                        )
                        q_index = q_start + lax.broadcasted_iota(jnp.int32, (1, rows), 1)
                        allowed = (k_index <= q_index) & (k_index >= begin_s[d])
                        probs = jnp.where(allowed, probs, 0.0)
                    weight_grad = nt(v_s[i, at], do_s[d])
                    score_grad = (weight_grad * (probs * probs * grown)).astype(BF16)
                    dv_acc[at] += nn(probs.astype(BF16), do_s[d])
                    dk_acc[at] += nn(score_grad, q_s[d])
                    dq_ref[d] += tn(score_grad, keys)

            pl.when(needed & full)(functools.partial(tile, False))
            pl.when(needed & jnp.logical_not(full))(functools.partial(tile, True))

        dkv_s[i, :, :HD] = (dk_acc[...] * FACTOR).astype(dkv_s.dtype)
        dkv_s[i, :, HD:] = dv_acc[...].astype(dkv_s.dtype)

    for e in range(n_dr):
        for d in range(nz):
            dkv_refs[e][d] = dkv_s[e * nz + d]


def attend_back(
    place, ends, queries, out_grads, keys_values, before, nz, ring, first_dr, n_dr, kept, after=()
):
    rows = queries[0].shape[0]
    n_kv = nz * n_dr
    pairs = nz * n_kv / 2
    chained = before is not None
    return call(
        functools.partial(
            attend_back_body, nz, ring, n_dr, first_dr, chained, ends.shape[0]
        ),
        (jax.ShapeDtypeStruct((nz, rows, HD), F32),)
        + tuple(jax.ShapeDtypeStruct((nz, rows, 2 * HD), kept) for _ in range(n_dr)),
        [place, ends, *queries, *out_grads, *keys_values, *([before] if chained else [])],
        [whole(pltpu.SMEM)] * 2 + [whole(pltpu.VMEM)] * (2 * nz + n_kv + chained),
        pairs * 10 * rows * rows * HD * 2,
        2 * (2 * nz + 4 * n_kv) * rows * HD,
        pairs * 2 * rows * rows,
        after=after,
        out_specs=tuple(whole(pltpu.VMEM) for _ in range(1 + n_dr)),
        scratch_shapes=[
            pltpu.VMEM((nz, rows, HD), BF16),
            pltpu.VMEM((nz, rows, HD), BF16),
            pltpu.VMEM((n_kv, rows, HD), BF16),
            pltpu.VMEM((n_kv, rows, HD), BF16),
            pltpu.VMEM((nz, 1, rows), jnp.int32),
            pltpu.VMEM((nz, 1, rows), F32),
            pltpu.VMEM((n_kv, rows, 2 * HD), kept),
            pltpu.VMEM((rows, HD), F32),
            pltpu.VMEM((rows, HD), F32),
        ],
        vmem=16 + 2 * n_kv * rows * HD * 14 // MIB,
        name="attend_back",
    )


def finish_body(nz, dq_ref, dkv_ref, got_ref, cos_ref, sin_ref, *out_refs):
    for d in range(nz):
        cosine = cos_ref[d]
        signed = sin_ref[d]
        total = dkv_ref[d] + got_ref[d].astype(F32)
        out = out_refs[d]
        out[:, :HD] = unrotated(dq_ref[d] * FACTOR, cosine, signed).astype(BF16)
        out[:, HD : 2 * HD] = unrotated(total[:, :HD], cosine, signed).astype(BF16)
        out[:, 2 * HD :] = total[:, HD:].astype(BF16)


def finish_grads(dq, dkv, got, cosine, signed):
    nz, rows, _ = dq.shape
    return call(
        functools.partial(finish_body, nz),
        tuple(jax.ShapeDtypeStruct((rows, 3 * HD), BF16) for _ in range(nz)),
        [dq, dkv, got, cosine, signed],
        [whole(pltpu.VMEM)] * 5,
        12 * nz * rows * HD,
        nz * rows * HD * 30,
        out_specs=tuple(whole(pltpu.VMEM) for _ in range(nz)),
        name="finish_grads",
    )


def rows_at(place, width, height, tile_of):
    return pl.BlockSpec((height, width), lambda j, place: (tile_of(place), 0))


def place_rows(pieces, scratch, spot):
    size = pieces[0].shape[0]
    half = size * len(pieces)
    for i, piece in enumerate(pieces):
        at = pl.multiple_of(spot * half + i * size, size)
        scratch[pl.ds(at, size), :] = piece[...]


def upstream_body(place_ref, *refs):
    pieces, (w_ref, out_ref, x_s) = refs[:-3], refs[-3:]
    size = pieces[0].shape[0]

    @pl.when(pl.program_id(0) == 0)
    def _():
        for i, piece in enumerate(pieces):
            x_s[i * size : (i + 1) * size] = piece[...]

    out_ref[...] = nt(x_s[...], w_ref[...]).astype(BF16)


def hidden_upstream(place, pieces, weights, own, after=()):
    size, width = pieces[0].shape
    rows = size * len(pieces)
    units = weights.shape[0] // (2 if own else 1)
    tile = 512
    steps = units // tile
    first = (lambda place: place[3] * steps) if own else (lambda place: 0)
    return call(
        upstream_body,
        jax.ShapeDtypeStruct((rows, units), BF16),
        [place, *pieces, weights],
        [pl.BlockSpec((size, width), lambda j, place: (0, 0))] * len(pieces)
        + [pl.BlockSpec((tile, width), lambda j, place: (first(place) + j, 0))],
        2 * rows * width * units,
        2 * width * units + 4 * rows * units + 2 * rows * width,
        after=after,
        prefetch=1,
        grid=(steps,),
        out_specs=pl.BlockSpec((rows, tile), lambda j, place: (0, j)),
        scratch_shapes=[pltpu.VMEM((rows, width), BF16)],
        vmem=52,
        name="hidden_upstream",
    )


def hidden_body(place_ref, *refs):
    pieces, refs = refs[:-7], refs[-7:]
    wg_ref, wu_ref, dact_ref, act_ref, dg_ref, du_ref, x_s = refs
    size = pieces[0].shape[0]

    @pl.when(pl.program_id(0) == 0)
    def _():
        for i, piece in enumerate(pieces):
            x_s[i * size : (i + 1) * size] = piece[...]

    x = x_s[...]
    for first in range(0, act_ref.shape[1], 256):
        at = slice(first, first + 256)
        gate = nn(x, wg_ref[:, at])
        up = nn(x, wu_ref[:, at])
        dact = dact_ref[:, at].astype(F32)
        sig = jax.nn.sigmoid(gate)
        silu = gate * sig
        act_ref[:, at] = (silu * up).astype(BF16)
        dg_ref[:, at] = (dact * up * sig * (1.0 + gate * (1.0 - sig))).astype(BF16)
        du_ref[:, at] = (dact * silu).astype(BF16)


def hidden(place, pieces, w_gate, w_up, dact, own, after=()):
    size, width = pieces[0].shape
    rows = size * len(pieces)
    units = dact.shape[1]
    tile = 512
    steps = units // tile
    first = (lambda place: place[3] * steps) if own else (lambda place: 0)
    made = jax.ShapeDtypeStruct((rows, units), BF16)
    block = pl.BlockSpec((rows, tile), lambda j, place: (0, j))
    weight = pl.BlockSpec((width, tile), lambda j, place: (0, first(place) + j))
    return call(
        hidden_body,
        (made, made, made),
        [place, *pieces, w_gate, w_up, dact],
        [pl.BlockSpec((size, width), lambda j, place: (0, 0))] * len(pieces)
        + [weight, weight, block],
        4 * rows * width * units,
        4 * width * units + 8 * rows * units + 2 * rows * width,
        rows * units,
        after=after,
        prefetch=1,
        grid=(steps,),
        out_specs=(block, block, block),
        scratch_shapes=[pltpu.VMEM((rows, width), BF16)],
        vmem=52,
        name="hidden",
    )


def chunked(total, out_refs):
    size = out_refs[0].shape[0]
    for i, ref in enumerate(out_refs):
        ref[...] = total[i * size : (i + 1) * size].astype(ref.dtype)


def back_body(place_ref, dg_ref, dg_sib, du_ref, du_sib, wg_ref, wg_sib, wu_ref, wu_sib, *outs):
    chunked(
        nt(dg_ref[...], wg_ref[...])
        + nt(dg_sib[...], wg_sib[...])
        + nt(du_ref[...], wu_ref[...])
        + nt(du_sib[...], wu_sib[...]),
        outs,
    )


def hidden_back(place, dg, dg_sib, du, du_sib, w_gate, gate_sib, w_up, up_sib, chunks, after=()):
    rows, half = dg.shape
    width = w_gate.shape[0]
    tile = 512
    size = rows // chunks
    left = pl.BlockSpec((rows, half), lambda j, place: (0, 0))
    own = pl.BlockSpec((tile, half), lambda j, place: (j, place[3]))
    sib = pl.BlockSpec((tile, half), lambda j, place: (j, 0))
    return call(
        back_body,
        tuple(jax.ShapeDtypeStruct((size, width), BF16) for _ in range(chunks)),
        [place, dg, dg_sib, du, du_sib, w_gate, gate_sib, w_up, up_sib],
        [left] * 4 + [own, sib, own, sib],
        8 * rows * width * half,
        8 * width * half + 8 * rows * half + 2 * rows * width,
        after=after,
        prefetch=1,
        grid=(width // tile,),
        out_specs=tuple(pl.BlockSpec((size, tile), lambda j, place: (0, j)) for _ in range(chunks)),
        vmem=52,
        name="hidden_back",
    )


def down_body(place_ref, act_ref, act_sib, wd_ref, wd_sib, *outs):
    chunked(nn(act_ref[...], wd_ref[...]) + nn(act_sib[...], wd_sib[...]), outs)


def down(place, act, act_sib, w_down, down_sib, chunks, after=()):
    rows, half = act.shape
    width = w_down.shape[1]
    tile = 512
    size = rows // chunks
    left = pl.BlockSpec((rows, half), lambda j, place: (0, 0))
    return call(
        down_body,
        tuple(jax.ShapeDtypeStruct((size, width), BF16) for _ in range(chunks)),
        [place, act, act_sib, w_down, down_sib],
        [
            left,
            left,
            pl.BlockSpec((half, tile), lambda j, place: (place[3], j)),
            pl.BlockSpec((half, tile), lambda j, place: (0, j)),
        ],
        4 * rows * width * half,
        4 * width * half + 4 * rows * half + 2 * rows * width,
        after=after,
        prefetch=1,
        grid=(width // tile,),
        out_specs=tuple(pl.BlockSpec((size, tile), lambda j, place: (0, j)) for _ in range(chunks)),
        vmem=52,
        name="down",
    )


def heads_body(nz, contract, keep, place_ref, *refs):
    n_w = 1 if keep else 3
    pieces, refs = refs[:nz], refs[nz:]
    w_refs, (sib_ref, mine_ref), refs = refs[:n_w], refs[n_w : n_w + 2], refs[n_w + 2 :]
    joined = refs[:n_w]
    for d in range(nz):
        at = pl.multiple_of((place_ref[0] ^ d) * HD, HD)
        for i in range(n_w):
            joined[i][:, pl.ds(at, HD)] = pieces[d][:, i * HD : (i + 1) * HD]
    half = sib_ref.shape[0]
    core = place_ref[2] & 1

    def rows_of(start):
        start = pl.multiple_of(start, half)
        total = contract(joined[0][pl.ds(start, half), :], w_refs[0][...])
        for i in range(1, n_w):
            total = total + contract(joined[i][pl.ds(start, half), :], w_refs[i][...])
        return total

    sib_ref[...] = rows_of((1 - core) * half).astype(BF16)
    mine_ref[...] = rows_of(core * half)


def heads_project(place, pieces, weights, contract, keep, after=()):
    nz = len(pieces)
    rows = pieces[0].shape[0]
    n_w = len(weights)
    width = weights[0].shape[1] if contract is nn else weights[0].shape[0]
    half = rows // 2
    joined = (rows, nz * HD)
    out = (
        jax.ShapeDtypeStruct((half, width), BF16),
        jax.ShapeDtypeStruct((half, width), F32),
    ) + ((jax.ShapeDtypeStruct(joined, BF16),) if keep else ())
    return call(
        functools.partial(heads_body, nz, contract, keep),
        out,
        [place, *pieces, *weights],
        [whole(pltpu.SMEM)] + [whole(pltpu.VMEM)] * (nz + n_w),
        2 * rows * width * nz * HD * n_w,
        2 * n_w * (width * nz * HD + rows * nz * HD) + 3 * rows * width,
        after=after,
        out_specs=tuple(whole(pltpu.VMEM) for _ in out),
        scratch_shapes=() if keep else (pltpu.VMEM(joined, BF16),) * n_w,
        vmem=24,
        name="heads_project",
    )


def dheads_body(nz, n, place_ref, *refs):
    mine, refs = refs[:n], refs[n:]
    sibs, refs = refs[:n], refs[n:]
    w_ref, outs, x_s = refs[0], refs[1:-1], refs[-1]
    core = place_ref[2] & 1
    place_rows(mine, x_s, core)
    place_rows(sibs, x_s, 1 - core)
    x = x_s[...]
    wide = outs[0].shape[1]
    for d in range(nz):
        at = pl.multiple_of((place_ref[0] ^ d) * wide, wide)
        outs[d][...] = nt(x, w_ref[pl.ds(at, wide), :]).astype(BF16)


def heads_upstream(place, mine, sibs, w_out, nz, after=()):
    n = len(mine)
    size, width = mine[0].shape
    rows = 2 * n * size
    wide = w_out.shape[0] // nz
    return call(
        functools.partial(dheads_body, nz, n),
        tuple(jax.ShapeDtypeStruct((rows, wide), BF16) for _ in range(nz)),
        [place, *mine, *sibs, w_out],
        [whole(pltpu.SMEM)] + [whole(pltpu.VMEM)] * (2 * n + 1),
        2 * rows * width * nz * wide,
        2 * width * nz * wide + 2 * rows * nz * wide + 2 * rows * width,
        after=after,
        out_specs=tuple(whole(pltpu.VMEM) for _ in range(nz)),
        scratch_shapes=[pltpu.VMEM((rows, width), BF16)],
        name="heads_upstream",
    )


def sum_body(mine_ref, got_ref, *outs):
    chunked(mine_ref[...].astype(F32) + got_ref[...].astype(F32), outs)


def row_sum(mine, got, chunks, after=()):
    rows, width = mine.shape
    size = rows // chunks
    return call(
        sum_body,
        tuple(jax.ShapeDtypeStruct((size, width), BF16) for _ in range(chunks)),
        [mine, got],
        [whole(pltpu.VMEM)] * 2,
        rows * width,
        8 * rows * width,
        after=after,
        out_specs=tuple(whole(pltpu.VMEM) for _ in range(chunks)),
        name="row_sum",
    )


def scale_of(values):
    return lax.rsqrt(jnp.mean(values * values, axis=-1, keepdims=True) + EPSILON)


def norm_body(part_ref, got_ref, x_ref, gain_ref, res_ref, normed_ref):
    residual = x_ref[...].astype(F32) + (part_ref[...].astype(F32) + got_ref[...].astype(F32))
    res_ref[...] = residual
    normed_ref[...] = (residual * scale_of(residual) * gain_ref[...]).astype(BF16)


def norm_rows(part, got, x, gain, after=()):
    rows, width = part.shape
    return call(
        norm_body,
        (
            jax.ShapeDtypeStruct((rows, width), F32),
            jax.ShapeDtypeStruct((rows, width), BF16),
        ),
        [part, got, x, gain],
        [whole(pltpu.VMEM)] * 4,
        8 * rows * width,
        12 * rows * width,
        after=after,
        out_specs=(whole(pltpu.VMEM), whole(pltpu.VMEM)),
        name="norm_rows",
    )


def norm_back_body(part_ref, got_ref, values_ref, add_ref, gain_ref, *outs):
    upstream = part_ref[...].astype(F32) + got_ref[...].astype(F32)
    values = values_ref[...].astype(F32)
    scale = scale_of(values)
    normed = values * scale
    outs[-1][...] = jnp.sum(upstream * normed, axis=0, keepdims=True)
    weighted = upstream * gain_ref[...]
    grad = scale * (weighted - normed * jnp.mean(weighted * normed, axis=-1, keepdims=True))
    total = add_ref[...].astype(F32) + grad
    for ref in outs[:-1]:
        ref[...] = total.astype(ref.dtype)


def norm_back(part, got, values, add, gain, kinds, after=()):
    rows, width = part.shape
    return call(
        norm_back_body,
        tuple(jax.ShapeDtypeStruct((rows, width), kind) for kind in kinds)
        + (jax.ShapeDtypeStruct((1, width), F32),),
        [part, got, values, add, gain],
        [whole(pltpu.VMEM)] * 5,
        16 * rows * width,
        16 * rows * width,
        after=after,
        out_specs=tuple(whole(pltpu.VMEM) for _ in range(len(kinds) + 1)),
        name="norm_back",
    )


def add_body(part_ref, got_ref, res_ref, out_ref):
    out_ref[...] = (
        res_ref[...] + (part_ref[...].astype(F32) + got_ref[...].astype(F32))
    ).astype(BF16)


def add_rows(part, got, residual, after=()):
    return call(
        add_body,
        jax.ShapeDtypeStruct(part.shape, BF16),
        [part, got, residual],
        [whole(pltpu.VMEM)] * 3,
        part.size,
        10 * part.size,
        after=after,
        out_specs=whole(pltpu.VMEM),
        name="add_rows",
    )


def join_body(n, place_ref, *refs):
    core = place_ref[2] & 1
    place_rows(refs[:n], refs[-1], core)
    place_rows(refs[n : 2 * n], refs[-1], 1 - core)


def join_rows(place, mine, sibs, after=()):
    n = len(mine)
    size, width = mine[0].shape
    return call(
        functools.partial(join_body, n),
        jax.ShapeDtypeStruct((2 * n * size, width), BF16),
        [place, *mine, *sibs],
        [whole(pltpu.SMEM)] + [whole(pltpu.VMEM)] * (2 * n),
        0,
        8 * n * size * width,
        after=after,
        out_specs=whole(pltpu.VMEM),
        name="join_rows",
    )


def turn_body(n, block, offset_ref, order_ref, *refs):
    pieces, out_ref = refs[:n], refs[n]
    size, wide = pieces[0].shape
    unit = (
        lax.broadcasted_iota(jnp.int32, (block, block), 0)
        == lax.broadcasted_iota(jnp.int32, (block, block), 1)
    ).astype(F32).astype(BF16)
    for p in range(wide // block):
        at = pl.multiple_of(order_ref[p] * block, block)
        for j in range(n):
            to = pl.multiple_of(offset_ref[j] * size, size)
            made = nt(unit, pieces[j][:, pl.ds(at, block)]).astype(BF16)
            out_ref[p * block : (p + 1) * block, pl.ds(to, size)] = made


def turn(order, group, pieces, offsets=None, after=()):
    wide = pieces[0].shape[1]
    if group % 128 != 0:
        pieces = [
            jnp.concatenate(
                [
                    lax.dynamic_slice_in_dim(piece, order[p] * group, group, 1)
                    for p in range(order.shape[0])
                ],
                axis=1,
            )
            for piece in pieces
        ]
        block = math.gcd(256, wide)
        order_in = jnp.arange(wide // block, dtype=jnp.int32)
    else:
        block = group
        order_in = order
    n = len(pieces)
    size = pieces[0].shape[0]
    tokens = n * size
    if offsets is None:
        offsets = jnp.arange(n, dtype=jnp.int32)
    return call(
        functools.partial(turn_body, n, block),
        jax.ShapeDtypeStruct((wide, tokens), BF16),
        [offsets, order_in, *pieces],
        [whole(pltpu.SMEM)] * 2 + [whole(pltpu.VMEM)] * n,
        2 * tokens * wide * block,
        4 * tokens * wide,
        after=after,
        out_specs=whole(pltpu.VMEM),
        vmem=8 + 4 * tokens * wide // MIB,
        name="turn",
    )


def stack_body(*refs):
    for i, ref in enumerate(refs[:-1]):
        refs[-1][i] = ref[...]


def stack_rows(pieces):
    n = len(pieces)
    return call(
        stack_body,
        jax.ShapeDtypeStruct((n, *pieces[0].shape), BF16),
        list(pieces),
        [whole(pltpu.VMEM)] * n,
        0,
        4 * n * pieces[0].size,
        out_specs=whole(pltpu.VMEM),
        name="stack_rows",
    )


def turn_all_body(block, place_ref, order_ref, own_ref, *refs):
    parts, out_ref = refs[:-1], refs[-1]
    n = len(parts)
    size, wide = parts[0].shape[1:]
    unit = (
        lax.broadcasted_iota(jnp.int32, (block, block), 0)
        == lax.broadcasted_iota(jnp.int32, (block, block), 1)
    ).astype(F32).astype(BF16)

    @pl.when(pl.program_id(0) == 0)
    def _():
        for p in range(wide // block):
            at = pl.multiple_of(order_ref[p] * block, block)
            made = nt(unit, own_ref[:, pl.ds(at, block)]).astype(BF16)
            out_ref[p * block : (p + 1) * block, :] = made

    @pl.when(pl.program_id(0) > 0)
    def _():
        for p in range(wide // block):
            at = pl.multiple_of(order_ref[p] * block, block)
            for j in range(n):
                to = pl.multiple_of((place_ref[0] ^ j) * size, size)
                made = nt(unit, parts[j][0, :, pl.ds(at, block)]).astype(BF16)
                out_ref[p * block : (p + 1) * block, pl.ds(to, size)] = made


def turn_all(order, group, own, parts, m):
    tokens, wide = own.shape
    others, size, _ = parts[0].shape
    if group % 128 != 0:

        def ordered(values):
            axis = values.ndim - 1
            return jnp.concatenate(
                [
                    lax.dynamic_slice_in_dim(values, order[p] * group, group, axis)
                    for p in range(order.shape[0])
                ],
                axis=axis,
            )

        own = ordered(own)
        parts = [ordered(part) for part in parts]
        block = math.gcd(256, wide)
        order_in = jnp.arange(wide // block, dtype=jnp.int32)
    else:
        block = group
        order_in = order
    return call(
        functools.partial(turn_all_body, block),
        jax.ShapeDtypeStruct((wide, (others + 1) * tokens), BF16),
        [m.reshape(1).astype(jnp.int32), order_in, own, *parts],
        [pl.BlockSpec((tokens, wide), lambda d, place, order: (0, 0))]
        + [
            pl.BlockSpec((1, size, wide), lambda d, place, order: (jnp.maximum(d - 1, 0), 0, 0))
        ]
        * len(parts),
        2 * (others + 1) * tokens * wide * block,
        4 * (others + 1) * tokens * wide,
        prefetch=2,
        grid=(others + 1,),
        out_specs=pl.BlockSpec((wide, tokens), lambda d, place, order: (0, d)),
        vmem=52,
        name="turn_all",
    )


def weight_body(n, *refs):
    lefts, refs = refs[:n], refs[n:]
    rights, (sent_ref, kept_ref) = refs[:n], refs[n:]
    total = nn(lefts[0][...], rights[0][...])
    for i in range(1, n):
        total = total + nn(lefts[i][...], rights[i][...])
    half = pl.num_programs(0) // 2

    @pl.when(pl.program_id(0) < half)
    def _():
        sent_ref[...] = total.astype(BF16)

    @pl.when(pl.program_id(0) >= half)
    def _():
        kept_ref[...] = total.astype(BF16)


def weight_grad(lefts, rights, after=()):
    wide = lefts[0].shape[0]
    width = rights[0].shape[1]
    tokens = sum(left.shape[1] for left in lefts)
    steps = 4
    tile = wide // steps
    half = steps // 2
    made = jax.ShapeDtypeStruct((wide // 2, width), BF16)
    return call(
        functools.partial(weight_body, len(lefts)),
        (made,) * 2,
        [*lefts, *rights],
        [
            pl.BlockSpec((tile, left.shape[1]), lambda i: ((i + half) % steps, 0))
            for left in lefts
        ]
        + [pl.BlockSpec(right.shape, lambda i: (0, 0)) for right in rights],
        2 * tokens * wide * width,
        2 * (tokens * wide + tokens * width + wide * width),
        after=after,
        grid=(steps,),
        out_specs=(
            pl.BlockSpec((tile, width), lambda i: (jnp.minimum(i, half - 1), 0)),
            pl.BlockSpec((tile, width), lambda i: (jnp.maximum(i - half, 0), 0)),
        ),
        vmem=52,
        name="weight_grad",
    )


def sum3_body(n, *refs):
    total = refs[0][...].astype(F32)
    for ref in refs[1:n]:
        total = total + ref[...].astype(F32)
    low_ref, high_ref = refs[n:]
    low_ref[...] = total[0]
    high_ref[...] = total[1].astype(BF16)


def final_sum(terms, after=()):
    wide, width = terms[0].shape
    high = wide // 2
    tile = math.gcd(high, 128)
    block = pl.BlockSpec((2, tile, width), lambda i: (0, i, 0))
    out = pl.BlockSpec((tile, width), lambda i: (i, 0))
    return call(
        functools.partial(sum3_body, len(terms)),
        (
            jax.ShapeDtypeStruct((high, width), F32),
            jax.ShapeDtypeStruct((high, width), BF16),
        ),
        [term.reshape(2, high, width) for term in terms],
        [block] * len(terms),
        wide * width,
        wide * width * 8,
        after=after,
        grid=(high // tile,),
        out_specs=(out, out),
        name="final_sum",
    )


def merge_body(kept_ref, got_ref, low_ref, high_ref):
    total = kept_ref[...].astype(F32) + got_ref[...].astype(F32)
    low_ref[...] = total[0]
    high_ref[...] = total[1].astype(BF16)


def merge(kept, got, after=()):
    wide, width = kept.shape
    high = wide // 2
    tile = math.gcd(high, 128)
    operands = [kept.reshape(2, high, width), got.reshape(2, high, width)]
    block = pl.BlockSpec((2, tile, width), lambda i: (0, i, 0))
    out = pl.BlockSpec((tile, width), lambda i: (i, 0))
    return call(
        merge_body,
        (
            jax.ShapeDtypeStruct((high, width), F32),
            jax.ShapeDtypeStruct((high, width), BF16),
        ),
        operands,
        [block, block],
        wide * width,
        wide * width * 8,
        after=after,
        grid=(high // tile,),
        out_specs=(out, out),
        name="merge",
    )


def lay_body(turned, place_ref, own_ref, got_ref, out_ref):
    value = jnp.where(pl.program_id(0) == 0, own_ref[...], got_ref[...].astype(F32))
    out_ref[...] = value.T if turned else value


def lay(place, own, got, turned):
    rows, width = own.shape
    if turned:
        shape, block = (2 * width, rows), (width, rows)
        index = lambda i, place: (place[3] ^ i, 0)
    else:
        shape, block = (rows, 2 * width), (rows, width)
        index = lambda i, place: (0, place[3] ^ i)
    fixed = pl.BlockSpec((rows, width), lambda i, place: (0, 0))
    return call(
        functools.partial(lay_body, turned),
        jax.ShapeDtypeStruct(shape, F32),
        [place, own, got],
        [fixed, fixed],
        0,
        14 * rows * width,
        prefetch=1,
        grid=(2,),
        out_specs=pl.BlockSpec(block, index),
        name="lay",
    )


def qkv_sum_body(kept_ref, got_ref, own_ref, *outs):
    size = own_ref.shape[0]
    total = kept_ref[...].astype(F32) + got_ref[...].astype(F32)
    own_ref[...] = total[:size]
    for i, ref in enumerate(outs):
        ref[...] = total[(i + 1) * size : (i + 2) * size].astype(BF16)


def split_sum(kept, got, n):
    rows, width = kept.shape
    size = rows // n
    return call(
        qkv_sum_body,
        (jax.ShapeDtypeStruct((size, width), F32),)
        + (jax.ShapeDtypeStruct((size, width), BF16),) * (n - 1),
        [kept, got],
        [whole(pltpu.VMEM)] * 2,
        rows * width,
        8 * rows * width,
        out_specs=(whole(pltpu.VMEM),) * n,
        name="split_sum",
    )


def place_heads_body(nz, place_ref, *refs):
    pieces, outs = refs[:nz], refs[nz:]
    for d in range(nz):
        at = pl.multiple_of((place_ref[0] ^ d) * HD, HD)
        for i, out in enumerate(outs):
            out[:, pl.ds(at, HD)] = pieces[d][:, i * HD : (i + 1) * HD].astype(F32)


def place_heads(place, pieces):
    nz = len(pieces)
    rows = pieces[0].shape[0]
    return call(
        functools.partial(place_heads_body, nz),
        (jax.ShapeDtypeStruct((rows, nz * HD), F32),) * 3,
        [place, *pieces],
        [whole(pltpu.SMEM)] + [whole(pltpu.VMEM)] * nz,
        0,
        20 * rows * nz * HD,
        out_specs=(whole(pltpu.VMEM),) * 3,
        name="place_heads",
    )


def rope_tables(position):
    middle = HD // 2
    frequency = THETA ** (-(jnp.arange(middle, dtype=F32) * 2.0 / HD))
    angles = position.astype(F32)[..., None] * frequency
    cosine = jnp.cos(angles)
    sine = jnp.sin(angles)
    return (
        jnp.concatenate([cosine, cosine], axis=-1),
        jnp.concatenate([-sine, sine], axis=-1),
    )


def rms_scale(values):
    return lax.rsqrt(jnp.mean(values * values, axis=-1, keepdims=True) + EPSILON)


def layer(
    n_seq,
    n_mp,
    mixed_in,
    w_query,
    w_key,
    w_value,
    w_out,
    gain_attn,
    w_gate,
    w_up,
    w_down,
    gain_mlp,
    doc_ends,
    cotangent,
):
    rows, width = mixed_in.shape
    nz = w_query.shape[1] // HD
    ring = n_seq // nz
    bits = n_seq.bit_length() - 1
    low_bits = ring.bit_length() - 1
    units = w_gate.shape[1]
    half_units = units // 2
    half_rows = rows // 2
    group = width // n_seq
    pair_bit = bits - 2
    pair = 1 << pair_bit

    s = lax.axis_index("seq")
    m = lax.axis_index("mp")
    z, r = s // ring, s % ring
    core = m % 2
    side = m // 2
    low = (s >> pair_bit) & 1

    def seq_swap(v, distance):
        return lax.ppermute(v, "seq", [(i, i ^ distance) for i in range(n_seq)])

    def mp_swap(v, distance):
        return lax.ppermute(v, "mp", [(i, i ^ distance) for i in range(n_mp)])

    sum_bits = list(range(pair_bit)) + [bits - 1]
    places = []
    for p in range(n_seq):
        e = 0
        for at, bit in enumerate(sum_bits + [pair_bit]):
            if (p >> (bits - 1 - at)) & 1:
                e |= 1 << bit
        places.append(e)
    order = s ^ jnp.array(places, dtype=jnp.int32)

    ORDER.clear()

    place = jnp.stack([z, r, m, low]).astype(jnp.int32)
    blocks = (z ^ jnp.arange(nz, dtype=jnp.int32)) * ring + r
    token_index = blocks[:, None] * rows + jnp.arange(rows, dtype=jnp.int32)[None, :]
    ends_below = doc_ends[None, None, :] <= token_index[..., None]
    begin = jnp.max(jnp.where(ends_below, doc_ends, 0), axis=-1)
    cos_own, sin_own = rope_tables(token_index[0] - begin[0])
    cos_all, sin_all = rope_tables(token_index - begin)
    weights = [w_query, w_key, w_value]
    half_z = nz // 2
    made = project_qkv(
        place,
        mixed_in,
        gain_attn.reshape(1, width),
        weights,
        cos_own,
        sin_own,
        list(range(half_z, nz)),
    )
    normed = made[-1]
    pieces = {half_z + i: made[i] for i in range(half_z)}
    made = project_qkv(place, normed, None, weights, cos_own, sin_own, list(range(half_z)))
    pieces.update({i: made[i] for i in range(half_z)})
    pieces = [pieces[0]] + [seq_swap(pieces[d], d * ring) for d in range(1, nz)]
    near = pieces
    keys_values = [near, [seq_swap(piece[:, HD:], 1) for piece in pieces]]
    for b in range(1, low_bits):
        keys_values = keys_values + [
            [seq_swap(kv[:, -2 * HD :], 1 << b) for kv in kvs] for kvs in keys_values
        ]
    queries = pieces

    quarter = rows // n_mp
    my_quarter = lax.dynamic_slice_in_dim(normed, m * quarter, quarter, 0)
    halves = [
        lax.dynamic_slice_in_dim(w_down, low * half_units, half_units, 0),
        lax.dynamic_slice_in_dim(w_gate, low * half_units, half_units, 1),
        lax.dynamic_slice_in_dim(w_up, low * half_units, half_units, 1),
    ]
    cot_half = lax.dynamic_slice_in_dim(cotangent, core * half_rows, half_rows, 0)

    flat = [kv for kvs in keys_values for kv in kvs]
    far = [kv for kvs in keys_values[1:] for kv in kvs]
    cot_half, *halves = hold([cot_half, *halves], after=pieces)
    cot_pair = seq_swap(cot_half, pair)
    outs = attend(place, doc_ends, queries, flat, nz, ring, after=[cos_all, sin_all])
    heads = [outs[0]] + [seq_swap(outs[d], d * ring) for d in range(1, nz)]

    size = half_rows // CHUNKS
    last_low = 1 << sum_bits[pair_bit - 1]
    high = 1 << sum_bits[pair_bit]
    gain_mlp_row = gain_mlp.reshape(1, width)
    gain_attn_row = gain_attn.reshape(1, width)

    def chunks_of(values):
        return [values[i * size : (i + 1) * size] for i in range(CHUNKS)]

    def low_sums(sent, kept):
        for bit in sum_bits[: pair_bit - 1]:
            kept, sent = merge(kept, seq_swap(sent, 1 << bit))
        return kept, seq_swap(sent, last_low)

    x_chunks = chunks_of(lax.dynamic_slice_in_dim(mixed_in, core * half_rows, half_rows, 0))
    cot_chunks = chunks_of(cot_half)
    cot_all = cot_chunks + chunks_of(cot_pair)
    spots = jnp.concatenate(
        [core * CHUNKS + jnp.arange(CHUNKS), (1 - core) * CHUNKS + jnp.arange(CHUNKS)]
    ).astype(jnp.int32)
    v = types.SimpleNamespace(
        residual=[None] * CHUNKS,
        normed=[None] * (2 * CHUNKS),
        back=[None] * CHUNKS,
        back_across=[None] * CHUNKS,
        residual_grad=[None] * CHUNKS,
        branch=[None] * CHUNKS,
        branch_sib=[None] * CHUNKS,
        gain_mlp=[None] * CHUNKS,
        gain_attn=[None] * CHUNKS,
        grad_rows=[None] * CHUNKS,
        grad_sib=[None] * CHUNKS,
        quarters={0: my_quarter},
        out_grads=(),
    )
    def heads_out():
        sib, v.mine, v.heads_placed = heads_project(
            place, heads, [w_out], nn, True, after=[cot_pair]
        )
        v.sib = mp_swap(sib, 1)

    def out_sum():
        v.parts = row_sum(v.mine, v.sib, CHUNKS)
        v.across = [mp_swap(part, 2) for part in v.parts]

    def swap_weights():
        v.down_sib, v.gate_sib, v.up_sib = [mp_swap(half, 1) for half in hold(halves)]

    def dact_own():
        v.dact = hidden_upstream(place, cot_all, w_down, True)

    def dact_sib():
        v.dact_sib = hidden_upstream(place, cot_all, v.down_sib, False)

    def norm_chunk(i):
        v.residual[i], v.normed[i] = norm_rows(
            v.parts[i], v.across[i], x_chunks[i], gain_mlp_row
        )
        v.normed[CHUNKS + i] = seq_swap(v.normed[i], pair)

    def turn_cot():
        v.cot_turned = turn(order, group, cot_all)

    def swap_cot():
        (turned,) = hold([v.cot_turned])
        v.cot_both = [turned, mp_swap(turned, 1)]

    def hidden_sib():
        v.act_sib, dg_sib, du_sib = hidden(
            place, v.normed, v.gate_sib, v.up_sib, v.dact_sib, False
        )
        v.act_got = mp_swap(v.act_sib, 1)
        v.dg_sib, v.du_sib = dg_sib, du_sib

    def swap_dg():
        (part,) = hold([v.dg_sib])
        v.dg_got = mp_swap(part, 1)

    def swap_du():
        (part,) = hold([v.du_sib])
        v.du_got = mp_swap(part, 1)

    def hidden_own():
        v.act, v.dg, v.du = hidden(place, v.normed, w_gate, w_up, v.dact, True)

    def turn_normed():
        v.normed_turned = turn(order, group, v.normed)

    def swap_normed():
        (turned,) = hold([v.normed_turned])
        v.normed_both = [turned, mp_swap(turned, 1)]

    def grad_down():
        v.sent_down, v.part_down = weight_grad(v.cot_both, [v.act, v.act_got])

    def send_down():
        (sent,) = hold([v.sent_down])
        v.low_down = low_sums(sent, v.part_down)

    def hidden_in():
        v.made = hidden_back(
            place,
            v.dg,
            v.dg_sib,
            v.du,
            v.du_sib,
            w_gate,
            v.gate_sib,
            w_up,
            v.up_sib,
            2 * CHUNKS,
        )
        v.made_got = [seq_swap(v.made[CHUNKS + i], pair) for i in range(CHUNKS)]

    def back_chunk(i):
        (v.back[i],) = row_sum(v.made[i], v.made_got[i], 1)
        v.back_across[i] = mp_swap(v.back[i], 2)

    def norm_back_chunk(i):
        v.residual_grad[i], v.branch[i], v.gain_mlp[i] = norm_back(
            v.back[i], v.back_across[i], v.residual[i], cot_chunks[i], gain_mlp_row, (F32, BF16)
        )
        v.branch_sib[i] = mp_swap(v.branch[i], 1)

    def grad_gate():
        v.sent_gate, v.part_gate = weight_grad(v.normed_both, [v.dg, v.dg_got])

    def send_gate():
        (sent,) = hold([v.sent_gate])
        v.low_gate = low_sums(sent, v.part_gate)

    def grad_up():
        v.sent_up, v.part_up = weight_grad(v.normed_both, [v.du, v.du_got])

    def send_up():
        (sent,) = hold([v.sent_up])
        v.low_up = low_sums(sent, v.part_up)

    def merge_down():
        v.kept_down, v.high_down = merge(*v.low_down)

    def high_down():
        (sent,) = hold([v.high_down], after=v.out_grads)
        v.come_down = seq_swap(sent, high)

    def merge_gate():
        v.kept_gate, v.high_gate = merge(*v.low_gate)

    def high_gate():
        (sent,) = hold([v.high_gate])
        v.come_gate = seq_swap(sent, high)

    def merge_up():
        v.kept_up, v.high_up = merge(*v.low_up)

    def high_up():
        (sent,) = hold([v.high_up])
        v.come_up = seq_swap(sent, high)

    def sum_down():
        v.own_down, v.pair_down = final_sum([v.kept_down, v.come_down])

    def sum_gate():
        v.own_gate, v.pair_gate = final_sum([v.kept_gate, v.come_gate])

    def sum_up():
        v.own_up, v.pair_up = final_sum([v.kept_up, v.come_up])

    def pair_down():
        (sent,) = hold([v.pair_down])
        v.theirs_down = seq_swap(sent, pair)

    def pair_gate():
        (sent,) = hold([v.pair_gate])
        v.theirs_gate = seq_swap(sent, pair)

    def pair_up():
        (sent,) = hold([v.pair_up])
        v.theirs_up = seq_swap(sent, pair)

    def lay_down():
        v.down_share = lay(place, v.own_down, v.theirs_down, True)

    def lay_gate():
        v.gate_share = lay(place, v.own_gate, v.theirs_gate, False)

    def lay_up():
        v.up_share = lay(place, v.own_up, v.theirs_up, False)

    def gather_z(d):
        (part,) = hold([v.quarters[d & (d - 1)]])
        v.quarters[d] = seq_swap(part, ring * (d & -d))

    def gather_x():
        v.rows = stack_rows([v.quarters[d] for d in range(1, nz)])
        v.rows_x = mp_swap(v.rows, 2)

    def gather_core():
        v.rows_core = [mp_swap(part, 1) for part in hold([v.rows, v.rows_x])]

    def heads_in():
        made = heads_upstream(place, v.branch, v.branch_sib, w_out, nz)
        v.out_grads = [made[0]] + [seq_swap(made[d], d * ring) for d in range(1, nz)]

    def attend_far():
        v.dq_far, *summed = attend_back(
            place, doc_ends, queries, v.out_grads, far, None, nz, ring, 1, ring - 1, BF16
        )
        summed = [None] + summed
        for b in reversed(range(low_bits)):
            bit = 1 << b
            for e in range(bit):
                got = seq_swap(summed[e | bit], bit)
                summed[e] = (
                    got
                    if summed[e] is None
                    else (summed[e].astype(F32) + got.astype(F32)).astype(BF16)
                )
        v.dkv_got = summed[0]

    def attend_near():
        v.dq, v.dkv = attend_back(
            place, doc_ends, queries, v.out_grads, near, v.dq_far, nz, ring, 0, 1, F32
        )

    def head_grads():
        v.grads = finish_grads(v.dq, v.dkv, v.dkv_got, cos_all, sin_all)
        v.own_grads = [v.grads[0]] + [
            seq_swap(v.grads[d], d * ring) for d in range(1, nz)
        ]

    def turn_branch():
        v.branch_turned = turn(order, group, v.branch + v.branch_sib, spots)

    def grad_out():
        v.sent_out, v.part_out = weight_grad([v.branch_turned], [v.heads_placed])

    def send_out():
        (sent,) = hold([v.sent_out])
        v.low_out = low_sums(sent, v.part_out)

    def merge_out():
        v.kept_out, v.high_out = merge(*v.low_out)

    def high_out():
        (sent,) = hold([v.high_out])
        v.come_out = seq_swap(sent, high)

    def sum_out():
        v.own_out, sent = final_sum([v.kept_out, v.come_out])
        v.pair_out = seq_swap(sent, pair)

    def turn_rows():
        v.all_turned = turn_all(
            order, group, normed, [v.rows, v.rows_core[0], v.rows_x, v.rows_core[1]], m
        )

    def grad_qkv():
        v.sent_qkv, v.part_qkv = weight_grad(
            [v.all_turned], [jnp.concatenate(v.grads, axis=0)]
        )

    def send_qkv():
        (sent,) = hold([v.sent_qkv])
        v.low_qkv = low_sums(sent, v.part_qkv)

    def split_qkv():
        own, *sent = split_sum(*v.low_qkv, nz)
        v.qkv_heads = [own] + [seq_swap(sent[d - 1], d * ring) for d in range(1, nz)]

    def lay_qkv():
        v.shares = place_heads(place, v.qkv_heads)

    def rows_in():
        sib, v.in_mine = heads_project(place, v.own_grads, weights, nt, False)
        v.in_sib = mp_swap(sib, 1)

    def in_sum():
        v.in_parts = row_sum(v.in_mine, v.in_sib, CHUNKS)
        v.in_across = [mp_swap(part, 2) for part in v.in_parts]

    def norm_in_chunk(i):
        v.grad_rows[i], v.gain_attn[i] = norm_back(
            v.in_parts[i], v.in_across[i], x_chunks[i], v.residual_grad[i], gain_attn_row, (BF16,)
        )
        v.grad_sib[i] = mp_swap(v.grad_rows[i], 1)

    def join_in():
        v.input_grad = join_rows(place, v.grad_rows, v.grad_sib)

    def down_rows():
        v.down_mine, v.down_theirs = down(place, v.act, v.act_sib, w_down, v.down_sib, 2)

    def pair_rows():
        (sent,) = hold([v.down_theirs])
        v.down_got = seq_swap(sent, pair)

    def sum_rows():
        (v.down_part,) = row_sum(v.down_mine, v.down_got, 1)
        v.down_across = mp_swap(v.down_part, 2)

    def add_out():
        v.out_rows = add_rows(
            v.down_part, v.down_across, jnp.concatenate(v.residual, axis=0)
        )
        v.out_sib = mp_swap(v.out_rows, 1)

    def join_out():
        v.mixed_out = join_rows(place, [v.out_rows], [v.out_sib])

    def gains_core():
        (v.gains,) = hold([jnp.concatenate([sum(v.gain_attn), sum(v.gain_mlp)])])
        v.gains = v.gains + mp_swap(v.gains, 1)

    def gains_seq(bit):
        (v.gains,) = hold([v.gains])
        v.gains = v.gains + seq_swap(v.gains, 1 << bit)

    loose(heads_out)
    dact_own()
    gather_z(1)
    out_sum()
    swap_weights()
    norm_chunk(1)
    dact_sib()
    norm_chunk(0)
    turn_cot()
    swap_cot()
    gather_z(2)
    hidden_sib()
    swap_dg()
    hidden_own()
    swap_du()
    turn_normed()
    swap_normed()
    grad_down()
    hidden_in()
    send_down()
    grad_gate()
    gather_z(3)
    back_chunk(1)
    back_chunk(0)
    send_gate()
    gather_x()
    norm_back_chunk(1)
    norm_back_chunk(0)
    heads_in()
    merge_down()
    turn_branch()
    high_down()
    attend_far()
    grad_up()
    send_up()
    gather_core()
    merge_gate()
    attend_near()
    high_gate()
    loose(sum_down)
    head_grads()
    pair_down()
    rows_in()
    merge_up()
    grad_out()
    loose(high_up)
    in_sum()
    down_rows()
    pair_rows()
    norm_in_chunk(0)
    send_out()
    turn_rows()
    lay_down()
    grad_qkv()
    merge_out()
    high_out()
    sum_gate()
    norm_in_chunk(1)
    send_qkv()
    gains_core()
    gains_seq(0)
    loose(pair_gate)
    sum_rows()
    join_in()
    gains_seq(2)
    split_qkv()
    sum_up()
    pair_up()
    sum_out()
    lay_gate()
    loose(add_out)
    lay_up()
    gains_seq(1)
    join_out()
    lay_qkv()
    for bit in range(3, bits):
        gains_seq(bit)
    gains = lax.dynamic_slice_in_dim(v.gains, s * group, group, 1)

    return (
        v.mixed_out,
        v.input_grad,
        *v.shares,
        (v.own_out + v.pair_out.astype(F32)).T,
        gains[0],
        v.gate_share,
        v.up_share,
        v.down_share,
        gains[1],
    )


def solution(mesh):
    placed = (
        P("seq", None),
        P(None, "mp"),
        P(None, "mp"),
        P(None, "mp"),
        P("mp", None),
        P(),
        P(None, "mp"),
        P(None, "mp"),
        P("mp", None),
        P(),
        P(),
        P("seq", None),
    )
    return jax.shard_map(
        functools.partial(layer, mesh.shape["seq"], mesh.shape["mp"]),
        mesh=mesh,
        in_specs=placed,
        out_specs=(
            P("seq", None),
            P("seq", None),
            P("seq", "mp"),
            P("seq", "mp"),
            P("seq", "mp"),
            P("mp", "seq"),
            P("seq"),
            P("seq", "mp"),
            P("seq", "mp"),
            P("mp", "seq"),
            P("seq"),
        ),
        check_vma=False,
    )
```

```python
import functools
import math
import types

import jax
import jax.numpy as jnp
from jax import lax
from jax.experimental import pallas as pl
from jax.experimental.pallas import tpu as pltpu
from jax.sharding import PartitionSpec as P

HD = 128
EPSILON = 1e-05
THETA = 10000.0
FACTOR = 1.0 / math.sqrt(HD)
CLAMP = 80.0
CHUNKS = 2
SHARE = 0.5
ORDER = []
LOOSE = [False]
MIB = 1024 * 1024
F32 = jnp.float32
BF16 = jnp.bfloat16


def nn(left, right):
    return lax.dot_general(left, right, (((1,), (0,)), ((), ())), preferred_element_type=F32)


def nt(left, right):
    return lax.dot_general(left, right, (((1,), (1,)), ((), ())), preferred_element_type=F32)


def tn(left, right):
    return lax.dot_general(left, right, (((0,), (0,)), ((), ())), preferred_element_type=F32)


def call(
    body,
    out_shape,
    operands,
    in_specs,
    flops,
    moved,
    transcendentals=0,
    after=(),
    prefetch=0,
    chain=True,
    vmem=20,
    **kwargs,
):
    n = prefetch + len(in_specs)
    chain = chain and not LOOSE[0]
    after = list(after) + (ORDER if chain else [])

    def kernel(*refs):
        body(*refs[:n], *refs[n + len(after) :])

    in_specs = list(in_specs) + [pl.BlockSpec(memory_space=pl.ANY)] * len(after)
    if prefetch:
        kwargs = {
            "name": kwargs.pop("name"),
            "grid_spec": pltpu.PrefetchScalarGridSpec(
                num_scalar_prefetch=prefetch, in_specs=in_specs, **kwargs
            ),
        }
    else:
        kwargs["in_specs"] = in_specs
    made = pl.pallas_call(
        kernel,
        out_shape=out_shape,
        compiler_params=pltpu.CompilerParams(vmem_limit_bytes=vmem * MIB),
        cost_estimate=pl.CostEstimate(
            flops=int(flops / SHARE),
            bytes_accessed=int(moved / SHARE),
            transcendentals=int(transcendentals / SHARE),
        ),
        **kwargs,
    )(*operands, *after)
    if chain:
        ORDER[:] = [made[0] if isinstance(made, (tuple, list)) else made]
    return made


def hold(values, after=()):
    n = len(values)
    if LOOSE[0]:
        return list(lax.optimization_barrier((*values, *after))[:n])
    made = lax.optimization_barrier((*values, *ORDER, *after))
    ORDER[:] = made[n : n + len(ORDER)]
    return list(made[:n])


def loose(step, *args):
    LOOSE[0] = True
    step(*args)
    LOOSE[0] = False


def whole(memory):
    return pl.BlockSpec(memory_space=memory)


def rotated(values, cosine, signed):
    return values * cosine + pltpu.roll(values, HD // 2, 1) * signed


def unrotated(values, cosine, signed):
    return values * cosine - pltpu.roll(values, HD // 2, 1) * signed


def qkv_body(n, fresh, place_ref, *refs):
    if fresh:
        x_ref, gain_ref, refs = refs[0], refs[1], refs[2:]
    else:
        x_ref, refs = refs[0], refs[1:]
    wq_ref, wk_ref, wv_ref, cos_ref, sin_ref = refs[:5]
    outs, (w_s, x_s) = refs[5 : 5 + n], refs[-2:]
    step = pl.program_id(0)

    @pl.when(step == 0)
    def _():
        if fresh:
            x = x_ref[...].astype(F32)
            x_s[...] = (x * scale_of(x) * gain_ref[...]).astype(BF16)
            refs[5 + n][...] = x_s[...]
        else:
            x_s[...] = x_ref[...]

    w_s[:, :HD] = wq_ref[...]
    w_s[:, HD : 2 * HD] = wk_ref[...]
    w_s[:, 2 * HD :] = wv_ref[...]
    made = nn(x_s[...], w_s[...])
    cosine = cos_ref[...]
    signed = sin_ref[...]
    query = rotated(made[:, :HD], cosine, signed).astype(BF16)
    key = rotated(made[:, HD : 2 * HD], cosine, signed).astype(BF16)
    value = made[:, 2 * HD :].astype(BF16)
    for i in range(n):

        @pl.when(step == i)
        def _(i=i):
            outs[i][:, :HD] = query
            outs[i][:, HD : 2 * HD] = key
            outs[i][:, 2 * HD :] = value


def project_qkv(place, x, gain, weights, cosine, signed, spots):
    n = len(spots)
    rows, width = x.shape
    fresh = gain is not None
    fixed = pl.BlockSpec((rows, width), lambda i, place: (0, 0))
    table = pl.BlockSpec((rows, HD), lambda i, place: (0, 0))
    first = spots[0]
    assert list(spots) == [first ^ i for i in range(n)]
    weight = pl.BlockSpec((width, HD), lambda i, place: (0, place[0] ^ first ^ i))
    piece = jax.ShapeDtypeStruct((rows, 3 * HD), BF16)
    return call(
        functools.partial(qkv_body, n, fresh),
        (piece,) * n + ((jax.ShapeDtypeStruct(x.shape, BF16),) if fresh else ()),
        [place, x] + ([gain] if fresh else []) + [*weights, cosine, signed],
        [fixed]
        + ([pl.BlockSpec((1, width), lambda i, place: (0, 0))] if fresh else [])
        + [weight] * 3
        + [table] * 2,
        6 * n * rows * width * HD,
        4 * rows * width + 6 * n * width * HD + 6 * n * rows * HD,
        prefetch=1,
        grid=(n,),
        out_specs=(pl.BlockSpec((rows, 3 * HD), lambda i, place: (0, 0)),) * n
        + ((fixed,) if fresh else ()),
        scratch_shapes=[pltpu.VMEM((width, 3 * HD), BF16), pltpu.VMEM((rows, width), BF16)],
        vmem=60,
        name="project_qkv",
    )


def begin_of(index, ends_ref, count):
    begin = jnp.zeros_like(index)
    for e in range(count):
        end = ends_ref[e]
        begin = jnp.where(end <= index, jnp.maximum(begin, end), begin)
    return begin


def finish_of(index, ends_ref, count):
    finish = jnp.zeros_like(index) + ends_ref[count - 1]
    for e in range(count):
        end = ends_ref[e]
        finish = jnp.where(end > index, jnp.minimum(finish, end), finish)
    return finish


def attend_body(nz, ring, count, place_ref, ends_ref, *refs):
    n_kv = nz * ring
    q_refs, refs = refs[:nz], refs[nz:]
    kv_refs, refs = refs[:n_kv], refs[n_kv:]
    o_refs, refs = refs[:nz], refs[nz:]
    q_s, k_s, v_s, o_s, acc = refs
    z, r = place_ref[0], place_ref[1]
    rows = q_s.shape[1]
    for d in range(nz):
        q_s[d] = q_refs[d][:, :HD]
    for i in range(n_kv):
        first = kv_refs[i].shape[1] - 2 * HD
        k_s[i] = kv_refs[i][:, first : first + HD]
        v_s[i] = kv_refs[i][:, first + HD :]

    @pl.loop(0, nz)
    def per_query(d):
        q_block = (z ^ d) * ring + r
        q_start = q_block * rows
        q_index = q_start + lax.broadcasted_iota(jnp.int32, (rows, 1), 0)
        begin = begin_of(q_index, ends_ref, count)
        shift = jnp.log((finish_of(q_index, ends_ref, count) - begin).astype(F32))
        first_begin = begin_of(q_start, ends_ref, count)
        last_begin = begin_of(q_start + (rows - 1), ends_ref, count)
        acc[...] = jnp.zeros_like(acc)

        @pl.loop(0, n_kv)
        def per_key(i):
            k_block = (z ^ (i & (nz - 1))) * ring + (r ^ (i // nz))
            k_start = k_block * rows
            needed = (k_block <= q_block) & (k_start + rows > first_begin)
            full = (k_block < q_block) & (k_start >= last_begin)

            def tile(masked):
                half = rows // 2
                for part in range(2):
                    at = slice(part * half, (part + 1) * half)
                    scores = nt(q_s[d, at], k_s[i])
                    grown = jnp.exp(jnp.minimum(shift[at] - scores * FACTOR, CLAMP))
                    probs = pl.reciprocal(1.0 + grown, approx=True)
                    if masked:
                        k_index = k_start + lax.broadcasted_iota(jnp.int32, (1, rows), 1)
                        allowed = (k_index <= q_index[at]) & (k_index >= begin[at])
                        probs = jnp.where(allowed, probs, 0.0)
                    acc[at] += nn(probs.astype(BF16), v_s[i])

            pl.when(needed & full)(functools.partial(tile, False))
            pl.when(needed & jnp.logical_not(full))(functools.partial(tile, True))

        o_s[d] = acc[...].astype(BF16)

    for d in range(nz):
        o_refs[d][...] = o_s[d]


def attend(place, ends, queries, keys_values, nz, ring, after=()):
    rows = queries[0].shape[0]
    n_kv = nz * ring
    pairs = nz * n_kv / 2
    return call(
        functools.partial(attend_body, nz, ring, ends.shape[0]),
        tuple(jax.ShapeDtypeStruct((rows, HD), BF16) for _ in range(nz)),
        [place, ends, *queries, *keys_values],
        [whole(pltpu.SMEM)] * 2 + [whole(pltpu.VMEM)] * (nz + n_kv),
        pairs * 4 * rows * rows * HD * 2,
        2 * (2 * nz + 2 * n_kv) * rows * HD,
        pairs * 2 * rows * rows,
        after=after,
        out_specs=tuple(whole(pltpu.VMEM) for _ in range(nz)),
        scratch_shapes=[
            pltpu.VMEM((nz, rows, HD), BF16),
            pltpu.VMEM((n_kv, rows, HD), BF16),
            pltpu.VMEM((n_kv, rows, HD), BF16),
            pltpu.VMEM((nz, rows, HD), BF16),
            pltpu.VMEM((rows, HD), F32),
        ],
        vmem=12 + 2 * n_kv * rows * HD * 8 // MIB,
        name="attend",
    )


def attend_back_body(nz, ring, n_dr, first_dr, chained, count, place_ref, ends_ref, *refs):
    n_kv = nz * n_dr
    q_refs, refs = refs[:nz], refs[nz:]
    do_refs, refs = refs[:nz], refs[nz:]
    kv_refs, refs = refs[:n_kv], refs[n_kv:]
    if chained:
        before_ref, refs = refs[0], refs[1:]
    dq_ref, refs = refs[0], refs[1:]
    dkv_refs, refs = refs[:n_dr], refs[n_dr:]
    q_s, do_s, k_s, v_s, begin_s, shift_s, dkv_s, dk_acc, dv_acc = refs
    z, r = place_ref[0], place_ref[1]
    rows = q_s.shape[1]
    for d in range(nz):
        q_s[d] = q_refs[d][:, :HD]
        do_s[d] = do_refs[d][...]
    for i in range(n_kv):
        first = kv_refs[i].shape[1] - 2 * HD
        k_s[i] = kv_refs[i][:, first : first + HD]
        v_s[i] = kv_refs[i][:, first + HD :]
    if chained:
        dq_ref[...] = before_ref[...]
    else:
        dq_ref[...] = jnp.zeros_like(dq_ref)

    @pl.loop(0, nz)
    def tables(d):
        q_index = ((z ^ d) * ring + r) * rows + lax.broadcasted_iota(jnp.int32, (1, rows), 1)
        begin = begin_of(q_index, ends_ref, count)
        begin_s[d] = begin
        shift_s[d] = jnp.log((finish_of(q_index, ends_ref, count) - begin).astype(F32))

    @pl.loop(0, n_kv)
    def per_key(i):
        k_block = (z ^ (i & (nz - 1))) * ring + (r ^ (first_dr + i // nz))
        k_start = k_block * rows
        dk_acc[...] = jnp.zeros_like(dk_acc)
        dv_acc[...] = jnp.zeros_like(dv_acc)

        @pl.loop(0, nz)
        def per_query(d):
            q_block = (z ^ d) * ring + r
            q_start = q_block * rows
            first_begin = begin_of(q_start, ends_ref, count)
            last_begin = begin_of(q_start + (rows - 1), ends_ref, count)
            needed = (k_block <= q_block) & (k_start + rows > first_begin)
            full = (k_block < q_block) & (k_start >= last_begin)

            def tile(masked):
                half = rows // 2
                for part in range(2):
                    at = slice(part * half, (part + 1) * half)
                    keys = k_s[i, at]
                    scores = nt(keys, q_s[d])
                    grown = jnp.exp(jnp.minimum(shift_s[d] - scores * FACTOR, CLAMP))
                    probs = pl.reciprocal(1.0 + grown, approx=True)
                    if masked:
                        k_index = (
                            k_start
                            + part * half
                            + lax.broadcasted_iota(jnp.int32, (half, 1), 0)
                        )
                        q_index = q_start + lax.broadcasted_iota(jnp.int32, (1, rows), 1)
                        allowed = (k_index <= q_index) & (k_index >= begin_s[d])
                        probs = jnp.where(allowed, probs, 0.0)
                    weight_grad = nt(v_s[i, at], do_s[d])
                    score_grad = (weight_grad * (probs * probs * grown)).astype(BF16)
                    dv_acc[at] += nn(probs.astype(BF16), do_s[d])
                    dk_acc[at] += nn(score_grad, q_s[d])
                    dq_ref[d] += tn(score_grad, keys)

            pl.when(needed & full)(functools.partial(tile, False))
            pl.when(needed & jnp.logical_not(full))(functools.partial(tile, True))

        dkv_s[i, :, :HD] = (dk_acc[...] * FACTOR).astype(dkv_s.dtype)
        dkv_s[i, :, HD:] = dv_acc[...].astype(dkv_s.dtype)

    for e in range(n_dr):
        for d in range(nz):
            dkv_refs[e][d] = dkv_s[e * nz + d]


def attend_back(
    place, ends, queries, out_grads, keys_values, before, nz, ring, first_dr, n_dr, kept, after=()
):
    rows = queries[0].shape[0]
    n_kv = nz * n_dr
    pairs = nz * n_kv / 2
    chained = before is not None
    return call(
        functools.partial(
            attend_back_body, nz, ring, n_dr, first_dr, chained, ends.shape[0]
        ),
        (jax.ShapeDtypeStruct((nz, rows, HD), F32),)
        + tuple(jax.ShapeDtypeStruct((nz, rows, 2 * HD), kept) for _ in range(n_dr)),
        [place, ends, *queries, *out_grads, *keys_values, *([before] if chained else [])],
        [whole(pltpu.SMEM)] * 2 + [whole(pltpu.VMEM)] * (2 * nz + n_kv + chained),
        pairs * 10 * rows * rows * HD * 2,
        2 * (2 * nz + 4 * n_kv) * rows * HD,
        pairs * 2 * rows * rows,
        after=after,
        out_specs=tuple(whole(pltpu.VMEM) for _ in range(1 + n_dr)),
        scratch_shapes=[
            pltpu.VMEM((nz, rows, HD), BF16),
            pltpu.VMEM((nz, rows, HD), BF16),
            pltpu.VMEM((n_kv, rows, HD), BF16),
            pltpu.VMEM((n_kv, rows, HD), BF16),
            pltpu.VMEM((nz, 1, rows), jnp.int32),
            pltpu.VMEM((nz, 1, rows), F32),
            pltpu.VMEM((n_kv, rows, 2 * HD), kept),
            pltpu.VMEM((rows, HD), F32),
            pltpu.VMEM((rows, HD), F32),
        ],
        vmem=16 + 2 * n_kv * rows * HD * 14 // MIB,
        name="attend_back",
    )


def finish_body(nz, dq_ref, dkv_ref, got_ref, cos_ref, sin_ref, *out_refs):
    for d in range(nz):
        cosine = cos_ref[d]
        signed = sin_ref[d]
        total = dkv_ref[d] + got_ref[d].astype(F32)
        out = out_refs[d]
        out[:, :HD] = unrotated(dq_ref[d] * FACTOR, cosine, signed).astype(BF16)
        out[:, HD : 2 * HD] = unrotated(total[:, :HD], cosine, signed).astype(BF16)
        out[:, 2 * HD :] = total[:, HD:].astype(BF16)


def finish_grads(dq, dkv, got, cosine, signed):
    nz, rows, _ = dq.shape
    return call(
        functools.partial(finish_body, nz),
        tuple(jax.ShapeDtypeStruct((rows, 3 * HD), BF16) for _ in range(nz)),
        [dq, dkv, got, cosine, signed],
        [whole(pltpu.VMEM)] * 5,
        12 * nz * rows * HD,
        nz * rows * HD * 30,
        out_specs=tuple(whole(pltpu.VMEM) for _ in range(nz)),
        name="finish_grads",
    )


def rows_at(place, width, height, tile_of):
    return pl.BlockSpec((height, width), lambda j, place: (tile_of(place), 0))


def place_rows(pieces, scratch, spot):
    size = pieces[0].shape[0]
    half = size * len(pieces)
    for i, piece in enumerate(pieces):
        at = pl.multiple_of(spot * half + i * size, size)
        scratch[pl.ds(at, size), :] = piece[...]


def upstream_body(place_ref, *refs):
    pieces, (w_ref, out_ref, x_s) = refs[:-3], refs[-3:]
    size = pieces[0].shape[0]

    @pl.when(pl.program_id(0) == 0)
    def _():
        for i, piece in enumerate(pieces):
            x_s[i * size : (i + 1) * size] = piece[...]

    out_ref[...] = nt(x_s[...], w_ref[...]).astype(BF16)


def hidden_upstream(place, pieces, weights, own, after=()):
    size, width = pieces[0].shape
    rows = size * len(pieces)
    units = weights.shape[0] // (2 if own else 1)
    tile = 512
    steps = units // tile
    first = (lambda place: place[3] * steps) if own else (lambda place: 0)
    return call(
        upstream_body,
        jax.ShapeDtypeStruct((rows, units), BF16),
        [place, *pieces, weights],
        [pl.BlockSpec((size, width), lambda j, place: (0, 0))] * len(pieces)
        + [pl.BlockSpec((tile, width), lambda j, place: (first(place) + j, 0))],
        2 * rows * width * units,
        2 * width * units + 4 * rows * units + 2 * rows * width,
        after=after,
        prefetch=1,
        grid=(steps,),
        out_specs=pl.BlockSpec((rows, tile), lambda j, place: (0, j)),
        scratch_shapes=[pltpu.VMEM((rows, width), BF16)],
        vmem=52,
        name="hidden_upstream",
    )


def hidden_body(place_ref, *refs):
    pieces, refs = refs[:-7], refs[-7:]
    wg_ref, wu_ref, dact_ref, act_ref, dg_ref, du_ref, x_s = refs
    size = pieces[0].shape[0]

    @pl.when(pl.program_id(0) == 0)
    def _():
        for i, piece in enumerate(pieces):
            x_s[i * size : (i + 1) * size] = piece[...]

    x = x_s[...]
    for first in range(0, act_ref.shape[1], 256):
        at = slice(first, first + 256)
        gate = nn(x, wg_ref[:, at])
        up = nn(x, wu_ref[:, at])
        dact = dact_ref[:, at].astype(F32)
        sig = jax.nn.sigmoid(gate)
        silu = gate * sig
        act_ref[:, at] = (silu * up).astype(BF16)
        dg_ref[:, at] = (dact * up * sig * (1.0 + gate * (1.0 - sig))).astype(BF16)
        du_ref[:, at] = (dact * silu).astype(BF16)


def hidden(place, pieces, w_gate, w_up, dact, own, after=()):
    size, width = pieces[0].shape
    rows = size * len(pieces)
    units = dact.shape[1]
    tile = 512
    steps = units // tile
    first = (lambda place: place[3] * steps) if own else (lambda place: 0)
    made = jax.ShapeDtypeStruct((rows, units), BF16)
    block = pl.BlockSpec((rows, tile), lambda j, place: (0, j))
    weight = pl.BlockSpec((width, tile), lambda j, place: (0, first(place) + j))
    return call(
        hidden_body,
        (made, made, made),
        [place, *pieces, w_gate, w_up, dact],
        [pl.BlockSpec((size, width), lambda j, place: (0, 0))] * len(pieces)
        + [weight, weight, block],
        4 * rows * width * units,
        4 * width * units + 8 * rows * units + 2 * rows * width,
        rows * units,
        after=after,
        prefetch=1,
        grid=(steps,),
        out_specs=(block, block, block),
        scratch_shapes=[pltpu.VMEM((rows, width), BF16)],
        vmem=52,
        name="hidden",
    )


def chunked(total, out_refs):
    size = out_refs[0].shape[0]
    for i, ref in enumerate(out_refs):
        ref[...] = total[i * size : (i + 1) * size].astype(ref.dtype)


def back_body(place_ref, dg_ref, dg_sib, du_ref, du_sib, wg_ref, wg_sib, wu_ref, wu_sib, *outs):
    chunked(
        nt(dg_ref[...], wg_ref[...])
        + nt(dg_sib[...], wg_sib[...])
        + nt(du_ref[...], wu_ref[...])
        + nt(du_sib[...], wu_sib[...]),
        outs,
    )


def hidden_back(place, dg, dg_sib, du, du_sib, w_gate, gate_sib, w_up, up_sib, chunks, after=()):
    rows, half = dg.shape
    width = w_gate.shape[0]
    tile = 512
    size = rows // chunks
    left = pl.BlockSpec((rows, half), lambda j, place: (0, 0))
    own = pl.BlockSpec((tile, half), lambda j, place: (j, place[3]))
    sib = pl.BlockSpec((tile, half), lambda j, place: (j, 0))
    return call(
        back_body,
        tuple(jax.ShapeDtypeStruct((size, width), BF16) for _ in range(chunks)),
        [place, dg, dg_sib, du, du_sib, w_gate, gate_sib, w_up, up_sib],
        [left] * 4 + [own, sib, own, sib],
        8 * rows * width * half,
        8 * width * half + 8 * rows * half + 2 * rows * width,
        after=after,
        prefetch=1,
        grid=(width // tile,),
        out_specs=tuple(pl.BlockSpec((size, tile), lambda j, place: (0, j)) for _ in range(chunks)),
        vmem=52,
        name="hidden_back",
    )


def down_body(place_ref, act_ref, act_sib, wd_ref, wd_sib, *outs):
    chunked(nn(act_ref[...], wd_ref[...]) + nn(act_sib[...], wd_sib[...]), outs)


def down(place, act, act_sib, w_down, down_sib, chunks, after=()):
    rows, half = act.shape
    width = w_down.shape[1]
    tile = 512
    size = rows // chunks
    left = pl.BlockSpec((rows, half), lambda j, place: (0, 0))
    return call(
        down_body,
        tuple(jax.ShapeDtypeStruct((size, width), BF16) for _ in range(chunks)),
        [place, act, act_sib, w_down, down_sib],
        [
            left,
            left,
            pl.BlockSpec((half, tile), lambda j, place: (place[3], j)),
            pl.BlockSpec((half, tile), lambda j, place: (0, j)),
        ],
        4 * rows * width * half,
        4 * width * half + 4 * rows * half + 2 * rows * width,
        after=after,
        prefetch=1,
        grid=(width // tile,),
        out_specs=tuple(pl.BlockSpec((size, tile), lambda j, place: (0, j)) for _ in range(chunks)),
        vmem=52,
        name="down",
    )


def heads_body(nz, contract, keep, place_ref, *refs):
    n_w = 1 if keep else 3
    pieces, refs = refs[:nz], refs[nz:]
    w_refs, (sib_ref, mine_ref), refs = refs[:n_w], refs[n_w : n_w + 2], refs[n_w + 2 :]
    joined = refs[:n_w]
    for d in range(nz):
        at = pl.multiple_of((place_ref[0] ^ d) * HD, HD)
        for i in range(n_w):
            joined[i][:, pl.ds(at, HD)] = pieces[d][:, i * HD : (i + 1) * HD]
    half = sib_ref.shape[0]
    core = place_ref[2] & 1

    def rows_of(start):
        start = pl.multiple_of(start, half)
        total = contract(joined[0][pl.ds(start, half), :], w_refs[0][...])
        for i in range(1, n_w):
            total = total + contract(joined[i][pl.ds(start, half), :], w_refs[i][...])
        return total

    sib_ref[...] = rows_of((1 - core) * half).astype(BF16)
    mine_ref[...] = rows_of(core * half)


def heads_project(place, pieces, weights, contract, keep, after=()):
    nz = len(pieces)
    rows = pieces[0].shape[0]
    n_w = len(weights)
    width = weights[0].shape[1] if contract is nn else weights[0].shape[0]
    half = rows // 2
    joined = (rows, nz * HD)
    out = (
        jax.ShapeDtypeStruct((half, width), BF16),
        jax.ShapeDtypeStruct((half, width), F32),
    ) + ((jax.ShapeDtypeStruct(joined, BF16),) if keep else ())
    return call(
        functools.partial(heads_body, nz, contract, keep),
        out,
        [place, *pieces, *weights],
        [whole(pltpu.SMEM)] + [whole(pltpu.VMEM)] * (nz + n_w),
        2 * rows * width * nz * HD * n_w,
        2 * n_w * (width * nz * HD + rows * nz * HD) + 3 * rows * width,
        after=after,
        out_specs=tuple(whole(pltpu.VMEM) for _ in out),
        scratch_shapes=() if keep else (pltpu.VMEM(joined, BF16),) * n_w,
        vmem=24,
        name="heads_project",
    )


def dheads_body(nz, n, place_ref, *refs):
    mine, refs = refs[:n], refs[n:]
    sibs, refs = refs[:n], refs[n:]
    w_ref, outs, x_s = refs[0], refs[1:-1], refs[-1]
    core = place_ref[2] & 1
    place_rows(mine, x_s, core)
    place_rows(sibs, x_s, 1 - core)
    x = x_s[...]
    wide = outs[0].shape[1]
    for d in range(nz):
        at = pl.multiple_of((place_ref[0] ^ d) * wide, wide)
        outs[d][...] = nt(x, w_ref[pl.ds(at, wide), :]).astype(BF16)


def heads_upstream(place, mine, sibs, w_out, nz, after=()):
    n = len(mine)
    size, width = mine[0].shape
    rows = 2 * n * size
    wide = w_out.shape[0] // nz
    return call(
        functools.partial(dheads_body, nz, n),
        tuple(jax.ShapeDtypeStruct((rows, wide), BF16) for _ in range(nz)),
        [place, *mine, *sibs, w_out],
        [whole(pltpu.SMEM)] + [whole(pltpu.VMEM)] * (2 * n + 1),
        2 * rows * width * nz * wide,
        2 * width * nz * wide + 2 * rows * nz * wide + 2 * rows * width,
        after=after,
        out_specs=tuple(whole(pltpu.VMEM) for _ in range(nz)),
        scratch_shapes=[pltpu.VMEM((rows, width), BF16)],
        name="heads_upstream",
    )


def sum_body(mine_ref, got_ref, *outs):
    chunked(mine_ref[...].astype(F32) + got_ref[...].astype(F32), outs)


def row_sum(mine, got, chunks, after=()):
    rows, width = mine.shape
    size = rows // chunks
    return call(
        sum_body,
        tuple(jax.ShapeDtypeStruct((size, width), BF16) for _ in range(chunks)),
        [mine, got],
        [whole(pltpu.VMEM)] * 2,
        rows * width,
        8 * rows * width,
        after=after,
        out_specs=tuple(whole(pltpu.VMEM) for _ in range(chunks)),
        name="row_sum",
    )


def scale_of(values):
    return lax.rsqrt(jnp.mean(values * values, axis=-1, keepdims=True) + EPSILON)


def norm_body(part_ref, got_ref, x_ref, gain_ref, res_ref, normed_ref):
    residual = x_ref[...].astype(F32) + (part_ref[...].astype(F32) + got_ref[...].astype(F32))
    res_ref[...] = residual
    normed_ref[...] = (residual * scale_of(residual) * gain_ref[...]).astype(BF16)


def norm_rows(part, got, x, gain, after=()):
    rows, width = part.shape
    return call(
        norm_body,
        (
            jax.ShapeDtypeStruct((rows, width), F32),
            jax.ShapeDtypeStruct((rows, width), BF16),
        ),
        [part, got, x, gain],
        [whole(pltpu.VMEM)] * 4,
        8 * rows * width,
        12 * rows * width,
        after=after,
        out_specs=(whole(pltpu.VMEM), whole(pltpu.VMEM)),
        name="norm_rows",
    )


def norm_back_body(part_ref, got_ref, values_ref, add_ref, gain_ref, *outs):
    upstream = part_ref[...].astype(F32) + got_ref[...].astype(F32)
    values = values_ref[...].astype(F32)
    scale = scale_of(values)
    normed = values * scale
    outs[-1][...] = jnp.sum(upstream * normed, axis=0, keepdims=True)
    weighted = upstream * gain_ref[...]
    grad = scale * (weighted - normed * jnp.mean(weighted * normed, axis=-1, keepdims=True))
    total = add_ref[...].astype(F32) + grad
    for ref in outs[:-1]:
        ref[...] = total.astype(ref.dtype)


def norm_back(part, got, values, add, gain, kinds, after=()):
    rows, width = part.shape
    return call(
        norm_back_body,
        tuple(jax.ShapeDtypeStruct((rows, width), kind) for kind in kinds)
        + (jax.ShapeDtypeStruct((1, width), F32),),
        [part, got, values, add, gain],
        [whole(pltpu.VMEM)] * 5,
        16 * rows * width,
        16 * rows * width,
        after=after,
        out_specs=tuple(whole(pltpu.VMEM) for _ in range(len(kinds) + 1)),
        name="norm_back",
    )


def add_body(part_ref, got_ref, res_ref, out_ref):
    out_ref[...] = (
        res_ref[...] + (part_ref[...].astype(F32) + got_ref[...].astype(F32))
    ).astype(BF16)


def add_rows(part, got, residual, after=()):
    return call(
        add_body,
        jax.ShapeDtypeStruct(part.shape, BF16),
        [part, got, residual],
        [whole(pltpu.VMEM)] * 3,
        part.size,
        10 * part.size,
        after=after,
        out_specs=whole(pltpu.VMEM),
        name="add_rows",
    )


def join_body(n, place_ref, *refs):
    core = place_ref[2] & 1
    place_rows(refs[:n], refs[-1], core)
    place_rows(refs[n : 2 * n], refs[-1], 1 - core)


def join_rows(place, mine, sibs, after=()):
    n = len(mine)
    size, width = mine[0].shape
    return call(
        functools.partial(join_body, n),
        jax.ShapeDtypeStruct((2 * n * size, width), BF16),
        [place, *mine, *sibs],
        [whole(pltpu.SMEM)] + [whole(pltpu.VMEM)] * (2 * n),
        0,
        8 * n * size * width,
        after=after,
        out_specs=whole(pltpu.VMEM),
        name="join_rows",
    )


def turn_body(n, block, offset_ref, order_ref, *refs):
    pieces, out_ref = refs[:n], refs[n]
    size, wide = pieces[0].shape
    unit = (
        lax.broadcasted_iota(jnp.int32, (block, block), 0)
        == lax.broadcasted_iota(jnp.int32, (block, block), 1)
    ).astype(F32).astype(BF16)
    for p in range(wide // block):
        at = pl.multiple_of(order_ref[p] * block, block)
        for j in range(n):
            to = pl.multiple_of(offset_ref[j] * size, size)
            made = nt(unit, pieces[j][:, pl.ds(at, block)]).astype(BF16)
            out_ref[p * block : (p + 1) * block, pl.ds(to, size)] = made


def turn(order, group, pieces, offsets=None, after=()):
    wide = pieces[0].shape[1]
    if group % 128 != 0:
        pieces = [
            jnp.concatenate(
                [
                    lax.dynamic_slice_in_dim(piece, order[p] * group, group, 1)
                    for p in range(order.shape[0])
                ],
                axis=1,
            )
            for piece in pieces
        ]
        block = math.gcd(256, wide)
        order_in = jnp.arange(wide // block, dtype=jnp.int32)
    else:
        block = group
        order_in = order
    n = len(pieces)
    size = pieces[0].shape[0]
    tokens = n * size
    if offsets is None:
        offsets = jnp.arange(n, dtype=jnp.int32)
    return call(
        functools.partial(turn_body, n, block),
        jax.ShapeDtypeStruct((wide, tokens), BF16),
        [offsets, order_in, *pieces],
        [whole(pltpu.SMEM)] * 2 + [whole(pltpu.VMEM)] * n,
        2 * tokens * wide * block,
        4 * tokens * wide,
        after=after,
        out_specs=whole(pltpu.VMEM),
        vmem=8 + 4 * tokens * wide // MIB,
        name="turn",
    )


def stack_body(*refs):
    for i, ref in enumerate(refs[:-1]):
        refs[-1][i] = ref[...]


def stack_rows(pieces):
    n = len(pieces)
    return call(
        stack_body,
        jax.ShapeDtypeStruct((n, *pieces[0].shape), BF16),
        list(pieces),
        [whole(pltpu.VMEM)] * n,
        0,
        4 * n * pieces[0].size,
        out_specs=whole(pltpu.VMEM),
        name="stack_rows",
    )


def turn_all_body(block, place_ref, order_ref, own_ref, *refs):
    parts, out_ref = refs[:-1], refs[-1]
    n = len(parts)
    size, wide = parts[0].shape[1:]
    unit = (
        lax.broadcasted_iota(jnp.int32, (block, block), 0)
        == lax.broadcasted_iota(jnp.int32, (block, block), 1)
    ).astype(F32).astype(BF16)

    @pl.when(pl.program_id(0) == 0)
    def _():
        for p in range(wide // block):
            at = pl.multiple_of(order_ref[p] * block, block)
            made = nt(unit, own_ref[:, pl.ds(at, block)]).astype(BF16)
            out_ref[p * block : (p + 1) * block, :] = made

    @pl.when(pl.program_id(0) > 0)
    def _():
        for p in range(wide // block):
            at = pl.multiple_of(order_ref[p] * block, block)
            for j in range(n):
                to = pl.multiple_of((place_ref[0] ^ j) * size, size)
                made = nt(unit, parts[j][0, :, pl.ds(at, block)]).astype(BF16)
                out_ref[p * block : (p + 1) * block, pl.ds(to, size)] = made


def turn_all(order, group, own, parts, m):
    tokens, wide = own.shape
    others, size, _ = parts[0].shape
    if group % 128 != 0:

        def ordered(values):
            axis = values.ndim - 1
            return jnp.concatenate(
                [
                    lax.dynamic_slice_in_dim(values, order[p] * group, group, axis)
                    for p in range(order.shape[0])
                ],
                axis=axis,
            )

        own = ordered(own)
        parts = [ordered(part) for part in parts]
        block = math.gcd(256, wide)
        order_in = jnp.arange(wide // block, dtype=jnp.int32)
    else:
        block = group
        order_in = order
    return call(
        functools.partial(turn_all_body, block),
        jax.ShapeDtypeStruct((wide, (others + 1) * tokens), BF16),
        [m.reshape(1).astype(jnp.int32), order_in, own, *parts],
        [pl.BlockSpec((tokens, wide), lambda d, place, order: (0, 0))]
        + [
            pl.BlockSpec((1, size, wide), lambda d, place, order: (jnp.maximum(d - 1, 0), 0, 0))
        ]
        * len(parts),
        2 * (others + 1) * tokens * wide * block,
        4 * (others + 1) * tokens * wide,
        prefetch=2,
        grid=(others + 1,),
        out_specs=pl.BlockSpec((wide, tokens), lambda d, place, order: (0, d)),
        vmem=52,
        name="turn_all",
    )


def weight_body(n, *refs):
    lefts, refs = refs[:n], refs[n:]
    rights, (sent_ref, kept_ref) = refs[:n], refs[n:]
    total = nn(lefts[0][...], rights[0][...])
    for i in range(1, n):
        total = total + nn(lefts[i][...], rights[i][...])
    half = pl.num_programs(0) // 2

    @pl.when(pl.program_id(0) < half)
    def _():
        sent_ref[...] = total.astype(BF16)

    @pl.when(pl.program_id(0) >= half)
    def _():
        kept_ref[...] = total.astype(BF16)


def weight_grad(lefts, rights, after=()):
    wide = lefts[0].shape[0]
    width = rights[0].shape[1]
    tokens = sum(left.shape[1] for left in lefts)
    steps = 4
    tile = wide // steps
    half = steps // 2
    made = jax.ShapeDtypeStruct((wide // 2, width), BF16)
    return call(
        functools.partial(weight_body, len(lefts)),
        (made,) * 2,
        [*lefts, *rights],
        [
            pl.BlockSpec((tile, left.shape[1]), lambda i: ((i + half) % steps, 0))
            for left in lefts
        ]
        + [pl.BlockSpec(right.shape, lambda i: (0, 0)) for right in rights],
        2 * tokens * wide * width,
        2 * (tokens * wide + tokens * width + wide * width),
        after=after,
        grid=(steps,),
        out_specs=(
            pl.BlockSpec((tile, width), lambda i: (jnp.minimum(i, half - 1), 0)),
            pl.BlockSpec((tile, width), lambda i: (jnp.maximum(i - half, 0), 0)),
        ),
        vmem=52,
        name="weight_grad",
    )


def sum3_body(n, *refs):
    total = refs[0][...].astype(F32)
    for ref in refs[1:n]:
        total = total + ref[...].astype(F32)
    low_ref, high_ref = refs[n:]
    low_ref[...] = total[0]
    high_ref[...] = total[1].astype(BF16)


def final_sum(terms, after=()):
    wide, width = terms[0].shape
    high = wide // 2
    tile = math.gcd(high, 128)
    block = pl.BlockSpec((2, tile, width), lambda i: (0, i, 0))
    out = pl.BlockSpec((tile, width), lambda i: (i, 0))
    return call(
        functools.partial(sum3_body, len(terms)),
        (
            jax.ShapeDtypeStruct((high, width), F32),
            jax.ShapeDtypeStruct((high, width), BF16),
        ),
        [term.reshape(2, high, width) for term in terms],
        [block] * len(terms),
        wide * width,
        wide * width * 8,
        after=after,
        grid=(high // tile,),
        out_specs=(out, out),
        name="final_sum",
    )


def merge_body(kept_ref, got_ref, low_ref, high_ref):
    total = kept_ref[...].astype(F32) + got_ref[...].astype(F32)
    low_ref[...] = total[0]
    high_ref[...] = total[1].astype(BF16)


def merge(kept, got, after=()):
    wide, width = kept.shape
    high = wide // 2
    tile = math.gcd(high, 128)
    operands = [kept.reshape(2, high, width), got.reshape(2, high, width)]
    block = pl.BlockSpec((2, tile, width), lambda i: (0, i, 0))
    out = pl.BlockSpec((tile, width), lambda i: (i, 0))
    return call(
        merge_body,
        (
            jax.ShapeDtypeStruct((high, width), F32),
            jax.ShapeDtypeStruct((high, width), BF16),
        ),
        operands,
        [block, block],
        wide * width,
        wide * width * 8,
        after=after,
        grid=(high // tile,),
        out_specs=(out, out),
        name="merge",
    )


def lay_body(turned, place_ref, own_ref, got_ref, out_ref):
    value = jnp.where(pl.program_id(0) == 0, own_ref[...], got_ref[...].astype(F32))
    out_ref[...] = value.T if turned else value


def lay(place, own, got, turned):
    rows, width = own.shape
    if turned:
        shape, block = (2 * width, rows), (width, rows)
        index = lambda i, place: (place[3] ^ i, 0)
    else:
        shape, block = (rows, 2 * width), (rows, width)
        index = lambda i, place: (0, place[3] ^ i)
    fixed = pl.BlockSpec((rows, width), lambda i, place: (0, 0))
    return call(
        functools.partial(lay_body, turned),
        jax.ShapeDtypeStruct(shape, F32),
        [place, own, got],
        [fixed, fixed],
        0,
        14 * rows * width,
        prefetch=1,
        grid=(2,),
        out_specs=pl.BlockSpec(block, index),
        name="lay",
    )


def qkv_sum_body(kept_ref, got_ref, own_ref, *outs):
    size = own_ref.shape[0]
    total = kept_ref[...].astype(F32) + got_ref[...].astype(F32)
    own_ref[...] = total[:size]
    for i, ref in enumerate(outs):
        ref[...] = total[(i + 1) * size : (i + 2) * size].astype(BF16)


def split_sum(kept, got, n):
    rows, width = kept.shape
    size = rows // n
    return call(
        qkv_sum_body,
        (jax.ShapeDtypeStruct((size, width), F32),)
        + (jax.ShapeDtypeStruct((size, width), BF16),) * (n - 1),
        [kept, got],
        [whole(pltpu.VMEM)] * 2,
        rows * width,
        8 * rows * width,
        out_specs=(whole(pltpu.VMEM),) * n,
        name="split_sum",
    )


def place_heads_body(nz, place_ref, *refs):
    pieces, outs = refs[:nz], refs[nz:]
    for d in range(nz):
        at = pl.multiple_of((place_ref[0] ^ d) * HD, HD)
        for i, out in enumerate(outs):
            out[:, pl.ds(at, HD)] = pieces[d][:, i * HD : (i + 1) * HD].astype(F32)


def place_heads(place, pieces):
    nz = len(pieces)
    rows = pieces[0].shape[0]
    return call(
        functools.partial(place_heads_body, nz),
        (jax.ShapeDtypeStruct((rows, nz * HD), F32),) * 3,
        [place, *pieces],
        [whole(pltpu.SMEM)] + [whole(pltpu.VMEM)] * nz,
        0,
        20 * rows * nz * HD,
        out_specs=(whole(pltpu.VMEM),) * 3,
        name="place_heads",
    )


def rope_tables(position):
    middle = HD // 2
    frequency = THETA ** (-(jnp.arange(middle, dtype=F32) * 2.0 / HD))
    angles = position.astype(F32)[..., None] * frequency
    cosine = jnp.cos(angles)
    sine = jnp.sin(angles)
    return (
        jnp.concatenate([cosine, cosine], axis=-1),
        jnp.concatenate([-sine, sine], axis=-1),
    )


def rms_scale(values):
    return lax.rsqrt(jnp.mean(values * values, axis=-1, keepdims=True) + EPSILON)


def layer(
    n_seq,
    n_mp,
    mixed_in,
    w_query,
    w_key,
    w_value,
    w_out,
    gain_attn,
    w_gate,
    w_up,
    w_down,
    gain_mlp,
    doc_ends,
    cotangent,
):
    rows, width = mixed_in.shape
    nz = w_query.shape[1] // HD
    ring = n_seq // nz
    bits = n_seq.bit_length() - 1
    low_bits = ring.bit_length() - 1
    units = w_gate.shape[1]
    half_units = units // 2
    half_rows = rows // 2
    group = width // n_seq
    pair_bit = bits - 2
    pair = 1 << pair_bit

    s = lax.axis_index("seq")
    m = lax.axis_index("mp")
    z, r = s // ring, s % ring
    core = m % 2
    side = m // 2
    low = (s >> pair_bit) & 1

    def seq_swap(v, distance):
        return lax.ppermute(v, "seq", [(i, i ^ distance) for i in range(n_seq)])

    def mp_swap(v, distance):
        return lax.ppermute(v, "mp", [(i, i ^ distance) for i in range(n_mp)])

    sum_bits = list(range(pair_bit)) + [bits - 1]
    places = []
    for p in range(n_seq):
        e = 0
        for at, bit in enumerate(sum_bits + [pair_bit]):
            if (p >> (bits - 1 - at)) & 1:
                e |= 1 << bit
        places.append(e)
    order = s ^ jnp.array(places, dtype=jnp.int32)

    ORDER.clear()

    place = jnp.stack([z, r, m, low]).astype(jnp.int32)
    blocks = (z ^ jnp.arange(nz, dtype=jnp.int32)) * ring + r
    token_index = blocks[:, None] * rows + jnp.arange(rows, dtype=jnp.int32)[None, :]
    ends_below = doc_ends[None, None, :] <= token_index[..., None]
    begin = jnp.max(jnp.where(ends_below, doc_ends, 0), axis=-1)
    cos_own, sin_own = rope_tables(token_index[0] - begin[0])
    cos_all, sin_all = rope_tables(token_index - begin)
    weights = [w_query, w_key, w_value]
    half_z = nz // 2
    made = project_qkv(
        place,
        mixed_in,
        gain_attn.reshape(1, width),
        weights,
        cos_own,
        sin_own,
        list(range(half_z, nz)),
    )
    normed = made[-1]
    pieces = {half_z + i: made[i] for i in range(half_z)}
    made = project_qkv(place, normed, None, weights, cos_own, sin_own, list(range(half_z)))
    pieces.update({i: made[i] for i in range(half_z)})
    pieces = [pieces[0]] + [seq_swap(pieces[d], d * ring) for d in range(1, nz)]
    near = pieces
    keys_values = [near, [seq_swap(piece[:, HD:], 1) for piece in pieces]]
    for b in range(1, low_bits):
        keys_values = keys_values + [
            [seq_swap(kv[:, -2 * HD :], 1 << b) for kv in kvs] for kvs in keys_values
        ]
    queries = pieces

    quarter = rows // n_mp
    my_quarter = lax.dynamic_slice_in_dim(normed, m * quarter, quarter, 0)
    halves = [
        lax.dynamic_slice_in_dim(w_down, low * half_units, half_units, 0),
        lax.dynamic_slice_in_dim(w_gate, low * half_units, half_units, 1),
        lax.dynamic_slice_in_dim(w_up, low * half_units, half_units, 1),
    ]
    cot_half = lax.dynamic_slice_in_dim(cotangent, core * half_rows, half_rows, 0)

    flat = [kv for kvs in keys_values for kv in kvs]
    far = [kv for kvs in keys_values[1:] for kv in kvs]
    cot_half, *halves = hold([cot_half, *halves], after=pieces)
    cot_pair = seq_swap(cot_half, pair)
    outs = attend(place, doc_ends, queries, flat, nz, ring, after=[cos_all, sin_all])
    heads = [outs[0]] + [seq_swap(outs[d], d * ring) for d in range(1, nz)]

    size = half_rows // CHUNKS
    last_low = 1 << sum_bits[pair_bit - 1]
    high = 1 << sum_bits[pair_bit]
    gain_mlp_row = gain_mlp.reshape(1, width)
    gain_attn_row = gain_attn.reshape(1, width)

    def chunks_of(values):
        return [values[i * size : (i + 1) * size] for i in range(CHUNKS)]

    def low_sums(sent, kept):
        for bit in sum_bits[: pair_bit - 1]:
            kept, sent = merge(kept, seq_swap(sent, 1 << bit))
        return kept, seq_swap(sent, last_low)

    x_chunks = chunks_of(lax.dynamic_slice_in_dim(mixed_in, core * half_rows, half_rows, 0))
    cot_chunks = chunks_of(cot_half)
    cot_all = cot_chunks + chunks_of(cot_pair)
    spots = jnp.concatenate(
        [core * CHUNKS + jnp.arange(CHUNKS), (1 - core) * CHUNKS + jnp.arange(CHUNKS)]
    ).astype(jnp.int32)
    v = types.SimpleNamespace(
        residual=[None] * CHUNKS,
        normed=[None] * (2 * CHUNKS),
        back=[None] * CHUNKS,
        back_across=[None] * CHUNKS,
        residual_grad=[None] * CHUNKS,
        branch=[None] * CHUNKS,
        branch_sib=[None] * CHUNKS,
        gain_mlp=[None] * CHUNKS,
        gain_attn=[None] * CHUNKS,
        grad_rows=[None] * CHUNKS,
        grad_sib=[None] * CHUNKS,
        quarters={0: my_quarter},
        out_grads=(),
    )
    def heads_out():
        sib, v.mine, v.heads_placed = heads_project(
            place, heads, [w_out], nn, True, after=[cot_pair]
        )
        v.sib = mp_swap(sib, 1)

    def out_sum():
        v.parts = row_sum(v.mine, v.sib, CHUNKS)
        v.across = [mp_swap(part, 2) for part in v.parts]

    def swap_weights():
        v.down_sib, v.gate_sib, v.up_sib = [mp_swap(half, 1) for half in hold(halves)]

    def dact_own():
        v.dact = hidden_upstream(place, cot_all, w_down, True)

    def dact_sib():
        v.dact_sib = hidden_upstream(place, cot_all, v.down_sib, False)

    def norm_chunk(i):
        v.residual[i], v.normed[i] = norm_rows(
            v.parts[i], v.across[i], x_chunks[i], gain_mlp_row
        )
        v.normed[CHUNKS + i] = seq_swap(v.normed[i], pair)

    def turn_cot():
        v.cot_turned = turn(order, group, cot_all)

    def swap_cot():
        (turned,) = hold([v.cot_turned])
        v.cot_both = [turned, mp_swap(turned, 1)]

    def hidden_sib():
        v.act_sib, dg_sib, du_sib = hidden(
            place, v.normed, v.gate_sib, v.up_sib, v.dact_sib, False
        )
        v.act_got = mp_swap(v.act_sib, 1)
        v.dg_sib, v.du_sib = dg_sib, du_sib

    def swap_dg():
        (part,) = hold([v.dg_sib])
        v.dg_got = mp_swap(part, 1)

    def swap_du():
        (part,) = hold([v.du_sib])
        v.du_got = mp_swap(part, 1)

    def hidden_own():
        v.act, v.dg, v.du = hidden(place, v.normed, w_gate, w_up, v.dact, True)

    def turn_normed():
        v.normed_turned = turn(order, group, v.normed)

    def swap_normed():
        (turned,) = hold([v.normed_turned])
        v.normed_both = [turned, mp_swap(turned, 1)]

    def grad_down():
        v.sent_down, v.part_down = weight_grad(v.cot_both, [v.act, v.act_got])

    def send_down():
        (sent,) = hold([v.sent_down])
        v.low_down = low_sums(sent, v.part_down)

    def hidden_in():
        v.made = hidden_back(
            place,
            v.dg,
            v.dg_sib,
            v.du,
            v.du_sib,
            w_gate,
            v.gate_sib,
            w_up,
            v.up_sib,
            2 * CHUNKS,
        )
        v.made_got = [seq_swap(v.made[CHUNKS + i], pair) for i in range(CHUNKS)]

    def back_chunk(i):
        (v.back[i],) = row_sum(v.made[i], v.made_got[i], 1)
        v.back_across[i] = mp_swap(v.back[i], 2)

    def norm_back_chunk(i):
        v.residual_grad[i], v.branch[i], v.gain_mlp[i] = norm_back(
            v.back[i], v.back_across[i], v.residual[i], cot_chunks[i], gain_mlp_row, (F32, BF16)
        )
        v.branch_sib[i] = mp_swap(v.branch[i], 1)

    def grad_gate():
        v.sent_gate, v.part_gate = weight_grad(v.normed_both, [v.dg, v.dg_got])

    def send_gate():
        (sent,) = hold([v.sent_gate])
        v.low_gate = low_sums(sent, v.part_gate)

    def grad_up():
        v.sent_up, v.part_up = weight_grad(v.normed_both, [v.du, v.du_got])

    def send_up():
        (sent,) = hold([v.sent_up])
        v.low_up = low_sums(sent, v.part_up)

    def merge_down():
        v.kept_down, v.high_down = merge(*v.low_down)

    def high_down():
        (sent,) = hold([v.high_down], after=v.out_grads)
        v.come_down = seq_swap(sent, high)

    def merge_gate():
        v.kept_gate, v.high_gate = merge(*v.low_gate)

    def high_gate():
        (sent,) = hold([v.high_gate])
        v.come_gate = seq_swap(sent, high)

    def merge_up():
        v.kept_up, v.high_up = merge(*v.low_up)

    def high_up():
        (sent,) = hold([v.high_up])
        v.come_up = seq_swap(sent, high)

    def sum_down():
        v.own_down, v.pair_down = final_sum([v.kept_down, v.come_down])

    def sum_gate():
        v.own_gate, v.pair_gate = final_sum([v.kept_gate, v.come_gate])

    def sum_up():
        v.own_up, v.pair_up = final_sum([v.kept_up, v.come_up])

    def pair_down():
        (sent,) = hold([v.pair_down])
        v.theirs_down = seq_swap(sent, pair)

    def pair_gate():
        (sent,) = hold([v.pair_gate])
        v.theirs_gate = seq_swap(sent, pair)

    def pair_up():
        (sent,) = hold([v.pair_up])
        v.theirs_up = seq_swap(sent, pair)

    def lay_down():
        v.down_share = lay(place, v.own_down, v.theirs_down, True)

    def lay_gate():
        v.gate_share = lay(place, v.own_gate, v.theirs_gate, False)

    def lay_up():
        v.up_share = lay(place, v.own_up, v.theirs_up, False)

    def gather_z(d):
        (part,) = hold([v.quarters[d & (d - 1)]])
        v.quarters[d] = seq_swap(part, ring * (d & -d))

    def gather_x():
        v.rows = stack_rows([v.quarters[d] for d in range(1, nz)])
        v.rows_x = mp_swap(v.rows, 2)

    def gather_core():
        v.rows_core = [mp_swap(part, 1) for part in hold([v.rows, v.rows_x])]

    def heads_in():
        made = heads_upstream(place, v.branch, v.branch_sib, w_out, nz)
        v.out_grads = [made[0]] + [seq_swap(made[d], d * ring) for d in range(1, nz)]

    def attend_far():
        v.dq_far, *summed = attend_back(
            place, doc_ends, queries, v.out_grads, far, None, nz, ring, 1, ring - 1, BF16
        )
        summed = [None] + summed
        for b in reversed(range(low_bits)):
            bit = 1 << b
            for e in range(bit):
                got = seq_swap(summed[e | bit], bit)
                summed[e] = (
                    got
                    if summed[e] is None
                    else (summed[e].astype(F32) + got.astype(F32)).astype(BF16)
                )
        v.dkv_got = summed[0]

    def attend_near():
        v.dq, v.dkv = attend_back(
            place, doc_ends, queries, v.out_grads, near, v.dq_far, nz, ring, 0, 1, F32
        )

    def head_grads():
        v.grads = finish_grads(v.dq, v.dkv, v.dkv_got, cos_all, sin_all)
        v.own_grads = [v.grads[0]] + [
            seq_swap(v.grads[d], d * ring) for d in range(1, nz)
        ]

    def turn_branch():
        v.branch_turned = turn(order, group, v.branch + v.branch_sib, spots)

    def grad_out():
        v.sent_out, v.part_out = weight_grad([v.branch_turned], [v.heads_placed])

    def send_out():
        (sent,) = hold([v.sent_out])
        v.low_out = low_sums(sent, v.part_out)

    def merge_out():
        v.kept_out, v.high_out = merge(*v.low_out)

    def high_out():
        (sent,) = hold([v.high_out])
        v.come_out = seq_swap(sent, high)

    def sum_out():
        v.own_out, sent = final_sum([v.kept_out, v.come_out])
        v.pair_out = seq_swap(sent, pair)

    def turn_rows():
        v.all_turned = turn_all(
            order, group, normed, [v.rows, v.rows_core[0], v.rows_x, v.rows_core[1]], m
        )

    def grad_qkv():
        v.sent_qkv, v.part_qkv = weight_grad(
            [v.all_turned], [jnp.concatenate(v.grads, axis=0)]
        )

    def send_qkv():
        (sent,) = hold([v.sent_qkv])
        v.low_qkv = low_sums(sent, v.part_qkv)

    def split_qkv():
        own, *sent = split_sum(*v.low_qkv, nz)
        v.qkv_heads = [own] + [seq_swap(sent[d - 1], d * ring) for d in range(1, nz)]

    def lay_qkv():
        v.shares = place_heads(place, v.qkv_heads)

    def rows_in():
        sib, v.in_mine = heads_project(place, v.own_grads, weights, nt, False)
        v.in_sib = mp_swap(sib, 1)

    def in_sum():
        v.in_parts = row_sum(v.in_mine, v.in_sib, CHUNKS)
        v.in_across = [mp_swap(part, 2) for part in v.in_parts]

    def norm_in_chunk(i):
        v.grad_rows[i], v.gain_attn[i] = norm_back(
            v.in_parts[i], v.in_across[i], x_chunks[i], v.residual_grad[i], gain_attn_row, (BF16,)
        )
        v.grad_sib[i] = mp_swap(v.grad_rows[i], 1)

    def join_in():
        v.input_grad = join_rows(place, v.grad_rows, v.grad_sib)

    def down_rows():
        v.down_mine, v.down_theirs = down(place, v.act, v.act_sib, w_down, v.down_sib, 2)

    def pair_rows():
        (sent,) = hold([v.down_theirs])
        v.down_got = seq_swap(sent, pair)

    def sum_rows():
        (v.down_part,) = row_sum(v.down_mine, v.down_got, 1)
        v.down_across = mp_swap(v.down_part, 2)

    def add_out():
        v.out_rows = add_rows(
            v.down_part, v.down_across, jnp.concatenate(v.residual, axis=0)
        )
        v.out_sib = mp_swap(v.out_rows, 1)

    def join_out():
        v.mixed_out = join_rows(place, [v.out_rows], [v.out_sib])

    def gains_core():
        (v.gains,) = hold([jnp.concatenate([sum(v.gain_attn), sum(v.gain_mlp)])])
        v.gains = v.gains + mp_swap(v.gains, 1)

    def gains_seq(bit):
        (v.gains,) = hold([v.gains])
        v.gains = v.gains + seq_swap(v.gains, 1 << bit)

    loose(heads_out)
    gather_z(1)
    out_sum()
    swap_weights()
    dact_own()
    norm_chunk(1)
    dact_sib()
    norm_chunk(0)
    turn_cot()
    swap_cot()
    gather_z(2)
    hidden_sib()
    swap_dg()
    hidden_own()
    swap_du()
    turn_normed()
    swap_normed()
    grad_down()
    hidden_in()
    send_down()
    grad_gate()
    gather_z(3)
    back_chunk(1)
    back_chunk(0)
    send_gate()
    gather_x()
    norm_back_chunk(1)
    norm_back_chunk(0)
    heads_in()
    merge_down()
    turn_branch()
    high_down()
    attend_far()
    grad_up()
    send_up()
    gather_core()
    merge_gate()
    attend_near()
    high_gate()
    loose(sum_down)
    head_grads()
    pair_down()
    rows_in()
    merge_up()
    grad_out()
    loose(high_up)
    in_sum()
    down_rows()
    pair_rows()
    norm_in_chunk(0)
    send_out()
    turn_rows()
    lay_down()
    grad_qkv()
    merge_out()
    high_out()
    sum_gate()
    norm_in_chunk(1)
    send_qkv()
    gains_core()
    gains_seq(0)
    loose(pair_gate)
    sum_rows()
    join_in()
    gains_seq(2)
    split_qkv()
    sum_up()
    pair_up()
    sum_out()
    lay_gate()
    loose(add_out)
    lay_up()
    gains_seq(1)
    join_out()
    lay_qkv()
    for bit in range(3, bits):
        gains_seq(bit)
    gains = lax.dynamic_slice_in_dim(v.gains, s * group, group, 1)

    return (
        v.mixed_out,
        v.input_grad,
        *v.shares,
        (v.own_out + v.pair_out.astype(F32)).T,
        gains[0],
        v.gate_share,
        v.up_share,
        v.down_share,
        gains[1],
    )


def solution(mesh):
    placed = (
        P("seq", None),
        P(None, "mp"),
        P(None, "mp"),
        P(None, "mp"),
        P("mp", None),
        P(),
        P(None, "mp"),
        P(None, "mp"),
        P("mp", None),
        P(),
        P(),
        P("seq", None),
    )
    return jax.shard_map(
        functools.partial(layer, mesh.shape["seq"], mesh.shape["mp"]),
        mesh=mesh,
        in_specs=placed,
        out_specs=(
            P("seq", None),
            P("seq", None),
            P("seq", "mp"),
            P("seq", "mp"),
            P("seq", "mp"),
            P("mp", "seq"),
            P("seq"),
            P("seq", "mp"),
            P("seq", "mp"),
            P("mp", "seq"),
            P("seq"),
        ),
        check_vma=False,
    )
```
